32 devices in a mesh: rows: 8 (over y, x, core), mem: 4 (over z).
Axes of the slice: x: 2, y: 2, z: 4, core: 2. Of those that a mesh axis runs over, the one named last changes fastest.
Arguments:
- questions: bfloat16 [16, 1024, 768], P('rows', 'mem'), may hold values from -6 to 6
- answers: bfloat16 [16, 1024, 768], P('rows', 'mem'), may hold values from -6 to 6
- q_segments: int32 [16, 1024], P('rows'), may hold values from 0 to 7, never falling along the last dimension, each value on 1 to 769 neighbouring positions
- a_segments: int32 [16, 1024], P('rows'), may hold values from 0 to 7, never falling along the last dimension, each value on 1 to 769 neighbouring positions
- entry_ids: int32 [16, 8, 12], P('rows', None, 'mem'), may hold values from 0 to 4095
- entry_alive_flags: int32 [16, 8, 12], P('rows'), may hold values from 0 to 1, as said below
- memory_table: bfloat16 [4096, 2, 768], replicated, may hold values from -6 to 6
- enc_params: bfloat16 [768, 9216], P(None, ('rows', 'mem')), as said below
- dec_params: bfloat16 [768, 12288], P(None, ('rows', 'mem')), as said below
- norm_gains: float32 [6, 768], replicated, may hold values from 0.1 to 1.9
- cotangent: float32 [16, 1024, 768], P('rows', 'mem'), may hold values from -6 to 6
Outputs:
- decoded: bfloat16 [16, 1024, 768], P('rows', 'mem')
- grad_questions: float32 [16, 1024, 768], P('rows', 'mem')
- grad_answers: float32 [16, 1024, 768], P('rows', 'mem')
- grad_encoder: float32 [768, 9216], P(None, ('rows', 'mem'))
- grad_decoder: float32 [768, 12288], P(None, ('rows', 'mem'))
- grad_gains: float32 [6, 768], replicated
The draws below stay inside these ranges and needn't reach their ends.
Inputs may be any that keep to these rules, and one draw needn't show every extreme that they name: `entry_alive_flags`: each question has exactly 10 live slots of its 12. `enc_params`: entries lie within 9 / sqrt(768) in magnitude. `dec_params`: entries lie within 9 / sqrt(768) in magnitude.
All inputs are finite; a program needn't handle non-finite values.
Results may differ from the reference program's by a relative error of at most 0.025.
Values may be sent and summed in bfloat16 or wider, within the bound.
A program may use at most 384 MiB of HBM per device.

```python
import math
import jax
import jax.numpy as jnp
import numpy as np
from jax import lax

D = 768
H = 12
HD = 64
FF = 3072
LEN = 1024
QROW = 8
SLOTS = 12
TOPK = 10
ENTRIES = 4096
NROWS = 16
N_MEM = 4


def column_scales(pairs):
    return jnp.concatenate([jnp.full((width,), factor, jnp.float32) for width, factor in pairs])


def draw_enc_params(key, part):
    key = jax.random.fold_in(key, 1)
    root = D ** (-0.5)
    root_ff = FF ** (-0.5)
    scales = column_scales(((D, 1.5 * root), (D, root), (D, root), (D, 3.0 * root), (FF, root), (FF, 1.5 * root_ff)))
    base = jax.random.truncated_normal(key, -3.0, 3.0, (D, 4 * D + 2 * FF), jnp.float32)
    return (base * scales[None, :]).astype(jnp.bfloat16)


def draw_dec_params(key, part):
    key = jax.random.fold_in(key, 2)
    root = D ** (-0.5)
    root_ff = FF ** (-0.5)
    scales = column_scales(((D, 1.5 * root), (D, root), (D, root), (D, 3.0 * root), (D, 1.5 * root), (D, root), (D, root), (D, 3.0 * root), (FF, root), (FF, 1.5 * root_ff)))
    base = jax.random.truncated_normal(key, -3.0, 3.0, (D, 8 * D + 2 * FF), jnp.float32)
    return (base * scales[None, :]).astype(jnp.bfloat16)


def draw_entry_alive_flags(key, part):
    key = jax.random.fold_in(key, 3)
    scores = jax.random.randint(key, (NROWS, QROW, SLOTS), 0, 1 << 20) * SLOTS + jnp.arange(SLOTS, dtype=jnp.int32)
    ranks = jnp.argsort(jnp.argsort(scores, axis=-1), axis=-1)
    return (ranks >= SLOTS - TOPK).astype(jnp.int32)


def plant(array, stream_key, low, high):
    place = [jax.random.randint(jax.random.fold_in(stream_key, axis), (), 0, length) for axis, length in enumerate(array.shape)]
    longest = array.shape.index(max(array.shape))
    neighbour = place[:longest] + [(place[longest] + 1) % array.shape[longest]] + place[longest + 1:]
    return array.at[tuple(place)].set(low).at[tuple(neighbour)].set(high)


def level_of(key, shape, cuts, least, top_value):
    level = 1.0
    for axis_at, parts in cuts:
        draws = jax.random.uniform(jax.random.fold_in(jax.random.fold_in(key, 6), axis_at), (parts,), jnp.float32, least / len(cuts), top_value / len(cuts))
        level = level * jnp.repeat(jnp.exp(draws), shape[axis_at] // parts).reshape((-1,) + (1,) * (len(shape) - 1 - axis_at))
    return level


def length_profile(number_of, total, bound, skew):
    weights = [(1 << 20) // math.isqrt(grade ** skew) + 1 for grade in range(2, number_of + 1)]
    surplus, given = total - bound - (number_of - 1), [1] * (number_of - 1)
    while surplus > 0:
        candidates = [i for i in range(number_of - 1) if given[i] < bound]
        whole, budget = sum([weights[i] for i in candidates]), surplus
        for i in candidates:
            addition = min(bound - given[i], max(1, budget * weights[i] // whole), surplus)
            given[i] = given[i] + addition
            surplus = surplus - addition
    return np.array([bound] + given)


def uneven_parts(key, number_of, total, reach, skew):
    if number_of == 2:
        one = jax.random.randint(key, (), max(1, total - reach), min(reach, total - 1) + 1)
        return jnp.stack([one, total - one])
    sizes = jnp.asarray(length_profile(number_of, total, reach, skew), jnp.int32)
    pairs = (number_of - 1) // 2
    source_of, receiver = sizes[1:1 + 2 * pairs:2], sizes[2:2 + 2 * pairs:2]
    margin = jnp.minimum(source_of - 1, reach - receiver)
    shifted = jax.random.randint(jax.random.fold_in(key, 1), (pairs,), 0, 1 << 20) % (margin + 1)
    sizes = sizes.at[1:1 + 2 * pairs:2].set(source_of - shifted).at[2:2 + 2 * pairs:2].set(receiver + shifted)
    return sizes[jax.random.permutation(jax.random.fold_in(key, 2), number_of)]


def centred(stream_key, extent, spread, most, pieces=(), kind=jnp.bfloat16):
    level = level_of(stream_key, extent, pieces, -0.22, 0.18) if pieces else 1.0
    values = jax.random.normal(stream_key, extent, jnp.float32) * spread * level
    return jnp.minimum(jnp.maximum(values, -most), most).astype(kind)


def setup_inputs(seed: int = 0) -> dict:
    key_of = jax.random.split(jax.random.key(seed), 12)
    return {
        "questions": centred(key_of[0], (NROWS, LEN, D), 1.0, 6.0, ((0, 8), (1, 4))),
        "answers": centred(key_of[1], (NROWS, LEN, D), 1.0, 6.0, ((0, 8), (1, 4))),
        "q_segments": jax.vmap(lambda own: jnp.searchsorted(jnp.cumsum(uneven_parts(own, QROW, LEN, LEN - LEN // N_MEM + 1, 0)), jnp.arange(LEN), side="right"))(jax.random.split(key_of[2], NROWS)).reshape((NROWS, LEN)).astype(jnp.int32),
        "a_segments": jax.vmap(lambda own: jnp.searchsorted(jnp.cumsum(uneven_parts(own, QROW, LEN, LEN - LEN // N_MEM + 1, 0)), jnp.arange(LEN), side="right"))(jax.random.split(key_of[3], NROWS)).reshape((NROWS, LEN)).astype(jnp.int32),
        "entry_ids": plant(jax.random.randint(key_of[4], (NROWS, QROW, SLOTS), 0, ENTRIES), jax.random.fold_in(key_of[4], 1), 0, ENTRIES - 1).astype(jnp.int32),
        "entry_alive_flags": draw_entry_alive_flags(jax.random.fold_in(key_of[11], 71), 0),
        "memory_table": centred(key_of[6], (ENTRIES, 2, D), 1.0, 6.0),
        "enc_params": draw_enc_params(jax.random.fold_in(key_of[11], 71), 0),
        "dec_params": draw_dec_params(jax.random.fold_in(key_of[11], 71), 0),
        "norm_gains": jnp.clip(1.0 + 0.18 * jax.random.normal(key_of[9], (6, D), jnp.float32), 0.1, 1.9),
        "cotangent": centred(key_of[10], (NROWS, LEN, D), 1.0, 6.0, ((0, 8), (1, 4)), jnp.float32),
    }


epsilon = 1e-06
masked_score = -1e+30

@jax.custom_vjp
def low(v):
    return lax.optimization_barrier(v.astype(jnp.bfloat16)).astype(jnp.float32)

@jax.custom_vjp
def low_back(v):
    return v

def low_keep(v):
    return (low(v), None)

def low_pass(kept, grad):
    return (grad,)

def back_keep(v):
    return (v, None)

def backward_lowered(kept, grad):
    return (low(grad),)
low.defvjp(low_keep, low_pass)
low_back.defvjp(back_keep, backward_lowered)

def rms_norm(values, gain):
    return values * lax.rsqrt(lax.optimization_barrier(jnp.mean(values * values, -1, keepdims=True)) + epsilon) * gain

def matmul(left, weight):
    return jnp.dot(left, weight, precision=lax.Precision.HIGHEST)

def matmul_t(left, weight):
    return jnp.dot(left, weight.T, precision=lax.Precision.HIGHEST)

def projected(left, weight):
    return low(low_back(matmul(left, weight)))

def attention(queries, keys, values, mask):
    count_q = queries.shape[0]
    count_k = keys.shape[0]
    heads_q = queries.reshape(count_q, H, HD)
    heads_k = keys.reshape(count_k, H, HD)
    heads_v = values.reshape(count_k, H, HD)
    scores = jnp.einsum('qhd,khd->hqk', heads_q, heads_k, precision=lax.Precision.HIGHEST) * HD ** (-0.5)
    scores = low_back(scores)
    scores = jnp.where(mask[None], scores, masked_score)
    probs = low(jax.nn.softmax(scores, axis=-1))
    mixed = jnp.einsum('hqk,khd->qhd', probs, heads_v, precision=lax.Precision.HIGHEST).reshape(count_q, D)
    return low(low_back(mixed))

def feed_forward(values, gain, w_in, w_out):
    normed = low(rms_norm(values, gain))
    hidden = low(jax.nn.gelu(low_back(matmul(normed, w_in))))
    return low_back(matmul_t(hidden, w_out))

def layer_pair(x_question, x_answer, q_seg, a_seg, ids, live, table, enc_w, dec_w, gains):
    positions = jnp.arange(LEN).astype(jnp.int32)
    normed = low(rms_norm(x_question, gains[0]))
    query_e = projected(normed, enc_w[:, :D])
    key_e = projected(normed, enc_w[:, D:2 * D])
    value_e = projected(normed, enc_w[:, 2 * D:3 * D])
    entries = table[ids].reshape(QROW * SLOTS * 2, D)
    prefix_n = low(rms_norm(entries, gains[0]))
    prefix_k = projected(prefix_n, enc_w[:, D:2 * D])
    prefix_v = projected(prefix_n, enc_w[:, 2 * D:3 * D])
    index = jnp.arange(QROW * SLOTS * 2).astype(jnp.int32)
    question = index // (SLOTS * 2)
    slot = index // 2 % SLOTS
    prefix_mask = (q_seg[:, None] == question[None, :]) & (live[question, slot] == 1)[None, :]
    enc_mask = jnp.concatenate([q_seg[:, None] == q_seg[None, :], prefix_mask], 1)
    mixed = attention(query_e, jnp.concatenate([key_e, prefix_k], 0), jnp.concatenate([value_e, prefix_v], 0), enc_mask)
    hidden_one = x_question + low_back(matmul_t(mixed, enc_w[:, 3 * D:4 * D]))
    hidden_two = hidden_one + feed_forward(hidden_one, gains[1], enc_w[:, 4 * D:4 * D + FF], enc_w[:, 4 * D + FF:])
    encoded = low(rms_norm(hidden_two, gains[5]))
    normed_a = low(rms_norm(x_answer, gains[2]))
    query_s = projected(normed_a, dec_w[:, :D])
    key_s = projected(normed_a, dec_w[:, D:2 * D])
    value_s = projected(normed_a, dec_w[:, 2 * D:3 * D])
    self_mask = (a_seg[:, None] == a_seg[None, :]) & (positions[None, :] <= positions[:, None])
    mixed_s = attention(query_s, key_s, value_s, self_mask)
    dec_one = x_answer + low_back(matmul_t(mixed_s, dec_w[:, 3 * D:4 * D]))
    normed_c = low(rms_norm(dec_one, gains[3]))
    query_c = projected(normed_c, dec_w[:, 4 * D:5 * D])
    key_c = projected(encoded, dec_w[:, 5 * D:6 * D])
    value_c = projected(encoded, dec_w[:, 6 * D:7 * D])
    cross_mask = a_seg[:, None] == q_seg[None, :]
    mixed_c = attention(query_c, key_c, value_c, cross_mask)
    dec_two = dec_one + low_back(matmul_t(mixed_c, dec_w[:, 7 * D:8 * D]))
    return dec_two + feed_forward(dec_two, gains[4], dec_w[:, 8 * D:8 * D + FF], dec_w[:, 8 * D + FF:])

def reference(questions, answers, q_segments, a_segments, entry_ids, entry_alive_flags, memory_table, enc_params, dec_params, norm_gains, cotangent):
    table_full = memory_table.astype(jnp.float32)

    def forward(x_question, x_answer, enc_w, dec_w, gains):

        def one_row(items):
            return layer_pair(items[0], items[1], items[2], items[3], items[4], items[5], table_full, enc_w, dec_w, gains)
        return lax.map(jax.checkpoint(one_row), (x_question, x_answer, q_segments, a_segments, entry_ids, entry_alive_flags))
    result, pull = jax.vjp(forward, questions.astype(jnp.float32), answers.astype(jnp.float32), enc_params.astype(jnp.float32), dec_params.astype(jnp.float32), norm_gains)
    grad_q, grad_a, grad_e, grad_d, grad_g = pull(cotangent)
    return (result.astype(jnp.bfloat16), grad_q, grad_a, grad_e, grad_d, grad_g)
```

```python
import functools
import jax
import jax.numpy as jnp
from jax import lax
from jax.experimental import pallas as pl
from jax.experimental.pallas import tpu as pltpu
from jax.sharding import PartitionSpec as P

D = 768
H = 12
HD = 64
FF = 3072
QB = 256
masked_score = -1e30


def key_chunks(own_len, extra):
    chunks = []
    for side in (0, 1):
        for at in range(own_len // QB):
            chunks.append((side, at * QB, QB))
        if extra:
            chunks.append((side, own_len, extra))
    return chunks


def attend_kernel(causal, own_len, extra, act, q_ref, qaug_ref, own_k, own_v, oth_k, oth_v, kaug_ref, o_ref, lse_ref, s_ref, m_ref, l_ref, acc_ref):
    low = lax.broadcasted_iota(jnp.int32, (1, 128), 1) < HD
    chunks = key_chunks(own_len, extra)
    nk = own_len + extra
    for qb in range(own_len // QB):
        rows = pl.ds(qb * QB, QB)
        q = q_ref[rows, :] * jnp.bfloat16(HD ** (-0.5))
        qaug = qaug_ref[rows, :]
        queries = (jnp.where(low, q, qaug), jnp.where(low, qaug, q))
        m_ref[...] = jnp.full(m_ref.shape, -3e30, jnp.float32)
        l_ref[...] = jnp.zeros(l_ref.shape, jnp.float32)
        acc_ref[...] = jnp.zeros(acc_ref.shape, jnp.float32)
        for ci, (side, at, size) in enumerate(chunks):

            def score(side=side, at=at, size=size):
                k = (own_k, oth_k)[side][at : at + size, :]
                place = slice(side * nk + at, side * nk + at + size)
                kaug = kaug_ref[place, :]
                for h in (0, 1):
                    cols = slice(h * QB, (h + 1) * QB)
                    keys = jnp.where(low, k, kaug) if h == 0 else jnp.where(low, kaug, k)
                    s = lax.dot_general(keys, queries[h], (((1,), (1,)), ((), ())), preferred_element_type=jnp.float32)
                    if causal and side == 0 and at == qb * QB:
                        tri = lax.broadcasted_iota(jnp.int32, (size, QB), 0) <= lax.broadcasted_iota(jnp.int32, (size, QB), 1)
                        s = jnp.where(tri, s, masked_score)
                    s_ref[place, cols] = s
                    m_ref[:, cols] = jnp.maximum(m_ref[:, cols], jnp.max(s.reshape(size // 8, 8, QB), 0))

            pl.when(act[qb, ci] != 0)(score)
        m = jnp.max(m_ref[...], 0, keepdims=True)
        for ci, (side, at, size) in enumerate(chunks):

            def mix(side=side, at=at, size=size):
                v = (own_v, oth_v)[side][at : at + size, :]
                zero = jnp.zeros_like(v)
                place = slice(side * nk + at, side * nk + at + size)
                p = jnp.exp(s_ref[place, :] - m)
                l_ref[...] += jnp.sum(p.reshape(size // 8, 8, 2 * QB), 0)
                pb = p.astype(jnp.bfloat16)
                pb = jnp.concatenate([pb[:, :QB], pb[:, QB:]], 0)
                v_split = jnp.concatenate([jnp.where(low, v, zero), jnp.where(low, zero, v)], 0)
                acc_ref[...] += lax.dot_general(pb, v_split, (((0,), (0,)), ((), ())), preferred_element_type=jnp.float32)

            pl.when(act[qb, ci] != 0)(mix)
        total = jnp.sum(l_ref[...], 0, keepdims=True)
        lse = m + jnp.log(total)
        rec = 1.0 / total
        wide = lambda row, h: jnp.broadcast_to(row[:, h * QB : (h + 1) * QB], (HD, QB))
        o_ref[rows, :] = (acc_ref[...] * jnp.concatenate([wide(rec, 0), wide(rec, 1)], 0).T).astype(jnp.bfloat16)
        lse_ref[rows, :] = jnp.concatenate([wide(lse, 1), wide(lse, 0)], 0).T


def attend(causal, act, q, qaug, own_kv, oth_kv, kaug):
    t = q.shape[0]
    nk = own_kv.shape[0]
    col = lambda first: pl.BlockSpec((nk, 128), lambda i, a: (0, first + i))
    return pl.pallas_call(
        functools.partial(attend_kernel, causal, t, nk - t),
        grid_spec=pltpu.PrefetchScalarGridSpec(
            num_scalar_prefetch=1,
            grid=(H // 2,),
            in_specs=[
                pl.BlockSpec((t, 128), lambda i, a: (0, i)),
                pl.BlockSpec((t, 128), lambda i, a: (0, 0)),
                col(0), col(H // 2), col(0), col(H // 2),
                pl.BlockSpec((2 * nk, 128), lambda i, a: (0, 0)),
            ],
            out_specs=[pl.BlockSpec((t, 128), lambda i, a: (0, i))] * 2,
            scratch_shapes=[pltpu.VMEM((2 * nk, 2 * QB), jnp.float32), pltpu.VMEM((8, 2 * QB), jnp.float32), pltpu.VMEM((8, 2 * QB), jnp.float32), pltpu.VMEM((QB, 128), jnp.float32)],
        ),
        out_shape=[jax.ShapeDtypeStruct((t, D), jnp.bfloat16), jax.ShapeDtypeStruct((t, D), jnp.float32)],
        compiler_params=pltpu.CompilerParams(vmem_limit_bytes=40 * 1024 * 1024),
        cost_estimate=pl.CostEstimate(flops=4 * t * 2 * nk * D, bytes_accessed=8 * nk * D, transcendentals=t * 2 * nk * H),
        name="attend",
    )(act, q, qaug, own_kv, own_kv, oth_kv, oth_kv, kaug)


def three_parts(value):
    hi = value.astype(jnp.bfloat16).astype(jnp.float32)
    mid = (value - hi).astype(jnp.bfloat16).astype(jnp.float32)
    return hi, mid, value - hi - mid


def spread(base, lane64, value):
    hi, mid, lo = three_parts(value)
    return jnp.where(lane64 == 8, hi, jnp.where(lane64 == 9, mid, jnp.where(lane64 == 10, lo, base)))


def back_kernel(causal, own_len, extra, act, q_ref, qaug_ref, own_k, own_v, oth_k, oth_v, kaug_ref, o_ref, lse_ref, g_ref, dq_ref, dko_ref, dvo_ref, dkt_ref, dvt_ref, dk_acc, dv_acc, dq_acc):
    lane = lax.broadcasted_iota(jnp.int32, (1, 128), 1)
    low = lane < HD
    lane64 = lane % HD
    chunks = key_chunks(own_len, extra)
    nk = own_len + extra
    dk_acc[...] = jnp.zeros(dk_acc.shape, jnp.float32)
    dv_acc[...] = jnp.zeros(dv_acc.shape, jnp.float32)
    ones_aug = jnp.where((lane64 >= 8) & (lane64 <= 10), 1.0, 0.0).astype(jnp.bfloat16)
    for qb in range(own_len // QB):
        rows = pl.ds(qb * QB, QB)
        q = q_ref[rows, :] * jnp.bfloat16(HD ** (-0.5))
        g = g_ref[rows, :]
        qaug = spread(qaug_ref[rows, :].astype(jnp.float32), lane64, -lse_ref[rows, :]).astype(jnp.bfloat16)
        prod = g.astype(jnp.float32) * o_ref[rows, :].astype(jnp.float32)
        d_even = jnp.sum(jnp.where(low, prod, 0.0), -1, keepdims=True)
        d_odd = jnp.sum(jnp.where(low, 0.0, prod), -1, keepdims=True)
        gaug = spread(jnp.zeros((QB, 128), jnp.float32), lane64, -jnp.where(low, d_odd, d_even)).astype(jnp.bfloat16)
        queries = (jnp.where(low, q, qaug), jnp.where(low, qaug, q))
        grads = (jnp.where(low, g, gaug), jnp.where(low, gaug, g))
        zero = jnp.zeros_like(q)
        q_split = jnp.concatenate([jnp.where(low, q, zero), jnp.where(low, zero, q)], 0)
        g_split = jnp.concatenate([jnp.where(low, g, zero), jnp.where(low, zero, g)], 0)
        dq_acc[...] = jnp.zeros(dq_acc.shape, jnp.float32)
        for ci, (side, at, size) in enumerate(chunks):

            def work(side=side, at=at, size=size):
                k = (own_k, oth_k)[side][at : at + size, :]
                v = (own_v, oth_v)[side][at : at + size, :]
                place = slice(side * nk + at, side * nk + at + size)
                kaug = kaug_ref[place, :]
                vaug = jnp.broadcast_to(ones_aug, v.shape)
                zk = jnp.zeros_like(k)
                probs, dscores = [], []
                for h in (0, 1):
                    keys = jnp.where(low, k, kaug) if h == 0 else jnp.where(low, kaug, k)
                    vals = jnp.where(low, v, vaug) if h == 0 else jnp.where(low, vaug, v)
                    s = lax.dot_general(keys, queries[h], (((1,), (1,)), ((), ())), preferred_element_type=jnp.float32)
                    if causal and side == 0 and at == qb * QB:
                        tri = lax.broadcasted_iota(jnp.int32, (size, QB), 0) <= lax.broadcasted_iota(jnp.int32, (size, QB), 1)
                        s = jnp.where(tri, s, masked_score)
                    p = jnp.exp(s)
                    dp = lax.dot_general(vals, grads[h], (((1,), (1,)), ((), ())), preferred_element_type=jnp.float32)
                    dscores.append((p * dp).astype(jnp.bfloat16))
                    probs.append(p.astype(jnp.bfloat16))
                ds = jnp.concatenate(dscores, 1)
                pb = jnp.concatenate(probs, 1)
                dk_acc[place, :] += jnp.dot(ds, q_split, preferred_element_type=jnp.float32)
                dv_acc[place, :] += jnp.dot(pb, g_split, preferred_element_type=jnp.float32)
                k_split = jnp.concatenate([jnp.where(low, k, zk), jnp.where(low, zk, k)], 0)
                dst = jnp.concatenate(dscores, 0)
                dq_acc[...] += lax.dot_general(dst, k_split, (((0,), (0,)), ((), ())), preferred_element_type=jnp.float32)

            pl.when(act[qb, ci] != 0)(work)
        dq_ref[rows, :] = (dq_acc[...] * HD ** (-0.5)).astype(jnp.bfloat16)
    dko_ref[...] = dk_acc[:nk, :]
    dvo_ref[...] = dv_acc[:nk, :]
    dkt_ref[...] = dk_acc[nk:, :].astype(jnp.bfloat16)
    dvt_ref[...] = dv_acc[nk:, :].astype(jnp.bfloat16)


def attend_back(causal, act, q, qaug, own_kv, oth_kv, kaug, mixed, lse, grad):
    t = q.shape[0]
    nk = own_kv.shape[0]
    col = lambda first: pl.BlockSpec((nk, 128), lambda i, a: (0, first + i))
    tok = pl.BlockSpec((t, 128), lambda i, a: (0, i))
    return pl.pallas_call(
        functools.partial(back_kernel, causal, t, nk - t),
        grid_spec=pltpu.PrefetchScalarGridSpec(
            num_scalar_prefetch=1,
            grid=(H // 2,),
            in_specs=[
                tok,
                pl.BlockSpec((t, 128), lambda i, a: (0, 0)),
                col(0), col(H // 2), col(0), col(H // 2),
                pl.BlockSpec((2 * nk, 128), lambda i, a: (0, 0)),
                tok, tok, tok,
            ],
            out_specs=[tok, col(0), col(0), col(0), col(0)],
            scratch_shapes=[pltpu.VMEM((2 * nk, 128), jnp.float32), pltpu.VMEM((2 * nk, 128), jnp.float32), pltpu.VMEM((QB, 128), jnp.float32)],
        ),
        out_shape=[
            jax.ShapeDtypeStruct((t, D), jnp.bfloat16),
            jax.ShapeDtypeStruct((nk, D), jnp.float32),
            jax.ShapeDtypeStruct((nk, D), jnp.float32),
            jax.ShapeDtypeStruct((nk, D), jnp.bfloat16),
            jax.ShapeDtypeStruct((nk, D), jnp.bfloat16),
        ],
        compiler_params=pltpu.CompilerParams(vmem_limit_bytes=40 * 1024 * 1024),
        cost_estimate=pl.CostEstimate(flops=10 * t * 2 * nk * D, bytes_accessed=24 * nk * D, transcendentals=t * 2 * nk * H),
        name="attend_back",
    )(act, q, qaug, own_kv, own_kv, oth_kv, oth_kv, kaug, mixed, lse, grad)


def seg_aug_q(seg):
    j = jnp.arange(128, dtype=jnp.int32) % HD
    return ((j[None, :] < 8) & (j[None, :] == seg[:, None])).astype(jnp.bfloat16)


def seg_aug_k(seg):
    j = jnp.arange(128, dtype=jnp.int32)[None, :] % HD
    bad = (j < 8) & (j != seg[:, None])
    return jnp.where(bad, masked_score, jnp.where((j >= 8) & (j <= 10), 1.0, 0.0)).astype(jnp.bfloat16)


epsilon = 1e-06


def rms_norm(values, gain):
    return values * lax.rsqrt(jnp.mean(values * values, -1, keepdims=True) + epsilon) * gain


def norm_back(values, gain, grad):
    unused, pull = jax.vjp(rms_norm, values, gain)
    return pull(grad)


def project(left, weight_t):
    return jnp.einsum("nd,ed->ne", left, weight_t, preferred_element_type=jnp.float32)


def project_back(left, weight_t):
    return jnp.einsum("ne,ed->nd", left, weight_t, preferred_element_type=jnp.float32)


def outer_sum(wide, narrow):
    return jnp.einsum("ne,nd->ed", wide, narrow, preferred_element_type=jnp.float32).astype(jnp.bfloat16)


def output_back(grad, mixed_b, w_out):
    grad_b = grad.astype(jnp.bfloat16)
    return (outer_sum(mixed_b, grad_b), project(grad_b, w_out).astype(jnp.bfloat16))


def feed_back(grad, normed_b, pre_act, act_b, w_in, w_out):
    grad_b = grad.astype(jnp.bfloat16)
    grad_wout = outer_sum(act_b, grad_b)
    grad_act = project(grad_b, w_out)
    unused, pull = jax.vjp(jax.nn.gelu, pre_act)
    grad_pre = pull(grad_act)[0].astype(jnp.bfloat16)
    return (outer_sum(grad_pre, normed_b), grad_wout, project_back(grad_pre, w_in))


def partner(values):
    n_rows = lax.axis_size("rows")
    return lax.ppermute(values, "rows", [(i, i ^ 1) for i in range(n_rows)])


def my_row(values):
    core = lax.axis_index("rows") % 2
    mem = lax.axis_index("mem")
    chosen = jnp.where(mem // 2 == core, values, partner(values))
    return lax.dynamic_index_in_dim(chosen, mem % 2, 0, keepdims=False)


def quarters_of(core):
    return (jnp.where(core == 0, 0, 1), jnp.where(core == 0, 3, 2))


def own_quarters(row, core, quarter):
    return jnp.concatenate(
        [lax.dynamic_slice_in_dim(row, place * quarter, quarter, 0) for place in quarters_of(core)], 0
    )


def to_rows(values):
    quarter = values.shape[1]
    row = my_row(lax.all_gather(values, "mem", axis=1, tiled=True))
    return own_quarters(row, lax.axis_index("rows") % 2, quarter)


def from_rows(values):
    quarter = values.shape[0] // 2
    core = lax.axis_index("rows") % 2
    mem = lax.axis_index("mem")
    gathered = lax.all_gather(values, "mem", axis=0)
    other = partner(gathered)
    holder = jnp.where((mem == 0) | (mem == 3), 0, 1)
    chosen = jnp.where(holder == core, gathered, other)
    return lax.dynamic_slice(
        chosen, (2 * core, jnp.where(mem < 2, 0, quarter), 0), (2, quarter, values.shape[1])
    )


def gather_weights(params):
    return lax.all_gather(params.T, ("rows", "mem"), axis=0, tiled=True)


def reduce_weights(grads):
    return lax.psum_scatter(grads, ("rows", "mem"), scatter_dimension=0, tiled=True)


def flags_of(q_row, k_row, core, quarter, extra, causal):
    n = q_row.shape[0] // quarter
    ends_q = q_row.reshape(n, quarter)
    ends_k = k_row.reshape(n, quarter)
    meets = (ends_k[None, :, 0] <= ends_q[:, None, -1]) & (ends_q[:, None, 0] <= ends_k[None, :, -1])
    if causal:
        meets &= jnp.arange(n)[None, :] <= jnp.arange(n)[:, None]
    mine = jnp.stack(quarters_of(core))
    others = jnp.stack(quarters_of(1 - core))
    meets = meets[mine]
    always = [jnp.ones((2, 1), bool)] if extra else []
    return jnp.concatenate([meets[:, mine]] + always + [meets[:, others]] + always, 1).astype(jnp.int32)


def both_parts(own, other):
    return jnp.concatenate([own, other], 0)


def on_device(
    questions,
    answers,
    q_segments,
    a_segments,
    entry_ids,
    entry_alive_flags,
    memory_table,
    enc_params,
    dec_params,
    norm_gains,
    cotangent,
):
    quarter = questions.shape[1]
    core = lax.axis_index("rows") % 2
    per_row, slots = entry_alive_flags.shape[1], entry_alive_flags.shape[2]
    half = per_row // 2
    enc_w = gather_weights(enc_params)
    dec_w = gather_weights(dec_params)
    all_ids = lax.all_gather(entry_ids, "mem", axis=2, tiled=True)
    rows_here = questions.shape[0]
    numbers = my_row(
        jnp.concatenate(
            [
                q_segments,
                a_segments,
                entry_alive_flags.reshape(rows_here, -1),
                all_ids.reshape(rows_here, -1),
            ],
            1,
        )
    )
    row_len = q_segments.shape[1]
    q_row = numbers[:row_len]
    a_row = numbers[row_len : 2 * row_len]
    alive = numbers[2 * row_len : 2 * row_len + per_row * slots]
    ids = numbers[2 * row_len + per_row * slots :]
    x_question = to_rows(questions).astype(jnp.float32)
    x_answer = to_rows(answers).astype(jnp.float32)
    grad_top = to_rows(cotangent.astype(jnp.bfloat16)).astype(jnp.float32)

    own_ids = lax.dynamic_slice_in_dim(ids, core * half * slots, half * slots, 0)
    entry_vals = memory_table[own_ids].reshape(half * slots * 2, D).astype(jnp.float32)
    n_prefix = entry_vals.shape[0]
    extra = -(-n_prefix // 128) * 128
    place = jnp.arange(extra, dtype=jnp.int32)

    def prefix_segments(which):
        question = which * half + place // (2 * slots)
        live = lax.dynamic_slice_in_dim(alive, which * half * slots, half * slots, 0)
        live = jnp.pad(jnp.repeat(live, 2), (0, extra - n_prefix))
        return jnp.where(live == 1, question, -1)

    tokens = 2 * quarter
    own_q = own_quarters(q_row, core, quarter)
    other_q = own_quarters(q_row, 1 - core, quarter)
    own_a = own_quarters(a_row, core, quarter)
    other_a = own_quarters(a_row, 1 - core, quarter)
    q_aug, a_aug = seg_aug_q(own_q), seg_aug_q(own_a)
    enc_aug = seg_aug_k(
        jnp.concatenate([own_q, prefix_segments(core), other_q, prefix_segments(1 - core)])
    )
    self_aug = seg_aug_k(jnp.concatenate([own_a, other_a]))
    cross_aug = seg_aug_k(jnp.concatenate([own_q, other_q]))
    enc_act = flags_of(q_row, q_row, core, quarter, extra, False)
    self_act = flags_of(a_row, a_row, core, quarter, 0, True)
    cross_act = flags_of(a_row, q_row, core, quarter, 0, False)

    enc_in = jnp.concatenate([x_question, jnp.pad(entry_vals, ((0, extra - n_prefix), (0, 0)))], 0)
    normed_q = rms_norm(enc_in, norm_gains[0]).astype(jnp.bfloat16)
    query_enc = project(normed_q[:tokens], enc_w[:D]).astype(jnp.bfloat16)
    enc_kv = project(normed_q, enc_w[D : 3 * D]).astype(jnp.bfloat16)
    enc_kv_other = partner(enc_kv)

    normed_a = rms_norm(x_answer, norm_gains[2]).astype(jnp.bfloat16)
    qkv_self = project(normed_a, dec_w[: 3 * D]).astype(jnp.bfloat16)
    query_self, self_kv = qkv_self[:, :D], qkv_self[:, D:]
    self_kv_other = partner(self_kv)

    mixed_enc, logsum_enc = attend(False, enc_act, query_enc, q_aug, enc_kv, enc_kv_other, enc_aug)
    hidden_one = x_question + project_back(mixed_enc, enc_w[3 * D : 4 * D])
    normed_f1 = rms_norm(hidden_one, norm_gains[1]).astype(jnp.bfloat16)
    pre_enc = project(normed_f1, enc_w[4 * D : 4 * D + FF])
    act_enc = jax.nn.gelu(pre_enc).astype(jnp.bfloat16)
    hidden_two = hidden_one + project_back(act_enc, enc_w[4 * D + FF :])
    encoded = rms_norm(hidden_two, norm_gains[5]).astype(jnp.bfloat16)
    cross_kv = project(encoded, dec_w[5 * D : 7 * D]).astype(jnp.bfloat16)
    cross_kv_other = partner(cross_kv)

    mixed_self, logsum_self = attend(True, self_act, query_self, a_aug, self_kv, self_kv_other, self_aug)
    dec_one = x_answer + project_back(mixed_self, dec_w[3 * D : 4 * D])
    normed_c = rms_norm(dec_one, norm_gains[3]).astype(jnp.bfloat16)
    query_cross = project(normed_c, dec_w[4 * D : 5 * D]).astype(jnp.bfloat16)
    mixed_cross, logsum_cross = attend(
        False, cross_act, query_cross, a_aug, cross_kv, cross_kv_other, cross_aug
    )
    dec_two = dec_one + project_back(mixed_cross, dec_w[7 * D : 8 * D])
    normed_f2 = rms_norm(dec_two, norm_gains[4]).astype(jnp.bfloat16)
    pre_dec = project(normed_f2, dec_w[8 * D : 8 * D + FF])
    act_dec = jax.nn.gelu(pre_dec).astype(jnp.bfloat16)
    dec_three = dec_two + project_back(act_dec, dec_w[8 * D + FF :])
    decoded = from_rows(dec_three.astype(jnp.bfloat16))

    grad_w1d, grad_w2d, grad_nf2 = feed_back(
        grad_top, normed_f2, pre_dec, act_dec, dec_w[8 * D : 8 * D + FF], dec_w[8 * D + FF :]
    )
    grad_x, grad_gain4 = norm_back(dec_two, norm_gains[4], grad_nf2)
    grad_two = grad_top + grad_x
    grad_woc, grad_mixc = output_back(grad_two, mixed_cross, dec_w[7 * D : 8 * D])
    grad_qc, dk_own, dv_own, dk_other, dv_other = attend_back(
        False, cross_act, query_cross, a_aug, cross_kv, cross_kv_other, cross_aug,
        mixed_cross, logsum_cross, grad_mixc,
    )
    more = partner(jnp.concatenate([dk_other, dv_other], 1)).astype(jnp.float32)
    grad_ckv = (jnp.concatenate([dk_own, dv_own], 1) + more).astype(jnp.bfloat16)
    grad_wqc = outer_sum(grad_qc, normed_c)
    grad_x, grad_gain3 = norm_back(
        dec_one, norm_gains[3], project_back(grad_qc, dec_w[4 * D : 5 * D])
    )
    grad_one = grad_two + grad_x
    grad_wckv = outer_sum(grad_ckv, encoded)
    grad_encoded, grad_gain5 = norm_back(
        hidden_two, norm_gains[5], project_back(grad_ckv, dec_w[5 * D : 7 * D])
    )
    grad_wos, grad_mixs = output_back(grad_one, mixed_self, dec_w[3 * D : 4 * D])
    grad_qs, dk_own, dv_own, dk_other, dv_other = attend_back(
        True, self_act, query_self, a_aug, self_kv, self_kv_other, self_aug,
        mixed_self, logsum_self, grad_mixs,
    )
    more = partner(jnp.concatenate([dk_other, dv_other], 1)).astype(jnp.float32)
    grad_skv = (jnp.concatenate([dk_own, dv_own], 1) + more).astype(jnp.bfloat16)
    grad_self = jnp.concatenate([grad_qs, grad_skv], 1)
    grad_wself = outer_sum(grad_self, normed_a)
    grad_x, grad_gain2 = norm_back(x_answer, norm_gains[2], project_back(grad_self, dec_w[: 3 * D]))
    grad_answers = from_rows((grad_one + grad_x).astype(jnp.bfloat16)).astype(jnp.float32)
    dec_full = jnp.concatenate(
        [grad_wself, grad_wos, grad_wqc, grad_wckv, grad_woc, grad_w1d, grad_w2d], 0
    )
    grad_decoder = reduce_weights(dec_full).astype(jnp.float32).T

    grad_w1e, grad_w2e, grad_nf1 = feed_back(
        grad_encoded, normed_f1, pre_enc, act_enc, enc_w[4 * D : 4 * D + FF], enc_w[4 * D + FF :]
    )
    grad_x, grad_gain1 = norm_back(hidden_one, norm_gains[1], grad_nf1)
    grad_hidden = grad_encoded + grad_x
    grad_woe, grad_mixe = output_back(grad_hidden, mixed_enc, enc_w[3 * D : 4 * D])
    grad_qe, dk_own, dv_own, dk_other, dv_other = attend_back(
        False, enc_act, query_enc, q_aug, enc_kv, enc_kv_other, enc_aug,
        mixed_enc, logsum_enc, grad_mixe,
    )
    more = partner(jnp.concatenate([dk_other, dv_other], 1)).astype(jnp.float32)
    grad_ekv = (jnp.concatenate([dk_own, dv_own], 1) + more).astype(jnp.bfloat16)
    grad_wqe = outer_sum(grad_qe, normed_q[:tokens])
    grad_wkve = outer_sum(grad_ekv, normed_q)
    grad_in = project_back(grad_ekv, enc_w[D : 3 * D])
    grad_in = grad_in + jnp.pad(project_back(grad_qe, enc_w[:D]), ((0, extra), (0, 0)))
    grad_x, grad_gain0 = norm_back(enc_in, norm_gains[0], grad_in)
    grad_questions = from_rows((grad_hidden + grad_x[:tokens]).astype(jnp.bfloat16)).astype(jnp.float32)
    enc_full = jnp.concatenate([grad_wqe, grad_wkve, grad_woe, grad_w1e, grad_w2e], 0)
    gain_terms = jnp.stack(
        [grad_gain0, grad_gain1, grad_gain2, grad_gain3, grad_gain4, grad_gain5]
    )
    grad_gains = lax.psum(gain_terms, ("rows", "mem"))
    grad_encoder = reduce_weights(enc_full).astype(jnp.float32).T
    return (decoded, grad_questions, grad_answers, grad_encoder, grad_decoder, grad_gains)


def solution(mesh):
    return jax.shard_map(
        on_device,
        mesh=mesh,
        in_specs=(
            P("rows", "mem", None),
            P("rows", "mem", None),
            P("rows", None),
            P("rows", None),
            P("rows", None, "mem"),
            P("rows", None, None),
            P(),
            P(None, ("rows", "mem")),
            P(None, ("rows", "mem")),
            P(),
            P("rows", "mem", None),
        ),
        out_specs=(
            P("rows", "mem", None),
            P("rows", "mem", None),
            P("rows", "mem", None),
            P(None, ("rows", "mem")),
            P(None, ("rows", "mem")),
            P(),
        ),
        check_vma=False,
    )
```

```python
import functools
import jax
import jax.numpy as jnp
from jax import lax
from jax.experimental import pallas as pl
from jax.experimental.pallas import tpu as pltpu
from jax.sharding import PartitionSpec as P

D = 768
H = 12
HD = 64
FF = 3072
QB = 256
masked_score = -1e30


def key_chunks(own_len, extra):
    chunks = []
    for side in (0, 1):
        for at in range(own_len // QB):
            chunks.append((side, at * QB, QB))
        if extra:
            chunks.append((side, own_len, extra))
    return chunks


def attend_kernel(causal, own_len, extra, act, q_ref, qaug_ref, own_k, own_v, oth_k, oth_v, kaug_ref, o_ref, lse_ref, s_ref, m_ref, l_ref, acc_ref):
    low = lax.broadcasted_iota(jnp.int32, (1, 128), 1) < HD
    chunks = key_chunks(own_len, extra)
    nk = own_len + extra
    for qb in range(own_len // QB):
        rows = pl.ds(qb * QB, QB)
        q = q_ref[rows, :] * jnp.bfloat16(HD ** (-0.5))
        qaug = qaug_ref[rows, :]
        queries = (jnp.where(low, q, qaug), jnp.where(low, qaug, q))
        m_ref[...] = jnp.full(m_ref.shape, -3e30, jnp.float32)
        l_ref[...] = jnp.zeros(l_ref.shape, jnp.float32)
        acc_ref[...] = jnp.zeros(acc_ref.shape, jnp.float32)
        for ci, (side, at, size) in enumerate(chunks):

            def score(side=side, at=at, size=size):
                k = (own_k, oth_k)[side][at : at + size, :]
                place = slice(side * nk + at, side * nk + at + size)
                kaug = kaug_ref[place, :]
                for h in (0, 1):
                    cols = slice(h * QB, (h + 1) * QB)
                    keys = jnp.where(low, k, kaug) if h == 0 else jnp.where(low, kaug, k)
                    s = lax.dot_general(keys, queries[h], (((1,), (1,)), ((), ())), preferred_element_type=jnp.float32)
                    if causal and side == 0 and at == qb * QB:
                        tri = lax.broadcasted_iota(jnp.int32, (size, QB), 0) <= lax.broadcasted_iota(jnp.int32, (size, QB), 1)
                        s = jnp.where(tri, s, masked_score)
                    s_ref[place, cols] = s
                    m_ref[:, cols] = jnp.maximum(m_ref[:, cols], jnp.max(s.reshape(size // 8, 8, QB), 0))

            pl.when(act[qb, ci] != 0)(score)
        m = jnp.max(m_ref[...], 0, keepdims=True)
        for ci, (side, at, size) in enumerate(chunks):

            def mix(side=side, at=at, size=size):
                v = (own_v, oth_v)[side][at : at + size, :]
                zero = jnp.zeros_like(v)
                place = slice(side * nk + at, side * nk + at + size)
                p = jnp.exp(s_ref[place, :] - m)
                l_ref[...] += jnp.sum(p.reshape(size // 8, 8, 2 * QB), 0)
                pb = p.astype(jnp.bfloat16)
                pb = jnp.concatenate([pb[:, :QB], pb[:, QB:]], 0)
                v_split = jnp.concatenate([jnp.where(low, v, zero), jnp.where(low, zero, v)], 0)
                acc_ref[...] += lax.dot_general(pb, v_split, (((0,), (0,)), ((), ())), preferred_element_type=jnp.float32)

            pl.when(act[qb, ci] != 0)(mix)
        total = jnp.sum(l_ref[...], 0, keepdims=True)
        lse = m + jnp.log(total)
        rec = 1.0 / total
        wide = lambda row, h: jnp.broadcast_to(row[:, h * QB : (h + 1) * QB], (HD, QB))
        o_ref[rows, :] = (acc_ref[...] * jnp.concatenate([wide(rec, 0), wide(rec, 1)], 0).T).astype(jnp.bfloat16)
        lse_ref[rows, :] = jnp.concatenate([wide(lse, 1), wide(lse, 0)], 0).T


def attend(causal, act, q, qaug, own_kv, oth_kv, kaug):
    t = q.shape[0]
    nk = own_kv.shape[0]
    col = lambda first: pl.BlockSpec((nk, 128), lambda i, a: (0, first + i))
    return pl.pallas_call(
        functools.partial(attend_kernel, causal, t, nk - t),
        grid_spec=pltpu.PrefetchScalarGridSpec(
            num_scalar_prefetch=1,
            grid=(H // 2,),
            in_specs=[
                pl.BlockSpec((t, 128), lambda i, a: (0, i)),
                pl.BlockSpec((t, 128), lambda i, a: (0, 0)),
                col(0), col(H // 2), col(0), col(H // 2),
                pl.BlockSpec((2 * nk, 128), lambda i, a: (0, 0)),
            ],
            out_specs=[pl.BlockSpec((t, 128), lambda i, a: (0, i))] * 2,
            scratch_shapes=[pltpu.VMEM((2 * nk, 2 * QB), jnp.float32), pltpu.VMEM((8, 2 * QB), jnp.float32), pltpu.VMEM((8, 2 * QB), jnp.float32), pltpu.VMEM((QB, 128), jnp.float32)],
        ),
        out_shape=[jax.ShapeDtypeStruct((t, D), jnp.bfloat16), jax.ShapeDtypeStruct((t, D), jnp.float32)],
        compiler_params=pltpu.CompilerParams(vmem_limit_bytes=40 * 1024 * 1024),
        cost_estimate=pl.CostEstimate(flops=4 * t * 2 * nk * D, bytes_accessed=8 * nk * D, transcendentals=t * 2 * nk * H),
        name="attend",
    )(act, q, qaug, own_kv, own_kv, oth_kv, oth_kv, kaug)


def three_parts(value):
    hi = value.astype(jnp.bfloat16).astype(jnp.float32)
    mid = (value - hi).astype(jnp.bfloat16).astype(jnp.float32)
    return hi, mid, value - hi - mid


def spread(base, lane64, value):
    hi, mid, lo = three_parts(value)
    return jnp.where(lane64 == 8, hi, jnp.where(lane64 == 9, mid, jnp.where(lane64 == 10, lo, base)))


def back_kernel(causal, own_len, extra, act, q_ref, qaug_ref, own_k, own_v, oth_k, oth_v, kaug_ref, o_ref, lse_ref, g_ref, dq_ref, dko_ref, dvo_ref, dkt_ref, dvt_ref, dk_acc, dv_acc, dq_acc):
    lane = lax.broadcasted_iota(jnp.int32, (1, 128), 1)
    low = lane < HD
    lane64 = lane % HD
    chunks = key_chunks(own_len, extra)
    nk = own_len + extra
    dk_acc[...] = jnp.zeros(dk_acc.shape, jnp.float32)
    dv_acc[...] = jnp.zeros(dv_acc.shape, jnp.float32)
    ones_aug = jnp.where((lane64 >= 8) & (lane64 <= 10), 1.0, 0.0).astype(jnp.bfloat16)
    for qb in range(own_len // QB):
        rows = pl.ds(qb * QB, QB)
        q = q_ref[rows, :] * jnp.bfloat16(HD ** (-0.5))
        g = g_ref[rows, :]
        qaug = spread(qaug_ref[rows, :].astype(jnp.float32), lane64, -lse_ref[rows, :]).astype(jnp.bfloat16)
        prod = g.astype(jnp.float32) * o_ref[rows, :].astype(jnp.float32)
        d_even = jnp.sum(jnp.where(low, prod, 0.0), -1, keepdims=True)
        d_odd = jnp.sum(jnp.where(low, 0.0, prod), -1, keepdims=True)
        gaug = spread(jnp.zeros((QB, 128), jnp.float32), lane64, -jnp.where(low, d_odd, d_even)).astype(jnp.bfloat16)
        queries = (jnp.where(low, q, qaug), jnp.where(low, qaug, q))
        grads = (jnp.where(low, g, gaug), jnp.where(low, gaug, g))
        zero = jnp.zeros_like(q)
        q_split = jnp.concatenate([jnp.where(low, q, zero), jnp.where(low, zero, q)], 0)
        g_split = jnp.concatenate([jnp.where(low, g, zero), jnp.where(low, zero, g)], 0)
        dq_acc[...] = jnp.zeros(dq_acc.shape, jnp.float32)
        for ci, (side, at, size) in enumerate(chunks):

            def work(side=side, at=at, size=size):
                k = (own_k, oth_k)[side][at : at + size, :]
                v = (own_v, oth_v)[side][at : at + size, :]
                place = slice(side * nk + at, side * nk + at + size)
                kaug = kaug_ref[place, :]
                vaug = jnp.broadcast_to(ones_aug, v.shape)
                zk = jnp.zeros_like(k)
                probs, dscores = [], []
                for h in (0, 1):
                    keys = jnp.where(low, k, kaug) if h == 0 else jnp.where(low, kaug, k)
                    vals = jnp.where(low, v, vaug) if h == 0 else jnp.where(low, vaug, v)
                    s = lax.dot_general(keys, queries[h], (((1,), (1,)), ((), ())), preferred_element_type=jnp.float32)
                    if causal and side == 0 and at == qb * QB:
                        tri = lax.broadcasted_iota(jnp.int32, (size, QB), 0) <= lax.broadcasted_iota(jnp.int32, (size, QB), 1)
                        s = jnp.where(tri, s, masked_score)
                    p = jnp.exp(s)
                    dp = lax.dot_general(vals, grads[h], (((1,), (1,)), ((), ())), preferred_element_type=jnp.float32)
                    dscores.append((p * dp).astype(jnp.bfloat16))
                    probs.append(p.astype(jnp.bfloat16))
                ds = jnp.concatenate(dscores, 1)
                pb = jnp.concatenate(probs, 1)
                dk_acc[place, :] += jnp.dot(ds, q_split, preferred_element_type=jnp.float32)
                dv_acc[place, :] += jnp.dot(pb, g_split, preferred_element_type=jnp.float32)
                k_split = jnp.concatenate([jnp.where(low, k, zk), jnp.where(low, zk, k)], 0)
                dst = jnp.concatenate(dscores, 0)
                dq_acc[...] += lax.dot_general(dst, k_split, (((0,), (0,)), ((), ())), preferred_element_type=jnp.float32)

            pl.when(act[qb, ci] != 0)(work)
        dq_ref[rows, :] = (dq_acc[...] * HD ** (-0.5)).astype(jnp.bfloat16)
    dko_ref[...] = dk_acc[:nk, :]
    dvo_ref[...] = dv_acc[:nk, :]
    dkt_ref[...] = dk_acc[nk:, :].astype(jnp.bfloat16)
    dvt_ref[...] = dv_acc[nk:, :].astype(jnp.bfloat16)


def attend_back(causal, act, q, qaug, own_kv, oth_kv, kaug, mixed, lse, grad):
    t = q.shape[0]
    nk = own_kv.shape[0]
    col = lambda first: pl.BlockSpec((nk, 128), lambda i, a: (0, first + i))
    tok = pl.BlockSpec((t, 128), lambda i, a: (0, i))
    return pl.pallas_call(
        functools.partial(back_kernel, causal, t, nk - t),
        grid_spec=pltpu.PrefetchScalarGridSpec(
            num_scalar_prefetch=1,
            grid=(H // 2,),
            in_specs=[
                tok,
                pl.BlockSpec((t, 128), lambda i, a: (0, 0)),
                col(0), col(H // 2), col(0), col(H // 2),
                pl.BlockSpec((2 * nk, 128), lambda i, a: (0, 0)),
                tok, tok, tok,
            ],
            out_specs=[tok, col(0), col(0), col(0), col(0)],
            scratch_shapes=[pltpu.VMEM((2 * nk, 128), jnp.float32), pltpu.VMEM((2 * nk, 128), jnp.float32), pltpu.VMEM((QB, 128), jnp.float32)],
        ),
        out_shape=[
            jax.ShapeDtypeStruct((t, D), jnp.bfloat16),
            jax.ShapeDtypeStruct((nk, D), jnp.float32),
            jax.ShapeDtypeStruct((nk, D), jnp.float32),
            jax.ShapeDtypeStruct((nk, D), jnp.bfloat16),
            jax.ShapeDtypeStruct((nk, D), jnp.bfloat16),
        ],
        compiler_params=pltpu.CompilerParams(vmem_limit_bytes=40 * 1024 * 1024),
        cost_estimate=pl.CostEstimate(flops=10 * t * 2 * nk * D, bytes_accessed=24 * nk * D, transcendentals=t * 2 * nk * H),
        name="attend_back",
    )(act, q, qaug, own_kv, own_kv, oth_kv, oth_kv, kaug, mixed, lse, grad)


def seg_aug_q(seg):
    j = jnp.arange(128, dtype=jnp.int32) % HD
    return ((j[None, :] < 8) & (j[None, :] == seg[:, None])).astype(jnp.bfloat16)


def seg_aug_k(seg):
    j = jnp.arange(128, dtype=jnp.int32)[None, :] % HD
    bad = (j < 8) & (j != seg[:, None])
    return jnp.where(bad, masked_score, jnp.where((j >= 8) & (j <= 10), 1.0, 0.0)).astype(jnp.bfloat16)


MESH = pl.DeviceIdType.MESH


def position():
    r, m = lax.axis_index("rows"), lax.axis_index("mem")
    core = lax.rem(r, 2)
    x_at = lax.rem(lax.div(r, 2), 2)
    y_at = lax.div(r, 4)
    near = r + 1 - 2 * core
    x_near = r + 2 - 4 * x_at
    y_near = r + 4 - 8 * y_at
    first = x_near + core * (y_near - x_near)
    second = y_near + core * (x_near - y_near)
    both = first + second - r
    return r, m, core, near, first, second, both


def greet(r, m, core, first, second):
    barrier = pltpu.get_barrier_semaphore()
    base = r - core
    count = 0
    for c in (0, 1):
        for step in range(4):
            if c == 0 and step == 0:
                continue
            to = r if c == 0 else base + 1 - core
            pl.semaphore_signal(barrier, inc=1, device_id=(to, lax.rem(m + step, 4)), device_id_type=MESH)
            count += 1
    for to in (first, second):
        pl.semaphore_signal(barrier, inc=1, device_id=(to, m), device_id_type=MESH)
        count += 1
    pl.semaphore_wait(barrier, count)


def remote(src, dst, send, recv, to):
    return pltpu.make_async_remote_copy(
        src_ref=src, dst_ref=dst, send_sem=send, recv_sem=recv, device_id=to, device_id_type=MESH
    )


def gather_kernel(
    enc_in, dec_in, q_in, a_in, g_in, seg_in, ids_in,
    enc_out, dec_out, q_out, a_out, g_out, seg_out, ids_out,
    z_s, z_r, a_s, a_r, b_s, b_r, c_s, c_r, t_s, t_r, t_l, i_s, i_r, i_l, w_l, n_s, n_r,
):
    r, m, core, near, first, second, both = position()
    base = r - core
    ins, outs = (enc_in, dec_in), (enc_out, dec_out)
    greet(r, m, core, first, second)

    def at(which, row, mem):
        size = ins[which].shape[0]
        return outs[which].at[pl.ds(pl.multiple_of((row * 4 + mem) * size, 32), size)]

    waits = []
    locals_ = []
    for w in (0, 1):
        copy = pltpu.make_async_copy(ins[w], at(w, r, m), w_l.at[w])
        copy.start()
        locals_.append(copy)

    def send(src, dst, s, v, to):
        copy = remote(src, dst, s, v, to)
        copy.start()
        waits.append(copy)

    send(seg_in.at[lax.rem(m, 2)], seg_out, n_s, n_r, (near, m))
    holder = lax.div(m * (3 - m), 2)
    slot = lax.div(m, 2)
    cond_sends = []
    for i in (0, 1):
        for e in (0, 1):
            to = (r if e == 0 else near, 2 * core + i)
            copy = remote(ids_in.at[i], ids_out.at[m], i_s.at[i, e], i_r.at[m], to)
            if e == 1:
                copy.start()
                waits.append(copy)
                continue
            here = 2 * core + i == m
            mine = pltpu.make_async_copy(ids_in.at[i], ids_out.at[m], i_l)
            pl.when(here)(mine.start)
            pl.when(jnp.logical_not(here))(copy.start)
            cond_sends.append((here, copy))

    def tokens(n, src, dst):
        for i in (0, 1):
            here = jnp.logical_and(2 * core + i == m, holder == core)
            place = dst.at[pl.ds(pl.multiple_of(slot * 256, 256), 256)]
            copy = remote(src.at[i], place, t_s.at[n, i], t_r.at[n, slot], (base + holder, 2 * core + i))
            mine = pltpu.make_async_copy(src.at[i], place, t_l.at[n])
            pl.when(here)(mine.start)
            pl.when(jnp.logical_not(here))(copy.start)
            cond_sends.append((here, copy))

    def forward(step, which):
        mem = lax.rem(m - step + 4, 4)
        for w in (0, 1):
            here = at(w, r, mem)
            src = ins[w] if step == 0 else here
            if step < 3:
                send(src, here, z_s.at[step, w], z_r.at[step, w], (r, lax.rem(m + 1, 4)))
            send(src, here, b_s.at[step, 0, w], b_r.at[step, 0, w], (second, m))
            send(src, here, a_s.at[step, w], a_r.at[step, w], (first, m))
            send(src, here, c_s.at[step, 0, w], c_r.at[step, 0, w], (near, m))

    def stage_a(step):
        if step > 0:
            mem = lax.rem(m - step + 4, 4)
            for w in (0, 1):
                here = at(w, r, mem)
                remote(here, here, z_s.at[step - 1, w], z_r.at[step - 1, w], (near, m)).wait_recv()
        forward(step, 0)

    def stage_b(step):
        mem = lax.rem(m - step + 4, 4)
        for w in (0, 1):
            here = at(w, first, mem)
            remote(here, here, a_s.at[step, w], a_r.at[step, w], (near, m)).wait_recv()
            send(here, here, b_s.at[step, 1, w], b_r.at[step, 1, w], (second, m))
            send(here, here, c_s.at[step, 1, w], c_r.at[step, 1, w], (near, m))

    def stage_c(step):
        mem = lax.rem(m - step + 4, 4)
        for k, row in ((0, second), (1, both)):
            for w in (0, 1):
                here = at(w, row, mem)
                remote(here, here, b_s.at[step, k, w], b_r.at[step, k, w], (near, m)).wait_recv()
                send(here, here, c_s.at[step, 2 + k, w], c_r.at[step, 2 + k, w], (near, m))

    tokens(0, q_in, q_out)
    stage_a(0)
    tokens(1, a_in, a_out)
    stage_a(1)
    stage_b(0)
    tokens(2, g_in, g_out)
    stage_a(2)
    stage_b(1)
    stage_c(0)
    stage_a(3)
    stage_b(2)
    stage_c(1)
    stage_b(3)
    stage_c(2)
    stage_c(3)

    turn = 1 - 2 * core
    others = (r + turn, first_of(r, core), second_of(r, core), both + turn)
    for step in range(4):
        mem = lax.rem(m - step + 4, 4)
        for k in range(4):
            for w in (0, 1):
                here = at(w, others[k], mem)
                remote(here, here, c_s.at[step, k, w], c_r.at[step, k, w], (near, m)).wait_recv()
    remote(seg_out, seg_out, n_s, n_r, (near, m)).wait_recv()
    mine_row = lax.div(m, 2) == core
    for mem in range(4):
        here = jnp.logical_and(mine_row, m == mem)
        got = remote(ids_out.at[mem], ids_out.at[mem], i_s.at[0, 0], i_r.at[mem], (near, m))
        mine = pltpu.make_async_copy(ids_in.at[0], ids_out.at[mem], i_l)
        pl.when(here)(mine.wait)
        pl.when(jnp.logical_not(here))(got.wait_recv)
    for n, dst in enumerate((q_out, a_out, g_out)):
        for li in (0, 1):
            source = core if li == 0 else 3 - core
            here = jnp.logical_and(mine_row, m == source)
            place = dst.at[pl.ds(li * 256, 256)]
            got = remote(place, place, t_s.at[n, 0], t_r.at[n, li], (near, m))
            mine = pltpu.make_async_copy(place, place, t_l.at[n])
            pl.when(here)(mine.wait)
            pl.when(jnp.logical_not(here))(got.wait_recv)
    for copy in locals_:
        copy.wait()
    for copy in waits:
        copy.wait_send()
    for here, copy in cond_sends:
        pl.when(jnp.logical_not(here))(copy.wait_send)


def first_of(r, core):
    turn = 1 - 2 * core
    x_step = 2 - 4 * lax.rem(lax.div(r, 2), 2)
    y_step = 4 - 8 * lax.div(r, 4)
    return r + turn + y_step + core * (x_step - y_step)


def second_of(r, core):
    turn = 1 - 2 * core
    x_step = 2 - 4 * lax.rem(lax.div(r, 2), 2)
    y_step = 4 - 8 * lax.div(r, 4)
    return r + turn + x_step + core * (y_step - x_step)


def gather_fast(enc_t, dec_t, q, a, g, seg, ids):
    dma = pltpu.SemaphoreType.DMA
    tokens = 2 * q.shape[1]
    any_ = pl.BlockSpec(memory_space=pl.ANY)
    out = lambda shape, kind=jnp.bfloat16: jax.ShapeDtypeStruct(shape, kind)
    return pl.pallas_call(
        gather_kernel,
        in_specs=[any_] * 7,
        out_specs=[any_] * 7,
        out_shape=[
            out((32 * enc_t.shape[0], D)),
            out((32 * dec_t.shape[0], D)),
            out((tokens, D)), out((tokens, D)), out((tokens, D)),
            out(seg.shape[1:], jnp.int32),
            out((4,) + ids.shape[1:], jnp.int32),
        ],
        scratch_shapes=[
            dma((3, 2)), dma((3, 2)), dma((4, 2)), dma((4, 2)), dma((4, 2, 2)), dma((4, 2, 2)),
            dma((4, 4, 2)), dma((4, 4, 2)), dma((3, 2)), dma((3, 2)), dma((3,)), dma((2, 2)), dma((4,)), dma,
            dma((2,)), dma, dma,
        ],
        compiler_params=pltpu.CompilerParams(collective_id=0, has_side_effects=True),
        name="gather_fast",
    )(enc_t, dec_t, q, a, g, seg, ids)


def add_to(total, more):
    def step(i, unused):
        rows = pl.ds(pl.multiple_of(i * 32, 32), 32)
        total[rows, :] = total[rows, :] + more[rows, :]
        return unused

    lax.fori_loop(0, total.shape[0] // 32, step, 0)


def reduce_kernel(
    enc_in, dec_in, y_in, q_in, a_in, gain_in,
    enc_out, dec_out, y_out, q_out, a_out, gain_out,
    held_e, held_d, rc_e, rc_d, rb_e, rb_d, ra_e, ra_d, rz_e, rz_d, rg, gs, gz,
    l_l, c_s, c_r, b_s, b_r, a_s, a_r, z_s, z_r, t_s, t_r, t_l, g_s, g_r, gz_s, gz_r, o_l,
):
    r, m, core, near, first, second, both = position()
    base = r - core
    ins, outs = (enc_in, dec_in), (enc_out, dec_out)
    held, rc, rb, ra, rz = (held_e, held_d), (rc_e, rc_d), (rb_e, rb_d), (ra_e, ra_d), (rz_e, rz_d)
    greet(r, m, core, first, second)
    turn = 1 - 2 * core
    mine_rows = (r, first, second, both)
    others = (r + turn, first_of(r, core), second_of(r, core), both + turn)
    x_near = first + core * (second - first)
    y_near = second + core * (first - second)
    waits = []
    cond_sends = []

    def send(src, dst, s, v, to):
        copy = remote(src, dst, s, v, to)
        copy.start()
        waits.append(copy)

    def arrived(dst, s, v):
        remote(dst, dst, s, v, (near, m)).wait_recv()

    def at(w, row, mem):
        size = outs[w].shape[0]
        return ins[w].at[pl.ds(pl.multiple_of((row * 4 + mem) * size, 32), size)]

    send(gain_in, rg.at[0], g_s.at[0], g_r.at[0], (near, m))

    order = (3, 2, 1, 0)
    loads = {}
    for j in range(4):
        mem = lax.rem(m - 1 - j + 8, 4)
        for k in order:
            for w in (0, 1):
                send(at(w, others[k], mem), rc[w].at[j, k], c_s.at[j, k, w], c_r.at[j, k, w], (near, m))
                loads[j, k, w] = pltpu.make_async_copy(at(w, mine_rows[k], mem), held[w].at[j, k], l_l.at[j, k, w])
                loads[j, k, w].start()

    def tokens(n, src, dst):
        for li in (0, 1):
            to_mem = core if li == 0 else 3 - core
            here = jnp.logical_and(to_mem == m, lax.div(m, 2) == core)
            place = src.at[pl.ds(li * 256, 256)]
            target = dst.at[lax.rem(m, 2)]
            copy = remote(place, target, t_s.at[n, li], t_r.at[n, lax.rem(m, 2)], (base + lax.div(m, 2), to_mem))
            mine = pltpu.make_async_copy(place, target, t_l.at[n])
            pl.when(here)(mine.start)
            pl.when(jnp.logical_not(here))(copy.start)
            cond_sends.append((here, copy))

    def from_core(j):
        for k in order:
            for w in (0, 1):
                loads[j, k, w].wait()
                arrived(rc[w].at[j, k], c_s.at[j, k, w], c_r.at[j, k, w])
                add_to(held[w].at[j, k], rc[w].at[j, k])
                if k >= 2:
                    send(held[w].at[j, k], rb[w].at[j, k - 2], b_s.at[j, k - 2, w], b_r.at[j, k - 2, w], (second, m))

    def from_second(j):
        for k in (1, 0):
            for w in (0, 1):
                arrived(rb[w].at[j, k], b_s.at[j, k, w], b_r.at[j, k, w])
                add_to(held[w].at[j, k], rb[w].at[j, k])
                if k == 1:
                    send(held[w].at[j, 1], ra[w].at[j], a_s.at[j, w], a_r.at[j, w], (first, m))

    def from_first(j):
        for w in (0, 1):
            arrived(ra[w].at[j], a_s.at[j, w], a_r.at[j, w])
            add_to(held[w].at[j, 0], ra[w].at[j])
            if j > 0:
                arrived(rz[w].at[j - 1], z_s.at[j - 1, w], z_r.at[j - 1, w])
                add_to(held[w].at[j, 0], rz[w].at[j - 1])
            if j < 3:
                send(held[w].at[j, 0], rz[w].at[j], z_s.at[j, w], z_r.at[j, w], (r, lax.rem(m + 1, 4)))
            else:
                pltpu.make_async_copy(held[w].at[3, 0], outs[w], o_l.at[w]).start()

    tokens(0, y_in, y_out)
    from_core(0)
    arrived(rg.at[0], g_s.at[0], g_r.at[0])
    gs[0] = gain_in[...] + rg[0]
    send(gs.at[0], rg.at[1], g_s.at[1], g_r.at[1], (x_near, m))
    from_core(1)
    tokens(1, q_in, q_out)
    arrived(rg.at[1], g_s.at[1], g_r.at[1])
    gs[1] = gs[0] + rg[1]
    send(gs.at[1], rg.at[2], g_s.at[2], g_r.at[2], (y_near, m))
    from_second(0)
    from_core(2)
    from_second(1)
    tokens(2, a_in, a_out)
    from_first(0)
    arrived(rg.at[2], g_s.at[2], g_r.at[2])
    gs[2] = gs[1] + rg[2]
    gz[m] = gs[2]
    for hop in (1, 2, 3):
        send(gs.at[2], gz.at[m], gz_s.at[hop - 1], gz_r.at[m], (r, lax.rem(m + hop, 4)))
    from_core(3)
    from_second(2)
    from_first(1)
    from_second(3)
    from_first(2)
    from_first(3)
    for mem in range(4):
        pl.when(m != mem)(remote(gz.at[mem], gz.at[mem], gz_s.at[0], gz_r.at[mem], (near, m)).wait_recv)
    gain_out[...] = (gz[0] + gz[1]) + (gz[2] + gz[3])
    holder = lax.div(m * (3 - m), 2)
    for n, dst in enumerate((y_out, q_out, a_out)):
        for i in (0, 1):
            here = jnp.logical_and(2 * core + i == m, holder == core)
            got = remote(dst.at[i], dst.at[i], t_s.at[n, 0], t_r.at[n, i], (near, m))
            mine = pltpu.make_async_copy(dst.at[i], dst.at[i], t_l.at[n])
            pl.when(here)(mine.wait)
            pl.when(jnp.logical_not(here))(got.wait_recv)
    for w in (0, 1):
        pltpu.make_async_copy(held[w].at[3, 0], outs[w], o_l.at[w]).wait()
    for copy in waits:
        copy.wait_send()
    for here, copy in cond_sends:
        pl.when(jnp.logical_not(here))(copy.wait_send)


def reduce_fast(enc_g, dec_g, y, q, a, gains):
    dma = pltpu.SemaphoreType.DMA
    any_ = pl.BlockSpec(memory_space=pl.ANY)
    vmem = pl.BlockSpec(memory_space=pltpu.VMEM)
    out = lambda shape, kind=jnp.bfloat16: jax.ShapeDtypeStruct(shape, kind)
    n_e, n_d = enc_g.shape[0] // 32, dec_g.shape[0] // 32
    quarter = y.shape[0] // 2
    held = lambda *lead: [pltpu.VMEM(lead + (n, D), jnp.bfloat16) for n in (n_e, n_d)]
    small = lambda n: pltpu.VMEM((n,) + gains.shape, jnp.float32)
    return pl.pallas_call(
        reduce_kernel,
        in_specs=[any_] * 5 + [vmem],
        out_specs=[any_] * 5 + [vmem],
        out_shape=[out((n_e, D)), out((n_d, D))] + [out((2, quarter, D))] * 3 + [out(gains.shape, jnp.float32)],
        scratch_shapes=held(4, 4) + held(4, 4) + held(4, 2) + held(4) + held(3) + [small(3), small(3), small(4)] + [
            dma((4, 4, 2)), dma((4, 4, 2)), dma((4, 4, 2)), dma((4, 2, 2)), dma((4, 2, 2)), dma((4, 2)), dma((4, 2)),
            dma((3, 2)), dma((3, 2)), dma((3, 2)), dma((3, 2)), dma((3,)), dma((3,)), dma((3,)), dma((3,)), dma((4,)), dma((2,)),
        ],
        compiler_params=pltpu.CompilerParams(collective_id=1, has_side_effects=True, vmem_limit_bytes=56 * 1024 * 1024),
        name="reduce_fast",
    )(enc_g, dec_g, y, q, a, gains)


epsilon = 1e-06


def rms_norm(values, gain):
    return values * lax.rsqrt(jnp.mean(values * values, -1, keepdims=True) + epsilon) * gain


def norm_back(values, gain, grad):
    unused, pull = jax.vjp(rms_norm, values, gain)
    return pull(grad)


def project(left, weight_t):
    return jnp.einsum("nd,ed->ne", left, weight_t, preferred_element_type=jnp.float32)


def project_back(left, weight_t):
    return jnp.einsum("ne,ed->nd", left, weight_t, preferred_element_type=jnp.float32)


def outer_sum(wide, narrow):
    return jnp.einsum("ne,nd->ed", wide, narrow, preferred_element_type=jnp.float32).astype(jnp.bfloat16)


def output_back(grad, mixed_b, w_out):
    grad_b = grad.astype(jnp.bfloat16)
    return (outer_sum(mixed_b, grad_b), project(grad_b, w_out).astype(jnp.bfloat16))


def feed_back(grad, normed_b, pre_act, act_b, w_in, w_out):
    grad_b = grad.astype(jnp.bfloat16)
    grad_wout = outer_sum(act_b, grad_b)
    grad_act = project(grad_b, w_out)
    unused, pull = jax.vjp(jax.nn.gelu, pre_act)
    grad_pre = pull(grad_act)[0].astype(jnp.bfloat16)
    return (outer_sum(grad_pre, normed_b), grad_wout, project_back(grad_pre, w_in))


def partner(values):
    n_rows = lax.axis_size("rows")
    return lax.ppermute(values, "rows", [(i, i ^ 1) for i in range(n_rows)])


def my_row(values):
    core = lax.axis_index("rows") % 2
    mem = lax.axis_index("mem")
    chosen = jnp.where(mem // 2 == core, values, partner(values))
    return lax.dynamic_index_in_dim(chosen, mem % 2, 0, keepdims=False)


def quarters_of(core):
    return (jnp.where(core == 0, 0, 1), jnp.where(core == 0, 3, 2))


def own_quarters(row, core, quarter):
    return jnp.concatenate(
        [lax.dynamic_slice_in_dim(row, place * quarter, quarter, 0) for place in quarters_of(core)], 0
    )


def to_rows(values):
    quarter = values.shape[1]
    row = my_row(lax.all_gather(values, "mem", axis=1, tiled=True))
    return own_quarters(row, lax.axis_index("rows") % 2, quarter)


def from_rows(values):
    quarter = values.shape[0] // 2
    core = lax.axis_index("rows") % 2
    mem = lax.axis_index("mem")
    gathered = lax.all_gather(values, "mem", axis=0)
    other = partner(gathered)
    holder = jnp.where((mem == 0) | (mem == 3), 0, 1)
    chosen = jnp.where(holder == core, gathered, other)
    return lax.dynamic_slice(
        chosen, (2 * core, jnp.where(mem < 2, 0, quarter), 0), (2, quarter, values.shape[1])
    )


def gather_weights(params):
    return lax.all_gather(params.T, ("rows", "mem"), axis=0, tiled=True)


def reduce_weights(grads):
    return lax.psum_scatter(grads, ("rows", "mem"), scatter_dimension=0, tiled=True)


def flags_of(q_row, k_row, core, quarter, extra, causal):
    n = q_row.shape[0] // quarter
    ends_q = q_row.reshape(n, quarter)
    ends_k = k_row.reshape(n, quarter)
    meets = (ends_k[None, :, 0] <= ends_q[:, None, -1]) & (ends_q[:, None, 0] <= ends_k[None, :, -1])
    if causal:
        meets &= jnp.arange(n)[None, :] <= jnp.arange(n)[:, None]
    mine = jnp.stack(quarters_of(core))
    others = jnp.stack(quarters_of(1 - core))
    meets = meets[mine]
    always = [jnp.ones((2, 1), bool)] if extra else []
    return jnp.concatenate([meets[:, mine]] + always + [meets[:, others]] + always, 1).astype(jnp.int32)


def both_parts(own, other):
    return jnp.concatenate([own, other], 0)


def on_device(
    fast,
    questions,
    answers,
    q_segments,
    a_segments,
    entry_ids,
    entry_alive_flags,
    memory_table,
    enc_params,
    dec_params,
    norm_gains,
    cotangent,
):
    quarter = questions.shape[1]
    core = lax.axis_index("rows") % 2
    per_row, slots = entry_alive_flags.shape[1], entry_alive_flags.shape[2]
    half = per_row // 2
    rows_here, row_len = q_segments.shape
    segs = jnp.concatenate([q_segments, a_segments, entry_alive_flags.reshape(rows_here, -1)], 1)
    if fast:
        segs = jnp.pad(segs, ((0, 0), (0, -segs.shape[1] % 1024))).reshape(rows_here, -1, 128)
        own_ids = entry_ids.reshape(rows_here, -1)
        n_ids = own_ids.shape[1]
        own_ids = jnp.pad(own_ids, ((0, 0), (0, 1024 - n_ids))).reshape(rows_here, 8, 128)
        enc_w, dec_w, x_question, x_answer, grad_top, other_segs, ids = gather_fast(
            enc_params.T, dec_params.T, questions, answers, cotangent.astype(jnp.bfloat16), segs, own_ids
        )
        mem = lax.axis_index("mem")
        numbers = jnp.where(
            mem // 2 == core, lax.dynamic_index_in_dim(segs, mem % 2, 0, keepdims=False), other_segs
        ).reshape(-1)
        ids = ids.reshape(ids.shape[0], -1)[:, :n_ids].reshape(ids.shape[0], per_row, -1)
        ids = ids.transpose(1, 0, 2).reshape(-1)
    else:
        enc_w, dec_w = gather_weights(enc_params), gather_weights(dec_params)
        ids = my_row(lax.all_gather(entry_ids, "mem", axis=2, tiled=True)).reshape(-1)
        numbers = my_row(segs)
        x_question, x_answer = to_rows(questions), to_rows(answers)
        grad_top = to_rows(cotangent.astype(jnp.bfloat16))
    x_question, x_answer = x_question.astype(jnp.float32), x_answer.astype(jnp.float32)
    grad_top = grad_top.astype(jnp.float32)
    q_row = numbers[:row_len]
    a_row = numbers[row_len : 2 * row_len]
    alive = numbers[2 * row_len : 2 * row_len + per_row * slots]

    own_ids = lax.dynamic_slice_in_dim(ids, core * half * slots, half * slots, 0)
    entry_vals = memory_table[own_ids].reshape(half * slots * 2, D).astype(jnp.float32)
    n_prefix = entry_vals.shape[0]
    extra = -(-n_prefix // 128) * 128
    place = jnp.arange(extra, dtype=jnp.int32)

    def prefix_segments(which):
        question = which * half + place // (2 * slots)
        live = lax.dynamic_slice_in_dim(alive, which * half * slots, half * slots, 0)
        live = jnp.pad(jnp.repeat(live, 2), (0, extra - n_prefix))
        return jnp.where(live == 1, question, -1)

    tokens = 2 * quarter
    own_q = own_quarters(q_row, core, quarter)
    other_q = own_quarters(q_row, 1 - core, quarter)
    own_a = own_quarters(a_row, core, quarter)
    other_a = own_quarters(a_row, 1 - core, quarter)
    q_aug, a_aug = seg_aug_q(own_q), seg_aug_q(own_a)
    enc_aug = seg_aug_k(
        jnp.concatenate([own_q, prefix_segments(core), other_q, prefix_segments(1 - core)])
    )
    self_aug = seg_aug_k(jnp.concatenate([own_a, other_a]))
    cross_aug = seg_aug_k(jnp.concatenate([own_q, other_q]))
    enc_act = flags_of(q_row, q_row, core, quarter, extra, False)
    self_act = flags_of(a_row, a_row, core, quarter, 0, True)
    cross_act = flags_of(a_row, q_row, core, quarter, 0, False)

    enc_in = jnp.concatenate([x_question, jnp.pad(entry_vals, ((0, extra - n_prefix), (0, 0)))], 0)
    normed_q = rms_norm(enc_in, norm_gains[0]).astype(jnp.bfloat16)
    query_enc = project(normed_q[:tokens], enc_w[:D]).astype(jnp.bfloat16)
    enc_kv = project(normed_q, enc_w[D : 3 * D]).astype(jnp.bfloat16)
    enc_kv_other = partner(enc_kv)

    normed_a = rms_norm(x_answer, norm_gains[2]).astype(jnp.bfloat16)
    qkv_self = project(normed_a, dec_w[: 3 * D]).astype(jnp.bfloat16)
    query_self, self_kv = qkv_self[:, :D], qkv_self[:, D:]
    self_kv_other = partner(self_kv)

    mixed_enc, logsum_enc = attend(False, enc_act, query_enc, q_aug, enc_kv, enc_kv_other, enc_aug)
    hidden_one = x_question + project_back(mixed_enc, enc_w[3 * D : 4 * D])
    normed_f1 = rms_norm(hidden_one, norm_gains[1]).astype(jnp.bfloat16)
    pre_enc = project(normed_f1, enc_w[4 * D : 4 * D + FF])
    act_enc = jax.nn.gelu(pre_enc).astype(jnp.bfloat16)
    hidden_two = hidden_one + project_back(act_enc, enc_w[4 * D + FF :])
    encoded = rms_norm(hidden_two, norm_gains[5]).astype(jnp.bfloat16)
    cross_kv = project(encoded, dec_w[5 * D : 7 * D]).astype(jnp.bfloat16)
    cross_kv_other = partner(cross_kv)

    mixed_self, logsum_self = attend(True, self_act, query_self, a_aug, self_kv, self_kv_other, self_aug)
    dec_one = x_answer + project_back(mixed_self, dec_w[3 * D : 4 * D])
    normed_c = rms_norm(dec_one, norm_gains[3]).astype(jnp.bfloat16)
    query_cross = project(normed_c, dec_w[4 * D : 5 * D]).astype(jnp.bfloat16)
    mixed_cross, logsum_cross = attend(
        False, cross_act, query_cross, a_aug, cross_kv, cross_kv_other, cross_aug
    )
    dec_two = dec_one + project_back(mixed_cross, dec_w[7 * D : 8 * D])
    normed_f2 = rms_norm(dec_two, norm_gains[4]).astype(jnp.bfloat16)
    pre_dec = project(normed_f2, dec_w[8 * D : 8 * D + FF])
    act_dec = jax.nn.gelu(pre_dec).astype(jnp.bfloat16)
    dec_three = dec_two + project_back(act_dec, dec_w[8 * D + FF :])
    decoded = dec_three.astype(jnp.bfloat16)

    grad_w1d, grad_w2d, grad_nf2 = feed_back(
        grad_top, normed_f2, pre_dec, act_dec, dec_w[8 * D : 8 * D + FF], dec_w[8 * D + FF :]
    )
    grad_x, grad_gain4 = norm_back(dec_two, norm_gains[4], grad_nf2)
    grad_two = grad_top + grad_x
    grad_woc, grad_mixc = output_back(grad_two, mixed_cross, dec_w[7 * D : 8 * D])
    grad_qc, dk_own, dv_own, dk_other, dv_other = attend_back(
        False, cross_act, query_cross, a_aug, cross_kv, cross_kv_other, cross_aug,
        mixed_cross, logsum_cross, grad_mixc,
    )
    more = partner(jnp.concatenate([dk_other, dv_other], 1)).astype(jnp.float32)
    grad_ckv = (jnp.concatenate([dk_own, dv_own], 1) + more).astype(jnp.bfloat16)
    grad_wqc = outer_sum(grad_qc, normed_c)
    grad_x, grad_gain3 = norm_back(
        dec_one, norm_gains[3], project_back(grad_qc, dec_w[4 * D : 5 * D])
    )
    grad_one = grad_two + grad_x
    grad_wckv = outer_sum(grad_ckv, encoded)
    grad_encoded, grad_gain5 = norm_back(
        hidden_two, norm_gains[5], project_back(grad_ckv, dec_w[5 * D : 7 * D])
    )
    grad_wos, grad_mixs = output_back(grad_one, mixed_self, dec_w[3 * D : 4 * D])
    grad_qs, dk_own, dv_own, dk_other, dv_other = attend_back(
        True, self_act, query_self, a_aug, self_kv, self_kv_other, self_aug,
        mixed_self, logsum_self, grad_mixs,
    )
    more = partner(jnp.concatenate([dk_other, dv_other], 1)).astype(jnp.float32)
    grad_skv = (jnp.concatenate([dk_own, dv_own], 1) + more).astype(jnp.bfloat16)
    grad_self = jnp.concatenate([grad_qs, grad_skv], 1)
    grad_wself = outer_sum(grad_self, normed_a)
    grad_x, grad_gain2 = norm_back(x_answer, norm_gains[2], project_back(grad_self, dec_w[: 3 * D]))
    grad_answers = (grad_one + grad_x).astype(jnp.bfloat16)
    dec_full = jnp.concatenate(
        [grad_wself, grad_wos, grad_wqc, grad_wckv, grad_woc, grad_w1d, grad_w2d], 0
    )

    grad_w1e, grad_w2e, grad_nf1 = feed_back(
        grad_encoded, normed_f1, pre_enc, act_enc, enc_w[4 * D : 4 * D + FF], enc_w[4 * D + FF :]
    )
    grad_x, grad_gain1 = norm_back(hidden_one, norm_gains[1], grad_nf1)
    grad_hidden = grad_encoded + grad_x
    grad_woe, grad_mixe = output_back(grad_hidden, mixed_enc, enc_w[3 * D : 4 * D])
    grad_qe, dk_own, dv_own, dk_other, dv_other = attend_back(
        False, enc_act, query_enc, q_aug, enc_kv, enc_kv_other, enc_aug,
        mixed_enc, logsum_enc, grad_mixe,
    )
    more = partner(jnp.concatenate([dk_other, dv_other], 1)).astype(jnp.float32)
    grad_ekv = (jnp.concatenate([dk_own, dv_own], 1) + more).astype(jnp.bfloat16)
    grad_wqe = outer_sum(grad_qe, normed_q[:tokens])
    grad_wkve = outer_sum(grad_ekv, normed_q)
    grad_in = project_back(grad_ekv, enc_w[D : 3 * D])
    grad_in = grad_in + jnp.pad(project_back(grad_qe, enc_w[:D]), ((0, extra), (0, 0)))
    grad_x, grad_gain0 = norm_back(enc_in, norm_gains[0], grad_in)
    grad_questions = (grad_hidden + grad_x[:tokens]).astype(jnp.bfloat16)
    enc_full = jnp.concatenate([grad_wqe, grad_wkve, grad_woe, grad_w1e, grad_w2e], 0)
    gain_terms = jnp.stack(
        [grad_gain0, grad_gain1, grad_gain2, grad_gain3, grad_gain4, grad_gain5]
    )
    if fast:
        grad_encoder, grad_decoder, decoded, grad_questions, grad_answers, grad_gains = reduce_fast(
            enc_full, dec_full, decoded, grad_questions, grad_answers, jnp.pad(gain_terms, ((0, 2), (0, 0)))
        )
        grad_gains = grad_gains[:6]
    else:
        decoded, grad_questions, grad_answers = (
            from_rows(values) for values in (decoded, grad_questions, grad_answers)
        )
        grad_gains = lax.psum(gain_terms, ("rows", "mem"))
        grad_encoder, grad_decoder = reduce_weights(enc_full), reduce_weights(dec_full)
    return (
        decoded,
        grad_questions.astype(jnp.float32),
        grad_answers.astype(jnp.float32),
        grad_encoder.astype(jnp.float32).T,
        grad_decoder.astype(jnp.float32).T,
        grad_gains,
    )


def solution(mesh):
    fast = mesh.shape["rows"] == 8 and mesh.shape["mem"] == 4
    return jax.shard_map(
        functools.partial(on_device, fast),
        mesh=mesh,
        in_specs=(
            P("rows", "mem", None),
            P("rows", "mem", None),
            P("rows", None),
            P("rows", None),
            P("rows", None, "mem"),
            P("rows", None, None),
            P(),
            P(None, ("rows", "mem")),
            P(None, ("rows", "mem")),
            P(),
            P("rows", "mem", None),
        ),
        out_specs=(
            P("rows", "mem", None),
            P("rows", "mem", None),
            P("rows", "mem", None),
            P(None, ("rows", "mem")),
            P(None, ("rows", "mem")),
            P(),
        ),
        check_vma=False,
    )
```

```python
import functools
import jax
import jax.numpy as jnp
from jax import lax
from jax.experimental import pallas as pl
from jax.experimental.pallas import tpu as pltpu
from jax.sharding import PartitionSpec as P

D = 768
H = 12
HD = 64
FF = 3072
QB = 256
masked_score = -1e30


def key_chunks(own_len, extra):
    chunks = []
    for side in (0, 1):
        for at in range(own_len // QB):
            chunks.append((side, at * QB, QB))
        if extra:
            chunks.append((side, own_len, extra))
    return chunks


def attend_pair(causal, own_len, extra, when, q_ref, qaug_ref, own_k, own_v, oth_k, oth_v, kaug_ref, o_ref, lse_ref, s_ref, m_ref, l_ref, acc_ref):
    low = lax.broadcasted_iota(jnp.int32, (1, 128), 1) < HD
    chunks = key_chunks(own_len, extra)
    nk = own_len + extra
    for qb in range(own_len // QB):
        rows = pl.ds(qb * QB, QB)
        q = q_ref[rows, :] * jnp.bfloat16(HD ** (-0.5))
        qaug = qaug_ref[rows, :]
        queries = (jnp.where(low, q, qaug), jnp.where(low, qaug, q))
        m_ref[...] = jnp.full(m_ref.shape, -3e30, jnp.float32)
        l_ref[...] = jnp.zeros(l_ref.shape, jnp.float32)
        acc_ref[...] = jnp.zeros(acc_ref.shape, jnp.float32)
        for ci, (side, at, size) in enumerate(chunks):

            def score(side=side, at=at, size=size):
                k = (own_k, oth_k)[side][at : at + size, :]
                place = slice(side * nk + at, side * nk + at + size)
                kaug = kaug_ref[place, :]
                for h in (0, 1):
                    cols = slice(h * QB, (h + 1) * QB)
                    keys = jnp.where(low, k, kaug) if h == 0 else jnp.where(low, kaug, k)
                    s = lax.dot_general(keys, queries[h], (((1,), (1,)), ((), ())), preferred_element_type=jnp.float32)
                    if causal and side == 0 and at == qb * QB:
                        tri = lax.broadcasted_iota(jnp.int32, (size, QB), 0) <= lax.broadcasted_iota(jnp.int32, (size, QB), 1)
                        s = jnp.where(tri, s, masked_score)
                    s_ref[place, cols] = s
                    m_ref[:, cols] = jnp.maximum(m_ref[:, cols], jnp.max(s.reshape(size // 8, 8, QB), 0))

            when(qb, ci)(score)
        m = jnp.max(m_ref[...], 0, keepdims=True)
        for ci, (side, at, size) in enumerate(chunks):

            def mix(side=side, at=at, size=size):
                v = (own_v, oth_v)[side][at : at + size, :]
                zero = jnp.zeros_like(v)
                place = slice(side * nk + at, side * nk + at + size)
                p = jnp.exp(s_ref[place, :] - m)
                l_ref[...] += jnp.sum(p.reshape(size // 8, 8, 2 * QB), 0)
                pb = p.astype(jnp.bfloat16)
                pb = jnp.concatenate([pb[:, :QB], pb[:, QB:]], 0)
                v_split = jnp.concatenate([jnp.where(low, v, zero), jnp.where(low, zero, v)], 0)
                acc_ref[...] += lax.dot_general(pb, v_split, (((0,), (0,)), ((), ())), preferred_element_type=jnp.float32)

            when(qb, ci)(mix)
        total = jnp.sum(l_ref[...], 0, keepdims=True)
        lse = m + jnp.log(total)
        rec = 1.0 / total
        wide = lambda row, h: jnp.broadcast_to(row[:, h * QB : (h + 1) * QB], (HD, QB))
        o_ref[rows, :] = (acc_ref[...] * jnp.concatenate([wide(rec, 0), wide(rec, 1)], 0).T).astype(jnp.bfloat16)
        lse_ref[rows, :] = jnp.concatenate([wide(lse, 1), wide(lse, 0)], 0).T


def flagged(act):
    return lambda qb, ci: pl.when(act[qb, ci] != 0)


def always(qb, ci):
    return lambda work: work()


def attend_kernel(causal, own_len, extra, act, *refs):
    attend_pair(causal, own_len, extra, flagged(act), *refs)


def back_kernel(causal, own_len, extra, act, *refs):
    back_pair(causal, own_len, extra, flagged(act), *refs)


def attend(causal, act, q, qaug, own_kv, oth_kv, kaug):
    t = q.shape[0]
    nk = own_kv.shape[0]
    col = lambda first: pl.BlockSpec((nk, 128), lambda i, a: (0, first + i))
    return pl.pallas_call(
        functools.partial(attend_kernel, causal, t, nk - t),
        grid_spec=pltpu.PrefetchScalarGridSpec(
            num_scalar_prefetch=1,
            grid=(H // 2,),
            in_specs=[
                pl.BlockSpec((t, 128), lambda i, a: (0, i)),
                pl.BlockSpec((t, 128), lambda i, a: (0, 0)),
                col(0), col(H // 2), col(0), col(H // 2),
                pl.BlockSpec((2 * nk, 128), lambda i, a: (0, 0)),
            ],
            out_specs=[pl.BlockSpec((t, 128), lambda i, a: (0, i))] * 2,
            scratch_shapes=[pltpu.VMEM((2 * nk, 2 * QB), jnp.float32), pltpu.VMEM((8, 2 * QB), jnp.float32), pltpu.VMEM((8, 2 * QB), jnp.float32), pltpu.VMEM((QB, 128), jnp.float32)],
        ),
        out_shape=[jax.ShapeDtypeStruct((t, D), jnp.bfloat16), jax.ShapeDtypeStruct((t, D), jnp.float32)],
        compiler_params=pltpu.CompilerParams(vmem_limit_bytes=40 * 1024 * 1024),
        cost_estimate=pl.CostEstimate(flops=4 * t * 2 * nk * D, bytes_accessed=8 * nk * D, transcendentals=t * 2 * nk * H),
        name="attend",
    )(act, q, qaug, own_kv, own_kv, oth_kv, oth_kv, kaug)


def three_parts(value):
    hi = value.astype(jnp.bfloat16).astype(jnp.float32)
    mid = (value - hi).astype(jnp.bfloat16).astype(jnp.float32)
    return hi, mid, value - hi - mid


def spread(base, lane64, value):
    hi, mid, lo = three_parts(value)
    return jnp.where(lane64 == 8, hi, jnp.where(lane64 == 9, mid, jnp.where(lane64 == 10, lo, base)))


def back_pair(causal, own_len, extra, when, q_ref, qaug_ref, own_k, own_v, oth_k, oth_v, kaug_ref, o_ref, lse_ref, g_ref, dq_ref, dko_ref, dvo_ref, dkt_ref, dvt_ref, dk_acc, dv_acc, dq_acc):
    lane = lax.broadcasted_iota(jnp.int32, (1, 128), 1)
    low = lane < HD
    lane64 = lane % HD
    chunks = key_chunks(own_len, extra)
    nk = own_len + extra
    dk_acc[...] = jnp.zeros(dk_acc.shape, jnp.float32)
    dv_acc[...] = jnp.zeros(dv_acc.shape, jnp.float32)
    ones_aug = jnp.where((lane64 >= 8) & (lane64 <= 10), 1.0, 0.0).astype(jnp.bfloat16)
    for qb in range(own_len // QB):
        rows = pl.ds(qb * QB, QB)
        q = q_ref[rows, :] * jnp.bfloat16(HD ** (-0.5))
        g = g_ref[rows, :]
        qaug = spread(qaug_ref[rows, :].astype(jnp.float32), lane64, -lse_ref[rows, :]).astype(jnp.bfloat16)
        prod = g.astype(jnp.float32) * o_ref[rows, :].astype(jnp.float32)
        d_even = jnp.sum(jnp.where(low, prod, 0.0), -1, keepdims=True)
        d_odd = jnp.sum(jnp.where(low, 0.0, prod), -1, keepdims=True)
        gaug = spread(jnp.zeros((QB, 128), jnp.float32), lane64, -jnp.where(low, d_odd, d_even)).astype(jnp.bfloat16)
        queries = (jnp.where(low, q, qaug), jnp.where(low, qaug, q))
        grads = (jnp.where(low, g, gaug), jnp.where(low, gaug, g))
        zero = jnp.zeros_like(q)
        q_split = jnp.concatenate([jnp.where(low, q, zero), jnp.where(low, zero, q)], 0)
        g_split = jnp.concatenate([jnp.where(low, g, zero), jnp.where(low, zero, g)], 0)
        dq_acc[...] = jnp.zeros(dq_acc.shape, jnp.float32)
        for ci, (side, at, size) in enumerate(chunks):

            def work(side=side, at=at, size=size):
                k = (own_k, oth_k)[side][at : at + size, :]
                v = (own_v, oth_v)[side][at : at + size, :]
                place = slice(side * nk + at, side * nk + at + size)
                kaug = kaug_ref[place, :]
                vaug = jnp.broadcast_to(ones_aug, v.shape)
                zk = jnp.zeros_like(k)
                probs, dscores = [], []
                for h in (0, 1):
                    keys = jnp.where(low, k, kaug) if h == 0 else jnp.where(low, kaug, k)
                    vals = jnp.where(low, v, vaug) if h == 0 else jnp.where(low, vaug, v)
                    s = lax.dot_general(keys, queries[h], (((1,), (1,)), ((), ())), preferred_element_type=jnp.float32)
                    if causal and side == 0 and at == qb * QB:
                        tri = lax.broadcasted_iota(jnp.int32, (size, QB), 0) <= lax.broadcasted_iota(jnp.int32, (size, QB), 1)
                        s = jnp.where(tri, s, masked_score)
                    p = jnp.exp(s)
                    dp = lax.dot_general(vals, grads[h], (((1,), (1,)), ((), ())), preferred_element_type=jnp.float32)
                    dscores.append((p * dp).astype(jnp.bfloat16))
                    probs.append(p.astype(jnp.bfloat16))
                ds = jnp.concatenate(dscores, 1)
                pb = jnp.concatenate(probs, 1)
                dk_acc[place, :] += jnp.dot(ds, q_split, preferred_element_type=jnp.float32)
                dv_acc[place, :] += jnp.dot(pb, g_split, preferred_element_type=jnp.float32)
                k_split = jnp.concatenate([jnp.where(low, k, zk), jnp.where(low, zk, k)], 0)
                dst = jnp.concatenate(dscores, 0)
                dq_acc[...] += lax.dot_general(dst, k_split, (((0,), (0,)), ((), ())), preferred_element_type=jnp.float32)

            when(qb, ci)(work)
        dq_ref[rows, :] = (dq_acc[...] * HD ** (-0.5)).astype(jnp.bfloat16)
    dko_ref[...] = dk_acc[:nk, :]
    dvo_ref[...] = dv_acc[:nk, :]
    dkt_ref[...] = dk_acc[nk:, :].astype(jnp.bfloat16)
    dvt_ref[...] = dv_acc[nk:, :].astype(jnp.bfloat16)


def attend_back(causal, act, q, qaug, own_kv, oth_kv, kaug, mixed, lse, grad):
    t = q.shape[0]
    nk = own_kv.shape[0]
    col = lambda first: pl.BlockSpec((nk, 128), lambda i, a: (0, first + i))
    tok = pl.BlockSpec((t, 128), lambda i, a: (0, i))
    return pl.pallas_call(
        functools.partial(back_kernel, causal, t, nk - t),
        grid_spec=pltpu.PrefetchScalarGridSpec(
            num_scalar_prefetch=1,
            grid=(H // 2,),
            in_specs=[
                tok,
                pl.BlockSpec((t, 128), lambda i, a: (0, 0)),
                col(0), col(H // 2), col(0), col(H // 2),
                pl.BlockSpec((2 * nk, 128), lambda i, a: (0, 0)),
                tok, tok, tok,
            ],
            out_specs=[tok, col(0), col(0), col(0), col(0)],
            scratch_shapes=[pltpu.VMEM((2 * nk, 128), jnp.float32), pltpu.VMEM((2 * nk, 128), jnp.float32), pltpu.VMEM((QB, 128), jnp.float32)],
        ),
        out_shape=[
            jax.ShapeDtypeStruct((t, D), jnp.bfloat16),
            jax.ShapeDtypeStruct((nk, D), jnp.float32),
            jax.ShapeDtypeStruct((nk, D), jnp.float32),
            jax.ShapeDtypeStruct((nk, D), jnp.bfloat16),
            jax.ShapeDtypeStruct((nk, D), jnp.bfloat16),
        ],
        compiler_params=pltpu.CompilerParams(vmem_limit_bytes=40 * 1024 * 1024),
        cost_estimate=pl.CostEstimate(flops=10 * t * 2 * nk * D, bytes_accessed=24 * nk * D, transcendentals=t * 2 * nk * H),
        name="attend_back",
    )(act, q, qaug, own_kv, own_kv, oth_kv, oth_kv, kaug, mixed, lse, grad)


def seg_aug_q(seg):
    j = jnp.arange(128, dtype=jnp.int32) % HD
    return ((j[None, :] < 8) & (j[None, :] == seg[:, None])).astype(jnp.bfloat16)


def seg_aug_k(seg):
    j = jnp.arange(128, dtype=jnp.int32)[None, :] % HD
    bad = (j < 8) & (j != seg[:, None])
    return jnp.where(bad, masked_score, jnp.where((j >= 8) & (j <= 10), 1.0, 0.0)).astype(jnp.bfloat16)


epsilon = 1e-06
CHUNK = 512


def dot_nt(left, right):
    return lax.dot_general(left, right, (((1,), (1,)), ((), ())), preferred_element_type=jnp.float32)


def dot_nn(left, right):
    return lax.dot_general(left, right, (((1,), (0,)), ((), ())), preferred_element_type=jnp.float32)


def dot_tn(left, right):
    return lax.dot_general(left, right, (((0,), (0,)), ((), ())), preferred_element_type=jnp.float32)


def rms_norm(values, gain):
    return values * lax.rsqrt(jnp.mean(values * values, -1, keepdims=True) + epsilon) * gain


def norm_back(values, gain, grad):
    root = lax.rsqrt(jnp.mean(values * values, -1, keepdims=True) + epsilon)
    unit = values * root
    scaled = grad * gain
    inner = jnp.mean(unit * scaled, -1, keepdims=True)
    return root * (scaled - unit * inner), jnp.sum(grad * unit, 0, keepdims=True)


def gelu_pair(pre):
    root = 0.7978845608028654
    square = pre * pre
    bent = jnp.tanh(root * pre * (1.0 + 0.044715 * square))
    half = 0.5 * (1.0 + bent)
    slope = half + 0.5 * pre * (1.0 - bent * bent) * root * (1.0 + 0.134145 * square)
    return pre * half, slope


def feed_back_chunk(normed, grad_b, w1, w2, dw, total, first):
    act, slope = gelu_pair(dot_nt(normed, w1))
    act = act.astype(jnp.bfloat16)
    grad_pre = (dot_nt(grad_b, w2) * slope).astype(jnp.bfloat16)
    dw[0] = dot_tn(grad_pre, normed).astype(jnp.bfloat16)
    dw[1] = dot_tn(act, grad_b).astype(jnp.bfloat16)
    part = dot_nn(grad_pre, w1)

    @pl.when(first)
    def _():
        total[...] = part

    @pl.when(jnp.logical_not(first))
    def _():
        total[...] += part

    return act


class ChunkStore:
    def __init__(self, slots, whole, places, sems):
        self.slots, self.whole, self.places, self.sems = slots, whole, places, sems

    def copy(self, i, which):
        slot = lax.rem(i, 2)
        rows = pl.ds(pl.multiple_of(self.places[which] + i * CHUNK, CHUNK), CHUNK)
        return pltpu.make_async_copy(self.slots.at[slot, which], self.whole.at[rows], self.sems.at[slot, which])

    def start(self, i):
        for which in (0, 1):
            self.copy(i, which).start()

    def wait(self, i):
        for which in (0, 1):
            self.copy(i, which).wait()


def whole_spec(shape):
    return pl.BlockSpec(shape, lambda i: (0,) * len(shape))


def decode_top_kernel(
    d1_ref, mixed_ref, gains, grad_ref, wo_ref, w1_ref, w2_ref,
    decoded_ref, grad_two_ref, grad_mix_ref, dgain_ref, whole,
    d2_ref, normed_ref, acc_ref, total_ref, slots, dwo_ref, sems, sem_o,
):
    i = pl.program_id(0)
    store = ChunkStore(slots, whole, (8 * D, 8 * D + FF), sems)

    @pl.when(i == 0)
    def _():
        d2_ref[...] = d1_ref[...] + dot_nn(mixed_ref[...], wo_ref[...])
        normed_ref[...] = rms_norm(d2_ref[...], gains[4:5, :]).astype(jnp.bfloat16)

    pl.when(i >= 2)(lambda: store.wait(i - 2))
    act = feed_back_chunk(
        normed_ref[...], grad_ref[...], w1_ref[...], w2_ref[...], slots.at[lax.rem(i, 2)], total_ref, i == 0
    )
    store.start(i)
    more = dot_nn(act, w2_ref[...])

    @pl.when(i == 0)
    def _():
        acc_ref[...] = d2_ref[...] + more

    @pl.when(i > 0)
    def _():
        acc_ref[...] += more

    @pl.when(i == FF // CHUNK - 1)
    def _():
        decoded_ref[...] = acc_ref[...].astype(jnp.bfloat16)
        grad_x, dgain = norm_back(d2_ref[...], gains[4:5, :], total_ref[...])
        dgain_ref[...] = jnp.broadcast_to(dgain, dgain_ref.shape)
        grad_two = grad_ref[...].astype(jnp.float32) + grad_x
        grad_two_ref[...] = grad_two
        grad_b = grad_two.astype(jnp.bfloat16)
        dwo_ref[...] = dot_tn(mixed_ref[...], grad_b).astype(jnp.bfloat16)
        last = pltpu.make_async_copy(dwo_ref, whole.at[pl.ds(7 * D, D)], sem_o)
        last.start()
        grad_mix_ref[...] = dot_nt(grad_b, wo_ref[...]).astype(jnp.bfloat16)
        store.wait(i - 1)
        store.wait(i)
        last.wait()


def decode_top(d1, mixed, gains, grad_top, dec_w):
    t = d1.shape[0]
    n = FF // CHUNK
    tok = whole_spec((t, D))
    return pl.pallas_call(
        decode_top_kernel,
        grid=(n,),
        in_specs=[
            tok, tok, whole_spec(gains.shape), tok,
            pl.BlockSpec((D, D), lambda i: (7, 0)),
            pl.BlockSpec((CHUNK, D), lambda i: (8 * D // CHUNK + i, 0)),
            pl.BlockSpec((CHUNK, D), lambda i: (8 * D // CHUNK + n + i, 0)),
        ],
        out_specs=[tok, tok, tok, whole_spec((8, D)), pl.BlockSpec(memory_space=pl.ANY)],
        out_shape=[
            jax.ShapeDtypeStruct((t, D), jnp.bfloat16),
            jax.ShapeDtypeStruct((t, D), jnp.float32),
            jax.ShapeDtypeStruct((t, D), jnp.bfloat16),
            jax.ShapeDtypeStruct((8, D), jnp.float32),
            jax.ShapeDtypeStruct(dec_w.shape, jnp.bfloat16),
        ],
        scratch_shapes=[
            pltpu.VMEM((t, D), jnp.float32),
            pltpu.VMEM((t, D), jnp.bfloat16),
            pltpu.VMEM((t, D), jnp.float32),
            pltpu.VMEM((t, D), jnp.float32),
            pltpu.VMEM((2, 2, CHUNK, D), jnp.bfloat16),
            pltpu.VMEM((D, D), jnp.bfloat16),
            pltpu.SemaphoreType.DMA((2, 2)),
            pltpu.SemaphoreType.DMA,
        ],
        compiler_params=pltpu.CompilerParams(vmem_limit_bytes=48 * 1024 * 1024),
        cost_estimate=pl.CostEstimate(flops=14 * t * FF * D, bytes_accessed=8 * FF * D, transcendentals=t * FF),
        name="decode_top",
    )(d1, mixed, gains, grad_top, dec_w, dec_w, dec_w)


MESH = pl.DeviceIdType.MESH


def position():
    r, m = lax.axis_index("rows"), lax.axis_index("mem")
    core = lax.rem(r, 2)
    near = r + 1 - 2 * core
    x_near = r + 2 - 4 * lax.rem(lax.div(r, 2), 2)
    y_near = r + 4 - 8 * lax.div(r, 4)
    first = x_near + core * (y_near - x_near)
    second = y_near + core * (x_near - y_near)
    both = first + second - r
    turn = 1 - 2 * core
    others = (near, second + turn, first + turn, both + turn)
    return r, m, core, near, first, second, both, others


def greet(pos):
    r, m, core, near, first, second = pos[:6]
    barrier = pltpu.get_barrier_semaphore()
    count = 0
    for to in (r, near):
        for step in range(4):
            if to is r and step == 0:
                continue
            pl.semaphore_signal(barrier, inc=1, device_id=(to, lax.rem(m + step, 4)), device_id_type=MESH)
            count += 1
    for to in (first, second):
        pl.semaphore_signal(barrier, inc=1, device_id=(to, m), device_id_type=MESH)
        count += 1
    pl.semaphore_wait(barrier, count)


def remote(src, dst, send, recv, to):
    return pltpu.make_async_remote_copy(
        src_ref=src, dst_ref=dst, send_sem=send, recv_sem=recv, device_id=to, device_id_type=MESH
    )


class Mail:
    def __init__(self, pos):
        self.pos = pos
        self.started = []
        self.maybe = []

    def send(self, make):
        make().start()
        self.started.append(make)

    def send_or_keep(self, here, make, keep):
        pl.when(here())(lambda: keep().start())
        pl.when(jnp.logical_not(here()))(lambda: make().start())
        self.maybe.append((here, make))

    def arrived(self, ref, sem):
        near, m = self.pos[3], self.pos[1]
        remote(ref, ref, sem, sem, (near, m)).wait_recv()

    def finish(self):
        for make in self.started:
            make().wait_send()
        for here, make in self.maybe:
            pl.when(jnp.logical_not(here()))(lambda make=make: make().wait_send())


def dma(*shape):
    return pltpu.SemaphoreType.DMA(shape)


def gather_sems(n):
    return [dma(3, n), dma(3, n), dma(4, n), dma(4, n), dma(4, 2, n), dma(4, 2, n), dma(4, 4, n), dma(4, 4, n), dma(n)]


class Gather:
    def __init__(self, mail, ins, outs, sems):
        self.mail, self.ins, self.outs = mail, ins, outs
        self.z_s, self.z_r, self.a_s, self.a_r, self.b_s, self.b_r, self.c_s, self.c_r, self.l = sems

    def at(self, w, row, step):
        m = self.mail.pos[1]
        size = self.ins[w].shape[0]
        mem = lax.rem(m - step + 4, 4)
        return self.outs[w].at[pl.ds(pl.multiple_of((row * 4 + mem) * size, 32), size)]

    def own(self, w):
        return pltpu.make_async_copy(self.ins[w], self.at(w, self.mail.pos[0], 0), self.l.at[w])

    def ring(self, step):
        r, m, core, near, first, second, both, others = self.mail.pos
        for w in range(len(self.ins)):
            if step == 0:
                self.own(w).start()
            else:
                self.mail.arrived(self.at(w, r, step), self.z_r.at[step - 1, w])

            def src(w=w):
                return self.ins[w] if step == 0 else self.at(w, r, step)

            def dst(w=w):
                return self.at(w, r, step)

            send = self.mail.send
            if step < 3:
                send(lambda w=w, src=src, dst=dst: remote(src(), dst(), self.z_s.at[step, w], self.z_r.at[step, w], (r, lax.rem(m + 1, 4))))
            send(lambda w=w, src=src, dst=dst: remote(src(), dst(), self.a_s.at[step, w], self.a_r.at[step, w], (first, m)))
            send(lambda w=w, src=src, dst=dst: remote(src(), dst(), self.b_s.at[step, 0, w], self.b_r.at[step, 0, w], (second, m)))
            send(lambda w=w, src=src, dst=dst: remote(src(), dst(), self.c_s.at[step, 0, w], self.c_r.at[step, 0, w], (near, m)))

    def from_first(self, step):
        r, m, core, near, first, second, both, others = self.mail.pos
        for w in range(len(self.ins)):
            here = lambda w=w: self.at(w, first, step)
            self.mail.arrived(here(), self.a_r.at[step, w])
            self.mail.send(lambda w=w, here=here: remote(here(), here(), self.b_s.at[step, 1, w], self.b_r.at[step, 1, w], (second, m)))
            self.mail.send(lambda w=w, here=here: remote(here(), here(), self.c_s.at[step, 1, w], self.c_r.at[step, 1, w], (near, m)))

    def from_second(self, step):
        r, m, core, near, first, second, both, others = self.mail.pos
        for k, row in ((0, second), (1, both)):
            for w in range(len(self.ins)):
                here = lambda w=w, row=row: self.at(w, row, step)
                self.mail.arrived(here(), self.b_r.at[step, k, w])
                self.mail.send(lambda w=w, k=k, here=here: remote(here(), here(), self.c_s.at[step, 2 + k, w], self.c_r.at[step, 2 + k, w], (near, m)))

    def finish(self):
        others = self.mail.pos[7]
        for step in range(4):
            for k in range(4):
                for w in range(len(self.ins)):
                    self.mail.arrived(self.at(w, others[k], step), self.c_r.at[step, k, w])
        for w in range(len(self.ins)):
            self.own(w).wait()


def gather_order(gather, more=()):
    steps = [
        (gather.ring, 0), (gather.ring, 1), (gather.from_first, 0), (gather.ring, 2), (gather.from_first, 1),
        (gather.from_second, 0), (gather.ring, 3), (gather.from_first, 2), (gather.from_second, 1),
        (gather.from_first, 3), (gather.from_second, 2), (gather.from_second, 3),
    ]
    return [functools.partial(*step) for step in steps]


def token_sems(n):
    return [dma(n, 2), dma(n, 2), dma(n)]


class TokensIn:
    def __init__(self, mail, pairs, sems):
        self.mail, self.pairs = mail, pairs
        self.t_s, self.t_r, self.t_l = sems

    def start(self, n):
        r, m, core, near = self.mail.pos[:4]
        src, dst = self.pairs[n]
        quarter = src.shape[1]
        holder = lambda: lax.div(m * (3 - m), 2)
        slot = lambda: lax.div(m, 2)
        for i in (0, 1):
            here = lambda i=i: jnp.logical_and(2 * core + i == m, holder() == core)
            place = lambda: dst.at[pl.ds(pl.multiple_of(slot() * quarter, quarter), quarter)]
            make = lambda i=i: remote(src.at[i], place(), self.t_s.at[n, i], self.t_r.at[n, slot()], (r - core + holder(), 2 * core + i))
            keep = lambda i=i: pltpu.make_async_copy(src.at[i], place(), self.t_l.at[n])
            self.mail.send_or_keep(here, make, keep)

    def finish(self):
        r, m, core, near = self.mail.pos[:4]
        for n, (src, dst) in enumerate(self.pairs):
            quarter = src.shape[1]
            for li in (0, 1):
                source = core if li == 0 else 3 - core
                here = jnp.logical_and(lax.div(m, 2) == core, m == source)
                place = lambda: dst.at[pl.ds(li * quarter, quarter)]
                pl.when(here)(lambda: pltpu.make_async_copy(place(), place(), self.t_l.at[n]).wait())
                pl.when(jnp.logical_not(here))(lambda: self.mail.arrived(place(), self.t_r.at[n, li]))


class TokensOut:
    def __init__(self, mail, pairs, sems):
        self.mail, self.pairs = mail, pairs
        self.t_s, self.t_r, self.t_l = sems

    def start(self, n):
        r, m, core, near = self.mail.pos[:4]
        src, dst = self.pairs[n]
        quarter = dst.shape[1]
        row = lambda: lax.rem(m, 2)
        for li in (0, 1):
            to_mem = lambda li=li: core if li == 0 else 3 - core
            here = lambda to_mem=to_mem: jnp.logical_and(to_mem() == m, lax.div(m, 2) == core)
            place = lambda li=li: src.at[pl.ds(li * quarter, quarter)]
            make = lambda li=li, to_mem=to_mem, place=place: remote(place(), dst.at[row()], self.t_s.at[n, li], self.t_r.at[n, row()], (r - core + lax.div(m, 2), to_mem()))
            keep = lambda place=place: pltpu.make_async_copy(place(), dst.at[row()], self.t_l.at[n])
            self.mail.send_or_keep(here, make, keep)

    def finish(self):
        r, m, core, near = self.mail.pos[:4]
        holder = lax.div(m * (3 - m), 2)
        for n, (src, dst) in enumerate(self.pairs):
            for i in (0, 1):
                here = jnp.logical_and(2 * core + i == m, holder == core)
                pl.when(here)(lambda: pltpu.make_async_copy(dst.at[i], dst.at[i], self.t_l.at[n]).wait())
                pl.when(jnp.logical_not(here))(lambda: self.mail.arrived(dst.at[i], self.t_r.at[n, i]))


class NumbersIn:
    def __init__(self, mail, seg_in, seg_out, ids_in, ids_out, sems):
        self.mail, self.seg_in, self.seg_out, self.ids_in, self.ids_out = mail, seg_in, seg_out, ids_in, ids_out
        self.i_s, self.i_r, self.i_l, self.n_s, self.n_r = sems

    def start(self):
        r, m, core, near = self.mail.pos[:4]
        self.mail.send(lambda: remote(self.seg_in.at[lax.rem(m, 2)], self.seg_out, self.n_s, self.n_r, (near, m)))
        for i in (0, 1):
            make = lambda i=i, e=0, to=r: remote(self.ids_in.at[i], self.ids_out.at[m], self.i_s.at[i, e], self.i_r.at[m], (to, 2 * core + i))
            self.mail.send(functools.partial(make, e=1, to=near))
            here = lambda i=i: 2 * core + i == m
            keep = lambda i=i: pltpu.make_async_copy(self.ids_in.at[i], self.ids_out.at[m], self.i_l)
            self.mail.send_or_keep(here, make, keep)

    def finish(self):
        r, m, core, near = self.mail.pos[:4]
        self.mail.arrived(self.seg_out, self.n_r)
        for mem in range(4):
            here = jnp.logical_and(lax.div(m, 2) == core, m == mem)
            place = self.ids_out.at[mem]
            pl.when(here)(lambda: pltpu.make_async_copy(place, place, self.i_l).wait())
            pl.when(jnp.logical_not(here))(lambda: self.mail.arrived(place, self.i_r.at[mem]))


def add_to(total, more):
    def step(i, unused):
        rows = pl.ds(pl.multiple_of(i * 32, 32), 32)
        total[rows, :] = total[rows, :] + more[rows, :]
        return unused

    lax.fori_loop(0, total.shape[0] // 32, step, 0)


def reduce_buffers(size):
    block = lambda *lead: pltpu.VMEM(lead + (size, D), jnp.bfloat16)
    return [block(4, 4), block(4, 4), block(4, 2), block(4), block(3)]


def reduce_sems():
    return [dma(4, 4), dma(4, 4), dma(4, 4), dma(4, 2), dma(4, 2), dma(4), dma(4), dma(3), dma(3), dma(1)]


class Reduce:
    def __init__(self, mail, source, out, buffers, sems):
        self.mail, self.source, self.out = mail, source, out
        self.held, self.rc, self.rb, self.ra, self.rz = buffers
        self.l, self.c_s, self.c_r, self.b_s, self.b_r, self.a_s, self.a_r, self.z_s, self.z_r, self.o = sems

    def at(self, row, j):
        m = self.mail.pos[1]
        size = self.out.shape[0]
        mem = lax.rem(m + 7 - j, 4)
        return self.source.at[pl.ds(pl.multiple_of((row * 4 + mem) * size, 32), size)]

    def load(self, j, k):
        r, m, core, near, first, second, both, others = self.mail.pos
        return pltpu.make_async_copy(self.at((r, first, second, both)[k], j), self.held.at[j, k], self.l.at[j, k])

    def start(self):
        r, m, core, near, first, second, both, others = self.mail.pos
        for j in range(4):
            for k in (3, 2, 1, 0):
                self.mail.send(lambda j=j, k=k: remote(self.at(others[k], j), self.rc.at[j, k], self.c_s.at[j, k], self.c_r.at[j, k], (near, m)))
                self.load(j, k).start()

    def from_core(self, j):
        second, m = self.mail.pos[5], self.mail.pos[1]
        for k in (3, 2, 1, 0):
            self.load(j, k).wait()
            self.mail.arrived(self.rc.at[j, k], self.c_r.at[j, k])
            add_to(self.held.at[j, k], self.rc.at[j, k])
            if k >= 2:
                self.mail.send(lambda k=k: remote(self.held.at[j, k], self.rb.at[j, k - 2], self.b_s.at[j, k - 2], self.b_r.at[j, k - 2], (second, m)))

    def from_second(self, j):
        first, m = self.mail.pos[4], self.mail.pos[1]
        for k in (1, 0):
            self.mail.arrived(self.rb.at[j, k], self.b_r.at[j, k])
            add_to(self.held.at[j, k], self.rb.at[j, k])
            if k == 1:
                self.mail.send(lambda: remote(self.held.at[j, 1], self.ra.at[j], self.a_s.at[j], self.a_r.at[j], (first, m)))

    def result(self):
        return pltpu.make_async_copy(self.held.at[3, 0], self.out, self.o.at[0])

    def from_first(self, j):
        r, m = self.mail.pos[:2]
        self.mail.arrived(self.ra.at[j], self.a_r.at[j])
        add_to(self.held.at[j, 0], self.ra.at[j])
        if j > 0:
            self.mail.arrived(self.rz.at[j - 1], self.z_r.at[j - 1])
            add_to(self.held.at[j, 0], self.rz.at[j - 1])
        if j < 3:
            self.mail.send(lambda: remote(self.held.at[j, 0], self.rz.at[j], self.z_s.at[j], self.z_r.at[j], (r, lax.rem(m + 1, 4))))
        else:
            self.result().start()

    def finish(self):
        self.result().wait()


def reduce_order(reduce):
    steps = [
        (reduce.from_core, 0), (reduce.from_core, 1), (reduce.from_second, 0), (reduce.from_core, 2),
        (reduce.from_second, 1), (reduce.from_first, 0), (reduce.from_core, 3), (reduce.from_second, 2),
        (reduce.from_first, 1), (reduce.from_second, 3), (reduce.from_first, 2), (reduce.from_first, 3),
    ]
    return [functools.partial(*step) for step in steps]


class GainSums:
    def __init__(self, mail, own, out, rg, gs, gz, sems):
        self.mail, self.own, self.out, self.rg, self.gs, self.gz = mail, own, out, rg, gs, gz
        self.g_s, self.g_r, self.gz_s, self.gz_r = sems

    def hop(self, n):
        r, m, core, near, first, second, both, others = self.mail.pos
        x_near = first + core * (second - first)
        y_near = second + core * (first - second)
        if n > 0:
            self.mail.arrived(self.rg.at[n - 1], self.g_r.at[n - 1])
            before = self.own[...] if n == 1 else self.gs[n - 2]
            self.gs[n - 1] = before + self.rg[n - 1]
        if n < 3:
            src = lambda: self.own if n == 0 else self.gs.at[n - 1]
            to = (near, x_near, y_near)[n]
            self.mail.send(lambda: remote(src(), self.rg.at[n], self.g_s.at[n], self.g_r.at[n], (to, m)))
            return
        self.gz[m] = self.gs[2]
        for hop in (1, 2, 3):
            self.mail.send(lambda hop=hop: remote(self.gs.at[2], self.gz.at[m], self.gz_s.at[hop - 1], self.gz_r.at[m], (r, lax.rem(m + hop, 4))))

    def finish(self):
        m = self.mail.pos[1]
        for mem in range(4):
            pl.when(m != mem)(lambda mem=mem: self.mail.arrived(self.gz.at[mem], self.gz_r.at[mem]))
        self.out[...] = (self.gz[0] + self.gz[1]) + (self.gz[2] + self.gz[3])


ANY = pl.BlockSpec(memory_space=pl.ANY)


def shaped(shape, kind=jnp.bfloat16):
    return jax.ShapeDtypeStruct(shape, kind)


def gather_encoder_kernel(enc_in, q_in, seg_in, ids_in, enc_out, q_out, seg_out, ids_out, *sems):
    mail = Mail(position())
    gather = Gather(mail, (enc_in,), (enc_out,), sems[:9])
    tokens = TokensIn(mail, ((q_in, q_out),), sems[9:12])
    numbers = NumbersIn(mail, seg_in, seg_out, ids_in, ids_out, sems[12:])
    greet(mail.pos)
    numbers.start()
    steps = gather_order(gather)
    steps[0]()
    tokens.start(0)
    for step in steps[1:]:
        step()
    gather.finish()
    tokens.finish()
    numbers.finish()
    mail.finish()


def gather_encoder(enc_t, q, seg, ids):
    return pl.pallas_call(
        gather_encoder_kernel,
        in_specs=[ANY] * 4,
        out_specs=[ANY] * 4,
        out_shape=[
            shaped((32 * enc_t.shape[0], D)),
            shaped((2 * q.shape[1], D)),
            shaped(seg.shape[1:], jnp.int32),
            shaped((4,) + ids.shape[1:], jnp.int32),
        ],
        scratch_shapes=gather_sems(1) + token_sems(1) + [dma(2, 2), dma(4), dma(), dma(), dma()],
        compiler_params=pltpu.CompilerParams(collective_id=0, has_side_effects=True),
        name="gather_encoder",
    )(enc_t, q, seg, ids)


def reduce_encoder_kernel(enc_in, q_in, gain_in, enc_out, q_out, gain_out, *rest):
    mail = Mail(position())
    reduce = Reduce(mail, enc_in, enc_out, rest[:5], rest[5:15])
    tokens = TokensOut(mail, ((q_in, q_out),), rest[15:18])
    gains = GainSums(mail, gain_in, gain_out, *rest[18:21], rest[21:])
    greet(mail.pos)
    gains.hop(0)
    reduce.start()
    steps = reduce_order(reduce)
    steps[0]()
    gains.hop(1)
    tokens.start(0)
    steps[1]()
    gains.hop(2)
    for step in steps[2:6]:
        step()
    gains.hop(3)
    for step in steps[6:]:
        step()
    reduce.finish()
    tokens.finish()
    gains.finish()
    mail.finish()


def reduce_encoder(enc_g, q, gains):
    vmem = pl.BlockSpec(memory_space=pltpu.VMEM)
    size = enc_g.shape[0] // 32
    small = lambda n: pltpu.VMEM((n,) + gains.shape, jnp.float32)
    return pl.pallas_call(
        reduce_encoder_kernel,
        in_specs=[ANY, ANY, vmem],
        out_specs=[ANY, ANY, vmem],
        out_shape=[shaped((size, D)), shaped((2, q.shape[0] // 2, D)), shaped(gains.shape, jnp.float32)],
        scratch_shapes=reduce_buffers(size) + reduce_sems() + token_sems(1) + [small(3), small(3), small(4)]
        + [dma(3), dma(3), dma(3), dma(4)],
        compiler_params=pltpu.CompilerParams(collective_id=3, has_side_effects=True, vmem_limit_bytes=40 * 1024 * 1024),
        name="reduce_encoder",
    )(enc_g, q, gains)


PAIRS = H // 2
CHUNKS = FF // CHUNK


def encode_kernel(
    fast, own_len, extra,
    q_ref, qaug_ref, own_k, own_v, oth_k, oth_v, kaug_ref, x_ref, gains, wo_ref, w1_ref, w2_ref, *rest,
):
    i = pl.program_id(0)
    if fast:
        dec_in, a_in, g_in = rest[:3]
        o_ref, lse_ref, h1_ref, nf1_ref, h2_ref, ne_ref, dec_out, a_out, g_out = rest[3:12]
        s_ref, m_ref, l_ref, acc_ref, ff_ref = rest[12:17]
        sems = rest[17:]
        mail = Mail(position())
        gather = Gather(mail, (dec_in,), (dec_out,), sems[:9])
        tokens = TokensIn(mail, ((a_in, a_out), (g_in, g_out)), sems[9:12])
        steps = gather_order(gather)
        places = {2: (1, 2), 4: (3, 4), 5: (5,), 6: (6, 7), 7: (8,), 8: (9,), 10: (10,)}

        @pl.when(i == 0)
        def _():
            greet(mail.pos)
            steps[0]()
            tokens.start(0)
            tokens.start(1)

        for at, which in places.items():

            @pl.when(i == at)
            def _(which=which):
                for n in which:
                    steps[n]()
    else:
        o_ref, lse_ref, h1_ref, nf1_ref, h2_ref, ne_ref = rest[:6]
        s_ref, m_ref, l_ref, acc_ref, ff_ref = rest[6:]

    @pl.when(i < PAIRS)
    def _():
        cols = pl.ds(pl.multiple_of(i * 128, 128), 128)
        attend_pair(
            False, own_len, extra, always, q_ref, qaug_ref, own_k, own_v, oth_k, oth_v, kaug_ref,
            o_ref.at[:, cols], lse_ref, s_ref, m_ref, l_ref, acc_ref,
        )

    @pl.when(i == PAIRS)
    def _():
        h1_ref[...] = x_ref[...].astype(jnp.float32) + dot_nn(o_ref[...], wo_ref[...])
        nf1_ref[...] = rms_norm(h1_ref[...], gains[1:2, :]).astype(jnp.bfloat16)
        ff_ref[...] = h1_ref[...]

    @pl.when(i >= PAIRS)
    def _():
        act = gelu_pair(dot_nt(nf1_ref[...], w1_ref[...]))[0].astype(jnp.bfloat16)
        ff_ref[...] += dot_nn(act, w2_ref[...])

    @pl.when(i == PAIRS + CHUNKS - 1)
    def _():
        h2_ref[...] = ff_ref[...]
        ne_ref[...] = rms_norm(ff_ref[...], gains[5:6, :]).astype(jnp.bfloat16)
        if fast:
            steps[11]()
            gather.finish()
            tokens.finish()
            mail.finish()


def encode(fast, q, qaug, own_kv, oth_kv, kaug, x, gains, enc_w, dec_t, a, g):
    t = q.shape[0]
    nk = own_kv.shape[0]
    pair = lambda i: jnp.minimum(i, PAIRS - 1)
    chunk = lambda i: jnp.maximum(i - PAIRS, 0)
    col = lambda first: pl.BlockSpec((nk, 128), lambda i: (0, first + pair(i)))
    tok = whole_spec((t, D))
    dims = lambda kind: jax.ShapeDtypeStruct((t, D), kind)
    in_specs = [
        pl.BlockSpec((t, 128), lambda i: (0, pair(i))), whole_spec((t, 128)),
        col(0), col(PAIRS), col(0), col(PAIRS), whole_spec((2 * nk, 128)), tok, whole_spec(gains.shape),
        pl.BlockSpec((D, D), lambda i: (3, 0)),
        pl.BlockSpec((CHUNK, D), lambda i: (4 * D // CHUNK + chunk(i), 0)),
        pl.BlockSpec((CHUNK, D), lambda i: (4 * D // CHUNK + CHUNKS + chunk(i), 0)),
    ]
    args = [q, qaug, own_kv, own_kv, oth_kv, oth_kv, kaug, x, gains, enc_w, enc_w, enc_w]
    out_specs = [tok, pl.BlockSpec((t, 128), lambda i: (0, pair(i))), tok, tok, tok, tok]
    out_shape = [dims(jnp.bfloat16), dims(jnp.float32), dims(jnp.float32), dims(jnp.bfloat16), dims(jnp.float32), dims(jnp.bfloat16)]
    scratch = [
        pltpu.VMEM((2 * nk, 2 * QB), jnp.float32), pltpu.VMEM((8, 2 * QB), jnp.float32),
        pltpu.VMEM((8, 2 * QB), jnp.float32), pltpu.VMEM((QB, 128), jnp.float32), pltpu.VMEM((t, D), jnp.float32),
    ]
    params = dict(vmem_limit_bytes=48 * 1024 * 1024)
    if fast:
        in_specs += [ANY] * 3
        args += [dec_t, a, g]
        out_specs += [ANY] * 3
        out_shape += [shaped((32 * dec_t.shape[0], D)), dims(jnp.bfloat16), dims(jnp.bfloat16)]
        scratch += gather_sems(1) + token_sems(2)
        params.update(collective_id=1, has_side_effects=True)
    return pl.pallas_call(
        functools.partial(encode_kernel, fast, t, nk - t),
        grid=(PAIRS + CHUNKS,),
        in_specs=in_specs,
        out_specs=out_specs,
        out_shape=out_shape,
        scratch_shapes=scratch,
        compiler_params=pltpu.CompilerParams(**params),
        name="encode",
    )(*args)


def encode_back_kernel(
    fast, own_len, extra,
    grad_ref, nf1_ref, h1_ref, gains, wo_ref, w1_ref, w2_ref, o_ref,
    q_ref, qaug_ref, own_k, own_v, oth_k, oth_v, kaug_ref, lse_ref, *rest,
):
    i = pl.program_id(0)
    if fast:
        dec_g, y_in, a_in = rest[:3]
        rest = rest[3:]
    whole, grad_h_ref, dgain_ref, dq_ref, dko_ref, dvo_ref, dkt_ref, dvt_ref = rest[:8]
    rest = rest[8:]
    if fast:
        dec_out, y_out, a_out = rest[:3]
        rest = rest[3:]
    total_ref, grad_b, mix_ref, slots, dwo_ref, sems, sem_o, dk_acc, dv_acc, dq_acc = rest[:10]
    store = ChunkStore(slots, whole, (4 * D, 4 * D + FF), sems)
    store_o = lambda: pltpu.make_async_copy(dwo_ref, whole.at[pl.ds(3 * D, D)], sem_o)
    if fast:
        rest = rest[10:]
        mail = Mail(position())
        reduce = Reduce(mail, dec_g, dec_out, rest[:5], rest[5:15])
        tokens = TokensOut(mail, ((y_in, y_out), (a_in, a_out)), rest[15:])
        steps = reduce_order(reduce)
        places = {1: (0,), 2: (1,), 4: (2, 3), 6: (4, 5, 6), 7: (7,), 8: (8,), 9: (9,), 11: (10,)}

        @pl.when(i == 0)
        def _():
            greet(mail.pos)
            reduce.start()
            tokens.start(0)
            tokens.start(1)

        for at, which in places.items():

            @pl.when(i == at)
            def _(which=which):
                for n in which:
                    steps[n]()

    @pl.when(i == 0)
    def _():
        grad_b[...] = grad_ref[...].astype(jnp.bfloat16)

    @pl.when(i < CHUNKS)
    def _():
        pl.when(i >= 2)(lambda: store.wait(i - 2))
        feed_back_chunk(
            nf1_ref[...], grad_b[...], w1_ref[...], w2_ref[...], slots.at[lax.rem(i, 2)], total_ref, i == 0
        )
        store.start(i)

    @pl.when(i == CHUNKS - 1)
    def _():
        grad_x, dgain = norm_back(h1_ref[...], gains[1:2, :], total_ref[...])
        dgain_ref[...] = jnp.broadcast_to(dgain, dgain_ref.shape)
        grad_h = grad_ref[...] + grad_x
        grad_h_ref[...] = grad_h
        top = grad_h.astype(jnp.bfloat16)
        dwo_ref[...] = dot_tn(o_ref[...], top).astype(jnp.bfloat16)
        store_o().start()
        mix_ref[...] = dot_nt(top, wo_ref[...]).astype(jnp.bfloat16)
        store.wait(i - 1)
        store.wait(i)

    @pl.when(i >= CHUNKS)
    def _():
        cols = pl.ds(pl.multiple_of((i - CHUNKS) * 128, 128), 128)
        back_pair(
            False, own_len, extra, always, q_ref, qaug_ref, own_k, own_v, oth_k, oth_v, kaug_ref,
            o_ref.at[:, cols], lse_ref, mix_ref.at[:, cols],
            dq_ref, dko_ref, dvo_ref, dkt_ref, dvt_ref, dk_acc, dv_acc, dq_acc,
        )

    @pl.when(i == PAIRS + CHUNKS - 1)
    def _():
        store_o().wait()
        if fast:
            steps[11]()
            reduce.finish()
            tokens.finish()
            mail.finish()


def encode_back(fast, grad, nf1, h1, gains, enc_w, o, q, qaug, own_kv, oth_kv, kaug, lse, dec_g, y, a):
    t = q.shape[0]
    nk = own_kv.shape[0]
    pair = lambda i: jnp.maximum(i - CHUNKS, 0)
    chunk = lambda i: jnp.minimum(i, CHUNKS - 1)
    col = lambda first: pl.BlockSpec((nk, 128), lambda i: (0, first + pair(i)))
    cols = pl.BlockSpec((t, 128), lambda i: (0, pair(i)))
    tok = whole_spec((t, D))
    dims = lambda kind, n=t: jax.ShapeDtypeStruct((n, D), kind)
    in_specs = [
        tok, tok, tok, whole_spec(gains.shape),
        pl.BlockSpec((D, D), lambda i: (3, 0)),
        pl.BlockSpec((CHUNK, D), lambda i: (4 * D // CHUNK + chunk(i), 0)),
        pl.BlockSpec((CHUNK, D), lambda i: (4 * D // CHUNK + CHUNKS + chunk(i), 0)),
        tok, cols, whole_spec((t, 128)), col(0), col(PAIRS), col(0), col(PAIRS), whole_spec((2 * nk, 128)), cols,
    ]
    args = [grad, nf1, h1, gains, enc_w, enc_w, enc_w, o, q, qaug, own_kv, own_kv, oth_kv, oth_kv, kaug, lse]
    out_specs = [pl.BlockSpec(memory_space=pl.ANY), tok, whole_spec((8, D)), cols, col(0), col(0), col(0), col(0)]
    out_shape = [
        jax.ShapeDtypeStruct(enc_w.shape, jnp.bfloat16), dims(jnp.float32), dims(jnp.float32, 8), dims(jnp.bfloat16),
        dims(jnp.float32, nk), dims(jnp.float32, nk), dims(jnp.bfloat16, nk), dims(jnp.bfloat16, nk),
    ]
    scratch = [
        pltpu.VMEM((t, D), jnp.float32), pltpu.VMEM((t, D), jnp.bfloat16), pltpu.VMEM((t, D), jnp.bfloat16),
        pltpu.VMEM((2, 2, CHUNK, D), jnp.bfloat16), pltpu.VMEM((D, D), jnp.bfloat16),
        pltpu.SemaphoreType.DMA((2, 2)), pltpu.SemaphoreType.DMA,
        pltpu.VMEM((2 * nk, 128), jnp.float32), pltpu.VMEM((2 * nk, 128), jnp.float32), pltpu.VMEM((QB, 128), jnp.float32),
    ]
    params = dict(vmem_limit_bytes=60 * 1024 * 1024)
    if fast:
        size = dec_g.shape[0] // 32
        in_specs += [ANY] * 3
        args += [dec_g, y, a]
        out_specs += [ANY] * 3
        out_shape += [shaped((size, D)), shaped((2, t // 2, D)), shaped((2, t // 2, D))]
        scratch += reduce_buffers(size) + reduce_sems() + token_sems(2)
        params.update(collective_id=2, has_side_effects=True)
    return pl.pallas_call(
        functools.partial(encode_back_kernel, fast, t, nk - t),
        grid=(PAIRS + CHUNKS,),
        in_specs=in_specs,
        out_specs=out_specs,
        out_shape=out_shape,
        scratch_shapes=scratch,
        compiler_params=pltpu.CompilerParams(**params),
        name="encode_back",
    )(*args)


def project(left, weight_t):
    return jnp.einsum("nd,ed->ne", left, weight_t, preferred_element_type=jnp.float32)


def project_back(left, weight_t):
    return jnp.einsum("ne,ed->nd", left, weight_t, preferred_element_type=jnp.float32)


def outer_sum(wide, narrow):
    return jnp.einsum("ne,nd->ed", wide, narrow, preferred_element_type=jnp.float32).astype(jnp.bfloat16)


def output_back(grad, mixed_b, w_out):
    grad_b = grad.astype(jnp.bfloat16)
    return (outer_sum(mixed_b, grad_b), project(grad_b, w_out).astype(jnp.bfloat16))


def partner(values):
    n_rows = lax.axis_size("rows")
    return lax.ppermute(values, "rows", [(i, i ^ 1) for i in range(n_rows)])


def my_row(values):
    core = lax.axis_index("rows") % 2
    mem = lax.axis_index("mem")
    chosen = jnp.where(mem // 2 == core, values, partner(values))
    return lax.dynamic_index_in_dim(chosen, mem % 2, 0, keepdims=False)


def quarters_of(core):
    return (jnp.where(core == 0, 0, 1), jnp.where(core == 0, 3, 2))


def own_quarters(row, core, quarter):
    return jnp.concatenate(
        [lax.dynamic_slice_in_dim(row, place * quarter, quarter, 0) for place in quarters_of(core)], 0
    )


def to_rows(values):
    quarter = values.shape[1]
    row = my_row(lax.all_gather(values, "mem", axis=1, tiled=True))
    return own_quarters(row, lax.axis_index("rows") % 2, quarter)


def from_rows(values):
    quarter = values.shape[0] // 2
    core = lax.axis_index("rows") % 2
    mem = lax.axis_index("mem")
    gathered = lax.all_gather(values, "mem", axis=0)
    other = partner(gathered)
    holder = jnp.where((mem == 0) | (mem == 3), 0, 1)
    chosen = jnp.where(holder == core, gathered, other)
    return lax.dynamic_slice(
        chosen, (2 * core, jnp.where(mem < 2, 0, quarter), 0), (2, quarter, values.shape[1])
    )


def gather_weights(params):
    return lax.all_gather(params.T, ("rows", "mem"), axis=0, tiled=True)


def reduce_weights(grads):
    return lax.psum_scatter(grads, ("rows", "mem"), scatter_dimension=0, tiled=True)


def flags_of(q_row, k_row, core, quarter, extra, causal):
    n = q_row.shape[0] // quarter
    ends_q = q_row.reshape(n, quarter)
    ends_k = k_row.reshape(n, quarter)
    meets = (ends_k[None, :, 0] <= ends_q[:, None, -1]) & (ends_q[:, None, 0] <= ends_k[None, :, -1])
    if causal:
        meets &= jnp.arange(n)[None, :] <= jnp.arange(n)[:, None]
    mine = jnp.stack(quarters_of(core))
    others = jnp.stack(quarters_of(1 - core))
    meets = meets[mine]
    always = [jnp.ones((2, 1), bool)] if extra else []
    return jnp.concatenate([meets[:, mine]] + always + [meets[:, others]] + always, 1).astype(jnp.int32)


def both_parts(own, other):
    return jnp.concatenate([own, other], 0)


def on_device(
    fast,
    questions,
    answers,
    q_segments,
    a_segments,
    entry_ids,
    entry_alive_flags,
    memory_table,
    enc_params,
    dec_params,
    norm_gains,
    cotangent,
):
    quarter = questions.shape[1]
    core = lax.axis_index("rows") % 2
    per_row, slots = entry_alive_flags.shape[1], entry_alive_flags.shape[2]
    half = per_row // 2
    rows_here, row_len = q_segments.shape
    segs = jnp.concatenate([q_segments, a_segments, entry_alive_flags.reshape(rows_here, -1)], 1)
    if fast:
        segs = jnp.pad(segs, ((0, 0), (0, -segs.shape[1] % 1024))).reshape(rows_here, -1, 128)
        own_ids = entry_ids.reshape(rows_here, -1)
        n_ids = own_ids.shape[1]
        own_ids = jnp.pad(own_ids, ((0, 0), (0, 1024 - n_ids))).reshape(rows_here, 8, 128)
        enc_w, x_question, other_segs, ids = gather_encoder(enc_params.T, questions, segs, own_ids)
        mem = lax.axis_index("mem")
        numbers = jnp.where(
            mem // 2 == core, lax.dynamic_index_in_dim(segs, mem % 2, 0, keepdims=False), other_segs
        ).reshape(-1)
        ids = ids.reshape(ids.shape[0], -1)[:, :n_ids].reshape(ids.shape[0], per_row, -1)
        ids = ids.transpose(1, 0, 2).reshape(-1)
    else:
        enc_w, dec_w = gather_weights(enc_params), gather_weights(dec_params)
        ids = my_row(lax.all_gather(entry_ids, "mem", axis=2, tiled=True)).reshape(-1)
        numbers = my_row(segs)
        x_question, x_answer = to_rows(questions), to_rows(answers)
        grad_top = to_rows(cotangent.astype(jnp.bfloat16))
    gains = jnp.pad(norm_gains, ((0, 2), (0, 0)))
    q_row = numbers[:row_len]
    a_row = numbers[row_len : 2 * row_len]
    alive = numbers[2 * row_len : 2 * row_len + per_row * slots]

    own_ids = lax.dynamic_slice_in_dim(ids, core * half * slots, half * slots, 0)
    entry_vals = memory_table[own_ids].reshape(half * slots * 2, D).astype(jnp.float32)
    n_prefix = entry_vals.shape[0]
    extra = -(-n_prefix // 128) * 128
    place = jnp.arange(extra, dtype=jnp.int32)

    def prefix_segments(which):
        question = which * half + place // (2 * slots)
        live = lax.dynamic_slice_in_dim(alive, which * half * slots, half * slots, 0)
        live = jnp.pad(jnp.repeat(live, 2), (0, extra - n_prefix))
        return jnp.where(live == 1, question, -1)

    tokens = 2 * quarter
    own_q = own_quarters(q_row, core, quarter)
    other_q = own_quarters(q_row, 1 - core, quarter)
    own_a = own_quarters(a_row, core, quarter)
    other_a = own_quarters(a_row, 1 - core, quarter)
    q_aug, a_aug = seg_aug_q(own_q), seg_aug_q(own_a)
    enc_aug = seg_aug_k(
        jnp.concatenate([own_q, prefix_segments(core), other_q, prefix_segments(1 - core)])
    )
    self_aug = seg_aug_k(jnp.concatenate([own_a, other_a]))
    cross_aug = seg_aug_k(jnp.concatenate([own_q, other_q]))
    enc_act = flags_of(q_row, q_row, core, quarter, extra, False)
    self_act = flags_of(a_row, a_row, core, quarter, 0, True)
    cross_act = flags_of(a_row, q_row, core, quarter, 0, False)

    enc_in = jnp.concatenate([x_question.astype(jnp.float32), jnp.pad(entry_vals, ((0, extra - n_prefix), (0, 0)))], 0)
    normed_q = rms_norm(enc_in, norm_gains[0]).astype(jnp.bfloat16)
    query_enc = project(normed_q[:tokens], enc_w[:D]).astype(jnp.bfloat16)
    enc_kv = project(normed_q, enc_w[D : 3 * D]).astype(jnp.bfloat16)
    enc_kv_other = partner(enc_kv)

    mixed_enc, logsum_enc, hidden_one, normed_f1, hidden_two, encoded, *gathered = encode(
        fast, query_enc, q_aug, enc_kv, enc_kv_other, enc_aug, x_question, gains, enc_w,
        dec_params.T, answers, cotangent.astype(jnp.bfloat16),
    )
    if fast:
        dec_w, x_answer, grad_top = gathered
    x_answer = x_answer.astype(jnp.float32)
    normed_a = rms_norm(x_answer, norm_gains[2]).astype(jnp.bfloat16)
    qkv_self = project(normed_a, dec_w[: 3 * D]).astype(jnp.bfloat16)
    query_self, self_kv = qkv_self[:, :D], qkv_self[:, D:]
    self_kv_other = partner(self_kv)
    cross_kv = project(encoded, dec_w[5 * D : 7 * D]).astype(jnp.bfloat16)
    cross_kv_other = partner(cross_kv)

    mixed_self, logsum_self = attend(True, self_act, query_self, a_aug, self_kv, self_kv_other, self_aug)
    dec_one = x_answer + project_back(mixed_self, dec_w[3 * D : 4 * D])
    normed_c = rms_norm(dec_one, norm_gains[3]).astype(jnp.bfloat16)
    query_cross = project(normed_c, dec_w[4 * D : 5 * D]).astype(jnp.bfloat16)
    mixed_cross, logsum_cross = attend(
        False, cross_act, query_cross, a_aug, cross_kv, cross_kv_other, cross_aug
    )
    decoded, grad_two, grad_mixc, grad_gain4, dec_full = decode_top(
        dec_one, mixed_cross, gains, grad_top, dec_w
    )
    grad_qc, dk_own, dv_own, dk_other, dv_other = attend_back(
        False, cross_act, query_cross, a_aug, cross_kv, cross_kv_other, cross_aug,
        mixed_cross, logsum_cross, grad_mixc,
    )
    more = partner(jnp.concatenate([dk_other, dv_other], 1)).astype(jnp.float32)
    grad_ckv = (jnp.concatenate([dk_own, dv_own], 1) + more).astype(jnp.bfloat16)
    grad_wqc = outer_sum(grad_qc, normed_c)
    grad_x, grad_gain3 = norm_back(
        dec_one, norm_gains[3], project_back(grad_qc, dec_w[4 * D : 5 * D])
    )
    grad_one = grad_two + grad_x
    grad_wckv = outer_sum(grad_ckv, encoded)
    grad_encoded, grad_gain5 = norm_back(
        hidden_two, norm_gains[5], project_back(grad_ckv, dec_w[5 * D : 7 * D])
    )
    grad_wos, grad_mixs = output_back(grad_one, mixed_self, dec_w[3 * D : 4 * D])
    grad_qs, dk_own, dv_own, dk_other, dv_other = attend_back(
        True, self_act, query_self, a_aug, self_kv, self_kv_other, self_aug,
        mixed_self, logsum_self, grad_mixs,
    )
    more = partner(jnp.concatenate([dk_other, dv_other], 1)).astype(jnp.float32)
    grad_skv = (jnp.concatenate([dk_own, dv_own], 1) + more).astype(jnp.bfloat16)
    grad_self = jnp.concatenate([grad_qs, grad_skv], 1)
    grad_wself = outer_sum(grad_self, normed_a)
    grad_x, grad_gain2 = norm_back(x_answer, norm_gains[2], project_back(grad_self, dec_w[: 3 * D]))
    grad_answers = (grad_one + grad_x).astype(jnp.bfloat16)
    dec_full = dec_full.at[: 3 * D].set(grad_wself)
    dec_full = dec_full.at[3 * D : 4 * D].set(grad_wos)
    dec_full = dec_full.at[4 * D : 5 * D].set(grad_wqc)
    dec_full = dec_full.at[5 * D : 7 * D].set(grad_wckv)

    enc_full, grad_hidden, grad_gain1, grad_qe, dk_own, dv_own, dk_other, dv_other, *reduced = encode_back(
        fast, grad_encoded, normed_f1, hidden_one, gains, enc_w, mixed_enc, query_enc, q_aug,
        enc_kv, enc_kv_other, enc_aug, logsum_enc, dec_full, decoded, grad_answers,
    )
    more = partner(jnp.concatenate([dk_other, dv_other], 1)).astype(jnp.float32)
    grad_ekv = (jnp.concatenate([dk_own, dv_own], 1) + more).astype(jnp.bfloat16)
    grad_wqe = outer_sum(grad_qe, normed_q[:tokens])
    grad_wkve = outer_sum(grad_ekv, normed_q)
    grad_in = project_back(grad_ekv, enc_w[D : 3 * D])
    grad_in = grad_in + jnp.pad(project_back(grad_qe, enc_w[:D]), ((0, extra), (0, 0)))
    grad_x, grad_gain0 = norm_back(enc_in, norm_gains[0], grad_in)
    grad_questions = (grad_hidden + grad_x[:tokens]).astype(jnp.bfloat16)
    enc_full = enc_full.at[:D].set(grad_wqe)
    enc_full = enc_full.at[D : 3 * D].set(grad_wkve)
    gain_terms = jnp.concatenate(
        [grad_gain0, grad_gain1[:1], grad_gain2, grad_gain3, grad_gain4[:1], grad_gain5], 0
    )
    if fast:
        grad_decoder, decoded, grad_answers = reduced
        grad_encoder, grad_questions, grad_gains = reduce_encoder(
            enc_full, grad_questions, jnp.pad(gain_terms, ((0, 2), (0, 0)))
        )
        grad_gains = grad_gains[:6]
    else:
        decoded, grad_questions, grad_answers = (
            from_rows(values) for values in (decoded, grad_questions, grad_answers)
        )
        grad_gains = lax.psum(gain_terms, ("rows", "mem"))
        grad_encoder, grad_decoder = reduce_weights(enc_full), reduce_weights(dec_full)
    return (
        decoded,
        grad_questions.astype(jnp.float32),
        grad_answers.astype(jnp.float32),
        grad_encoder.astype(jnp.float32).T,
        grad_decoder.astype(jnp.float32).T,
        grad_gains,
    )


def solution(mesh):
    fast = mesh.shape["rows"] == 8 and mesh.shape["mem"] == 4
    return jax.shard_map(
        functools.partial(on_device, fast),
        mesh=mesh,
        in_specs=(
            P("rows", "mem", None),
            P("rows", "mem", None),
            P("rows", None),
            P("rows", None),
            P("rows", None, "mem"),
            P("rows", None, None),
            P(),
            P(None, ("rows", "mem")),
            P(None, ("rows", "mem")),
            P(),
            P("rows", "mem", None),
        ),
        out_specs=(
            P("rows", "mem", None),
            P("rows", "mem", None),
            P("rows", "mem", None),
            P(None, ("rows", "mem")),
            P(None, ("rows", "mem")),
            P(),
        ),
        check_vma=False,
    )
```

```python
import functools
import jax
import jax.numpy as jnp
from jax import lax
from jax.experimental import pallas as pl
from jax.experimental.pallas import tpu as pltpu
from jax.sharding import PartitionSpec as P

D = 768
H = 12
HD = 64
FF = 3072
QB = 256
masked_score = -1e30


def key_chunks(own_len, extra):
    chunks = []
    for side in (0, 1):
        for at in range(own_len // QB):
            chunks.append((side, at * QB, QB))
        if extra:
            chunks.append((side, own_len, extra))
    return chunks


def chunk_sets(causal, own_len, extra):
    chunks = key_chunks(own_len, extra)
    if not causal:
        return [[list(range(len(chunks)))] * (own_len // QB)]
    quarters = ((0, 3), (1, 2))
    sets = []
    for core in (0, 1):
        held = (quarters[core], quarters[1 - core])
        sets.append([
            [n for n, (side, at, size) in enumerate(chunks) if held[side][at // QB] <= held[0][qb]]
            for qb in range(own_len // QB)
        ])
    return sets


def attend_pair(causal, own_len, extra, use, q_ref, qaug_ref, own_k, own_v, oth_k, oth_v, kaug_ref, o_ref, lse_ref, s_ref):
    low = lax.broadcasted_iota(jnp.int32, (1, 128), 1) < HD
    chunks = key_chunks(own_len, extra)
    nk = own_len + extra
    for qb in range(own_len // QB):
        rows = pl.ds(qb * QB, QB)
        q = q_ref[rows, :] * jnp.bfloat16(HD ** (-0.5))
        qaug = qaug_ref[rows, :]
        queries = (jnp.where(low, q, qaug), jnp.where(low, qaug, q))
        tops = [None, None]
        for ci in use[qb]:
            side, at, size = chunks[ci]
            k = (own_k, oth_k)[side][at : at + size, :]
            place = slice(side * nk + at, side * nk + at + size)
            kaug = kaug_ref[place, :]
            for h in (0, 1):
                keys = jnp.where(low, k, kaug) if h == 0 else jnp.where(low, kaug, k)
                s = lax.dot_general(keys, queries[h], (((1,), (1,)), ((), ())), preferred_element_type=jnp.float32)
                if causal and side == 0 and at == qb * QB:
                    tri = lax.broadcasted_iota(jnp.int32, (size, QB), 0) <= lax.broadcasted_iota(jnp.int32, (size, QB), 1)
                    s = jnp.where(tri, s, masked_score)
                s_ref[qb, place, h * QB : (h + 1) * QB] = s
                top = jnp.max(s.reshape(size // 8, 8, QB), 0)
                tops[h] = top if tops[h] is None else jnp.maximum(tops[h], top)
        m = jnp.max(jnp.concatenate(tops, 1), 0, keepdims=True)
        total, acc = None, None
        for ci in use[qb]:
            side, at, size = chunks[ci]
            v = (own_v, oth_v)[side][at : at + size, :]
            zero = jnp.zeros_like(v)
            place = slice(side * nk + at, side * nk + at + size)
            p = jnp.exp(s_ref[qb, place, :] - m)
            part = jnp.sum(p.reshape(size // 8, 8, 2 * QB), 0)
            total = part if total is None else total + part
            pb = p.astype(jnp.bfloat16)
            pb = jnp.concatenate([pb[:, :QB], pb[:, QB:]], 0)
            v_split = jnp.concatenate([jnp.where(low, v, zero), jnp.where(low, zero, v)], 0)
            part = lax.dot_general(pb, v_split, (((0,), (0,)), ((), ())), preferred_element_type=jnp.float32)
            acc = part if acc is None else acc + part
        total = jnp.sum(total, 0, keepdims=True)
        lse = m + jnp.log(total)
        rec = 1.0 / total
        wide = lambda row, h: jnp.broadcast_to(row[:, h * QB : (h + 1) * QB], (HD, QB))
        o_ref[rows, :] = (acc * jnp.concatenate([wide(rec, 0), wide(rec, 1)], 0).T).astype(jnp.bfloat16)
        lse_ref[rows, :] = jnp.concatenate([wide(lse, 1), wide(lse, 0)], 0).T


def by_core(core, sets, work):
    if len(sets) == 1:
        work(sets[0])
        return
    for n, use in enumerate(sets):
        pl.when(core[0] == n)(functools.partial(work, use))


def attend_kernel(causal, own_len, extra, core, *refs):
    by_core(core, chunk_sets(causal, own_len, extra), lambda use: attend_pair(causal, own_len, extra, use, *refs))


def back_kernel(causal, own_len, extra, core, *refs):
    by_core(core, chunk_sets(causal, own_len, extra), lambda use: back_pair(causal, own_len, extra, use, *refs))


def attend(causal, core, q, qaug, own_kv, oth_kv, kaug):
    t = q.shape[0]
    nk = own_kv.shape[0]
    col = lambda first: pl.BlockSpec((nk, 128), lambda i, a: (0, first + i))
    return pl.pallas_call(
        functools.partial(attend_kernel, causal, t, nk - t),
        grid_spec=pltpu.PrefetchScalarGridSpec(
            num_scalar_prefetch=1,
            grid=(H // 2,),
            in_specs=[
                pl.BlockSpec((t, 128), lambda i, a: (0, i)),
                pl.BlockSpec((t, 128), lambda i, a: (0, 0)),
                col(0), col(H // 2), col(0), col(H // 2),
                pl.BlockSpec((2 * nk, 128), lambda i, a: (0, 0)),
            ],
            out_specs=[pl.BlockSpec((t, 128), lambda i, a: (0, i))] * 2,
            scratch_shapes=[pltpu.VMEM((t // QB, 2 * nk, 2 * QB), jnp.float32)],
        ),
        out_shape=[jax.ShapeDtypeStruct((t, D), jnp.bfloat16), jax.ShapeDtypeStruct((t, D), jnp.float32)],
        compiler_params=pltpu.CompilerParams(vmem_limit_bytes=40 * 1024 * 1024),
        cost_estimate=pl.CostEstimate(flops=4 * t * 2 * nk * D, bytes_accessed=8 * nk * D, transcendentals=t * 2 * nk * H),
        name="attend",
    )(core.reshape(1), q, qaug, own_kv, own_kv, oth_kv, oth_kv, kaug)


def three_parts(value):
    hi = value.astype(jnp.bfloat16).astype(jnp.float32)
    mid = (value - hi).astype(jnp.bfloat16).astype(jnp.float32)
    return hi, mid, value - hi - mid


def spread(base, lane64, value):
    hi, mid, lo = three_parts(value)
    return jnp.where(lane64 == 8, hi, jnp.where(lane64 == 9, mid, jnp.where(lane64 == 10, lo, base)))


def back_pair(causal, own_len, extra, use, q_ref, qaug_ref, own_k, own_v, oth_k, oth_v, kaug_ref, o_ref, lse_ref, g_ref, dq_ref, dko_ref, dvo_ref, dkt_ref, dvt_ref, dk_acc, dv_acc):
    lane = lax.broadcasted_iota(jnp.int32, (1, 128), 1)
    low = lane < HD
    lane64 = lane % HD
    chunks = key_chunks(own_len, extra)
    nk = own_len + extra
    begun = set()
    ones_aug = jnp.where((lane64 >= 8) & (lane64 <= 10), 1.0, 0.0).astype(jnp.bfloat16)
    for qb in range(own_len // QB):
        rows = pl.ds(qb * QB, QB)
        q = q_ref[rows, :] * jnp.bfloat16(HD ** (-0.5))
        g = g_ref[rows, :]
        qaug = spread(qaug_ref[rows, :].astype(jnp.float32), lane64, -lse_ref[rows, :]).astype(jnp.bfloat16)
        prod = g.astype(jnp.float32) * o_ref[rows, :].astype(jnp.float32)
        d_even = jnp.sum(jnp.where(low, prod, 0.0), -1, keepdims=True)
        d_odd = jnp.sum(jnp.where(low, 0.0, prod), -1, keepdims=True)
        gaug = spread(jnp.zeros((QB, 128), jnp.float32), lane64, -jnp.where(low, d_odd, d_even)).astype(jnp.bfloat16)
        queries = (jnp.where(low, q, qaug), jnp.where(low, qaug, q))
        grads = (jnp.where(low, g, gaug), jnp.where(low, gaug, g))
        zero = jnp.zeros_like(q)
        q_split = jnp.concatenate([jnp.where(low, q, zero), jnp.where(low, zero, q)], 0)
        g_split = jnp.concatenate([jnp.where(low, g, zero), jnp.where(low, zero, g)], 0)
        dq = None
        for ci in use[qb]:
            side, at, size = chunks[ci]
            k = (own_k, oth_k)[side][at : at + size, :]
            v = (own_v, oth_v)[side][at : at + size, :]
            place = slice(side * nk + at, side * nk + at + size)
            kaug = kaug_ref[place, :]
            vaug = jnp.broadcast_to(ones_aug, v.shape)
            zk = jnp.zeros_like(k)
            probs, dscores = [], []
            for h in (0, 1):
                keys = jnp.where(low, k, kaug) if h == 0 else jnp.where(low, kaug, k)
                vals = jnp.where(low, v, vaug) if h == 0 else jnp.where(low, vaug, v)
                s = lax.dot_general(keys, queries[h], (((1,), (1,)), ((), ())), preferred_element_type=jnp.float32)
                if causal and side == 0 and at == qb * QB:
                    tri = lax.broadcasted_iota(jnp.int32, (size, QB), 0) <= lax.broadcasted_iota(jnp.int32, (size, QB), 1)
                    s = jnp.where(tri, s, masked_score)
                p = jnp.exp(s)
                dp = lax.dot_general(vals, grads[h], (((1,), (1,)), ((), ())), preferred_element_type=jnp.float32)
                dscores.append((p * dp).astype(jnp.bfloat16))
                probs.append(p.astype(jnp.bfloat16))
            dk = jnp.dot(jnp.concatenate(dscores, 1), q_split, preferred_element_type=jnp.float32)
            dv = jnp.dot(jnp.concatenate(probs, 1), g_split, preferred_element_type=jnp.float32)
            if ci in begun:
                dk_acc[place, :] += dk
                dv_acc[place, :] += dv
            else:
                begun.add(ci)
                dk_acc[place, :] = dk
                dv_acc[place, :] = dv
            k_split = jnp.concatenate([jnp.where(low, k, zk), jnp.where(low, zk, k)], 0)
            dst = jnp.concatenate(dscores, 0)
            part = lax.dot_general(dst, k_split, (((0,), (0,)), ((), ())), preferred_element_type=jnp.float32)
            dq = part if dq is None else dq + part
        dq_ref[rows, :] = (dq * HD ** (-0.5)).astype(jnp.bfloat16)
    for ci, (side, at, size) in enumerate(chunks):
        if ci not in begun:
            place = slice(side * nk + at, side * nk + at + size)
            dk_acc[place, :] = jnp.zeros((size, 128), jnp.float32)
            dv_acc[place, :] = jnp.zeros((size, 128), jnp.float32)
    dko_ref[...] = dk_acc[:nk, :]
    dvo_ref[...] = dv_acc[:nk, :]
    dkt_ref[...] = dk_acc[nk:, :].astype(jnp.bfloat16)
    dvt_ref[...] = dv_acc[nk:, :].astype(jnp.bfloat16)


def attend_back(causal, core, q, qaug, own_kv, oth_kv, kaug, mixed, lse, grad):
    t = q.shape[0]
    nk = own_kv.shape[0]
    col = lambda first: pl.BlockSpec((nk, 128), lambda i, a: (0, first + i))
    tok = pl.BlockSpec((t, 128), lambda i, a: (0, i))
    return pl.pallas_call(
        functools.partial(back_kernel, causal, t, nk - t),
        grid_spec=pltpu.PrefetchScalarGridSpec(
            num_scalar_prefetch=1,
            grid=(H // 2,),
            in_specs=[
                tok,
                pl.BlockSpec((t, 128), lambda i, a: (0, 0)),
                col(0), col(H // 2), col(0), col(H // 2),
                pl.BlockSpec((2 * nk, 128), lambda i, a: (0, 0)),
                tok, tok, tok,
            ],
            out_specs=[tok, col(0), col(0), col(0), col(0)],
            scratch_shapes=[pltpu.VMEM((2 * nk, 128), jnp.float32), pltpu.VMEM((2 * nk, 128), jnp.float32)],
        ),
        out_shape=[
            jax.ShapeDtypeStruct((t, D), jnp.bfloat16),
            jax.ShapeDtypeStruct((nk, D), jnp.float32),
            jax.ShapeDtypeStruct((nk, D), jnp.float32),
            jax.ShapeDtypeStruct((nk, D), jnp.bfloat16),
            jax.ShapeDtypeStruct((nk, D), jnp.bfloat16),
        ],
        compiler_params=pltpu.CompilerParams(vmem_limit_bytes=40 * 1024 * 1024),
        cost_estimate=pl.CostEstimate(flops=10 * t * 2 * nk * D, bytes_accessed=24 * nk * D, transcendentals=t * 2 * nk * H),
        name="attend_back",
    )(core.reshape(1), q, qaug, own_kv, own_kv, oth_kv, oth_kv, kaug, mixed, lse, grad)


def seg_aug_q(seg):
    j = jnp.arange(128, dtype=jnp.int32) % HD
    return ((j[None, :] < 8) & (j[None, :] == seg[:, None])).astype(jnp.bfloat16)


def seg_aug_k(seg):
    j = jnp.arange(128, dtype=jnp.int32)[None, :] % HD
    bad = (j < 8) & (j != seg[:, None])
    return jnp.where(bad, masked_score, jnp.where((j >= 8) & (j <= 10), 1.0, 0.0)).astype(jnp.bfloat16)


epsilon = 1e-06
CHUNK = 512


def dot_nt(left, right):
    return lax.dot_general(left, right, (((1,), (1,)), ((), ())), preferred_element_type=jnp.float32)


def dot_nn(left, right):
    return lax.dot_general(left, right, (((1,), (0,)), ((), ())), preferred_element_type=jnp.float32)


def dot_tn(left, right):
    return lax.dot_general(left, right, (((0,), (0,)), ((), ())), preferred_element_type=jnp.float32)


def rms_norm(values, gain):
    return values * lax.rsqrt(jnp.mean(values * values, -1, keepdims=True) + epsilon) * gain


def norm_back(values, gain, grad):
    root = lax.rsqrt(jnp.mean(values * values, -1, keepdims=True) + epsilon)
    unit = values * root
    scaled = grad * gain
    inner = jnp.mean(unit * scaled, -1, keepdims=True)
    return root * (scaled - unit * inner), jnp.sum(grad * unit, 0, keepdims=True)


def gelu_pair(pre):
    root = 0.7978845608028654
    square = pre * pre
    bent = jnp.tanh(root * pre * (1.0 + 0.044715 * square))
    half = 0.5 * (1.0 + bent)
    slope = half + 0.5 * pre * (1.0 - bent * bent) * root * (1.0 + 0.134145 * square)
    return pre * half, slope


def feed_back_chunk(normed, grad_b, w1, w2, dw, total, first):
    act, slope = gelu_pair(dot_nt(normed, w1))
    act = act.astype(jnp.bfloat16)
    grad_pre = (dot_nt(grad_b, w2) * slope).astype(jnp.bfloat16)
    dw[0] = dot_tn(grad_pre, normed).astype(jnp.bfloat16)
    dw[1] = dot_tn(act, grad_b).astype(jnp.bfloat16)
    part = dot_nn(grad_pre, w1)

    @pl.when(first)
    def _():
        total[...] = part

    @pl.when(jnp.logical_not(first))
    def _():
        total[...] += part

    return act


class ChunkStore:
    def __init__(self, slots, whole, places, sems):
        self.slots, self.whole, self.places, self.sems = slots, whole, places, sems

    def copy(self, i, which):
        slot = lax.rem(i, 2)
        rows = pl.ds(pl.multiple_of(self.places[which] + i * CHUNK, CHUNK), CHUNK)
        return pltpu.make_async_copy(self.slots.at[slot, which], self.whole.at[rows], self.sems.at[slot, which])

    def start(self, i):
        for which in (0, 1):
            self.copy(i, which).start()

    def wait(self, i):
        for which in (0, 1):
            self.copy(i, which).wait()


def whole_spec(shape):
    return pl.BlockSpec(shape, lambda i: (0,) * len(shape))


def decode_top_kernel(
    d1_ref, mixed_ref, gains, grad_ref, wo_ref, w1_ref, w2_ref,
    decoded_ref, grad_two_ref, grad_mix_ref, dgain_ref, whole,
    d2_ref, normed_ref, acc_ref, total_ref, slots, dwo_ref, sems, sem_o,
):
    i = pl.program_id(0)
    store = ChunkStore(slots, whole, (8 * D, 8 * D + FF), sems)

    @pl.when(i == 0)
    def _():
        d2_ref[...] = d1_ref[...] + dot_nn(mixed_ref[...], wo_ref[...])
        normed_ref[...] = rms_norm(d2_ref[...], gains[4:5, :]).astype(jnp.bfloat16)

    pl.when(i >= 2)(lambda: store.wait(i - 2))
    act = feed_back_chunk(
        normed_ref[...], grad_ref[...], w1_ref[...], w2_ref[...], slots.at[lax.rem(i, 2)], total_ref, i == 0
    )
    store.start(i)
    more = dot_nn(act, w2_ref[...])

    @pl.when(i == 0)
    def _():
        acc_ref[...] = d2_ref[...] + more

    @pl.when(i > 0)
    def _():
        acc_ref[...] += more

    @pl.when(i == FF // CHUNK - 1)
    def _():
        decoded_ref[...] = acc_ref[...].astype(jnp.bfloat16)
        grad_x, dgain = norm_back(d2_ref[...], gains[4:5, :], total_ref[...])
        dgain_ref[...] = jnp.broadcast_to(dgain, dgain_ref.shape)
        grad_two = grad_ref[...].astype(jnp.float32) + grad_x
        grad_two_ref[...] = grad_two
        grad_b = grad_two.astype(jnp.bfloat16)
        dwo_ref[...] = dot_tn(mixed_ref[...], grad_b).astype(jnp.bfloat16)
        last = pltpu.make_async_copy(dwo_ref, whole.at[pl.ds(7 * D, D)], sem_o)
        last.start()
        grad_mix_ref[...] = dot_nt(grad_b, wo_ref[...]).astype(jnp.bfloat16)
        store.wait(i - 1)
        store.wait(i)
        last.wait()


def decode_top(d1, mixed, gains, grad_top, dec_w):
    t = d1.shape[0]
    n = FF // CHUNK
    tok = whole_spec((t, D))
    return pl.pallas_call(
        decode_top_kernel,
        grid=(n,),
        in_specs=[
            tok, tok, whole_spec(gains.shape), tok,
            pl.BlockSpec((D, D), lambda i: (7, 0)),
            pl.BlockSpec((CHUNK, D), lambda i: (8 * D // CHUNK + i, 0)),
            pl.BlockSpec((CHUNK, D), lambda i: (8 * D // CHUNK + n + i, 0)),
        ],
        out_specs=[tok, tok, tok, whole_spec((8, D)), pl.BlockSpec(memory_space=pl.ANY)],
        out_shape=[
            jax.ShapeDtypeStruct((t, D), jnp.bfloat16),
            jax.ShapeDtypeStruct((t, D), jnp.float32),
            jax.ShapeDtypeStruct((t, D), jnp.bfloat16),
            jax.ShapeDtypeStruct((8, D), jnp.float32),
            jax.ShapeDtypeStruct(dec_w.shape, jnp.bfloat16),
        ],
        scratch_shapes=[
            pltpu.VMEM((t, D), jnp.float32),
            pltpu.VMEM((t, D), jnp.bfloat16),
            pltpu.VMEM((t, D), jnp.float32),
            pltpu.VMEM((t, D), jnp.float32),
            pltpu.VMEM((2, 2, CHUNK, D), jnp.bfloat16),
            pltpu.VMEM((D, D), jnp.bfloat16),
            pltpu.SemaphoreType.DMA((2, 2)),
            pltpu.SemaphoreType.DMA,
        ],
        compiler_params=pltpu.CompilerParams(vmem_limit_bytes=48 * 1024 * 1024),
        cost_estimate=pl.CostEstimate(flops=14 * t * FF * D, bytes_accessed=8 * FF * D, transcendentals=t * FF),
        name="decode_top",
    )(d1, mixed, gains, grad_top, dec_w, dec_w, dec_w)


MESH = pl.DeviceIdType.MESH


def position():
    r, m = lax.axis_index("rows"), lax.axis_index("mem")
    core = lax.rem(r, 2)
    near = r + 1 - 2 * core
    x_near = r + 2 - 4 * lax.rem(lax.div(r, 2), 2)
    y_near = r + 4 - 8 * lax.div(r, 4)
    first = x_near + core * (y_near - x_near)
    second = y_near + core * (x_near - y_near)
    both = first + second - r
    turn = 1 - 2 * core
    others = (near, second + turn, first + turn, both + turn)
    return r, m, core, near, first, second, both, others


def greet(pos):
    r, m, core, near, first, second = pos[:6]
    barrier = pltpu.get_barrier_semaphore()
    count = 0
    for to in (r, near):
        for step in range(4):
            if to is r and step == 0:
                continue
            pl.semaphore_signal(barrier, inc=1, device_id=(to, lax.rem(m + step, 4)), device_id_type=MESH)
            count += 1
    for to in (first, second):
        pl.semaphore_signal(barrier, inc=1, device_id=(to, m), device_id_type=MESH)
        count += 1
    pl.semaphore_wait(barrier, count)


def remote(src, dst, send, recv, to):
    return pltpu.make_async_remote_copy(
        src_ref=src, dst_ref=dst, send_sem=send, recv_sem=recv, device_id=to, device_id_type=MESH
    )


class Mail:
    def __init__(self, pos):
        self.pos = pos
        self.started = []
        self.maybe = []

    def send(self, make):
        make().start()
        self.started.append(make)

    def send_or_keep(self, here, make, keep):
        pl.when(here())(lambda: keep().start())
        pl.when(jnp.logical_not(here()))(lambda: make().start())
        self.maybe.append((here, make))

    def arrived(self, ref, sem):
        near, m = self.pos[3], self.pos[1]
        remote(ref, ref, sem, sem, (near, m)).wait_recv()

    def finish(self):
        for make in self.started:
            make().wait_send()
        for here, make in self.maybe:
            pl.when(jnp.logical_not(here()))(lambda make=make: make().wait_send())


def dma(*shape):
    return pltpu.SemaphoreType.DMA(shape)


def gather_sems(n):
    return [dma(3, n), dma(3, n), dma(4, n), dma(4, n), dma(4, 2, n), dma(4, 2, n), dma(4, 4, n), dma(4, 4, n), dma(n)]


class Gather:
    def __init__(self, mail, ins, outs, sems):
        self.mail, self.ins, self.outs = mail, ins, outs
        self.z_s, self.z_r, self.a_s, self.a_r, self.b_s, self.b_r, self.c_s, self.c_r, self.l = sems

    def at(self, w, row, step):
        m = self.mail.pos[1]
        size = self.ins[w].shape[0]
        mem = lax.rem(m - step + 4, 4)
        return self.outs[w].at[pl.ds(pl.multiple_of((row * 4 + mem) * size, 32), size)]

    def own(self, w):
        return pltpu.make_async_copy(self.ins[w], self.at(w, self.mail.pos[0], 0), self.l.at[w])

    def ring(self, step):
        r, m, core, near, first, second, both, others = self.mail.pos
        for w in range(len(self.ins)):
            if step == 0:
                self.own(w).start()
            else:
                self.mail.arrived(self.at(w, r, step), self.z_r.at[step - 1, w])

            def src(w=w):
                return self.ins[w] if step == 0 else self.at(w, r, step)

            def dst(w=w):
                return self.at(w, r, step)

            send = self.mail.send
            if step < 3:
                send(lambda w=w, src=src, dst=dst: remote(src(), dst(), self.z_s.at[step, w], self.z_r.at[step, w], (r, lax.rem(m + 1, 4))))
            send(lambda w=w, src=src, dst=dst: remote(src(), dst(), self.a_s.at[step, w], self.a_r.at[step, w], (first, m)))
            send(lambda w=w, src=src, dst=dst: remote(src(), dst(), self.b_s.at[step, 0, w], self.b_r.at[step, 0, w], (second, m)))
            send(lambda w=w, src=src, dst=dst: remote(src(), dst(), self.c_s.at[step, 0, w], self.c_r.at[step, 0, w], (near, m)))

    def from_first(self, step):
        r, m, core, near, first, second, both, others = self.mail.pos
        for w in range(len(self.ins)):
            here = lambda w=w: self.at(w, first, step)
            self.mail.arrived(here(), self.a_r.at[step, w])
            self.mail.send(lambda w=w, here=here: remote(here(), here(), self.b_s.at[step, 1, w], self.b_r.at[step, 1, w], (second, m)))
            self.mail.send(lambda w=w, here=here: remote(here(), here(), self.c_s.at[step, 1, w], self.c_r.at[step, 1, w], (near, m)))

    def from_second(self, step):
        r, m, core, near, first, second, both, others = self.mail.pos
        for k, row in ((0, second), (1, both)):
            for w in range(len(self.ins)):
                here = lambda w=w, row=row: self.at(w, row, step)
                self.mail.arrived(here(), self.b_r.at[step, k, w])
                self.mail.send(lambda w=w, k=k, here=here: remote(here(), here(), self.c_s.at[step, 2 + k, w], self.c_r.at[step, 2 + k, w], (near, m)))

    def finish(self):
        others = self.mail.pos[7]
        for step in range(4):
            for k in range(4):
                for w in range(len(self.ins)):
                    self.mail.arrived(self.at(w, others[k], step), self.c_r.at[step, k, w])
        for w in range(len(self.ins)):
            self.own(w).wait()


def gather_order(gather, more=()):
    steps = [
        (gather.ring, 0), (gather.ring, 1), (gather.from_first, 0), (gather.ring, 2), (gather.from_first, 1),
        (gather.from_second, 0), (gather.ring, 3), (gather.from_first, 2), (gather.from_second, 1),
        (gather.from_first, 3), (gather.from_second, 2), (gather.from_second, 3),
    ]
    return [functools.partial(*step) for step in steps]


def token_sems(n):
    return [dma(n, 2), dma(n, 2), dma(n)]


class TokensIn:
    def __init__(self, mail, pairs, sems):
        self.mail, self.pairs = mail, pairs
        self.t_s, self.t_r, self.t_l = sems

    def start(self, n):
        r, m, core, near = self.mail.pos[:4]
        src, dst = self.pairs[n]
        quarter = src.shape[1]
        holder = lambda: lax.div(m * (3 - m), 2)
        slot = lambda: lax.div(m, 2)
        for i in (0, 1):
            here = lambda i=i: jnp.logical_and(2 * core + i == m, holder() == core)
            place = lambda: dst.at[pl.ds(pl.multiple_of(slot() * quarter, quarter), quarter)]
            make = lambda i=i: remote(src.at[i], place(), self.t_s.at[n, i], self.t_r.at[n, slot()], (r - core + holder(), 2 * core + i))
            keep = lambda i=i: pltpu.make_async_copy(src.at[i], place(), self.t_l.at[n])
            self.mail.send_or_keep(here, make, keep)

    def finish(self):
        r, m, core, near = self.mail.pos[:4]
        for n, (src, dst) in enumerate(self.pairs):
            quarter = src.shape[1]
            for li in (0, 1):
                source = core if li == 0 else 3 - core
                here = jnp.logical_and(lax.div(m, 2) == core, m == source)
                place = lambda: dst.at[pl.ds(li * quarter, quarter)]
                pl.when(here)(lambda: pltpu.make_async_copy(place(), place(), self.t_l.at[n]).wait())
                pl.when(jnp.logical_not(here))(lambda: self.mail.arrived(place(), self.t_r.at[n, li]))


class TokensOut:
    def __init__(self, mail, pairs, sems):
        self.mail, self.pairs = mail, pairs
        self.t_s, self.t_r, self.t_l = sems

    def start(self, n):
        r, m, core, near = self.mail.pos[:4]
        src, dst = self.pairs[n]
        quarter = dst.shape[1]
        row = lambda: lax.rem(m, 2)
        for li in (0, 1):
            to_mem = lambda li=li: core if li == 0 else 3 - core
            here = lambda to_mem=to_mem: jnp.logical_and(to_mem() == m, lax.div(m, 2) == core)
            place = lambda li=li: src.at[pl.ds(li * quarter, quarter)]
            make = lambda li=li, to_mem=to_mem, place=place: remote(place(), dst.at[row()], self.t_s.at[n, li], self.t_r.at[n, row()], (r - core + lax.div(m, 2), to_mem()))
            keep = lambda place=place: pltpu.make_async_copy(place(), dst.at[row()], self.t_l.at[n])
            self.mail.send_or_keep(here, make, keep)

    def finish(self):
        r, m, core, near = self.mail.pos[:4]
        holder = lax.div(m * (3 - m), 2)
        for n, (src, dst) in enumerate(self.pairs):
            for i in (0, 1):
                here = jnp.logical_and(2 * core + i == m, holder == core)
                pl.when(here)(lambda: pltpu.make_async_copy(dst.at[i], dst.at[i], self.t_l.at[n]).wait())
                pl.when(jnp.logical_not(here))(lambda: self.mail.arrived(dst.at[i], self.t_r.at[n, i]))


class NumbersIn:
    def __init__(self, mail, seg_in, seg_out, ids_in, ids_out, sems):
        self.mail, self.seg_in, self.seg_out, self.ids_in, self.ids_out = mail, seg_in, seg_out, ids_in, ids_out
        self.i_s, self.i_r, self.i_l, self.n_s, self.n_r = sems

    def start(self):
        r, m, core, near = self.mail.pos[:4]
        self.mail.send(lambda: remote(self.seg_in.at[lax.rem(m, 2)], self.seg_out, self.n_s, self.n_r, (near, m)))
        for i in (0, 1):
            make = lambda i=i, e=0, to=r: remote(self.ids_in.at[i], self.ids_out.at[m], self.i_s.at[i, e], self.i_r.at[m], (to, 2 * core + i))
            self.mail.send(functools.partial(make, e=1, to=near))
            here = lambda i=i: 2 * core + i == m
            keep = lambda i=i: pltpu.make_async_copy(self.ids_in.at[i], self.ids_out.at[m], self.i_l)
            self.mail.send_or_keep(here, make, keep)

    def finish(self):
        r, m, core, near = self.mail.pos[:4]
        self.mail.arrived(self.seg_out, self.n_r)
        for mem in range(4):
            here = jnp.logical_and(lax.div(m, 2) == core, m == mem)
            place = self.ids_out.at[mem]
            pl.when(here)(lambda: pltpu.make_async_copy(place, place, self.i_l).wait())
            pl.when(jnp.logical_not(here))(lambda: self.mail.arrived(place, self.i_r.at[mem]))


def add_to(total, more):
    def step(i, unused):
        rows = pl.ds(pl.multiple_of(i * 32, 32), 32)
        total[rows, :] = total[rows, :] + more[rows, :]
        return unused

    lax.fori_loop(0, total.shape[0] // 32, step, 0)


def reduce_buffers(size):
    block = lambda *lead: pltpu.VMEM(lead + (size, D), jnp.bfloat16)
    return [block(4, 4), block(4, 4), block(4, 2), block(4), block(3)]


def reduce_sems():
    return [dma(4, 4), dma(4, 4), dma(4, 4), dma(4, 2), dma(4, 2), dma(4), dma(4), dma(3), dma(3), dma(1)]


class Reduce:
    def __init__(self, mail, source, out, buffers, sems):
        self.mail, self.source, self.out = mail, source, out
        self.held, self.rc, self.rb, self.ra, self.rz = buffers
        self.l, self.c_s, self.c_r, self.b_s, self.b_r, self.a_s, self.a_r, self.z_s, self.z_r, self.o = sems

    def at(self, row, j):
        m = self.mail.pos[1]
        size = self.out.shape[0]
        mem = lax.rem(m + 7 - j, 4)
        return self.source.at[pl.ds(pl.multiple_of((row * 4 + mem) * size, 32), size)]

    def load(self, j, k):
        r, m, core, near, first, second, both, others = self.mail.pos
        return pltpu.make_async_copy(self.at((r, first, second, both)[k], j), self.held.at[j, k], self.l.at[j, k])

    def start(self):
        r, m, core, near, first, second, both, others = self.mail.pos
        for j in range(4):
            for k in (3, 2, 1, 0):
                self.mail.send(lambda j=j, k=k: remote(self.at(others[k], j), self.rc.at[j, k], self.c_s.at[j, k], self.c_r.at[j, k], (near, m)))
                self.load(j, k).start()

    def from_core(self, j):
        second, m = self.mail.pos[5], self.mail.pos[1]
        for k in (3, 2, 1, 0):
            self.load(j, k).wait()
            self.mail.arrived(self.rc.at[j, k], self.c_r.at[j, k])
            add_to(self.held.at[j, k], self.rc.at[j, k])
            if k >= 2:
                self.mail.send(lambda k=k: remote(self.held.at[j, k], self.rb.at[j, k - 2], self.b_s.at[j, k - 2], self.b_r.at[j, k - 2], (second, m)))

    def from_second(self, j):
        first, m = self.mail.pos[4], self.mail.pos[1]
        for k in (1, 0):
            self.mail.arrived(self.rb.at[j, k], self.b_r.at[j, k])
            add_to(self.held.at[j, k], self.rb.at[j, k])
            if k == 1:
                self.mail.send(lambda: remote(self.held.at[j, 1], self.ra.at[j], self.a_s.at[j], self.a_r.at[j], (first, m)))

    def result(self):
        return pltpu.make_async_copy(self.held.at[3, 0], self.out, self.o.at[0])

    def from_first(self, j):
        r, m = self.mail.pos[:2]
        self.mail.arrived(self.ra.at[j], self.a_r.at[j])
        add_to(self.held.at[j, 0], self.ra.at[j])
        if j > 0:
            self.mail.arrived(self.rz.at[j - 1], self.z_r.at[j - 1])
            add_to(self.held.at[j, 0], self.rz.at[j - 1])
        if j < 3:
            self.mail.send(lambda: remote(self.held.at[j, 0], self.rz.at[j], self.z_s.at[j], self.z_r.at[j], (r, lax.rem(m + 1, 4))))
        else:
            self.result().start()

    def finish(self):
        self.result().wait()


def reduce_order(reduce):
    steps = [
        (reduce.from_core, 0), (reduce.from_core, 1), (reduce.from_second, 0), (reduce.from_core, 2),
        (reduce.from_second, 1), (reduce.from_first, 0), (reduce.from_core, 3), (reduce.from_second, 2),
        (reduce.from_first, 1), (reduce.from_second, 3), (reduce.from_first, 2), (reduce.from_first, 3),
    ]
    return [functools.partial(*step) for step in steps]


class GainSums:
    def __init__(self, mail, own, out, rg, gs, gz, sems):
        self.mail, self.own, self.out, self.rg, self.gs, self.gz = mail, own, out, rg, gs, gz
        self.g_s, self.g_r, self.gz_s, self.gz_r = sems

    def hop(self, n):
        r, m, core, near, first, second, both, others = self.mail.pos
        x_near = first + core * (second - first)
        y_near = second + core * (first - second)
        if n > 0:
            self.mail.arrived(self.rg.at[n - 1], self.g_r.at[n - 1])
            before = self.own[...] if n == 1 else self.gs[n - 2]
            self.gs[n - 1] = before + self.rg[n - 1]
        if n < 3:
            src = lambda: self.own if n == 0 else self.gs.at[n - 1]
            to = (near, x_near, y_near)[n]
            self.mail.send(lambda: remote(src(), self.rg.at[n], self.g_s.at[n], self.g_r.at[n], (to, m)))
            return
        self.gz[m] = self.gs[2]
        for hop in (1, 2, 3):
            self.mail.send(lambda hop=hop: remote(self.gs.at[2], self.gz.at[m], self.gz_s.at[hop - 1], self.gz_r.at[m], (r, lax.rem(m + hop, 4))))

    def finish(self):
        m = self.mail.pos[1]
        for mem in range(4):
            pl.when(m != mem)(lambda mem=mem: self.mail.arrived(self.gz.at[mem], self.gz_r.at[mem]))
        self.out[...] = (self.gz[0] + self.gz[1]) + (self.gz[2] + self.gz[3])


ANY = pl.BlockSpec(memory_space=pl.ANY)


def shaped(shape, kind=jnp.bfloat16):
    return jax.ShapeDtypeStruct(shape, kind)


def gather_encoder_kernel(enc_in, q_in, seg_in, ids_in, enc_out, q_out, seg_out, ids_out, *sems):
    mail = Mail(position())
    gather = Gather(mail, (enc_in,), (enc_out,), sems[:9])
    tokens = TokensIn(mail, ((q_in, q_out),), sems[9:12])
    numbers = NumbersIn(mail, seg_in, seg_out, ids_in, ids_out, sems[12:])
    greet(mail.pos)
    numbers.start()
    steps = gather_order(gather)
    steps[0]()
    tokens.start(0)
    for step in steps[1:]:
        step()
    gather.finish()
    tokens.finish()
    numbers.finish()
    mail.finish()


def gather_encoder(enc_t, q, seg, ids):
    return pl.pallas_call(
        gather_encoder_kernel,
        in_specs=[ANY] * 4,
        out_specs=[ANY] * 4,
        out_shape=[
            shaped((32 * enc_t.shape[0], D)),
            shaped((2 * q.shape[1], D)),
            shaped(seg.shape[1:], jnp.int32),
            shaped((4,) + ids.shape[1:], jnp.int32),
        ],
        scratch_shapes=gather_sems(1) + token_sems(1) + [dma(2, 2), dma(4), dma(), dma(), dma()],
        compiler_params=pltpu.CompilerParams(collective_id=0, has_side_effects=True),
        name="gather_encoder",
    )(enc_t, q, seg, ids)


def reduce_encoder_kernel(enc_in, q_in, gain_in, enc_out, q_out, gain_out, *rest):
    mail = Mail(position())
    reduce = Reduce(mail, enc_in, enc_out, rest[:5], rest[5:15])
    tokens = TokensOut(mail, ((q_in, q_out),), rest[15:18])
    gains = GainSums(mail, gain_in, gain_out, *rest[18:21], rest[21:])
    greet(mail.pos)
    gains.hop(0)
    reduce.start()
    steps = reduce_order(reduce)
    steps[0]()
    gains.hop(1)
    tokens.start(0)
    steps[1]()
    gains.hop(2)
    for step in steps[2:6]:
        step()
    gains.hop(3)
    for step in steps[6:]:
        step()
    reduce.finish()
    tokens.finish()
    gains.finish()
    mail.finish()


def reduce_encoder(enc_g, q, gains):
    vmem = pl.BlockSpec(memory_space=pltpu.VMEM)
    size = enc_g.shape[0] // 32
    small = lambda n: pltpu.VMEM((n,) + gains.shape, jnp.float32)
    return pl.pallas_call(
        reduce_encoder_kernel,
        in_specs=[ANY, ANY, vmem],
        out_specs=[ANY, ANY, vmem],
        out_shape=[shaped((size, D)), shaped((2, q.shape[0] // 2, D)), shaped(gains.shape, jnp.float32)],
        scratch_shapes=reduce_buffers(size) + reduce_sems() + token_sems(1) + [small(3), small(3), small(4)]
        + [dma(3), dma(3), dma(3), dma(4)],
        compiler_params=pltpu.CompilerParams(collective_id=3, has_side_effects=True, vmem_limit_bytes=40 * 1024 * 1024),
        name="reduce_encoder",
    )(enc_g, q, gains)


PAIRS = H // 2
CHUNKS = FF // CHUNK


def encode_kernel(
    fast, own_len, extra,
    q_ref, qaug_ref, own_k, own_v, oth_k, oth_v, kaug_ref, x_ref, gains, wo_ref, w1_ref, w2_ref, *rest,
):
    i = pl.program_id(0)
    if fast:
        dec_in, a_in, g_in = rest[:3]
        o_ref, lse_ref, h1_ref, nf1_ref, h2_ref, ne_ref, dec_out, a_out, g_out = rest[3:12]
        s_ref, ff_ref = rest[12:14]
        sems = rest[14:]
        mail = Mail(position())
        gather = Gather(mail, (dec_in,), (dec_out,), sems[:9])
        tokens = TokensIn(mail, ((a_in, a_out), (g_in, g_out)), sems[9:12])
        steps = gather_order(gather)
        places = {2: (1, 2), 4: (3, 4), 5: (5,), 6: (6, 7), 7: (8,), 8: (9,), 10: (10,)}

        @pl.when(i == 0)
        def _():
            greet(mail.pos)
            steps[0]()

        for at, which in places.items():

            @pl.when(i == at)
            def _(at=at, which=which):
                for n in which:
                    steps[n]()
                if at == 6:
                    tokens.start(0)
                    tokens.start(1)
    else:
        o_ref, lse_ref, h1_ref, nf1_ref, h2_ref, ne_ref = rest[:6]
        s_ref, ff_ref = rest[6:]

    @pl.when(i < PAIRS)
    def _():
        cols = pl.ds(pl.multiple_of(i * 128, 128), 128)
        attend_pair(
            False, own_len, extra, chunk_sets(False, own_len, extra)[0],
            q_ref, qaug_ref, own_k, own_v, oth_k, oth_v, kaug_ref, o_ref.at[:, cols], lse_ref, s_ref,
        )

    @pl.when(i == PAIRS)
    def _():
        h1_ref[...] = x_ref[...].astype(jnp.float32) + dot_nn(o_ref[...], wo_ref[...])
        nf1_ref[...] = rms_norm(h1_ref[...], gains[1:2, :]).astype(jnp.bfloat16)
        ff_ref[...] = h1_ref[...]

    @pl.when(i >= PAIRS)
    def _():
        act = gelu_pair(dot_nt(nf1_ref[...], w1_ref[...]))[0].astype(jnp.bfloat16)
        ff_ref[...] += dot_nn(act, w2_ref[...])

    @pl.when(i == PAIRS + CHUNKS - 1)
    def _():
        h2_ref[...] = ff_ref[...]
        ne_ref[...] = rms_norm(ff_ref[...], gains[5:6, :]).astype(jnp.bfloat16)
        if fast:
            steps[11]()
            gather.finish()
            tokens.finish()
            mail.finish()


def encode(fast, q, qaug, own_kv, oth_kv, kaug, x, gains, enc_w, dec_t, a, g):
    t = q.shape[0]
    nk = own_kv.shape[0]
    pair = lambda i: jnp.minimum(i, PAIRS - 1)
    chunk = lambda i: jnp.maximum(i - PAIRS, 0)
    col = lambda first: pl.BlockSpec((nk, 128), lambda i: (0, first + pair(i)))
    tok = whole_spec((t, D))
    dims = lambda kind: jax.ShapeDtypeStruct((t, D), kind)
    in_specs = [
        pl.BlockSpec((t, 128), lambda i: (0, pair(i))), whole_spec((t, 128)),
        col(0), col(PAIRS), col(0), col(PAIRS), whole_spec((2 * nk, 128)), tok, whole_spec(gains.shape),
        pl.BlockSpec((D, D), lambda i: (3, 0)),
        pl.BlockSpec((CHUNK, D), lambda i: (4 * D // CHUNK + chunk(i), 0)),
        pl.BlockSpec((CHUNK, D), lambda i: (4 * D // CHUNK + CHUNKS + chunk(i), 0)),
    ]
    args = [q, qaug, own_kv, own_kv, oth_kv, oth_kv, kaug, x, gains, enc_w, enc_w, enc_w]
    out_specs = [tok, pl.BlockSpec((t, 128), lambda i: (0, pair(i))), tok, tok, tok, tok]
    out_shape = [dims(jnp.bfloat16), dims(jnp.float32), dims(jnp.float32), dims(jnp.bfloat16), dims(jnp.float32), dims(jnp.bfloat16)]
    scratch = [
        pltpu.VMEM((t // QB, 2 * nk, 2 * QB), jnp.float32), pltpu.VMEM((t, D), jnp.float32),
    ]
    params = dict(vmem_limit_bytes=48 * 1024 * 1024)
    if fast:
        in_specs += [ANY] * 3
        args += [dec_t, a, g]
        out_specs += [ANY] * 3
        out_shape += [shaped((32 * dec_t.shape[0], D)), dims(jnp.bfloat16), dims(jnp.bfloat16)]
        scratch += gather_sems(1) + token_sems(2)
        params.update(collective_id=1, has_side_effects=True)
    return pl.pallas_call(
        functools.partial(encode_kernel, fast, t, nk - t),
        grid=(PAIRS + CHUNKS,),
        in_specs=in_specs,
        out_specs=out_specs,
        out_shape=out_shape,
        scratch_shapes=scratch,
        compiler_params=pltpu.CompilerParams(**params),
        name="encode",
    )(*args)


def encode_back_kernel(
    fast, own_len, extra,
    grad_ref, nf1_ref, h1_ref, gains, wo_ref, w1_ref, w2_ref, o_ref,
    q_ref, qaug_ref, own_k, own_v, oth_k, oth_v, kaug_ref, lse_ref, *rest,
):
    i = pl.program_id(0)
    if fast:
        dec_g, y_in, a_in = rest[:3]
        rest = rest[3:]
    whole, grad_h_ref, dgain_ref, dq_ref, dko_ref, dvo_ref, dkt_ref, dvt_ref = rest[:8]
    rest = rest[8:]
    if fast:
        dec_out, y_out, a_out = rest[:3]
        rest = rest[3:]
    total_ref, grad_b, mix_ref, slots, dwo_ref, sems, sem_o, dk_acc, dv_acc = rest[:9]
    store = ChunkStore(slots, whole, (4 * D, 4 * D + FF), sems)
    store_o = lambda: pltpu.make_async_copy(dwo_ref, whole.at[pl.ds(3 * D, D)], sem_o)
    if fast:
        rest = rest[9:]
        mail = Mail(position())
        reduce = Reduce(mail, dec_g, dec_out, rest[:5], rest[5:15])
        tokens = TokensOut(mail, ((y_in, y_out), (a_in, a_out)), rest[15:])
        steps = reduce_order(reduce)
        places = {1: (0,), 2: (1,), 4: (2, 3), 7: (4, 6), 8: (5,), 10: (7, 8)}

        @pl.when(i == 0)
        def _():
            greet(mail.pos)
            reduce.start()
            tokens.start(0)
            tokens.start(1)

        for at, which in places.items():

            @pl.when(i == at)
            def _(which=which):
                for n in which:
                    steps[n]()

    @pl.when(i == 0)
    def _():
        grad_b[...] = grad_ref[...].astype(jnp.bfloat16)

    @pl.when(i < CHUNKS)
    def _():
        pl.when(i >= 2)(lambda: store.wait(i - 2))
        feed_back_chunk(
            nf1_ref[...], grad_b[...], w1_ref[...], w2_ref[...], slots.at[lax.rem(i, 2)], total_ref, i == 0
        )
        store.start(i)

    @pl.when(i == CHUNKS - 1)
    def _():
        grad_x, dgain = norm_back(h1_ref[...], gains[1:2, :], total_ref[...])
        dgain_ref[...] = jnp.broadcast_to(dgain, dgain_ref.shape)
        grad_h = grad_ref[...] + grad_x
        grad_h_ref[...] = grad_h
        top = grad_h.astype(jnp.bfloat16)
        dwo_ref[...] = dot_tn(o_ref[...], top).astype(jnp.bfloat16)
        store_o().start()
        mix_ref[...] = dot_nt(top, wo_ref[...]).astype(jnp.bfloat16)
        store.wait(i - 1)
        store.wait(i)

    @pl.when(i >= CHUNKS)
    def _():
        cols = pl.ds(pl.multiple_of((i - CHUNKS) * 128, 128), 128)
        back_pair(
            False, own_len, extra, chunk_sets(False, own_len, extra)[0], q_ref, qaug_ref, own_k, own_v, oth_k, oth_v, kaug_ref,
            o_ref.at[:, cols], lse_ref, mix_ref.at[:, cols],
            dq_ref, dko_ref, dvo_ref, dkt_ref, dvt_ref, dk_acc, dv_acc,
        )

    @pl.when(i == PAIRS + CHUNKS - 1)
    def _():
        store_o().wait()
        if fast:
            for n in (9, 10, 11):
                steps[n]()
            reduce.finish()
            tokens.finish()
            mail.finish()


def encode_back(fast, grad, nf1, h1, gains, enc_w, o, q, qaug, own_kv, oth_kv, kaug, lse, dec_g, y, a):
    t = q.shape[0]
    nk = own_kv.shape[0]
    pair = lambda i: jnp.maximum(i - CHUNKS, 0)
    chunk = lambda i: jnp.minimum(i, CHUNKS - 1)
    col = lambda first: pl.BlockSpec((nk, 128), lambda i: (0, first + pair(i)))
    cols = pl.BlockSpec((t, 128), lambda i: (0, pair(i)))
    tok = whole_spec((t, D))
    dims = lambda kind, n=t: jax.ShapeDtypeStruct((n, D), kind)
    in_specs = [
        tok, tok, tok, whole_spec(gains.shape),
        pl.BlockSpec((D, D), lambda i: (3, 0)),
        pl.BlockSpec((CHUNK, D), lambda i: (4 * D // CHUNK + chunk(i), 0)),
        pl.BlockSpec((CHUNK, D), lambda i: (4 * D // CHUNK + CHUNKS + chunk(i), 0)),
        tok, cols, whole_spec((t, 128)), col(0), col(PAIRS), col(0), col(PAIRS), whole_spec((2 * nk, 128)), cols,
    ]
    args = [grad, nf1, h1, gains, enc_w, enc_w, enc_w, o, q, qaug, own_kv, own_kv, oth_kv, oth_kv, kaug, lse]
    out_specs = [pl.BlockSpec(memory_space=pl.ANY), tok, whole_spec((8, D)), cols, col(0), col(0), col(0), col(0)]
    out_shape = [
        jax.ShapeDtypeStruct(enc_w.shape, jnp.bfloat16), dims(jnp.float32), dims(jnp.float32, 8), dims(jnp.bfloat16),
        dims(jnp.float32, nk), dims(jnp.float32, nk), dims(jnp.bfloat16, nk), dims(jnp.bfloat16, nk),
    ]
    scratch = [
        pltpu.VMEM((t, D), jnp.float32), pltpu.VMEM((t, D), jnp.bfloat16), pltpu.VMEM((t, D), jnp.bfloat16),
        pltpu.VMEM((2, 2, CHUNK, D), jnp.bfloat16), pltpu.VMEM((D, D), jnp.bfloat16),
        pltpu.SemaphoreType.DMA((2, 2)), pltpu.SemaphoreType.DMA,
        pltpu.VMEM((2 * nk, 128), jnp.float32), pltpu.VMEM((2 * nk, 128), jnp.float32),
    ]
    params = dict(vmem_limit_bytes=60 * 1024 * 1024)
    if fast:
        size = dec_g.shape[0] // 32
        in_specs += [ANY] * 3
        args += [dec_g, y, a]
        out_specs += [ANY] * 3
        out_shape += [shaped((size, D)), shaped((2, t // 2, D)), shaped((2, t // 2, D))]
        scratch += reduce_buffers(size) + reduce_sems() + token_sems(2)
        params.update(collective_id=2, has_side_effects=True)
    return pl.pallas_call(
        functools.partial(encode_back_kernel, fast, t, nk - t),
        grid=(PAIRS + CHUNKS,),
        in_specs=in_specs,
        out_specs=out_specs,
        out_shape=out_shape,
        scratch_shapes=scratch,
        compiler_params=pltpu.CompilerParams(**params),
        name="encode_back",
    )(*args)


def project(left, weight_t):
    return jnp.einsum("nd,ed->ne", left, weight_t, preferred_element_type=jnp.float32)


def project_back(left, weight_t):
    return jnp.einsum("ne,ed->nd", left, weight_t, preferred_element_type=jnp.float32)


def outer_sum(wide, narrow):
    return jnp.einsum("ne,nd->ed", wide, narrow, preferred_element_type=jnp.float32).astype(jnp.bfloat16)


def output_back(grad, mixed_b, w_out):
    grad_b = grad.astype(jnp.bfloat16)
    return (outer_sum(mixed_b, grad_b), project(grad_b, w_out).astype(jnp.bfloat16))


def partner(values):
    n_rows = lax.axis_size("rows")
    return lax.ppermute(values, "rows", [(i, i ^ 1) for i in range(n_rows)])


def my_row(values):
    core = lax.axis_index("rows") % 2
    mem = lax.axis_index("mem")
    chosen = jnp.where(mem // 2 == core, values, partner(values))
    return lax.dynamic_index_in_dim(chosen, mem % 2, 0, keepdims=False)


def quarters_of(core):
    return (jnp.where(core == 0, 0, 1), jnp.where(core == 0, 3, 2))


def own_quarters(row, core, quarter):
    return jnp.concatenate(
        [lax.dynamic_slice_in_dim(row, place * quarter, quarter, 0) for place in quarters_of(core)], 0
    )


def to_rows(values):
    quarter = values.shape[1]
    row = my_row(lax.all_gather(values, "mem", axis=1, tiled=True))
    return own_quarters(row, lax.axis_index("rows") % 2, quarter)


def from_rows(values):
    quarter = values.shape[0] // 2
    core = lax.axis_index("rows") % 2
    mem = lax.axis_index("mem")
    gathered = lax.all_gather(values, "mem", axis=0)
    other = partner(gathered)
    holder = jnp.where((mem == 0) | (mem == 3), 0, 1)
    chosen = jnp.where(holder == core, gathered, other)
    return lax.dynamic_slice(
        chosen, (2 * core, jnp.where(mem < 2, 0, quarter), 0), (2, quarter, values.shape[1])
    )


def gather_weights(params):
    return lax.all_gather(params.T, ("rows", "mem"), axis=0, tiled=True)


def reduce_weights(grads):
    return lax.psum_scatter(grads, ("rows", "mem"), scatter_dimension=0, tiled=True)


def on_device(
    fast,
    questions,
    answers,
    q_segments,
    a_segments,
    entry_ids,
    entry_alive_flags,
    memory_table,
    enc_params,
    dec_params,
    norm_gains,
    cotangent,
):
    quarter = questions.shape[1]
    core = lax.axis_index("rows") % 2
    per_row, slots = entry_alive_flags.shape[1], entry_alive_flags.shape[2]
    half = per_row // 2
    rows_here, row_len = q_segments.shape
    segs = jnp.concatenate([q_segments, a_segments, entry_alive_flags.reshape(rows_here, -1)], 1)
    if fast:
        segs = jnp.pad(segs, ((0, 0), (0, -segs.shape[1] % 1024))).reshape(rows_here, -1, 128)
        own_ids = entry_ids.reshape(rows_here, -1)
        n_ids = own_ids.shape[1]
        own_ids = jnp.pad(own_ids, ((0, 0), (0, 1024 - n_ids))).reshape(rows_here, 8, 128)
        enc_w, x_question, other_segs, ids = gather_encoder(enc_params.T, questions, segs, own_ids)
        mem = lax.axis_index("mem")
        numbers = jnp.where(
            mem // 2 == core, lax.dynamic_index_in_dim(segs, mem % 2, 0, keepdims=False), other_segs
        ).reshape(-1)
        ids = ids.reshape(ids.shape[0], -1)[:, :n_ids].reshape(ids.shape[0], per_row, -1)
        ids = ids.transpose(1, 0, 2).reshape(-1)
    else:
        enc_w, dec_w = gather_weights(enc_params), gather_weights(dec_params)
        ids = my_row(lax.all_gather(entry_ids, "mem", axis=2, tiled=True)).reshape(-1)
        numbers = my_row(segs)
        x_question, x_answer = to_rows(questions), to_rows(answers)
        grad_top = to_rows(cotangent.astype(jnp.bfloat16))
    gains = jnp.pad(norm_gains, ((0, 2), (0, 0)))
    q_row = numbers[:row_len]
    a_row = numbers[row_len : 2 * row_len]
    alive = numbers[2 * row_len : 2 * row_len + per_row * slots]

    own_ids = lax.dynamic_slice_in_dim(ids, core * half * slots, half * slots, 0)
    entry_vals = memory_table[own_ids].reshape(half * slots * 2, D).astype(jnp.float32)
    n_prefix = entry_vals.shape[0]
    extra = -(-n_prefix // 128) * 128
    place = jnp.arange(extra, dtype=jnp.int32)

    def prefix_segments(which):
        question = which * half + place // (2 * slots)
        live = lax.dynamic_slice_in_dim(alive, which * half * slots, half * slots, 0)
        live = jnp.pad(jnp.repeat(live, 2), (0, extra - n_prefix))
        return jnp.where(live == 1, question, -1)

    tokens = 2 * quarter
    own_q = own_quarters(q_row, core, quarter)
    other_q = own_quarters(q_row, 1 - core, quarter)
    own_a = own_quarters(a_row, core, quarter)
    other_a = own_quarters(a_row, 1 - core, quarter)
    q_aug, a_aug = seg_aug_q(own_q), seg_aug_q(own_a)
    enc_aug = seg_aug_k(
        jnp.concatenate([own_q, prefix_segments(core), other_q, prefix_segments(1 - core)])
    )
    self_aug = seg_aug_k(jnp.concatenate([own_a, other_a]))
    cross_aug = seg_aug_k(jnp.concatenate([own_q, other_q]))

    enc_in = jnp.concatenate([x_question.astype(jnp.float32), jnp.pad(entry_vals, ((0, extra - n_prefix), (0, 0)))], 0)
    normed_q = rms_norm(enc_in, norm_gains[0]).astype(jnp.bfloat16)
    query_enc = project(normed_q[:tokens], enc_w[:D]).astype(jnp.bfloat16)
    enc_kv = project(normed_q, enc_w[D : 3 * D]).astype(jnp.bfloat16)
    enc_kv_other = partner(enc_kv)

    mixed_enc, logsum_enc, hidden_one, normed_f1, hidden_two, encoded, *gathered = encode(
        fast, query_enc, q_aug, enc_kv, enc_kv_other, enc_aug, x_question, gains, enc_w,
        dec_params.T, answers, cotangent.astype(jnp.bfloat16),
    )
    if fast:
        dec_w, x_answer, grad_top = gathered
    x_answer = x_answer.astype(jnp.float32)
    normed_a = rms_norm(x_answer, norm_gains[2]).astype(jnp.bfloat16)
    qkv_self = project(normed_a, dec_w[: 3 * D]).astype(jnp.bfloat16)
    query_self, self_kv = qkv_self[:, :D], qkv_self[:, D:]
    self_kv_other = partner(self_kv)
    cross_kv = project(encoded, dec_w[5 * D : 7 * D]).astype(jnp.bfloat16)
    cross_kv_other = partner(cross_kv)

    mixed_self, logsum_self = attend(True, core, query_self, a_aug, self_kv, self_kv_other, self_aug)
    dec_one = x_answer + project_back(mixed_self, dec_w[3 * D : 4 * D])
    normed_c = rms_norm(dec_one, norm_gains[3]).astype(jnp.bfloat16)
    query_cross = project(normed_c, dec_w[4 * D : 5 * D]).astype(jnp.bfloat16)
    mixed_cross, logsum_cross = attend(
        False, core, query_cross, a_aug, cross_kv, cross_kv_other, cross_aug
    )
    decoded, grad_two, grad_mixc, grad_gain4, dec_full = decode_top(
        dec_one, mixed_cross, gains, grad_top, dec_w
    )
    grad_qc, dk_own, dv_own, dk_other, dv_other = attend_back(
        False, core, query_cross, a_aug, cross_kv, cross_kv_other, cross_aug,
        mixed_cross, logsum_cross, grad_mixc,
    )
    more = partner(jnp.concatenate([dk_other, dv_other], 1)).astype(jnp.float32)
    grad_ckv = (jnp.concatenate([dk_own, dv_own], 1) + more).astype(jnp.bfloat16)
    grad_wqc = outer_sum(grad_qc, normed_c)
    grad_x, grad_gain3 = norm_back(
        dec_one, norm_gains[3], project_back(grad_qc, dec_w[4 * D : 5 * D])
    )
    grad_one = grad_two + grad_x
    grad_wckv = outer_sum(grad_ckv, encoded)
    grad_encoded, grad_gain5 = norm_back(
        hidden_two, norm_gains[5], project_back(grad_ckv, dec_w[5 * D : 7 * D])
    )
    grad_wos, grad_mixs = output_back(grad_one, mixed_self, dec_w[3 * D : 4 * D])
    grad_qs, dk_own, dv_own, dk_other, dv_other = attend_back(
        True, core, query_self, a_aug, self_kv, self_kv_other, self_aug,
        mixed_self, logsum_self, grad_mixs,
    )
    more = partner(jnp.concatenate([dk_other, dv_other], 1)).astype(jnp.float32)
    grad_skv = (jnp.concatenate([dk_own, dv_own], 1) + more).astype(jnp.bfloat16)
    grad_self = jnp.concatenate([grad_qs, grad_skv], 1)
    grad_wself = outer_sum(grad_self, normed_a)
    grad_x, grad_gain2 = norm_back(x_answer, norm_gains[2], project_back(grad_self, dec_w[: 3 * D]))
    grad_answers = (grad_one + grad_x).astype(jnp.bfloat16)
    dec_full = dec_full.at[: 3 * D].set(grad_wself)
    dec_full = dec_full.at[3 * D : 4 * D].set(grad_wos)
    dec_full = dec_full.at[4 * D : 5 * D].set(grad_wqc)
    dec_full = dec_full.at[5 * D : 7 * D].set(grad_wckv)

    enc_full, grad_hidden, grad_gain1, grad_qe, dk_own, dv_own, dk_other, dv_other, *reduced = encode_back(
        fast, grad_encoded, normed_f1, hidden_one, gains, enc_w, mixed_enc, query_enc, q_aug,
        enc_kv, enc_kv_other, enc_aug, logsum_enc, dec_full, decoded, grad_answers,
    )
    more = partner(jnp.concatenate([dk_other, dv_other], 1)).astype(jnp.float32)
    grad_ekv = (jnp.concatenate([dk_own, dv_own], 1) + more).astype(jnp.bfloat16)
    grad_wqe = outer_sum(grad_qe, normed_q[:tokens])
    grad_wkve = outer_sum(grad_ekv, normed_q)
    grad_in = project_back(grad_ekv, enc_w[D : 3 * D])
    grad_in = grad_in + jnp.pad(project_back(grad_qe, enc_w[:D]), ((0, extra), (0, 0)))
    grad_x, grad_gain0 = norm_back(enc_in, norm_gains[0], grad_in)
    grad_questions = (grad_hidden + grad_x[:tokens]).astype(jnp.bfloat16)
    enc_full = enc_full.at[:D].set(grad_wqe)
    enc_full = enc_full.at[D : 3 * D].set(grad_wkve)
    gain_terms = jnp.concatenate(
        [grad_gain0, grad_gain1[:1], grad_gain2, grad_gain3, grad_gain4[:1], grad_gain5], 0
    )
    if fast:
        grad_decoder, decoded, grad_answers = reduced
        grad_encoder, grad_questions, grad_gains = reduce_encoder(
            enc_full, grad_questions, jnp.pad(gain_terms, ((0, 2), (0, 0)))
        )
        grad_gains = grad_gains[:6]
    else:
        decoded, grad_questions, grad_answers = (
            from_rows(values) for values in (decoded, grad_questions, grad_answers)
        )
        grad_gains = lax.psum(gain_terms, ("rows", "mem"))
        grad_encoder, grad_decoder = reduce_weights(enc_full), reduce_weights(dec_full)
    return (
        decoded,
        grad_questions.astype(jnp.float32),
        grad_answers.astype(jnp.float32),
        grad_encoder.astype(jnp.float32).T,
        grad_decoder.astype(jnp.float32).T,
        grad_gains,
    )


def solution(mesh):
    fast = mesh.shape["rows"] == 8 and mesh.shape["mem"] == 4
    return jax.shard_map(
        functools.partial(on_device, fast),
        mesh=mesh,
        in_specs=(
            P("rows", "mem", None),
            P("rows", "mem", None),
            P("rows", None),
            P("rows", None),
            P("rows", None, "mem"),
            P("rows", None, None),
            P(),
            P(None, ("rows", "mem")),
            P(None, ("rows", "mem")),
            P(),
            P("rows", "mem", None),
        ),
        out_specs=(
            P("rows", "mem", None),
            P("rows", "mem", None),
            P("rows", "mem", None),
            P(None, ("rows", "mem")),
            P(None, ("rows", "mem")),
            P(),
        ),
        check_vma=False,
    )
```

```python
import functools
import jax
import jax.numpy as jnp
from jax import lax
from jax.experimental import pallas as pl
from jax.experimental.pallas import tpu as pltpu
from jax.sharding import PartitionSpec as P

D = 768
H = 12
HD = 64
FF = 3072
QB = 256
masked_score = -1e30


def key_chunks(own_len, extra):
    chunks = []
    for side in (0, 1):
        for at in range(own_len // QB):
            chunks.append((side, at * QB, QB))
        if extra:
            chunks.append((side, own_len, extra))
    return chunks


def chunk_sets(causal, own_len, extra):
    chunks = key_chunks(own_len, extra)
    if not causal:
        return [[list(range(len(chunks)))] * (own_len // QB)]
    quarters = ((0, 3), (1, 2))
    sets = []
    for core in (0, 1):
        held = (quarters[core], quarters[1 - core])
        sets.append([
            [n for n, (side, at, size) in enumerate(chunks) if held[side][at // QB] <= held[0][qb]]
            for qb in range(own_len // QB)
        ])
    return sets


def attend_pair(causal, own_len, extra, use, q_ref, qaug_ref, own_k, own_v, oth_k, oth_v, kaug_ref, o_ref, lse_ref, s_ref):
    low = lax.broadcasted_iota(jnp.int32, (1, 128), 1) < HD
    chunks = key_chunks(own_len, extra)
    nk = own_len + extra
    for qb in range(own_len // QB):
        rows = pl.ds(qb * QB, QB)
        q = q_ref[rows, :] * jnp.bfloat16(HD ** (-0.5))
        qaug = qaug_ref[rows, :]
        queries = (jnp.where(low, q, qaug), jnp.where(low, qaug, q))
        tops = [None, None]
        for ci in use[qb]:
            side, at, size = chunks[ci]
            k = (own_k, oth_k)[side][at : at + size, :]
            place = slice(side * nk + at, side * nk + at + size)
            kaug = kaug_ref[place, :]
            for h in (0, 1):
                keys = jnp.where(low, k, kaug) if h == 0 else jnp.where(low, kaug, k)
                s = lax.dot_general(keys, queries[h], (((1,), (1,)), ((), ())), preferred_element_type=jnp.float32)
                if causal and side == 0 and at == qb * QB:
                    tri = lax.broadcasted_iota(jnp.int32, (size, QB), 0) <= lax.broadcasted_iota(jnp.int32, (size, QB), 1)
                    s = jnp.where(tri, s, masked_score)
                s_ref[qb, place, h * QB : (h + 1) * QB] = s
                top = jnp.max(s.reshape(size // 8, 8, QB), 0)
                tops[h] = top if tops[h] is None else jnp.maximum(tops[h], top)
        m = jnp.max(jnp.concatenate(tops, 1), 0, keepdims=True)
        total, acc = None, None
        for ci in use[qb]:
            side, at, size = chunks[ci]
            v = (own_v, oth_v)[side][at : at + size, :]
            zero = jnp.zeros_like(v)
            place = slice(side * nk + at, side * nk + at + size)
            p = jnp.exp(s_ref[qb, place, :] - m)
            part = jnp.sum(p.reshape(size // 8, 8, 2 * QB), 0)
            total = part if total is None else total + part
            pb = p.astype(jnp.bfloat16)
            pb = jnp.concatenate([pb[:, :QB], pb[:, QB:]], 0)
            v_split = jnp.concatenate([jnp.where(low, v, zero), jnp.where(low, zero, v)], 0)
            part = lax.dot_general(pb, v_split, (((0,), (0,)), ((), ())), preferred_element_type=jnp.float32)
            acc = part if acc is None else acc + part
        total = jnp.sum(total, 0, keepdims=True)
        lse = m + jnp.log(total)
        rec = 1.0 / total
        wide = lambda row, h: jnp.broadcast_to(row[:, h * QB : (h + 1) * QB], (HD, QB))
        o_ref[rows, :] = (acc * jnp.concatenate([wide(rec, 0), wide(rec, 1)], 0).T).astype(jnp.bfloat16)
        lse_ref[rows, :] = jnp.concatenate([wide(lse, 1), wide(lse, 0)], 0).T


def by_core(core, sets, work):
    if len(sets) == 1:
        work(sets[0])
        return
    for n, use in enumerate(sets):
        pl.when(core[0] == n)(functools.partial(work, use))


def attend_kernel(causal, own_len, extra, core, *refs):
    by_core(core, chunk_sets(causal, own_len, extra), lambda use: attend_pair(causal, own_len, extra, use, *refs))


def back_kernel(causal, own_len, extra, core, *refs):
    by_core(core, chunk_sets(causal, own_len, extra), lambda use: back_pair(causal, own_len, extra, use, *refs))


def attend(causal, core, q, qaug, own_kv, oth_kv, kaug):
    t = q.shape[0]
    nk = own_kv.shape[0]
    col = lambda first: pl.BlockSpec((nk, 128), lambda i, a: (0, first + i))
    return pl.pallas_call(
        functools.partial(attend_kernel, causal, t, nk - t),
        grid_spec=pltpu.PrefetchScalarGridSpec(
            num_scalar_prefetch=1,
            grid=(H // 2,),
            in_specs=[
                pl.BlockSpec((t, 128), lambda i, a: (0, i)),
                pl.BlockSpec((t, 128), lambda i, a: (0, 0)),
                col(0), col(H // 2), col(0), col(H // 2),
                pl.BlockSpec((2 * nk, 128), lambda i, a: (0, 0)),
            ],
            out_specs=[pl.BlockSpec((t, 128), lambda i, a: (0, i))] * 2,
            scratch_shapes=[pltpu.VMEM((t // QB, 2 * nk, 2 * QB), jnp.float32)],
        ),
        out_shape=[jax.ShapeDtypeStruct((t, D), jnp.bfloat16), jax.ShapeDtypeStruct((t, D), jnp.float32)],
        compiler_params=pltpu.CompilerParams(vmem_limit_bytes=32 * 1024 * 1024),
        cost_estimate=pl.CostEstimate(flops=4 * t * 2 * nk * D, bytes_accessed=8 * nk * D, transcendentals=t * 2 * nk * H),
        name="attend",
    )(core.reshape(1), q, qaug, own_kv, own_kv, oth_kv, oth_kv, kaug)


def three_parts(value):
    hi = value.astype(jnp.bfloat16).astype(jnp.float32)
    mid = (value - hi).astype(jnp.bfloat16).astype(jnp.float32)
    return hi, mid, value - hi - mid


def spread(base, lane64, value):
    hi, mid, lo = three_parts(value)
    return jnp.where(lane64 == 8, hi, jnp.where(lane64 == 9, mid, jnp.where(lane64 == 10, lo, base)))


def back_pair(causal, own_len, extra, use, q_ref, qaug_ref, own_k, own_v, oth_k, oth_v, kaug_ref, o_ref, lse_ref, g_ref, dq_ref, dko_ref, dvo_ref, dkt_ref, dvt_ref, dk_acc, dv_acc):
    lane = lax.broadcasted_iota(jnp.int32, (1, 128), 1)
    low = lane < HD
    lane64 = lane % HD
    chunks = key_chunks(own_len, extra)
    nk = own_len + extra
    begun = set()
    ones_aug = jnp.where((lane64 >= 8) & (lane64 <= 10), 1.0, 0.0).astype(jnp.bfloat16)
    for qb in range(own_len // QB):
        rows = pl.ds(qb * QB, QB)
        q = q_ref[rows, :] * jnp.bfloat16(HD ** (-0.5))
        g = g_ref[rows, :]
        qaug = spread(qaug_ref[rows, :].astype(jnp.float32), lane64, -lse_ref[rows, :]).astype(jnp.bfloat16)
        prod = g.astype(jnp.float32) * o_ref[rows, :].astype(jnp.float32)
        d_even = jnp.sum(jnp.where(low, prod, 0.0), -1, keepdims=True)
        d_odd = jnp.sum(jnp.where(low, 0.0, prod), -1, keepdims=True)
        gaug = spread(jnp.zeros((QB, 128), jnp.float32), lane64, -jnp.where(low, d_odd, d_even)).astype(jnp.bfloat16)
        queries = (jnp.where(low, q, qaug), jnp.where(low, qaug, q))
        grads = (jnp.where(low, g, gaug), jnp.where(low, gaug, g))
        zero = jnp.zeros_like(q)
        q_split = jnp.concatenate([jnp.where(low, q, zero), jnp.where(low, zero, q)], 0)
        g_split = jnp.concatenate([jnp.where(low, g, zero), jnp.where(low, zero, g)], 0)
        dq = None
        for ci in use[qb]:
            side, at, size = chunks[ci]
            k = (own_k, oth_k)[side][at : at + size, :]
            v = (own_v, oth_v)[side][at : at + size, :]
            place = slice(side * nk + at, side * nk + at + size)
            kaug = kaug_ref[place, :]
            vaug = jnp.broadcast_to(ones_aug, v.shape)
            zk = jnp.zeros_like(k)
            probs, dscores = [], []
            for h in (0, 1):
                keys = jnp.where(low, k, kaug) if h == 0 else jnp.where(low, kaug, k)
                vals = jnp.where(low, v, vaug) if h == 0 else jnp.where(low, vaug, v)
                s = lax.dot_general(keys, queries[h], (((1,), (1,)), ((), ())), preferred_element_type=jnp.float32)
                if causal and side == 0 and at == qb * QB:
                    tri = lax.broadcasted_iota(jnp.int32, (size, QB), 0) <= lax.broadcasted_iota(jnp.int32, (size, QB), 1)
                    s = jnp.where(tri, s, masked_score)
                p = jnp.exp(s)
                dp = lax.dot_general(vals, grads[h], (((1,), (1,)), ((), ())), preferred_element_type=jnp.float32)
                dscores.append((p * dp).astype(jnp.bfloat16))
                probs.append(p.astype(jnp.bfloat16))
            dk = jnp.dot(jnp.concatenate(dscores, 1), q_split, preferred_element_type=jnp.float32)
            dv = jnp.dot(jnp.concatenate(probs, 1), g_split, preferred_element_type=jnp.float32)
            if ci in begun:
                dk_acc[place, :] += dk
                dv_acc[place, :] += dv
            else:
                begun.add(ci)
                dk_acc[place, :] = dk
                dv_acc[place, :] = dv
            k_split = jnp.concatenate([jnp.where(low, k, zk), jnp.where(low, zk, k)], 0)
            dst = jnp.concatenate(dscores, 0)
            part = lax.dot_general(dst, k_split, (((0,), (0,)), ((), ())), preferred_element_type=jnp.float32)
            dq = part if dq is None else dq + part
        dq_ref[rows, :] = (dq * HD ** (-0.5)).astype(jnp.bfloat16)
    for ci, (side, at, size) in enumerate(chunks):
        if ci not in begun:
            place = slice(side * nk + at, side * nk + at + size)
            dk_acc[place, :] = jnp.zeros((size, 128), jnp.float32)
            dv_acc[place, :] = jnp.zeros((size, 128), jnp.float32)
    dko_ref[...] = dk_acc[:nk, :]
    dvo_ref[...] = dv_acc[:nk, :]
    dkt_ref[...] = dk_acc[nk:, :].astype(jnp.bfloat16)
    dvt_ref[...] = dv_acc[nk:, :].astype(jnp.bfloat16)


def attend_back(causal, core, q, qaug, own_kv, oth_kv, kaug, mixed, lse, grad):
    t = q.shape[0]
    nk = own_kv.shape[0]
    col = lambda first: pl.BlockSpec((nk, 128), lambda i, a: (0, first + i))
    tok = pl.BlockSpec((t, 128), lambda i, a: (0, i))
    return pl.pallas_call(
        functools.partial(back_kernel, causal, t, nk - t),
        grid_spec=pltpu.PrefetchScalarGridSpec(
            num_scalar_prefetch=1,
            grid=(H // 2,),
            in_specs=[
                tok,
                pl.BlockSpec((t, 128), lambda i, a: (0, 0)),
                col(0), col(H // 2), col(0), col(H // 2),
                pl.BlockSpec((2 * nk, 128), lambda i, a: (0, 0)),
                tok, tok, tok,
            ],
            out_specs=[tok, col(0), col(0), col(0), col(0)],
            scratch_shapes=[pltpu.VMEM((2 * nk, 128), jnp.float32), pltpu.VMEM((2 * nk, 128), jnp.float32)],
        ),
        out_shape=[
            jax.ShapeDtypeStruct((t, D), jnp.bfloat16),
            jax.ShapeDtypeStruct((nk, D), jnp.float32),
            jax.ShapeDtypeStruct((nk, D), jnp.float32),
            jax.ShapeDtypeStruct((nk, D), jnp.bfloat16),
            jax.ShapeDtypeStruct((nk, D), jnp.bfloat16),
        ],
        compiler_params=pltpu.CompilerParams(vmem_limit_bytes=32 * 1024 * 1024),
        cost_estimate=pl.CostEstimate(flops=10 * t * 2 * nk * D, bytes_accessed=24 * nk * D, transcendentals=t * 2 * nk * H),
        name="attend_back",
    )(core.reshape(1), q, qaug, own_kv, own_kv, oth_kv, oth_kv, kaug, mixed, lse, grad)


def seg_aug_q(seg):
    j = jnp.arange(128, dtype=jnp.int32) % HD
    return ((j[None, :] < 8) & (j[None, :] == seg[:, None])).astype(jnp.bfloat16)


def seg_aug_k(seg):
    j = jnp.arange(128, dtype=jnp.int32)[None, :] % HD
    bad = (j < 8) & (j != seg[:, None])
    return jnp.where(bad, masked_score, jnp.where((j >= 8) & (j <= 10), 1.0, 0.0)).astype(jnp.bfloat16)


epsilon = 1e-06
CHUNK = 512
TOP_CHUNK = 1024


def dot_nt(left, right):
    return lax.dot_general(left, right, (((1,), (1,)), ((), ())), preferred_element_type=jnp.float32)


def dot_nn(left, right):
    return lax.dot_general(left, right, (((1,), (0,)), ((), ())), preferred_element_type=jnp.float32)


def dot_tn(left, right):
    return lax.dot_general(left, right, (((0,), (0,)), ((), ())), preferred_element_type=jnp.float32)


def rms_norm(values, gain):
    return values * lax.rsqrt(jnp.mean(values * values, -1, keepdims=True) + epsilon) * gain


def norm_back(values, gain, grad):
    root = lax.rsqrt(jnp.mean(values * values, -1, keepdims=True) + epsilon)
    unit = values * root
    scaled = grad * gain
    inner = jnp.mean(unit * scaled, -1, keepdims=True)
    return root * (scaled - unit * inner), jnp.sum(grad * unit, 0, keepdims=True)


def gelu_pair(pre):
    root = 0.7978845608028654
    square = pre * pre
    bent = jnp.tanh(root * pre * (1.0 + 0.044715 * square))
    half = 0.5 * (1.0 + bent)
    slope = half + 0.5 * pre * (1.0 - bent * bent) * root * (1.0 + 0.134145 * square)
    return pre * half, slope


def feed_back_chunk(normed, grad_b, w1, w2, dw, total, first):
    act, slope = gelu_pair(dot_nt(normed, w1))
    act = act.astype(jnp.bfloat16)
    grad_pre = (dot_nt(grad_b, w2) * slope).astype(jnp.bfloat16)
    size = w1.shape[0]
    dw[:size, :] = dot_tn(grad_pre, normed).astype(jnp.bfloat16)
    dw[size:, :] = dot_tn(act, grad_b).astype(jnp.bfloat16)
    part = dot_nn(grad_pre, w1)

    @pl.when(first)
    def _():
        total[...] = part

    @pl.when(jnp.logical_not(first))
    def _():
        total[...] += part

    return act


class ChunkStore:
    def __init__(self, slots, whole, places, sems):
        self.slots, self.whole, self.places, self.sems = slots, whole, places, sems

    def copy(self, i, which):
        slot = lax.rem(i, 2)
        size = self.slots.shape[1] // 2
        rows = pl.ds(pl.multiple_of(self.places[which] + i * size, size), size)
        source = self.slots.at[slot, pl.ds(which * size, size)]
        return pltpu.make_async_copy(source, self.whole.at[rows], self.sems.at[slot, which])

    def start(self, i):
        for which in (0, 1):
            self.copy(i, which).start()

    def wait(self, i):
        for which in (0, 1):
            self.copy(i, which).wait()


def whole_spec(shape):
    return pl.BlockSpec(shape, lambda i: (0,) * len(shape))


def decode_top_kernel(
    d1_ref, mixed_ref, gains, grad_ref, wo_ref, w1_ref, w2_ref,
    decoded_ref, grad_two_ref, grad_mix_ref, dgain_ref, whole,
    d2_ref, normed_ref, acc_ref, total_ref, slots, dwo_ref, sems, sem_o,
):
    i = pl.program_id(0)
    store = ChunkStore(slots, whole, (8 * D, 8 * D + FF), sems)

    @pl.when(i == 0)
    def _():
        d2_ref[...] = d1_ref[...] + dot_nn(mixed_ref[...], wo_ref[...])
        normed_ref[...] = rms_norm(d2_ref[...], gains[4:5, :]).astype(jnp.bfloat16)

    pl.when(i >= 2)(lambda: store.wait(i - 2))
    act = feed_back_chunk(
        normed_ref[...], grad_ref[...], w1_ref[...], w2_ref[...], slots.at[lax.rem(i, 2)], total_ref, i == 0
    )
    store.start(i)
    more = dot_nn(act, w2_ref[...])

    @pl.when(i == 0)
    def _():
        acc_ref[...] = d2_ref[...] + more

    @pl.when(i > 0)
    def _():
        acc_ref[...] += more

    @pl.when(i == FF // TOP_CHUNK - 1)
    def _():
        decoded_ref[...] = acc_ref[...].astype(jnp.bfloat16)
        grad_x, dgain = norm_back(d2_ref[...], gains[4:5, :], total_ref[...])
        dgain_ref[...] = jnp.broadcast_to(dgain, dgain_ref.shape)
        grad_two = grad_ref[...].astype(jnp.float32) + grad_x
        grad_two_ref[...] = grad_two
        grad_b = grad_two.astype(jnp.bfloat16)
        dwo_ref[...] = dot_tn(mixed_ref[...], grad_b).astype(jnp.bfloat16)
        last = pltpu.make_async_copy(dwo_ref, whole.at[pl.ds(7 * D, D)], sem_o)
        last.start()
        grad_mix_ref[...] = dot_nt(grad_b, wo_ref[...]).astype(jnp.bfloat16)
        store.wait(i - 1)
        store.wait(i)
        last.wait()


def decode_top(d1, mixed, gains, grad_top, dec_w):
    t = d1.shape[0]
    n = FF // TOP_CHUNK
    tok = whole_spec((t, D))
    return pl.pallas_call(
        decode_top_kernel,
        grid=(n,),
        in_specs=[
            tok, tok, whole_spec(gains.shape), tok,
            pl.BlockSpec((D, D), lambda i: (7, 0)),
            pl.BlockSpec((TOP_CHUNK, D), lambda i: (8 * D // TOP_CHUNK + i, 0)),
            pl.BlockSpec((TOP_CHUNK, D), lambda i: (8 * D // TOP_CHUNK + n + i, 0)),
        ],
        out_specs=[tok, tok, tok, whole_spec((8, D)), pl.BlockSpec(memory_space=pl.ANY)],
        out_shape=[
            jax.ShapeDtypeStruct((t, D), jnp.bfloat16),
            jax.ShapeDtypeStruct((t, D), jnp.float32),
            jax.ShapeDtypeStruct((t, D), jnp.bfloat16),
            jax.ShapeDtypeStruct((8, D), jnp.float32),
            jax.ShapeDtypeStruct(dec_w.shape, jnp.bfloat16),
        ],
        scratch_shapes=[
            pltpu.VMEM((t, D), jnp.float32),
            pltpu.VMEM((t, D), jnp.bfloat16),
            pltpu.VMEM((t, D), jnp.float32),
            pltpu.VMEM((t, D), jnp.float32),
            pltpu.VMEM((2, 2 * TOP_CHUNK, D), jnp.bfloat16),
            pltpu.VMEM((D, D), jnp.bfloat16),
            pltpu.SemaphoreType.DMA((2, 2)),
            pltpu.SemaphoreType.DMA,
        ],
        compiler_params=pltpu.CompilerParams(vmem_limit_bytes=36 * 1024 * 1024),
        cost_estimate=pl.CostEstimate(flops=14 * t * FF * D, bytes_accessed=8 * FF * D, transcendentals=t * FF),
        name="decode_top",
    )(d1, mixed, gains, grad_top, dec_w, dec_w, dec_w)


def decode_dense_kernel(
    dqs_ref, dks_ref, dvs_ref, kvs_got, dqc_ref, dkc_ref, dvc_ref, kvc_got, na_ref, nc_ref, ne_ref, os_ref, one_ref,
    x_ref, h2_ref, gains, w_ref, unused, dw_ref, answers_ref, encoded_ref, dgain2_ref, dgain5_ref, g_ref, sum_ref,
):
    i = pl.program_id(0)

    def weight(n, wide, narrow):
        @pl.when(i == n)
        def _():
            dw_ref[...] = dot_tn(wide(), narrow[...]).astype(jnp.bfloat16)

    def total(own, got, which, slot):
        g_ref[slot] = (own[...] + got[:, which * D : (which + 1) * D].astype(jnp.float32)).astype(jnp.bfloat16)
        return g_ref[slot]

    def gather_back(n, begin, grads, finish):
        @pl.when(i == n)
        def _():
            part = dot_nn(grads(), w_ref[...])
            if begin:
                sum_ref[...] = part
            else:
                sum_ref[...] += part
            if finish is not None:
                finish()

    def encoded_done():
        grad, dgain = norm_back(h2_ref[...], gains[5:6, :], sum_ref[...])
        encoded_ref[...] = grad
        dgain5_ref[...] = jnp.broadcast_to(dgain, dgain5_ref.shape)

    def answers_done():
        grad, dgain = norm_back(x_ref[...].astype(jnp.float32), gains[2:3, :], sum_ref[...])
        answers_ref[...] = (one_ref[...] + grad).astype(jnp.bfloat16)
        dgain2_ref[...] = jnp.broadcast_to(dgain, dgain2_ref.shape)

    weight(0, lambda: total(dkc_ref, kvc_got, 0, 0), ne_ref)
    gather_back(0, True, lambda: g_ref[0], None)
    weight(1, lambda: total(dvc_ref, kvc_got, 1, 1), ne_ref)
    gather_back(1, False, lambda: g_ref[1], encoded_done)
    weight(2, lambda: dqc_ref[...], nc_ref)

    @pl.when(i == 3)
    def _():
        dw_ref[...] = dot_tn(os_ref[...], one_ref[...].astype(jnp.bfloat16)).astype(jnp.bfloat16)

    weight(4, lambda: dqs_ref[...], na_ref)
    gather_back(4, True, lambda: dqs_ref[...], None)
    weight(5, lambda: total(dks_ref, kvs_got, 0, 0), na_ref)
    gather_back(5, False, lambda: g_ref[0], None)
    weight(6, lambda: total(dvs_ref, kvs_got, 1, 1), na_ref)
    gather_back(6, False, lambda: g_ref[1], answers_done)


def decode_dense(dqs, dks, dvs, kvs_got, dqc, dkc, dvc, kvc_got, na, nc, ne, os, one, x, h2, gains, dec_w, dec_g):
    t = x.shape[0]
    block = lambda i: jnp.where(i < 2, i + 5, jnp.where(i == 2, 4, jnp.where(i == 3, 3, i - 4)))
    tok, wide = whole_spec((t, D)), whole_spec((t, 2 * D))
    f32, bf = jnp.float32, jnp.bfloat16
    dims = lambda kind, n=t: jax.ShapeDtypeStruct((n, D), kind)
    return pl.pallas_call(
        decode_dense_kernel,
        grid=(7,),
        in_specs=[tok, tok, tok, wide, tok, tok, tok, wide] + [tok] * 7 + [
            whole_spec(gains.shape), pl.BlockSpec((D, D), lambda i: (block(i), 0)), pl.BlockSpec(memory_space=pl.ANY),
        ],
        out_specs=[pl.BlockSpec((D, D), lambda i: (block(i), 0)), tok, tok, whole_spec((8, D)), whole_spec((8, D))],
        out_shape=[dims(bf, dec_g.shape[0]), dims(bf), dims(f32), dims(f32, 8), dims(f32, 8)],
        scratch_shapes=[pltpu.VMEM((2, t, D), bf), pltpu.VMEM((t, D), f32)],
        input_output_aliases={17: 0},
        compiler_params=pltpu.CompilerParams(vmem_limit_bytes=40 * 1024 * 1024),
        cost_estimate=pl.CostEstimate(flops=24 * t * D * D, bytes_accessed=50 * t * D, transcendentals=0),
        name="decode_dense",
    )(dqs, dks, dvs, kvs_got, dqc, dkc, dvc, kvc_got, na, nc, ne, os, one, x, h2, gains, dec_w, dec_g)


MESH = pl.DeviceIdType.MESH


def position():
    r, m = lax.axis_index("rows"), lax.axis_index("mem")
    core = lax.rem(r, 2)
    near = r + 1 - 2 * core
    x_near = r + 2 - 4 * lax.rem(lax.div(r, 2), 2)
    y_near = r + 4 - 8 * lax.div(r, 4)
    first = x_near + core * (y_near - x_near)
    second = y_near + core * (x_near - y_near)
    both = first + second - r
    turn = 1 - 2 * core
    others = (near, second + turn, first + turn, both + turn)
    return r, m, core, near, first, second, both, others


def greet(pos):
    r, m, core, near, first, second = pos[:6]
    barrier = pltpu.get_barrier_semaphore()
    count = 0
    for to in (r, near):
        for step in range(4):
            if to is r and step == 0:
                continue
            pl.semaphore_signal(barrier, inc=1, device_id=(to, lax.rem(m + step, 4)), device_id_type=MESH)
            count += 1
    for to in (first, second):
        pl.semaphore_signal(barrier, inc=1, device_id=(to, m), device_id_type=MESH)
        count += 1
    pl.semaphore_wait(barrier, count)


def remote(src, dst, send, recv, to):
    return pltpu.make_async_remote_copy(
        src_ref=src, dst_ref=dst, send_sem=send, recv_sem=recv, device_id=to, device_id_type=MESH
    )


class Mail:
    def __init__(self, pos):
        self.pos = pos
        self.started = []
        self.maybe = []

    def send(self, make):
        make().start()
        self.started.append(make)

    def send_or_keep(self, here, make, keep):
        pl.when(here())(lambda: keep().start())
        pl.when(jnp.logical_not(here()))(lambda: make().start())
        self.maybe.append((here, make))

    def arrived(self, ref, sem):
        near, m = self.pos[3], self.pos[1]
        remote(ref, ref, sem, sem, (near, m)).wait_recv()

    def finish(self):
        for make in self.started:
            make().wait_send()
        for here, make in self.maybe:
            pl.when(jnp.logical_not(here()))(lambda make=make: make().wait_send())


def dma(*shape):
    return pltpu.SemaphoreType.DMA(shape)


def gather_sems(n):
    return [dma(3, n), dma(3, n), dma(4, n), dma(4, n), dma(4, 2, n), dma(4, 2, n), dma(4, 4, n), dma(4, 4, n), dma(n)]


class Gather:
    def __init__(self, mail, ins, outs, sems):
        self.mail, self.ins, self.outs = mail, ins, outs
        self.z_s, self.z_r, self.a_s, self.a_r, self.b_s, self.b_r, self.c_s, self.c_r, self.l = sems

    def at(self, w, row, step):
        m = self.mail.pos[1]
        size = self.ins[w].shape[0]
        mem = lax.rem(m - step + 4, 4)
        return self.outs[w].at[pl.ds(pl.multiple_of((row * 4 + mem) * size, 32), size)]

    def own(self, w):
        return pltpu.make_async_copy(self.ins[w], self.at(w, self.mail.pos[0], 0), self.l.at[w])

    def ring(self, step):
        r, m, core, near, first, second, both, others = self.mail.pos
        for w in range(len(self.ins)):
            if step == 0:
                self.own(w).start()
            else:
                self.mail.arrived(self.at(w, r, step), self.z_r.at[step - 1, w])

            def src(w=w):
                return self.ins[w] if step == 0 else self.at(w, r, step)

            def dst(w=w):
                return self.at(w, r, step)

            send = self.mail.send
            if step < 3:
                send(lambda w=w, src=src, dst=dst: remote(src(), dst(), self.z_s.at[step, w], self.z_r.at[step, w], (r, lax.rem(m + 1, 4))))
            send(lambda w=w, src=src, dst=dst: remote(src(), dst(), self.a_s.at[step, w], self.a_r.at[step, w], (first, m)))
            send(lambda w=w, src=src, dst=dst: remote(src(), dst(), self.b_s.at[step, 0, w], self.b_r.at[step, 0, w], (second, m)))
            send(lambda w=w, src=src, dst=dst: remote(src(), dst(), self.c_s.at[step, 0, w], self.c_r.at[step, 0, w], (near, m)))

    def from_first(self, step):
        r, m, core, near, first, second, both, others = self.mail.pos
        for w in range(len(self.ins)):
            here = lambda w=w: self.at(w, first, step)
            self.mail.arrived(here(), self.a_r.at[step, w])
            self.mail.send(lambda w=w, here=here: remote(here(), here(), self.b_s.at[step, 1, w], self.b_r.at[step, 1, w], (second, m)))
            self.mail.send(lambda w=w, here=here: remote(here(), here(), self.c_s.at[step, 1, w], self.c_r.at[step, 1, w], (near, m)))

    def from_second(self, step):
        r, m, core, near, first, second, both, others = self.mail.pos
        for k, row in ((0, second), (1, both)):
            for w in range(len(self.ins)):
                here = lambda w=w, row=row: self.at(w, row, step)
                self.mail.arrived(here(), self.b_r.at[step, k, w])
                self.mail.send(lambda w=w, k=k, here=here: remote(here(), here(), self.c_s.at[step, 2 + k, w], self.c_r.at[step, 2 + k, w], (near, m)))

    def finish(self):
        others = self.mail.pos[7]
        for step in range(4):
            for k in range(4):
                for w in range(len(self.ins)):
                    self.mail.arrived(self.at(w, others[k], step), self.c_r.at[step, k, w])
        for w in range(len(self.ins)):
            self.own(w).wait()


def gather_order(gather, more=()):
    steps = [
        (gather.ring, 0), (gather.ring, 1), (gather.from_first, 0), (gather.ring, 2), (gather.from_first, 1),
        (gather.from_second, 0), (gather.ring, 3), (gather.from_first, 2), (gather.from_second, 1),
        (gather.from_first, 3), (gather.from_second, 2), (gather.from_second, 3),
    ]
    return [functools.partial(*step) for step in steps]


def token_sems(n):
    return [dma(n, 2), dma(n, 2), dma(n)]


class TokensIn:
    def __init__(self, mail, pairs, sems):
        self.mail, self.pairs = mail, pairs
        self.t_s, self.t_r, self.t_l = sems

    def start(self, n):
        r, m, core, near = self.mail.pos[:4]
        src, dst = self.pairs[n]
        quarter = src.shape[1]
        holder = lambda: lax.div(m * (3 - m), 2)
        slot = lambda: lax.div(m, 2)
        for i in (0, 1):
            here = lambda i=i: jnp.logical_and(2 * core + i == m, holder() == core)
            place = lambda: dst.at[pl.ds(pl.multiple_of(slot() * quarter, quarter), quarter)]
            make = lambda i=i: remote(src.at[i], place(), self.t_s.at[n, i], self.t_r.at[n, slot()], (r - core + holder(), 2 * core + i))
            keep = lambda i=i: pltpu.make_async_copy(src.at[i], place(), self.t_l.at[n])
            self.mail.send_or_keep(here, make, keep)

    def finish(self):
        r, m, core, near = self.mail.pos[:4]
        for n, (src, dst) in enumerate(self.pairs):
            quarter = src.shape[1]
            for li in (0, 1):
                source = core if li == 0 else 3 - core
                here = jnp.logical_and(lax.div(m, 2) == core, m == source)
                place = lambda: dst.at[pl.ds(li * quarter, quarter)]
                pl.when(here)(lambda: pltpu.make_async_copy(place(), place(), self.t_l.at[n]).wait())
                pl.when(jnp.logical_not(here))(lambda: self.mail.arrived(place(), self.t_r.at[n, li]))


class TokensOut:
    def __init__(self, mail, pairs, sems):
        self.mail, self.pairs = mail, pairs
        self.t_s, self.t_r, self.t_l = sems

    def start(self, n):
        r, m, core, near = self.mail.pos[:4]
        src, dst = self.pairs[n]
        quarter = dst.shape[1]
        row = lambda: lax.rem(m, 2)
        for li in (0, 1):
            to_mem = lambda li=li: core if li == 0 else 3 - core
            here = lambda to_mem=to_mem: jnp.logical_and(to_mem() == m, lax.div(m, 2) == core)
            place = lambda li=li: src.at[pl.ds(li * quarter, quarter)]
            make = lambda li=li, to_mem=to_mem, place=place: remote(place(), dst.at[row()], self.t_s.at[n, li], self.t_r.at[n, row()], (r - core + lax.div(m, 2), to_mem()))
            keep = lambda place=place: pltpu.make_async_copy(place(), dst.at[row()], self.t_l.at[n])
            self.mail.send_or_keep(here, make, keep)

    def finish(self):
        r, m, core, near = self.mail.pos[:4]
        holder = lax.div(m * (3 - m), 2)
        for n, (src, dst) in enumerate(self.pairs):
            for i in (0, 1):
                here = jnp.logical_and(2 * core + i == m, holder == core)
                pl.when(here)(lambda: pltpu.make_async_copy(dst.at[i], dst.at[i], self.t_l.at[n]).wait())
                pl.when(jnp.logical_not(here))(lambda: self.mail.arrived(dst.at[i], self.t_r.at[n, i]))


class NumbersIn:
    def __init__(self, mail, seg_ins, seg_outs, ent_in, ent_out, sems):
        self.mail, self.seg_ins, self.seg_outs, self.ent_in, self.ent_out = mail, seg_ins, seg_outs, ent_in, ent_out
        self.i_s, self.i_r, self.i_l, self.n_s, self.n_r = sems

    def start(self):
        r, m, core, near = self.mail.pos[:4]
        for n, (src, dst) in enumerate(zip(self.seg_ins, self.seg_outs)):
            self.mail.send(lambda n=n, src=src, dst=dst: remote(src, dst, self.n_s.at[n], self.n_r.at[n], (near, m)))
        for i in (0, 1):
            make = lambda i=i, e=0, to=r, half=core: remote(self.ent_in.at[i, half], self.ent_out.at[m], self.i_s.at[i, e], self.i_r.at[m], (to, 2 * core + i))
            self.mail.send(functools.partial(make, e=1, to=near, half=1 - core))
            here = lambda i=i: 2 * core + i == m
            keep = lambda i=i: pltpu.make_async_copy(self.ent_in.at[i, core], self.ent_out.at[m], self.i_l)
            self.mail.send_or_keep(here, make, keep)

    def finish(self):
        r, m, core, near = self.mail.pos[:4]
        for n, dst in enumerate(self.seg_outs):
            self.mail.arrived(dst, self.n_r.at[n])
        for mem in range(4):
            here = jnp.logical_and(lax.div(m, 2) == core, m == mem)
            place = self.ent_out.at[mem]
            pl.when(here)(lambda: pltpu.make_async_copy(place, place, self.i_l).wait())
            pl.when(jnp.logical_not(here))(lambda: self.mail.arrived(place, self.i_r.at[mem]))


def add_to(total, more):
    def step(i, unused):
        rows = pl.ds(pl.multiple_of(i * 32, 32), 32)
        total[rows, :] = total[rows, :] + more[rows, :]
        return unused

    lax.fori_loop(0, total.shape[0] // 32, step, 0)


def reduce_buffers(size):
    block = lambda *lead: pltpu.VMEM(lead + (size, D), jnp.bfloat16)
    return [block(4, 4), block(4, 4), block(4, 2), block(4), block(3)]


def reduce_sems():
    return [dma(4, 4), dma(4, 4), dma(4, 4), dma(4, 2), dma(4, 2), dma(4), dma(4), dma(3), dma(3), dma(1)]


class Reduce:
    def __init__(self, mail, source, out, buffers, sems):
        self.mail, self.source, self.out = mail, source, out
        self.held, self.rc, self.rb, self.ra, self.rz = buffers
        self.l, self.c_s, self.c_r, self.b_s, self.b_r, self.a_s, self.a_r, self.z_s, self.z_r, self.o = sems

    def at(self, row, j):
        m = self.mail.pos[1]
        size = self.out.shape[0]
        mem = lax.rem(m + 7 - j, 4)
        return self.source.at[pl.ds(pl.multiple_of((row * 4 + mem) * size, 32), size)]

    def load(self, j, k):
        r, m, core, near, first, second, both, others = self.mail.pos
        return pltpu.make_async_copy(self.at((r, first, second, both)[k], j), self.held.at[j, k], self.l.at[j, k])

    def start(self):
        r, m, core, near, first, second, both, others = self.mail.pos
        order = [(0, 3), (1, 3), (0, 1), (0, 2), (2, 3), (1, 1), (0, 0), (1, 2), (3, 3), (2, 1), (1, 0), (2, 2), (3, 1), (2, 0), (3, 2), (3, 0)]
        for j, k in order:
            self.mail.send(lambda j=j, k=k: remote(self.at(others[k], j), self.rc.at[j, k], self.c_s.at[j, k], self.c_r.at[j, k], (near, m)))
            self.load(j, k).start()

    def from_core(self, j, k):
        second, m = self.mail.pos[5], self.mail.pos[1]
        self.load(j, k).wait()
        self.mail.arrived(self.rc.at[j, k], self.c_r.at[j, k])
        add_to(self.held.at[j, k], self.rc.at[j, k])
        if k >= 2:
            self.mail.send(lambda: remote(self.held.at[j, k], self.rb.at[j, k - 2], self.b_s.at[j, k - 2], self.b_r.at[j, k - 2], (second, m)))

    def to_first(self, j):
        first, m = self.mail.pos[4], self.mail.pos[1]
        self.mail.arrived(self.rb.at[j, 1], self.b_r.at[j, 1])
        add_to(self.held.at[j, 1], self.rb.at[j, 1])
        self.mail.send(lambda: remote(self.held.at[j, 1], self.ra.at[j], self.a_s.at[j], self.a_r.at[j], (first, m)))

    def result(self):
        return pltpu.make_async_copy(self.held.at[3, 0], self.out, self.o.at[0])

    def ring(self, j):
        r, m = self.mail.pos[:2]
        self.mail.arrived(self.ra.at[j], self.a_r.at[j])
        add_to(self.held.at[j, 0], self.ra.at[j])
        self.mail.arrived(self.rb.at[j, 0], self.b_r.at[j, 0])
        add_to(self.held.at[j, 0], self.rb.at[j, 0])
        if j > 0:
            self.mail.arrived(self.rz.at[j - 1], self.z_r.at[j - 1])
            add_to(self.held.at[j, 0], self.rz.at[j - 1])
        if j < 3:
            self.mail.send(lambda: remote(self.held.at[j, 0], self.rz.at[j], self.z_s.at[j], self.z_r.at[j], (r, lax.rem(m + 1, 4))))
        else:
            self.result().start()

    def finish(self):
        self.result().wait()


def reduce_order(reduce):
    core, first, ring = reduce.from_core, reduce.to_first, reduce.ring
    groups = [
        [(core, 0, 3), (core, 1, 3), (core, 0, 1)],
        [(first, 0), (core, 0, 2), (core, 2, 3), (core, 1, 1), (core, 0, 0)],
        [(first, 1), (core, 1, 2), (core, 3, 3), (core, 2, 1), (core, 1, 0)],
        [(ring, 0)],
        [(first, 2), (core, 2, 2), (core, 3, 1), (core, 2, 0)],
        [(ring, 1)],
        [(first, 3), (core, 3, 2), (core, 3, 0)],
        [(ring, 2)],
        [(ring, 3)],
    ]

    def run(group):
        for step in group:
            step[0](*step[1:])

    return [functools.partial(run, group) for group in groups]


class GainSums:
    def __init__(self, mail, own, out, rg, gs, gz, sems):
        self.mail, self.own, self.out, self.rg, self.gs, self.gz = mail, own, out, rg, gs, gz
        self.g_s, self.g_r, self.gz_s, self.gz_r = sems

    def hop(self, n):
        r, m, core, near, first, second, both, others = self.mail.pos
        x_near = first + core * (second - first)
        y_near = second + core * (first - second)
        if n > 0:
            self.mail.arrived(self.rg.at[n - 1], self.g_r.at[n - 1])
            before = self.own[...] if n == 1 else self.gs[n - 2]
            self.gs[n - 1] = before + self.rg[n - 1]
        if n < 3:
            src = lambda: self.own if n == 0 else self.gs.at[n - 1]
            to = (near, x_near, y_near)[n]
            self.mail.send(lambda: remote(src(), self.rg.at[n], self.g_s.at[n], self.g_r.at[n], (to, m)))
            return
        self.gz[m] = self.gs[2]
        for hop in (1, 2, 3):
            self.mail.send(lambda hop=hop: remote(self.gs.at[2], self.gz.at[m], self.gz_s.at[hop - 1], self.gz_r.at[m], (r, lax.rem(m + hop, 4))))

    def finish(self):
        m = self.mail.pos[1]
        for mem in range(4):
            pl.when(m != mem)(lambda mem=mem: self.mail.arrived(self.gz.at[mem], self.gz_r.at[mem]))
        self.out[...] = (self.gz[0] + self.gz[1]) + (self.gz[2] + self.gz[3])


ANY = pl.BlockSpec(memory_space=pl.ANY)


def shaped(shape, kind=jnp.bfloat16):
    return jax.ShapeDtypeStruct(shape, kind)


def gather_encoder_kernel(
    enc_in, q_in, qs_in, as_in, al_in, ent_in, dec_ref, enc_out, q_out, qs_out, as_out, al_out, ent_out, dect_ref, *sems
):
    mail = Mail(position())
    gather = Gather(mail, (enc_in,), (enc_out,), sems[:9])
    tokens = TokensIn(mail, ((q_in, q_out),), sems[9:12])
    numbers = NumbersIn(mail, (qs_in, as_in, al_in), (qs_out, as_out, al_out), ent_in, ent_out, sems[12:])
    greet(mail.pos)
    numbers.start()
    steps = gather_order(gather)
    steps[0]()
    dect_ref[...] = dec_ref[...].T
    for step in steps[1:4]:
        step()
    tokens.start(0)
    for step in steps[4:]:
        step()
    gather.finish()
    tokens.finish()
    numbers.finish()
    mail.finish()


def gather_encoder(enc_t, q, q_seg, a_seg, alive, entries, dec_params):
    vmem = pl.BlockSpec(memory_space=pltpu.VMEM)
    return pl.pallas_call(
        gather_encoder_kernel,
        in_specs=[ANY] * 6 + [vmem],
        out_specs=[ANY] * 6 + [vmem],
        out_shape=[
            shaped((32 * enc_t.shape[0], D)),
            shaped((2 * q.shape[1], D)),
            shaped(q_seg.shape, jnp.int32),
            shaped(a_seg.shape, jnp.int32),
            shaped(alive.shape, jnp.int32),
            shaped((4,) + entries.shape[2:]),
            shaped((dec_params.shape[1], D)),
        ],
        scratch_shapes=gather_sems(1) + token_sems(1) + [dma(2, 2), dma(4), dma(), dma(3), dma(3)],
        compiler_params=pltpu.CompilerParams(collective_id=0, has_side_effects=True, vmem_limit_bytes=16 * 1024 * 1024),
        name="gather_encoder",
    )(enc_t, q, q_seg, a_seg, alive, entries, dec_params)


def reduce_encoder_kernel(
    enc_in, x_ref, pre_ref, dq_ref, dkv_ref, w_ref, grad_h_ref, gains, gain_in,
    enc_out, q_out, gain_out, gq_ref, own_ref, *rest,
):
    mail = Mail(position())
    reduce = Reduce(mail, enc_in, enc_out, rest[:5], rest[5:15])
    tokens = TokensOut(mail, ((gq_ref, q_out),), rest[15:18])
    sums = GainSums(mail, own_ref, gain_out, *rest[18:21], rest[21:])
    greet(mail.pos)
    reduce.start()
    steps = reduce_order(reduce)
    steps[0]()
    steps[1]()
    t = x_ref.shape[0]
    back = dot_nn(dkv_ref[...], w_ref[D : 3 * D, :])
    both = back[:t] + dot_nn(dq_ref[...], w_ref[:D, :])
    grad_x, dgain = norm_back(x_ref[...].astype(jnp.float32), gains[0:1, :], both)
    gq_ref[...] = (grad_h_ref[...] + grad_x).astype(jnp.bfloat16)
    tokens.start(0)
    unused, more = norm_back(pre_ref[...].astype(jnp.float32), gains[0:1, :], back[t:])
    own_ref[...] = gain_in[...]
    own_ref[0:1, :] = dgain + more
    sums.hop(0)
    steps[2]()
    sums.hop(1)
    steps[3]()
    steps[4]()
    sums.hop(2)
    steps[5]()
    steps[6]()
    sums.hop(3)
    steps[7]()
    steps[8]()
    reduce.finish()
    tokens.finish()
    sums.finish()
    mail.finish()


def reduce_encoder(enc_g, x, pre, dq, dkv, enc_w, grad_h, gains, gain_terms):
    vmem = pl.BlockSpec(memory_space=pltpu.VMEM)
    size = enc_g.shape[0] // 32
    t = x.shape[0]
    small = lambda n: pltpu.VMEM((n, 8, D), jnp.float32)
    return pl.pallas_call(
        reduce_encoder_kernel,
        grid=(1,),
        in_specs=[ANY, whole_spec(x.shape), whole_spec(pre.shape), whole_spec(dq.shape), whole_spec(dkv.shape),
                  pl.BlockSpec((3 * D, D), lambda i: (0, 0)), whole_spec(x.shape), whole_spec(gains.shape), whole_spec((8, D))],
        out_specs=[ANY, ANY, whole_spec((8, D))],
        out_shape=[shaped((size, D)), shaped((2, t // 2, D)), shaped((8, D), jnp.float32)],
        scratch_shapes=[pltpu.VMEM(x.shape, jnp.bfloat16), pltpu.VMEM((8, D), jnp.float32)]
        + reduce_buffers(size) + reduce_sems() + token_sems(1) + [small(3), small(3), small(4)]
        + [dma(3), dma(3), dma(3), dma(4)],
        compiler_params=pltpu.CompilerParams(collective_id=3, has_side_effects=True, vmem_limit_bytes=52 * 1024 * 1024),
        name="reduce_encoder",
    )(enc_g, x, pre, dq, dkv, enc_w, grad_h, gains, gain_terms)


def fetch_kernel(ids, table, out, sems):
    n = out.shape[0]
    copies = [pltpu.make_async_copy(table.at[ids[i]], out.at[i], sems.at[i]) for i in range(n)]
    for copy in copies:
        copy.start()
    for copy in copies:
        copy.wait()


def fetch(ids, table):
    n = ids.shape[0]
    return pl.pallas_call(
        fetch_kernel,
        grid_spec=pltpu.PrefetchScalarGridSpec(
            num_scalar_prefetch=1, grid=(1,), in_specs=[ANY], out_specs=ANY,
            scratch_shapes=[dma(n)],
        ),
        out_shape=shaped((n,) + table.shape[1:], table.dtype),
        name="fetch",
    )(ids, table)


PAIRS = H // 2
CHUNKS = FF // CHUNK


def once(shape):
    return pl.BlockSpec(shape, lambda i: (0,) * len(shape), pipeline_mode=pl.Buffered(1))


def column(refs, first, i):
    return [ref.at[:, pl.ds(pl.multiple_of(first + i * 128, 128), 128)] for ref in refs]


def encode_kernel(
    x_ref, pre_ref, qaug_ref, kaug_ref, gains, wqkv_ref, wo_ref, w1_ref, w2_ref, dec_in, a_in, g_ref,
    nq_ref, q_ref, o_ref, lse_ref, h1_ref, nf1_ref, h2_ref, ne_ref, kvo_out, kvt_out, dec_out, a_out, g_out,
    kvo_ref, kvt_ref, s_ref, ff_ref, g_in, kv_sems, *sems,
):
    i = pl.program_id(0)
    t, extra = x_ref.shape[0], pre_ref.shape[0]
    mail = Mail(position())
    gather = Gather(mail, (dec_in,), (dec_out,), sems[:9])
    tokens = TokensIn(mail, ((a_in, a_out), (g_in, g_out)), sems[9:12])
    steps = gather_order(gather)
    places = {4: (1, 2), 9: (3, 4), 11: (5,)}
    near, m = mail.pos[3], mail.pos[1]
    keep_own = lambda: pltpu.make_async_copy(kvo_ref, kvo_out, kv_sems.at[2])
    keep_other = lambda: pltpu.make_async_copy(kvt_ref, kvt_out, kv_sems.at[3])

    @pl.when(i == 0)
    def _():
        greet(mail.pos)
        steps[0]()
        nq_ref[:t, :] = rms_norm(x_ref[...].astype(jnp.float32), gains[0:1, :]).astype(jnp.bfloat16)
        nq_ref[t:, :] = rms_norm(pre_ref[...].astype(jnp.float32), gains[0:1, :]).astype(jnp.bfloat16)
        for b in (1, 2):
            kvo_ref[:, (b - 1) * D : b * D] = dot_nt(nq_ref[...], wqkv_ref[b * D : (b + 1) * D, :]).astype(jnp.bfloat16)
        mail.send(lambda: remote(kvo_ref, kvt_ref, kv_sems.at[0], kv_sems.at[1], (near, m)))
        keep_own().start()
        q_ref[...] = dot_nt(nq_ref[:t, :], wqkv_ref[:D, :]).astype(jnp.bfloat16)

    @pl.when(i == 1)
    def _():
        g_in[...] = g_ref[...].astype(jnp.bfloat16)
        mail.arrived(kvt_ref, kv_sems.at[1])
        keep_other().start()

    for at, which in places.items():

        @pl.when(i == at)
        def _(which=which):
            for n in which:
                steps[n]()
                if n == 3:
                    tokens.start(0)
                    tokens.start(1)

    @pl.when((i >= 1) & (i <= PAIRS))
    def _():
        pair = jnp.maximum(i - 1, 0)
        own_k, oth_k = column((kvo_ref, kvt_ref), 0, pair)
        own_v, oth_v = column((kvo_ref, kvt_ref), D, pair)
        q, o, lse = column((q_ref, o_ref, lse_ref), 0, pair)
        attend_pair(
            False, t, extra, chunk_sets(False, t, extra)[0], q, qaug_ref, own_k, own_v, oth_k, oth_v, kaug_ref, o, lse, s_ref
        )

    @pl.when(i == PAIRS + 1)
    def _():
        h1_ref[...] = x_ref[...].astype(jnp.float32) + dot_nn(o_ref[...], wo_ref[...])
        nf1_ref[...] = rms_norm(h1_ref[...], gains[1:2, :]).astype(jnp.bfloat16)
        ff_ref[...] = h1_ref[...]

    @pl.when(i > PAIRS)
    def _():
        act = gelu_pair(dot_nt(nf1_ref[...], w1_ref[...]))[0].astype(jnp.bfloat16)
        ff_ref[...] += dot_nn(act, w2_ref[...])

    @pl.when(i == PAIRS + CHUNKS)
    def _():
        h2_ref[...] = ff_ref[...]
        ne_ref[...] = rms_norm(ff_ref[...], gains[5:6, :]).astype(jnp.bfloat16)
        for n in range(6, 12):
            steps[n]()
        gather.finish()
        tokens.finish()
        keep_own().wait()
        keep_other().wait()
        mail.finish()


def encode(x, pre, qaug, kaug, gains, enc_w, dec_t, a, g):
    t, extra = x.shape[0], pre.shape[0]
    nk = t + extra
    chunk = lambda i: jnp.maximum(i - PAIRS - 1, 0)
    tok = whole_spec((t, D))
    dims = lambda kind, n=t, width=D: jax.ShapeDtypeStruct((n, width), kind)
    bf, f32 = jnp.bfloat16, jnp.float32
    return pl.pallas_call(
        encode_kernel,
        grid=(1 + PAIRS + CHUNKS,),
        in_specs=[
            tok, whole_spec((extra, D)), whole_spec((t, 128)), whole_spec((2 * nk, 128)), whole_spec(gains.shape),
            pl.BlockSpec((3 * D, D), lambda i: (0, 0)),
            pl.BlockSpec((D, D), lambda i: (3, 0)),
            pl.BlockSpec((CHUNK, D), lambda i: (4 * D // CHUNK + chunk(i), 0)),
            pl.BlockSpec((CHUNK, D), lambda i: (4 * D // CHUNK + CHUNKS + chunk(i), 0)),
            ANY, ANY, whole_spec(g.shape),
        ],
        out_specs=[whole_spec((nk, D)), tok, tok, tok, tok, tok, tok, tok] + [ANY] * 5,
        out_shape=[
            dims(bf, nk), dims(bf), dims(bf), dims(f32), dims(f32), dims(bf), dims(f32), dims(bf),
            dims(bf, nk, 2 * D), dims(bf, nk, 2 * D), dims(bf, 32 * dec_t.shape[0]), dims(bf), dims(bf),
        ],
        scratch_shapes=[
            pltpu.VMEM((nk, 2 * D), bf), pltpu.VMEM((nk, 2 * D), bf),
            pltpu.VMEM((t // QB, 2 * nk, 2 * QB), f32), pltpu.VMEM((t, D), f32), pltpu.VMEM(g.shape, bf), dma(4),
        ] + gather_sems(1) + token_sems(2),
        compiler_params=pltpu.CompilerParams(collective_id=1, has_side_effects=True, vmem_limit_bytes=48 * 1024 * 1024),
        name="encode",
    )(x, pre, qaug, kaug, gains, enc_w, enc_w, enc_w, enc_w, dec_t, a, g)


def encode_back_kernel(
    grad_ref, nf1_ref, h1_ref, nq_ref, gains, wo_ref, w1_ref, w2_ref, o_ref,
    q_ref, qaug_ref, own_k, own_v, oth_k, oth_v, kaug_ref, lse_ref, dec_g, y_in, a_in,
    whole, grad_h_ref, dgain_ref, dq_ref, dkv_ref, dec_out, y_out, a_out,
    total_ref, grad_b, mix_ref, slots, dwo_ref, sems, sem_o, dk_acc, dv_acc, dko_ref, dvo_ref, dkt_ref, dvt_ref,
    dqp_ref, own_d, sent, got, x_s, x_r, sem_w, *rest,
):
    i = pl.program_id(0)
    t = q_ref.shape[0]
    nk = own_k.shape[0]
    store = ChunkStore(slots, whole, (4 * D, 4 * D + FF), sems)
    store_o = lambda: pltpu.make_async_copy(dwo_ref, whole.at[pl.ds(3 * D, D)], sem_o)
    mail = Mail(position())
    near, m = mail.pos[3], mail.pos[1]
    reduce = Reduce(mail, dec_g, dec_out, rest[:5], rest[5:15])
    tokens = TokensOut(mail, ((y_in, y_out), (a_in, a_out)), rest[15:])
    steps = reduce_order(reduce)
    places = {1: (0,), 2: (1,), 4: (2,), 7: (3,), 8: (4,), 10: (5,), 11: (6,)}

    @pl.when(i == 0)
    def _():
        greet(mail.pos)
        reduce.start()
        tokens.start(0)
        tokens.start(1)
        grad_b[...] = grad_ref[...].astype(jnp.bfloat16)

    for at, which in places.items():

        @pl.when(i == at)
        def _(which=which):
            for n in which:
                steps[n]()

    @pl.when(i < CHUNKS)
    def _():
        pl.when(i >= 2)(lambda: store.wait(i - 2))
        feed_back_chunk(
            nf1_ref[...], grad_b[...], w1_ref[...], w2_ref[...], slots.at[lax.rem(i, 2)], total_ref, i == 0
        )
        store.start(i)

    @pl.when(i == CHUNKS - 1)
    def _():
        grad_x, dgain = norm_back(h1_ref[...], gains[1:2, :], total_ref[...])
        dgain_ref[...] = jnp.broadcast_to(dgain, dgain_ref.shape)
        grad_h = grad_ref[...] + grad_x
        grad_h_ref[...] = grad_h
        top = grad_h.astype(jnp.bfloat16)
        dwo_ref[...] = dot_tn(o_ref[...], top).astype(jnp.bfloat16)
        store_o().start()
        mix_ref[...] = dot_nt(top, wo_ref[...]).astype(jnp.bfloat16)
        store.wait(i - 1)
        store.wait(i)

    def swap(n):
        slot = lax.rem(n, 2)
        return remote(sent.at[slot], got.at[n], x_s.at[slot], x_r.at[n], (near, m))

    @pl.when(i >= CHUNKS)
    def _():
        n = jnp.maximum(i - CHUNKS, 0)
        o, mix, dq = column((o_ref, mix_ref, dq_ref), 0, n)
        back_pair(
            False, t, nk - t, chunk_sets(False, t, nk - t)[0], q_ref, qaug_ref, own_k, own_v, oth_k, oth_v, kaug_ref,
            o, lse_ref, mix, dqp_ref, dko_ref, dvo_ref, dkt_ref, dvt_ref, dk_acc, dv_acc,
        )
        dq[...] = dqp_ref[...]
        own_d[n, 0] = dko_ref[...].astype(jnp.bfloat16)
        own_d[n, 1] = dvo_ref[...].astype(jnp.bfloat16)
        pl.when(n >= 2)(lambda: swap(n - 2).wait_send())
        sent[lax.rem(n, 2), 0] = dkt_ref[...]
        sent[lax.rem(n, 2), 1] = dvt_ref[...]
        swap(n).start()

    @pl.when(i == PAIRS + CHUNKS - 1)
    def _():
        store_o().wait()
        for n in range(PAIRS):
            swap(n).wait_recv()
            for b in (0, 1):
                at = b * D + n * 128
                dkv_ref[:, at : at + 128] = own_d[n, b] + got[n, b]
        dwo_ref[...] = dot_tn(dq_ref[...], nq_ref[:t, :]).astype(jnp.bfloat16)
        last = [pltpu.make_async_copy(dwo_ref, whole.at[pl.ds(0, D)], sem_w.at[0])]
        for b in (1, 2):
            slots[b - 1, :D, :] = dot_tn(dkv_ref[:, (b - 1) * D : b * D], nq_ref[...]).astype(jnp.bfloat16)
            last.append(pltpu.make_async_copy(slots.at[b - 1, pl.ds(0, D)], whole.at[pl.ds(b * D, D)], sem_w.at[b]))
        for copy in last:
            copy.start()
        for n in (7, 8):
            steps[n]()
        reduce.finish()
        tokens.finish()
        for copy in last:
            copy.wait()
        for n in (PAIRS - 2, PAIRS - 1):
            swap(n).wait_send()
        mail.finish()


def encode_back(grad, nf1, h1, nq, gains, enc_w, o, q, qaug, own_kv, oth_kv, kaug, lse, dec_g, y, a):
    t = q.shape[0]
    nk = own_kv.shape[0]
    size = dec_g.shape[0] // 32
    pair = lambda i: jnp.maximum(i - CHUNKS, 0)
    chunk = lambda i: jnp.minimum(i, CHUNKS - 1)
    col = lambda first: pl.BlockSpec((nk, 128), lambda i: (0, first + pair(i)))
    cols = pl.BlockSpec((t, 128), lambda i: (0, pair(i)))
    tok = whole_spec((t, D))
    bf, f32 = jnp.bfloat16, jnp.float32
    dims = lambda kind, n=t, width=D: jax.ShapeDtypeStruct((n, width), kind)
    return pl.pallas_call(
        encode_back_kernel,
        grid=(PAIRS + CHUNKS,),
        in_specs=[
            once((t, D)), once((t, D)), once((t, D)), once((nk, D)), whole_spec(gains.shape),
            pl.BlockSpec((D, D), lambda i: (3, 0)),
            pl.BlockSpec((CHUNK, D), lambda i: (4 * D // CHUNK + chunk(i), 0)),
            pl.BlockSpec((CHUNK, D), lambda i: (4 * D // CHUNK + CHUNKS + chunk(i), 0)),
            once((t, D)), cols, whole_spec((t, 128)), col(0), col(PAIRS), col(0), col(PAIRS), whole_spec((2 * nk, 128)), cols,
            ANY, ANY, ANY,
        ],
        out_specs=[ANY, tok, whole_spec((8, D)), tok, whole_spec((nk, 2 * D)), ANY, ANY, ANY],
        out_shape=[
            dims(bf, enc_w.shape[0]), dims(f32), dims(f32, 8), dims(bf), dims(bf, nk, 2 * D),
            shaped((size, D)), shaped((2, t // 2, D)), shaped((2, t // 2, D)),
        ],
        scratch_shapes=[
            pltpu.VMEM((t, D), f32), pltpu.VMEM((t, D), bf), pltpu.VMEM((t, D), bf),
            pltpu.VMEM((2, 2 * CHUNK, D), bf), pltpu.VMEM((D, D), bf), dma(2, 2), dma(),
            pltpu.VMEM((2 * nk, 128), f32), pltpu.VMEM((2 * nk, 128), f32),
            pltpu.VMEM((nk, 128), f32), pltpu.VMEM((nk, 128), f32), pltpu.VMEM((nk, 128), bf), pltpu.VMEM((nk, 128), bf),
            pltpu.VMEM((t, 128), bf), pltpu.VMEM((PAIRS, 2, nk, 128), bf),
            pltpu.VMEM((2, 2, nk, 128), bf), pltpu.VMEM((PAIRS, 2, nk, 128), bf), dma(2), dma(PAIRS),
            dma(3),
        ] + reduce_buffers(size) + reduce_sems() + token_sems(2),
        compiler_params=pltpu.CompilerParams(collective_id=2, has_side_effects=True, vmem_limit_bytes=63 * 1024 * 1024),
        name="encode_back",
    )(grad, nf1, h1, nq, gains, enc_w, enc_w, enc_w, o, q, qaug, own_kv, own_kv, oth_kv, oth_kv, kaug, lse, dec_g, y, a)


def project(left, weight_t):
    return jnp.einsum("nd,ed->ne", left, weight_t, preferred_element_type=jnp.float32)


def project_back(left, weight_t):
    return jnp.einsum("ne,ed->nd", left, weight_t, preferred_element_type=jnp.float32)


def outer_sum(wide, narrow):
    return jnp.einsum("ne,nd->ed", wide, narrow, preferred_element_type=jnp.float32).astype(jnp.bfloat16)


def output_back(grad, mixed_b, w_out):
    grad_b = grad.astype(jnp.bfloat16)
    return (outer_sum(mixed_b, grad_b), project(grad_b, w_out).astype(jnp.bfloat16))


def feed_back(grad, normed_b, pre_act, act_b, w_in, w_out):
    grad_b = grad.astype(jnp.bfloat16)
    grad_wout = outer_sum(act_b, grad_b)
    grad_act = project(grad_b, w_out)
    unused, pull = jax.vjp(jax.nn.gelu, pre_act)
    grad_pre = pull(grad_act)[0].astype(jnp.bfloat16)
    return (outer_sum(grad_pre, normed_b), grad_wout, project_back(grad_pre, w_in))


def partner(values):
    n_rows = lax.axis_size("rows")
    return lax.ppermute(values, "rows", [(i, i ^ 1) for i in range(n_rows)])


def my_row(values):
    core = lax.axis_index("rows") % 2
    mem = lax.axis_index("mem")
    chosen = jnp.where(mem // 2 == core, values, partner(values))
    return lax.dynamic_index_in_dim(chosen, mem % 2, 0, keepdims=False)


def quarters_of(core):
    return (jnp.where(core == 0, 0, 1), jnp.where(core == 0, 3, 2))


def own_quarters(row, core, quarter):
    return jnp.concatenate(
        [lax.dynamic_slice_in_dim(row, place * quarter, quarter, 0) for place in quarters_of(core)], 0
    )


def to_rows(values):
    quarter = values.shape[1]
    row = my_row(lax.all_gather(values, "mem", axis=1, tiled=True))
    return own_quarters(row, lax.axis_index("rows") % 2, quarter)


def from_rows(values):
    quarter = values.shape[0] // 2
    core = lax.axis_index("rows") % 2
    mem = lax.axis_index("mem")
    gathered = lax.all_gather(values, "mem", axis=0)
    other = partner(gathered)
    holder = jnp.where((mem == 0) | (mem == 3), 0, 1)
    chosen = jnp.where(holder == core, gathered, other)
    return lax.dynamic_slice(
        chosen, (2 * core, jnp.where(mem < 2, 0, quarter), 0), (2, quarter, values.shape[1])
    )


def gather_weights(params):
    return lax.all_gather(params.T, ("rows", "mem"), axis=0, tiled=True)


def reduce_weights(grads):
    return lax.psum_scatter(grads, ("rows", "mem"), scatter_dimension=0, tiled=True)


def on_device_general(
    questions,
    answers,
    q_segments,
    a_segments,
    entry_ids,
    entry_alive_flags,
    memory_table,
    enc_params,
    dec_params,
    norm_gains,
    cotangent,
):
    quarter = questions.shape[1]
    core = lax.axis_index("rows") % 2
    per_row, slots = entry_alive_flags.shape[1], entry_alive_flags.shape[2]
    half = per_row // 2
    enc_w = gather_weights(enc_params)
    dec_w = gather_weights(dec_params)
    all_ids = lax.all_gather(entry_ids, "mem", axis=2, tiled=True)
    rows_here = questions.shape[0]
    numbers = my_row(
        jnp.concatenate(
            [
                q_segments,
                a_segments,
                entry_alive_flags.reshape(rows_here, -1),
                all_ids.reshape(rows_here, -1),
            ],
            1,
        )
    )
    row_len = q_segments.shape[1]
    q_row = numbers[:row_len]
    a_row = numbers[row_len : 2 * row_len]
    alive = numbers[2 * row_len : 2 * row_len + per_row * slots]
    ids = numbers[2 * row_len + per_row * slots :]
    x_question = to_rows(questions).astype(jnp.float32)
    x_answer = to_rows(answers).astype(jnp.float32)
    grad_top = to_rows(cotangent.astype(jnp.bfloat16)).astype(jnp.float32)

    own_ids = lax.dynamic_slice_in_dim(ids, core * half * slots, half * slots, 0)
    entry_vals = memory_table[own_ids].reshape(half * slots * 2, D).astype(jnp.float32)
    n_prefix = entry_vals.shape[0]
    extra = -(-n_prefix // 128) * 128
    place = jnp.arange(extra, dtype=jnp.int32)

    def prefix_segments(which):
        question = which * half + place // (2 * slots)
        live = lax.dynamic_slice_in_dim(alive, which * half * slots, half * slots, 0)
        live = jnp.pad(jnp.repeat(live, 2), (0, extra - n_prefix))
        return jnp.where(live == 1, question, -1)

    tokens = 2 * quarter
    own_q = own_quarters(q_row, core, quarter)
    other_q = own_quarters(q_row, 1 - core, quarter)
    own_a = own_quarters(a_row, core, quarter)
    other_a = own_quarters(a_row, 1 - core, quarter)
    q_aug, a_aug = seg_aug_q(own_q), seg_aug_q(own_a)
    enc_aug = seg_aug_k(
        jnp.concatenate([own_q, prefix_segments(core), other_q, prefix_segments(1 - core)])
    )
    self_aug = seg_aug_k(jnp.concatenate([own_a, other_a]))
    cross_aug = seg_aug_k(jnp.concatenate([own_q, other_q]))

    enc_in = jnp.concatenate([x_question, jnp.pad(entry_vals, ((0, extra - n_prefix), (0, 0)))], 0)
    normed_q = rms_norm(enc_in, norm_gains[0]).astype(jnp.bfloat16)
    query_enc = project(normed_q[:tokens], enc_w[:D]).astype(jnp.bfloat16)
    enc_kv = project(normed_q, enc_w[D : 3 * D]).astype(jnp.bfloat16)
    enc_kv_other = partner(enc_kv)

    normed_a = rms_norm(x_answer, norm_gains[2]).astype(jnp.bfloat16)
    qkv_self = project(normed_a, dec_w[: 3 * D]).astype(jnp.bfloat16)
    query_self, self_kv = qkv_self[:, :D], qkv_self[:, D:]
    self_kv_other = partner(self_kv)

    mixed_enc, logsum_enc = attend(False, core, query_enc, q_aug, enc_kv, enc_kv_other, enc_aug)
    hidden_one = x_question + project_back(mixed_enc, enc_w[3 * D : 4 * D])
    normed_f1 = rms_norm(hidden_one, norm_gains[1]).astype(jnp.bfloat16)
    pre_enc = project(normed_f1, enc_w[4 * D : 4 * D + FF])
    act_enc = jax.nn.gelu(pre_enc).astype(jnp.bfloat16)
    hidden_two = hidden_one + project_back(act_enc, enc_w[4 * D + FF :])
    encoded = rms_norm(hidden_two, norm_gains[5]).astype(jnp.bfloat16)
    cross_kv = project(encoded, dec_w[5 * D : 7 * D]).astype(jnp.bfloat16)
    cross_kv_other = partner(cross_kv)

    mixed_self, logsum_self = attend(True, core, query_self, a_aug, self_kv, self_kv_other, self_aug)
    dec_one = x_answer + project_back(mixed_self, dec_w[3 * D : 4 * D])
    normed_c = rms_norm(dec_one, norm_gains[3]).astype(jnp.bfloat16)
    query_cross = project(normed_c, dec_w[4 * D : 5 * D]).astype(jnp.bfloat16)
    mixed_cross, logsum_cross = attend(
        False, core, query_cross, a_aug, cross_kv, cross_kv_other, cross_aug
    )
    dec_two = dec_one + project_back(mixed_cross, dec_w[7 * D : 8 * D])
    normed_f2 = rms_norm(dec_two, norm_gains[4]).astype(jnp.bfloat16)
    pre_dec = project(normed_f2, dec_w[8 * D : 8 * D + FF])
    act_dec = jax.nn.gelu(pre_dec).astype(jnp.bfloat16)
    dec_three = dec_two + project_back(act_dec, dec_w[8 * D + FF :])
    decoded = from_rows(dec_three.astype(jnp.bfloat16))

    grad_w1d, grad_w2d, grad_nf2 = feed_back(
        grad_top, normed_f2, pre_dec, act_dec, dec_w[8 * D : 8 * D + FF], dec_w[8 * D + FF :]
    )
    grad_x, grad_gain4 = norm_back(dec_two, norm_gains[4], grad_nf2)
    grad_two = grad_top + grad_x
    grad_woc, grad_mixc = output_back(grad_two, mixed_cross, dec_w[7 * D : 8 * D])
    grad_qc, dk_own, dv_own, dk_other, dv_other = attend_back(
        False, core, query_cross, a_aug, cross_kv, cross_kv_other, cross_aug,
        mixed_cross, logsum_cross, grad_mixc,
    )
    more = partner(jnp.concatenate([dk_other, dv_other], 1)).astype(jnp.float32)
    grad_ckv = (jnp.concatenate([dk_own, dv_own], 1) + more).astype(jnp.bfloat16)
    grad_wqc = outer_sum(grad_qc, normed_c)
    grad_x, grad_gain3 = norm_back(
        dec_one, norm_gains[3], project_back(grad_qc, dec_w[4 * D : 5 * D])
    )
    grad_one = grad_two + grad_x
    grad_wckv = outer_sum(grad_ckv, encoded)
    grad_encoded, grad_gain5 = norm_back(
        hidden_two, norm_gains[5], project_back(grad_ckv, dec_w[5 * D : 7 * D])
    )
    grad_wos, grad_mixs = output_back(grad_one, mixed_self, dec_w[3 * D : 4 * D])
    grad_qs, dk_own, dv_own, dk_other, dv_other = attend_back(
        True, core, query_self, a_aug, self_kv, self_kv_other, self_aug,
        mixed_self, logsum_self, grad_mixs,
    )
    more = partner(jnp.concatenate([dk_other, dv_other], 1)).astype(jnp.float32)
    grad_skv = (jnp.concatenate([dk_own, dv_own], 1) + more).astype(jnp.bfloat16)
    grad_self = jnp.concatenate([grad_qs, grad_skv], 1)
    grad_wself = outer_sum(grad_self, normed_a)
    grad_x, grad_gain2 = norm_back(x_answer, norm_gains[2], project_back(grad_self, dec_w[: 3 * D]))
    grad_answers = from_rows((grad_one + grad_x).astype(jnp.bfloat16)).astype(jnp.float32)
    dec_full = jnp.concatenate(
        [grad_wself, grad_wos, grad_wqc, grad_wckv, grad_woc, grad_w1d, grad_w2d], 0
    )
    grad_decoder = reduce_weights(dec_full).astype(jnp.float32).T

    grad_w1e, grad_w2e, grad_nf1 = feed_back(
        grad_encoded, normed_f1, pre_enc, act_enc, enc_w[4 * D : 4 * D + FF], enc_w[4 * D + FF :]
    )
    grad_x, grad_gain1 = norm_back(hidden_one, norm_gains[1], grad_nf1)
    grad_hidden = grad_encoded + grad_x
    grad_woe, grad_mixe = output_back(grad_hidden, mixed_enc, enc_w[3 * D : 4 * D])
    grad_qe, dk_own, dv_own, dk_other, dv_other = attend_back(
        False, core, query_enc, q_aug, enc_kv, enc_kv_other, enc_aug,
        mixed_enc, logsum_enc, grad_mixe,
    )
    more = partner(jnp.concatenate([dk_other, dv_other], 1)).astype(jnp.float32)
    grad_ekv = (jnp.concatenate([dk_own, dv_own], 1) + more).astype(jnp.bfloat16)
    grad_wqe = outer_sum(grad_qe, normed_q[:tokens])
    grad_wkve = outer_sum(grad_ekv, normed_q)
    grad_in = project_back(grad_ekv, enc_w[D : 3 * D])
    grad_in = grad_in + jnp.pad(project_back(grad_qe, enc_w[:D]), ((0, extra), (0, 0)))
    grad_x, grad_gain0 = norm_back(enc_in, norm_gains[0], grad_in)
    grad_questions = from_rows((grad_hidden + grad_x[:tokens]).astype(jnp.bfloat16)).astype(jnp.float32)
    enc_full = jnp.concatenate([grad_wqe, grad_wkve, grad_woe, grad_w1e, grad_w2e], 0)
    gain_terms = jnp.concatenate(
        [grad_gain0, grad_gain1, grad_gain2, grad_gain3, grad_gain4, grad_gain5], 0
    )
    grad_gains = lax.psum(gain_terms, ("rows", "mem"))
    grad_encoder = reduce_weights(enc_full).astype(jnp.float32).T
    return (decoded, grad_questions, grad_answers, grad_encoder, grad_decoder, grad_gains)


def on_device_fast(
    questions,
    answers,
    q_segments,
    a_segments,
    entry_ids,
    entry_alive_flags,
    memory_table,
    enc_params,
    dec_params,
    norm_gains,
    cotangent,
):
    quarter = questions.shape[1]
    core = lax.axis_index("rows") % 2
    mem = lax.axis_index("mem")
    per_row, slots = entry_alive_flags.shape[1], entry_alive_flags.shape[2]
    half = per_row // 2
    rows_here, row_len = q_segments.shape
    n_mem = slots // entry_ids.shape[2]
    entries = fetch(entry_ids.reshape(-1), memory_table).reshape(rows_here, 2, -1, D)
    n_entry = entries.shape[2]
    piece = -(-n_entry // 32) * 32
    entries = jnp.pad(entries, ((0, 0), (0, 0), (0, piece - n_entry), (0, 0)))
    enc_w, x_question, *others, prefix, dec_t = gather_encoder(
        enc_params.T, questions, q_segments, a_segments, entry_alive_flags, entries, dec_params
    )
    prefix = prefix.reshape(-1, D)
    gains = norm_gains

    def mine(own, other):
        return lax.dynamic_index_in_dim(jnp.where(mem // 2 == core, own, other), mem % 2, 0, keepdims=False)

    q_row, a_row, alive = (
        mine(own, other) for own, other in zip((q_segments, a_segments, entry_alive_flags), others)
    )
    alive = alive.reshape(per_row, n_mem, -1)

    def prefix_segments(which):
        live = lax.dynamic_slice_in_dim(alive, which * half, half, 0)
        question = which * half + jnp.arange(half, dtype=jnp.int32)[:, None, None]
        found = jnp.where(live == 1, question, -1).transpose(1, 0, 2).reshape(n_mem, -1)
        found = jnp.repeat(found, 2, axis=1)
        return jnp.pad(found, ((0, 0), (0, piece - n_entry)), constant_values=-1).reshape(-1)

    own_q = own_quarters(q_row, core, quarter)
    other_q = own_quarters(q_row, 1 - core, quarter)
    own_a = own_quarters(a_row, core, quarter)
    other_a = own_quarters(a_row, 1 - core, quarter)
    q_aug, a_aug = seg_aug_q(own_q), seg_aug_q(own_a)
    enc_aug = seg_aug_k(
        jnp.concatenate([own_q, prefix_segments(core), other_q, prefix_segments(1 - core)])
    )
    self_aug = seg_aug_k(jnp.concatenate([own_a, other_a]))
    cross_aug = seg_aug_k(jnp.concatenate([own_q, other_q]))

    (
        normed_q, query_enc, mixed_enc, logsum_enc, hidden_one, normed_f1, hidden_two, encoded,
        enc_kv, enc_kv_other, dec_w, x_answer, grad_top,
    ) = encode(
        x_question, prefix, q_aug, enc_aug, gains, enc_w, dec_t, answers, cotangent
    )
    normed_a = rms_norm(x_answer.astype(jnp.float32), norm_gains[2]).astype(jnp.bfloat16)
    qkv_self = project(normed_a, dec_w[: 3 * D]).astype(jnp.bfloat16)
    query_self, self_kv = qkv_self[:, :D], qkv_self[:, D:]
    self_kv_other = partner(self_kv)
    cross_kv = project(encoded, dec_w[5 * D : 7 * D]).astype(jnp.bfloat16)
    cross_kv_other = partner(cross_kv)

    mixed_self, logsum_self = attend(True, core, query_self, a_aug, self_kv, self_kv_other, self_aug)
    dec_one = x_answer.astype(jnp.float32) + project_back(mixed_self, dec_w[3 * D : 4 * D])
    normed_c = rms_norm(dec_one, norm_gains[3]).astype(jnp.bfloat16)
    query_cross = project(normed_c, dec_w[4 * D : 5 * D]).astype(jnp.bfloat16)
    mixed_cross, logsum_cross = attend(
        False, core, query_cross, a_aug, cross_kv, cross_kv_other, cross_aug
    )
    decoded, grad_two, grad_mixc, grad_gain4, dec_full = decode_top(
        dec_one, mixed_cross, gains, grad_top, dec_w
    )
    grad_qc, dk_own, dv_own, dk_other, dv_other = attend_back(
        False, core, query_cross, a_aug, cross_kv, cross_kv_other, cross_aug,
        mixed_cross, logsum_cross, grad_mixc,
    )
    cross_got = partner(jnp.concatenate([dk_other, dv_other], 1))
    grad_x, grad_gain3 = norm_back(dec_one, norm_gains[3], project_back(grad_qc, dec_w[4 * D : 5 * D]))
    grad_one = grad_two + grad_x
    grad_mixs = project(grad_one.astype(jnp.bfloat16), dec_w[3 * D : 4 * D]).astype(jnp.bfloat16)
    grad_qs, dk_self, dv_self, dk_other, dv_other = attend_back(
        True, core, query_self, a_aug, self_kv, self_kv_other, self_aug,
        mixed_self, logsum_self, grad_mixs,
    )
    self_got = partner(jnp.concatenate([dk_other, dv_other], 1))
    dec_full, grad_answers, grad_encoded, grad_gain2, grad_gain5 = decode_dense(
        grad_qs, dk_self, dv_self, self_got, grad_qc, dk_own, dv_own, cross_got, normed_a, normed_c, encoded,
        mixed_self, grad_one, x_answer, hidden_two, gains, dec_w, dec_full,
    )

    enc_full, grad_hidden, grad_gain1, grad_qe, grad_ekv, grad_decoder, decoded, grad_answers = encode_back(
        grad_encoded, normed_f1, hidden_one, normed_q, gains, enc_w, mixed_enc, query_enc, q_aug,
        enc_kv, enc_kv_other, enc_aug, logsum_enc, dec_full, decoded, grad_answers,
    )
    gain_terms = jnp.concatenate(
        [
            jnp.zeros_like(grad_gain3), grad_gain1[:1], grad_gain2[:1], grad_gain3, grad_gain4[:1], grad_gain5[:1],
            jnp.zeros((2, D), jnp.float32),
        ],
        0,
    )
    grad_encoder, grad_questions, grad_gains = reduce_encoder(
        enc_full, x_question, prefix, grad_qe, grad_ekv, enc_w, grad_hidden, gains, gain_terms
    )
    return (
        decoded,
        grad_questions.astype(jnp.float32),
        grad_answers.astype(jnp.float32),
        grad_encoder.astype(jnp.float32).T,
        grad_decoder.astype(jnp.float32).T,
        grad_gains[:6],
    )


def solution(mesh):
    fast = mesh.shape["rows"] == 8 and mesh.shape["mem"] == 4
    return jax.shard_map(
        on_device_fast if fast else on_device_general,
        mesh=mesh,
        in_specs=(
            P("rows", "mem", None),
            P("rows", "mem", None),
            P("rows", None),
            P("rows", None),
            P("rows", None, "mem"),
            P("rows", None, None),
            P(),
            P(None, ("rows", "mem")),
            P(None, ("rows", "mem")),
            P(),
            P("rows", "mem", None),
        ),
        out_specs=(
            P("rows", "mem", None),
            P("rows", "mem", None),
            P("rows", "mem", None),
            P(None, ("rows", "mem")),
            P(None, ("rows", "mem")),
            P(),
        ),
        check_vma=False,
    )
```

```python
import functools
import jax
import jax.numpy as jnp
from jax import lax
from jax.experimental import pallas as pl
from jax.experimental.pallas import tpu as pltpu
from jax.sharding import PartitionSpec as P

D = 768
H = 12
HD = 64
FF = 3072
QB = 256
masked_score = -1e30


def key_chunks(own_len, extra):
    chunks = []
    for side in (0, 1):
        for at in range(own_len // QB):
            chunks.append((side, at * QB, QB))
        if extra:
            chunks.append((side, own_len, extra))
    return chunks


def chunk_sets(causal, own_len, extra):
    chunks = key_chunks(own_len, extra)
    if not causal:
        return [[list(range(len(chunks)))] * (own_len // QB)]
    quarters = ((0, 3), (1, 2))
    sets = []
    for core in (0, 1):
        held = (quarters[core], quarters[1 - core])
        sets.append([
            [n for n, (side, at, size) in enumerate(chunks) if held[side][at // QB] <= held[0][qb]]
            for qb in range(own_len // QB)
        ])
    return sets


def attend_pair(causal, own_len, extra, use, q_ref, qaug_ref, own_k, own_v, oth_k, oth_v, kaug_ref, o_ref, lse_ref, s_ref):
    low = lax.broadcasted_iota(jnp.int32, (1, 128), 1) < HD
    chunks = key_chunks(own_len, extra)
    nk = own_len + extra
    for qb in range(own_len // QB):
        rows = pl.ds(qb * QB, QB)
        q = q_ref[rows, :] * jnp.bfloat16(HD ** (-0.5))
        qaug = qaug_ref[rows, :]
        queries = (jnp.where(low, q, qaug), jnp.where(low, qaug, q))
        tops = [None, None]
        for ci in use[qb]:
            side, at, size = chunks[ci]
            k = (own_k, oth_k)[side][at : at + size, :]
            place = slice(side * nk + at, side * nk + at + size)
            kaug = kaug_ref[place, :]
            for h in (0, 1):
                keys = jnp.where(low, k, kaug) if h == 0 else jnp.where(low, kaug, k)
                s = lax.dot_general(keys, queries[h], (((1,), (1,)), ((), ())), preferred_element_type=jnp.float32)
                if causal and side == 0 and at == qb * QB:
                    tri = lax.broadcasted_iota(jnp.int32, (size, QB), 0) <= lax.broadcasted_iota(jnp.int32, (size, QB), 1)
                    s = jnp.where(tri, s, masked_score)
                s_ref[qb, place, h * QB : (h + 1) * QB] = s
                top = jnp.max(s.reshape(size // 8, 8, QB), 0)
                tops[h] = top if tops[h] is None else jnp.maximum(tops[h], top)
        m = jnp.max(jnp.concatenate(tops, 1), 0, keepdims=True)
        total, acc = None, None
        for ci in use[qb]:
            side, at, size = chunks[ci]
            v = (own_v, oth_v)[side][at : at + size, :]
            zero = jnp.zeros_like(v)
            place = slice(side * nk + at, side * nk + at + size)
            p = jnp.exp(s_ref[qb, place, :] - m)
            part = jnp.sum(p.reshape(size // 8, 8, 2 * QB), 0)
            total = part if total is None else total + part
            pb = p.astype(jnp.bfloat16)
            pb = jnp.concatenate([pb[:, :QB], pb[:, QB:]], 0)
            v_split = jnp.concatenate([jnp.where(low, v, zero), jnp.where(low, zero, v)], 0)
            part = lax.dot_general(pb, v_split, (((0,), (0,)), ((), ())), preferred_element_type=jnp.float32)
            acc = part if acc is None else acc + part
        total = jnp.sum(total, 0, keepdims=True)
        lse = m + jnp.log(total)
        rec = 1.0 / total
        wide = lambda row, h: jnp.broadcast_to(row[:, h * QB : (h + 1) * QB], (HD, QB))
        o_ref[rows, :] = (acc * jnp.concatenate([wide(rec, 0), wide(rec, 1)], 0).T).astype(jnp.bfloat16)
        lse_ref[rows, :] = jnp.concatenate([wide(lse, 1), wide(lse, 0)], 0).T


def by_core(core, sets, work):
    if len(sets) == 1:
        work(sets[0])
        return
    for n, use in enumerate(sets):
        pl.when(core[0] == n)(functools.partial(work, use))


def attend_kernel(causal, own_len, extra, core, *refs):
    by_core(core, chunk_sets(causal, own_len, extra), lambda use: attend_pair(causal, own_len, extra, use, *refs))


def back_kernel(causal, own_len, extra, core, *refs):
    by_core(core, chunk_sets(causal, own_len, extra), lambda use: back_pair(causal, own_len, extra, use, *refs))


def attend(causal, core, q, qaug, own_kv, oth_kv, kaug):
    t = q.shape[0]
    nk = own_kv.shape[0]
    col = lambda first: pl.BlockSpec((nk, 128), lambda i, a: (0, first + i))
    return pl.pallas_call(
        functools.partial(attend_kernel, causal, t, nk - t),
        grid_spec=pltpu.PrefetchScalarGridSpec(
            num_scalar_prefetch=1,
            grid=(H // 2,),
            in_specs=[
                pl.BlockSpec((t, 128), lambda i, a: (0, i)),
                pl.BlockSpec((t, 128), lambda i, a: (0, 0)),
                col(0), col(H // 2), col(0), col(H // 2),
                pl.BlockSpec((2 * nk, 128), lambda i, a: (0, 0)),
            ],
            out_specs=[pl.BlockSpec((t, 128), lambda i, a: (0, i))] * 2,
            scratch_shapes=[pltpu.VMEM((t // QB, 2 * nk, 2 * QB), jnp.float32)],
        ),
        out_shape=[jax.ShapeDtypeStruct((t, D), jnp.bfloat16), jax.ShapeDtypeStruct((t, D), jnp.float32)],
        compiler_params=pltpu.CompilerParams(vmem_limit_bytes=32 * 1024 * 1024),
        cost_estimate=pl.CostEstimate(flops=4 * t * 2 * nk * D, bytes_accessed=8 * nk * D, transcendentals=t * 2 * nk * H),
        name="attend",
    )(core.reshape(1), q, qaug, own_kv, own_kv, oth_kv, oth_kv, kaug)


def three_parts(value):
    hi = value.astype(jnp.bfloat16).astype(jnp.float32)
    mid = (value - hi).astype(jnp.bfloat16).astype(jnp.float32)
    return hi, mid, value - hi - mid


def spread(base, lane64, value):
    hi, mid, lo = three_parts(value)
    return jnp.where(lane64 == 8, hi, jnp.where(lane64 == 9, mid, jnp.where(lane64 == 10, lo, base)))


def back_pair(causal, own_len, extra, use, q_ref, qaug_ref, own_k, own_v, oth_k, oth_v, kaug_ref, o_ref, lse_ref, g_ref, dq_ref, dko_ref, dvo_ref, dkt_ref, dvt_ref, dk_acc, dv_acc):
    lane = lax.broadcasted_iota(jnp.int32, (1, 128), 1)
    low = lane < HD
    lane64 = lane % HD
    chunks = key_chunks(own_len, extra)
    nk = own_len + extra
    begun = set()
    ones_aug = jnp.where((lane64 >= 8) & (lane64 <= 10), 1.0, 0.0).astype(jnp.bfloat16)
    def block(qb, use_here, begun):
        rows = pl.ds(pl.multiple_of(qb * QB, QB), QB)
        q = q_ref[rows, :] * jnp.bfloat16(HD ** (-0.5))
        g = g_ref[rows, :]
        qaug = spread(qaug_ref[rows, :].astype(jnp.float32), lane64, -lse_ref[rows, :]).astype(jnp.bfloat16)
        prod = g.astype(jnp.float32) * o_ref[rows, :].astype(jnp.float32)
        d_even = jnp.sum(jnp.where(low, prod, 0.0), -1, keepdims=True)
        d_odd = jnp.sum(jnp.where(low, 0.0, prod), -1, keepdims=True)
        gaug = spread(jnp.zeros((QB, 128), jnp.float32), lane64, -jnp.where(low, d_odd, d_even)).astype(jnp.bfloat16)
        queries = (jnp.where(low, q, qaug), jnp.where(low, qaug, q))
        grads = (jnp.where(low, g, gaug), jnp.where(low, gaug, g))
        zero = jnp.zeros_like(q)
        q_split = jnp.concatenate([jnp.where(low, q, zero), jnp.where(low, zero, q)], 0)
        g_split = jnp.concatenate([jnp.where(low, g, zero), jnp.where(low, zero, g)], 0)
        dq = None
        for ci in use_here:
            side, at, size = chunks[ci]
            k = (own_k, oth_k)[side][at : at + size, :]
            v = (own_v, oth_v)[side][at : at + size, :]
            place = slice(side * nk + at, side * nk + at + size)
            kaug = kaug_ref[place, :]
            vaug = jnp.broadcast_to(ones_aug, v.shape)
            zk = jnp.zeros_like(k)
            probs, dscores = [], []
            for h in (0, 1):
                keys = jnp.where(low, k, kaug) if h == 0 else jnp.where(low, kaug, k)
                vals = jnp.where(low, v, vaug) if h == 0 else jnp.where(low, vaug, v)
                s = lax.dot_general(keys, queries[h], (((1,), (1,)), ((), ())), preferred_element_type=jnp.float32)
                if causal and side == 0 and at == qb * QB:
                    tri = lax.broadcasted_iota(jnp.int32, (size, QB), 0) <= lax.broadcasted_iota(jnp.int32, (size, QB), 1)
                    s = jnp.where(tri, s, masked_score)
                p = jnp.exp(s)
                dp = lax.dot_general(vals, grads[h], (((1,), (1,)), ((), ())), preferred_element_type=jnp.float32)
                dscores.append((p * dp).astype(jnp.bfloat16))
                probs.append(p.astype(jnp.bfloat16))
            dk = jnp.dot(jnp.concatenate(dscores, 1), q_split, preferred_element_type=jnp.float32)
            dv = jnp.dot(jnp.concatenate(probs, 1), g_split, preferred_element_type=jnp.float32)
            if ci in begun:
                dk_acc[place, :] += dk
                dv_acc[place, :] += dv
            else:
                begun.add(ci)
                dk_acc[place, :] = dk
                dv_acc[place, :] = dv
            k_split = jnp.concatenate([jnp.where(low, k, zk), jnp.where(low, zk, k)], 0)
            dst = jnp.concatenate(dscores, 0)
            part = lax.dot_general(dst, k_split, (((0,), (0,)), ((), ())), preferred_element_type=jnp.float32)
            dq = part if dq is None else dq + part
        dq_ref[rows, :] = (dq * HD ** (-0.5)).astype(jnp.bfloat16)

    if causal:
        begun = set()
        for qb in range(own_len // QB):
            block(qb, use[qb], begun)
    else:
        begun = set(use[0])
        dk_acc[...] = jnp.zeros(dk_acc.shape, jnp.float32)
        dv_acc[...] = jnp.zeros(dv_acc.shape, jnp.float32)

        def step(qb, unused):
            block(qb, use[0], begun)
            return unused

        lax.fori_loop(0, own_len // QB, step, 0)
    for ci, (side, at, size) in enumerate(chunks):
        if ci not in begun:
            place = slice(side * nk + at, side * nk + at + size)
            dk_acc[place, :] = jnp.zeros((size, 128), jnp.float32)
            dv_acc[place, :] = jnp.zeros((size, 128), jnp.float32)
    dko_ref[...] = dk_acc[:nk, :]
    dvo_ref[...] = dv_acc[:nk, :]
    dkt_ref[...] = dk_acc[nk:, :].astype(jnp.bfloat16)
    dvt_ref[...] = dv_acc[nk:, :].astype(jnp.bfloat16)


def attend_back(causal, core, q, qaug, own_kv, oth_kv, kaug, mixed, lse, grad):
    t = q.shape[0]
    nk = own_kv.shape[0]
    col = lambda first: pl.BlockSpec((nk, 128), lambda i, a: (0, first + i))
    tok = pl.BlockSpec((t, 128), lambda i, a: (0, i))
    return pl.pallas_call(
        functools.partial(back_kernel, causal, t, nk - t),
        grid_spec=pltpu.PrefetchScalarGridSpec(
            num_scalar_prefetch=1,
            grid=(H // 2,),
            in_specs=[
                tok,
                pl.BlockSpec((t, 128), lambda i, a: (0, 0)),
                col(0), col(H // 2), col(0), col(H // 2),
                pl.BlockSpec((2 * nk, 128), lambda i, a: (0, 0)),
                tok, tok, tok,
            ],
            out_specs=[tok, col(0), col(0), col(0), col(0)],
            scratch_shapes=[pltpu.VMEM((2 * nk, 128), jnp.float32), pltpu.VMEM((2 * nk, 128), jnp.float32)],
        ),
        out_shape=[
            jax.ShapeDtypeStruct((t, D), jnp.bfloat16),
            jax.ShapeDtypeStruct((nk, D), jnp.float32),
            jax.ShapeDtypeStruct((nk, D), jnp.float32),
            jax.ShapeDtypeStruct((nk, D), jnp.bfloat16),
            jax.ShapeDtypeStruct((nk, D), jnp.bfloat16),
        ],
        compiler_params=pltpu.CompilerParams(vmem_limit_bytes=32 * 1024 * 1024),
        cost_estimate=pl.CostEstimate(flops=10 * t * 2 * nk * D, bytes_accessed=24 * nk * D, transcendentals=t * 2 * nk * H),
        name="attend_back",
    )(core.reshape(1), q, qaug, own_kv, own_kv, oth_kv, oth_kv, kaug, mixed, lse, grad)


def seg_aug_q(seg):
    j = jnp.arange(128, dtype=jnp.int32) % HD
    return ((j[None, :] < 8) & (j[None, :] == seg[:, None])).astype(jnp.bfloat16)


def seg_aug_k(seg):
    j = jnp.arange(128, dtype=jnp.int32)[None, :] % HD
    bad = (j < 8) & (j != seg[:, None])
    return jnp.where(bad, masked_score, jnp.where((j >= 8) & (j <= 10), 1.0, 0.0)).astype(jnp.bfloat16)


epsilon = 1e-06
CHUNK = 512
TOP_CHUNK = 1024


def dot_nt(left, right):
    return lax.dot_general(left, right, (((1,), (1,)), ((), ())), preferred_element_type=jnp.float32)


def dot_nn(left, right):
    return lax.dot_general(left, right, (((1,), (0,)), ((), ())), preferred_element_type=jnp.float32)


def dot_tn(left, right):
    return lax.dot_general(left, right, (((0,), (0,)), ((), ())), preferred_element_type=jnp.float32)


def rms_norm(values, gain):
    return values * lax.rsqrt(jnp.mean(values * values, -1, keepdims=True) + epsilon) * gain


def norm_back(values, gain, grad):
    root = lax.rsqrt(jnp.mean(values * values, -1, keepdims=True) + epsilon)
    unit = values * root
    scaled = grad * gain
    inner = jnp.mean(unit * scaled, -1, keepdims=True)
    return root * (scaled - unit * inner), jnp.sum(grad * unit, 0, keepdims=True)


def gelu_pair(pre):
    root = 0.7978845608028654
    square = pre * pre
    bent = jnp.tanh(root * pre * (1.0 + 0.044715 * square))
    half = 0.5 * (1.0 + bent)
    slope = half + 0.5 * pre * (1.0 - bent * bent) * root * (1.0 + 0.134145 * square)
    return pre * half, slope


def feed_back_chunk(normed, grad_b, w1, w2, dw, total, first):
    act, slope = gelu_pair(dot_nt(normed, w1))
    act = act.astype(jnp.bfloat16)
    grad_pre = (dot_nt(grad_b, w2) * slope).astype(jnp.bfloat16)
    size = w1.shape[0]
    dw[:size, :] = dot_tn(grad_pre, normed).astype(jnp.bfloat16)
    dw[size:, :] = dot_tn(act, grad_b).astype(jnp.bfloat16)
    part = dot_nn(grad_pre, w1)

    @pl.when(first)
    def _():
        total[...] = part

    @pl.when(jnp.logical_not(first))
    def _():
        total[...] += part

    return act


class ChunkStore:
    def __init__(self, slots, whole, places, sems):
        self.slots, self.whole, self.places, self.sems = slots, whole, places, sems

    def copy(self, i, which):
        slot = lax.rem(i, 2)
        size = self.slots.shape[1] // 2
        rows = pl.ds(pl.multiple_of(self.places[which] + i * size, size), size)
        source = self.slots.at[slot, pl.ds(which * size, size)]
        return pltpu.make_async_copy(source, self.whole.at[rows], self.sems.at[slot, which])

    def start(self, i):
        for which in (0, 1):
            self.copy(i, which).start()

    def wait(self, i):
        for which in (0, 1):
            self.copy(i, which).wait()


def whole_spec(shape):
    return pl.BlockSpec(shape, lambda i: (0,) * len(shape))


def decode_top_kernel(
    d1_ref, mixed_ref, gains, grad_ref, wo_ref, w1_ref, w2_ref,
    decoded_ref, grad_two_ref, grad_mix_ref, dgain_ref, whole,
    d2_ref, normed_ref, acc_ref, total_ref, slots, dwo_ref, sems, sem_o,
):
    i = pl.program_id(0)
    store = ChunkStore(slots, whole, (8 * D, 8 * D + FF), sems)

    @pl.when(i == 0)
    def _():
        d2_ref[...] = d1_ref[...] + dot_nn(mixed_ref[...], wo_ref[...])
        normed_ref[...] = rms_norm(d2_ref[...], gains[4:5, :]).astype(jnp.bfloat16)

    pl.when(i >= 2)(lambda: store.wait(i - 2))
    act = feed_back_chunk(
        normed_ref[...], grad_ref[...], w1_ref[...], w2_ref[...], slots.at[lax.rem(i, 2)], total_ref, i == 0
    )
    store.start(i)
    more = dot_nn(act, w2_ref[...])

    @pl.when(i == 0)
    def _():
        acc_ref[...] = d2_ref[...] + more

    @pl.when(i > 0)
    def _():
        acc_ref[...] += more

    @pl.when(i == FF // TOP_CHUNK - 1)
    def _():
        decoded_ref[...] = acc_ref[...].astype(jnp.bfloat16)
        grad_x, dgain = norm_back(d2_ref[...], gains[4:5, :], total_ref[...])
        dgain_ref[...] = jnp.broadcast_to(dgain, dgain_ref.shape)
        grad_two = grad_ref[...].astype(jnp.float32) + grad_x
        grad_two_ref[...] = grad_two
        grad_b = grad_two.astype(jnp.bfloat16)
        dwo_ref[...] = dot_tn(mixed_ref[...], grad_b).astype(jnp.bfloat16)
        last = pltpu.make_async_copy(dwo_ref, whole.at[pl.ds(7 * D, D)], sem_o)
        last.start()
        grad_mix_ref[...] = dot_nt(grad_b, wo_ref[...]).astype(jnp.bfloat16)
        store.wait(i - 1)
        store.wait(i)
        last.wait()


def decode_top(d1, mixed, gains, grad_top, dec_w):
    t = d1.shape[0]
    n = FF // TOP_CHUNK
    tok = whole_spec((t, D))
    return pl.pallas_call(
        decode_top_kernel,
        grid=(n,),
        in_specs=[
            tok, tok, whole_spec(gains.shape), tok,
            pl.BlockSpec((D, D), lambda i: (7, 0)),
            pl.BlockSpec((TOP_CHUNK, D), lambda i: (8 * D // TOP_CHUNK + i, 0)),
            pl.BlockSpec((TOP_CHUNK, D), lambda i: (8 * D // TOP_CHUNK + n + i, 0)),
        ],
        out_specs=[tok, tok, tok, whole_spec((8, D)), pl.BlockSpec(memory_space=pl.ANY)],
        out_shape=[
            jax.ShapeDtypeStruct((t, D), jnp.bfloat16),
            jax.ShapeDtypeStruct((t, D), jnp.float32),
            jax.ShapeDtypeStruct((t, D), jnp.bfloat16),
            jax.ShapeDtypeStruct((8, D), jnp.float32),
            jax.ShapeDtypeStruct(dec_w.shape, jnp.bfloat16),
        ],
        scratch_shapes=[
            pltpu.VMEM((t, D), jnp.float32),
            pltpu.VMEM((t, D), jnp.bfloat16),
            pltpu.VMEM((t, D), jnp.float32),
            pltpu.VMEM((t, D), jnp.float32),
            pltpu.VMEM((2, 2 * TOP_CHUNK, D), jnp.bfloat16),
            pltpu.VMEM((D, D), jnp.bfloat16),
            pltpu.SemaphoreType.DMA((2, 2)),
            pltpu.SemaphoreType.DMA,
        ],
        compiler_params=pltpu.CompilerParams(vmem_limit_bytes=36 * 1024 * 1024),
        cost_estimate=pl.CostEstimate(flops=14 * t * FF * D, bytes_accessed=8 * FF * D, transcendentals=t * FF),
        name="decode_top",
    )(d1, mixed, gains, grad_top, dec_w, dec_w, dec_w)


def decode_dense_kernel(
    dqs_ref, dks_ref, dvs_ref, ks_got, vs_got, dqc_ref, dkc_ref, dvc_ref, kc_got, vc_got, na_ref, nc_ref, ne_ref, os_ref, one_ref,
    x_ref, h2_ref, gains, w_ref, unused, dw_ref, answers_ref, encoded_ref, dgain2_ref, dgain5_ref, g_ref, sum_ref,
):
    i = pl.program_id(0)

    def weight(n, wide, narrow):
        @pl.when(i == n)
        def _():
            dw_ref[...] = dot_tn(wide(), narrow[...]).astype(jnp.bfloat16)

    def total(own, got, slot):
        g_ref[slot] = (own[...] + got[...].astype(jnp.float32)).astype(jnp.bfloat16)
        return g_ref[slot]

    def gather_back(n, begin, grads, finish):
        @pl.when(i == n)
        def _():
            part = dot_nn(grads(), w_ref[...])
            if begin:
                sum_ref[...] = part
            else:
                sum_ref[...] += part
            if finish is not None:
                finish()

    def encoded_done():
        grad, dgain = norm_back(h2_ref[...], gains[5:6, :], sum_ref[...])
        encoded_ref[...] = grad
        dgain5_ref[...] = jnp.broadcast_to(dgain, dgain5_ref.shape)

    def answers_done():
        grad, dgain = norm_back(x_ref[...].astype(jnp.float32), gains[2:3, :], sum_ref[...])
        answers_ref[...] = (one_ref[...] + grad).astype(jnp.bfloat16)
        dgain2_ref[...] = jnp.broadcast_to(dgain, dgain2_ref.shape)

    weight(0, lambda: total(dkc_ref, kc_got, 0), ne_ref)
    gather_back(0, True, lambda: g_ref[0], None)
    weight(1, lambda: total(dvc_ref, vc_got, 1), ne_ref)
    gather_back(1, False, lambda: g_ref[1], encoded_done)
    weight(2, lambda: dqc_ref[...], nc_ref)

    @pl.when(i == 3)
    def _():
        dw_ref[...] = dot_tn(os_ref[...], one_ref[...].astype(jnp.bfloat16)).astype(jnp.bfloat16)

    weight(4, lambda: dqs_ref[...], na_ref)
    gather_back(4, True, lambda: dqs_ref[...], None)
    weight(5, lambda: total(dks_ref, ks_got, 0), na_ref)
    gather_back(5, False, lambda: g_ref[0], None)
    weight(6, lambda: total(dvs_ref, vs_got, 1), na_ref)
    gather_back(6, False, lambda: g_ref[1], answers_done)


def decode_dense(dqs, dks, dvs, ks_got, vs_got, dqc, dkc, dvc, kc_got, vc_got, na, nc, ne, os, one, x, h2, gains, dec_w, dec_g):
    t = x.shape[0]
    block = lambda i: jnp.where(i < 2, i + 5, jnp.where(i == 2, 4, jnp.where(i == 3, 3, i - 4)))
    tok = whole_spec((t, D))
    f32, bf = jnp.float32, jnp.bfloat16
    dims = lambda kind, n=t: jax.ShapeDtypeStruct((n, D), kind)
    return pl.pallas_call(
        decode_dense_kernel,
        grid=(7,),
        in_specs=[tok] * 17 + [
            whole_spec(gains.shape), pl.BlockSpec((D, D), lambda i: (block(i), 0)), pl.BlockSpec(memory_space=pl.ANY),
        ],
        out_specs=[pl.BlockSpec((D, D), lambda i: (block(i), 0)), tok, tok, whole_spec((8, D)), whole_spec((8, D))],
        out_shape=[dims(bf, dec_g.shape[0]), dims(bf), dims(f32), dims(f32, 8), dims(f32, 8)],
        scratch_shapes=[pltpu.VMEM((2, t, D), bf), pltpu.VMEM((t, D), f32)],
        input_output_aliases={19: 0},
        compiler_params=pltpu.CompilerParams(vmem_limit_bytes=40 * 1024 * 1024),
        cost_estimate=pl.CostEstimate(flops=24 * t * D * D, bytes_accessed=50 * t * D, transcendentals=0),
        name="decode_dense",
    )(dqs, dks, dvs, ks_got, vs_got, dqc, dkc, dvc, kc_got, vc_got, na, nc, ne, os, one, x, h2, gains, dec_w, dec_g)


MESH = pl.DeviceIdType.MESH


def position():
    r, m = lax.axis_index("rows"), lax.axis_index("mem")
    core = lax.rem(r, 2)
    near = r + 1 - 2 * core
    x_near = r + 2 - 4 * lax.rem(lax.div(r, 2), 2)
    y_near = r + 4 - 8 * lax.div(r, 4)
    first = x_near + core * (y_near - x_near)
    second = y_near + core * (x_near - y_near)
    both = first + second - r
    turn = 1 - 2 * core
    others = (near, second + turn, first + turn, both + turn)
    return r, m, core, near, first, second, both, others


def greet(pos):
    r, m, core, near, first, second = pos[:6]
    barrier = pltpu.get_barrier_semaphore()
    count = 0
    for to in (r, near):
        for step in range(4):
            if to is r and step == 0:
                continue
            pl.semaphore_signal(barrier, inc=1, device_id=(to, lax.rem(m + step, 4)), device_id_type=MESH)
            count += 1
    for to in (first, second):
        pl.semaphore_signal(barrier, inc=1, device_id=(to, m), device_id_type=MESH)
        count += 1
    pl.semaphore_wait(barrier, count)


def remote(src, dst, send, recv, to):
    return pltpu.make_async_remote_copy(
        src_ref=src, dst_ref=dst, send_sem=send, recv_sem=recv, device_id=to, device_id_type=MESH
    )


class Mail:
    def __init__(self, pos):
        self.pos = pos
        self.started = []
        self.maybe = []

    def send(self, make):
        make().start()
        self.started.append(make)

    def send_or_keep(self, here, make, keep):
        pl.when(here())(lambda: keep().start())
        pl.when(jnp.logical_not(here()))(lambda: make().start())
        self.maybe.append((here, make))

    def arrived(self, ref, sem):
        near, m = self.pos[3], self.pos[1]
        remote(ref, ref, sem, sem, (near, m)).wait_recv()

    def finish(self):
        for make in self.started:
            make().wait_send()
        for here, make in self.maybe:
            pl.when(jnp.logical_not(here()))(lambda make=make: make().wait_send())


def dma(*shape):
    return pltpu.SemaphoreType.DMA(shape)


def gather_sems(n):
    return [dma(3, n), dma(3, n), dma(4, n), dma(4, n), dma(4, 2, n), dma(4, 2, n), dma(4, 4, n), dma(4, 4, n), dma(n)]


class Gather:
    def __init__(self, mail, ins, outs, sems):
        self.mail, self.ins, self.outs = mail, ins, outs
        self.z_s, self.z_r, self.a_s, self.a_r, self.b_s, self.b_r, self.c_s, self.c_r, self.l = sems

    def at(self, w, row, step):
        m = self.mail.pos[1]
        size = self.ins[w].shape[0]
        mem = lax.rem(m - step + 4, 4)
        return self.outs[w].at[pl.ds(pl.multiple_of((row * 4 + mem) * size, 32), size)]

    def own(self, w):
        return pltpu.make_async_copy(self.ins[w], self.at(w, self.mail.pos[0], 0), self.l.at[w])

    def ring(self, step):
        r, m = self.mail.pos[:2]
        if step == 0:
            self.own(0).start()
        else:
            self.mail.arrived(self.at(0, r, step), self.z_r.at[step - 1, 0])
        if step < 3:
            self.mail.send(lambda: remote(self.source(step), self.at(0, r, step), self.z_s.at[step, 0], self.z_r.at[step, 0], (r, lax.rem(m + 1, 4))))

    def source(self, step):
        return self.ins[0] if step == 0 else self.at(0, self.mail.pos[0], step)

    def spread(self, step):
        r, m, core, near, first, second, both, others = self.mail.pos
        src, dst, send = functools.partial(self.source, step), functools.partial(self.at, 0, r, step), self.mail.send
        send(lambda: remote(src(), dst(), self.a_s.at[step, 0], self.a_r.at[step, 0], (first, m)))
        send(lambda: remote(src(), dst(), self.b_s.at[step, 0, 0], self.b_r.at[step, 0, 0], (second, m)))
        send(lambda: remote(src(), dst(), self.c_s.at[step, 0, 0], self.c_r.at[step, 0, 0], (near, m)))

    def from_first(self, step):
        r, m, core, near, first, second, both, others = self.mail.pos
        for w in range(len(self.ins)):
            here = lambda w=w: self.at(w, first, step)
            self.mail.arrived(here(), self.a_r.at[step, w])
            self.mail.send(lambda w=w, here=here: remote(here(), here(), self.b_s.at[step, 1, w], self.b_r.at[step, 1, w], (second, m)))
            self.mail.send(lambda w=w, here=here: remote(here(), here(), self.c_s.at[step, 1, w], self.c_r.at[step, 1, w], (near, m)))

    def from_second(self, step):
        r, m, core, near, first, second, both, others = self.mail.pos
        for k, row in ((0, second), (1, both)):
            for w in range(len(self.ins)):
                here = lambda w=w, row=row: self.at(w, row, step)
                self.mail.arrived(here(), self.b_r.at[step, k, w])
                self.mail.send(lambda w=w, k=k, here=here: remote(here(), here(), self.c_s.at[step, 2 + k, w], self.c_r.at[step, 2 + k, w], (near, m)))

    def finish(self):
        others = self.mail.pos[7]
        for step in range(4):
            for k in range(4):
                for w in range(len(self.ins)):
                    self.mail.arrived(self.at(w, others[k], step), self.c_r.at[step, k, w])
        for w in range(len(self.ins)):
            self.own(w).wait()


def token_sems(n):
    return [dma(n, 2), dma(n, 2), dma(n)]


class TokensIn:
    def __init__(self, mail, pairs, sems):
        self.mail, self.pairs = mail, pairs
        self.t_s, self.t_r, self.t_l = sems

    def start(self, n):
        r, m, core, near = self.mail.pos[:4]
        src, dst = self.pairs[n]
        quarter = src.shape[1]
        holder = lambda: lax.div(m * (3 - m), 2)
        slot = lambda: lax.div(m, 2)
        for i in (0, 1):
            here = lambda i=i: jnp.logical_and(2 * core + i == m, holder() == core)
            place = lambda: dst.at[pl.ds(pl.multiple_of(slot() * quarter, quarter), quarter)]
            make = lambda i=i: remote(src.at[i], place(), self.t_s.at[n, i], self.t_r.at[n, slot()], (r - core + holder(), 2 * core + i))
            keep = lambda i=i: pltpu.make_async_copy(src.at[i], place(), self.t_l.at[n])
            self.mail.send_or_keep(here, make, keep)

    def finish(self, n):
        r, m, core, near = self.mail.pos[:4]
        src, dst = self.pairs[n]
        quarter = src.shape[1]
        for li in (0, 1):
            source = core if li == 0 else 3 - core
            here = jnp.logical_and(lax.div(m, 2) == core, m == source)
            place = lambda: dst.at[pl.ds(li * quarter, quarter)]
            pl.when(here)(lambda: pltpu.make_async_copy(place(), place(), self.t_l.at[n]).wait())
            pl.when(jnp.logical_not(here))(lambda: self.mail.arrived(place(), self.t_r.at[n, li]))


class TokensOut:
    def __init__(self, mail, pairs, sems):
        self.mail, self.pairs = mail, pairs
        self.t_s, self.t_r, self.t_l = sems

    def start(self, n):
        r, m, core, near = self.mail.pos[:4]
        src, dst = self.pairs[n]
        quarter = dst.shape[1]
        row = lambda: lax.rem(m, 2)
        for li in (0, 1):
            to_mem = lambda li=li: core if li == 0 else 3 - core
            here = lambda to_mem=to_mem: jnp.logical_and(to_mem() == m, lax.div(m, 2) == core)
            place = lambda li=li: src.at[pl.ds(li * quarter, quarter)]
            make = lambda li=li, to_mem=to_mem, place=place: remote(place(), dst.at[row()], self.t_s.at[n, li], self.t_r.at[n, row()], (r - core + lax.div(m, 2), to_mem()))
            keep = lambda place=place: pltpu.make_async_copy(place(), dst.at[row()], self.t_l.at[n])
            self.mail.send_or_keep(here, make, keep)

    def finish(self):
        r, m, core, near = self.mail.pos[:4]
        holder = lax.div(m * (3 - m), 2)
        for n, (src, dst) in enumerate(self.pairs):
            for i in (0, 1):
                here = jnp.logical_and(2 * core + i == m, holder == core)
                pl.when(here)(lambda: pltpu.make_async_copy(dst.at[i], dst.at[i], self.t_l.at[n]).wait())
                pl.when(jnp.logical_not(here))(lambda: self.mail.arrived(dst.at[i], self.t_r.at[n, i]))


class EntriesIn:
    def __init__(self, mail, ent_in, ent_out, sems):
        self.mail, self.ent_in, self.ent_out = mail, ent_in, ent_out
        self.i_s, self.i_r, self.i_l = sems

    def start(self):
        r, m, core, near = self.mail.pos[:4]
        for i in (0, 1):
            make = lambda i=i, e=0, to=r: remote(self.ent_in.at[i, 1 - core if e else core], self.ent_out.at[m], self.i_s.at[i, e], self.i_r.at[m], (to, 2 * core + i))
            self.mail.send(functools.partial(make, e=1, to=near))
            here = lambda i=i: 2 * core + i == m
            keep = lambda i=i: pltpu.make_async_copy(self.ent_in.at[i, core], self.ent_out.at[m], self.i_l)
            self.mail.send_or_keep(here, make, keep)

    def finish(self):
        r, m, core, near = self.mail.pos[:4]
        for mem in range(4):
            here = jnp.logical_and(lax.div(m, 2) == core, m == mem)
            place = self.ent_out.at[mem]
            pl.when(here)(lambda: pltpu.make_async_copy(place, place, self.i_l).wait())
            pl.when(jnp.logical_not(here))(lambda: self.mail.arrived(place, self.i_r.at[mem]))


def add_to(total, more):
    def step(i, unused):
        rows = pl.ds(pl.multiple_of(i * 32, 32), 32)
        total[rows, :] = total[rows, :] + more[rows, :]
        return unused

    lax.fori_loop(0, total.shape[0] // 32, step, 0)


def reduce_buffers(size):
    block = lambda *lead: pltpu.VMEM(lead + (size, D), jnp.bfloat16)
    return [block(4, 4), block(4, 4), block(4, 2), block(4), block(3)]


def reduce_sems():
    return [dma(4, 4), dma(4, 4), dma(4, 4), dma(4, 2), dma(4, 2), dma(4), dma(4), dma(3), dma(3), dma(1)]


class Reduce:
    def __init__(self, mail, source, out, buffers, sems):
        self.mail, self.source, self.out = mail, source, out
        self.held, self.rc, self.rb, self.ra, self.rz = buffers
        self.l, self.c_s, self.c_r, self.b_s, self.b_r, self.a_s, self.a_r, self.z_s, self.z_r, self.o = sems

    def at(self, row, j):
        m = self.mail.pos[1]
        size = self.out.shape[0]
        mem = lax.rem(m + 7 - j, 4)
        return self.source.at[pl.ds(pl.multiple_of((row * 4 + mem) * size, 32), size)]

    def load(self, j, k):
        r, m, core, near, first, second, both, others = self.mail.pos
        return pltpu.make_async_copy(self.at((r, first, second, both)[k], j), self.held.at[j, k], self.l.at[j, k])

    def start(self):
        r, m, core, near, first, second, both, others = self.mail.pos
        order = [(0, 3), (1, 3), (0, 1), (0, 2), (2, 3), (1, 1), (0, 0), (1, 2), (3, 3), (2, 1), (1, 0), (2, 2), (3, 1), (2, 0), (3, 2), (3, 0)]
        for j, k in order:
            self.mail.send(lambda j=j, k=k: remote(self.at(others[k], j), self.rc.at[j, k], self.c_s.at[j, k], self.c_r.at[j, k], (near, m)))
            self.load(j, k).start()

    def from_core(self, j, k):
        second, m = self.mail.pos[5], self.mail.pos[1]
        self.load(j, k).wait()
        self.mail.arrived(self.rc.at[j, k], self.c_r.at[j, k])
        add_to(self.held.at[j, k], self.rc.at[j, k])
        if k >= 2:
            self.mail.send(lambda: remote(self.held.at[j, k], self.rb.at[j, k - 2], self.b_s.at[j, k - 2], self.b_r.at[j, k - 2], (second, m)))

    def to_first(self, j):
        first, m = self.mail.pos[4], self.mail.pos[1]
        self.mail.arrived(self.rb.at[j, 1], self.b_r.at[j, 1])
        add_to(self.held.at[j, 1], self.rb.at[j, 1])
        self.mail.send(lambda: remote(self.held.at[j, 1], self.ra.at[j], self.a_s.at[j], self.a_r.at[j], (first, m)))

    def result(self):
        return pltpu.make_async_copy(self.held.at[3, 0], self.out, self.o.at[0])

    def ring(self, j):
        r, m = self.mail.pos[:2]
        self.mail.arrived(self.ra.at[j], self.a_r.at[j])
        add_to(self.held.at[j, 0], self.ra.at[j])
        self.mail.arrived(self.rb.at[j, 0], self.b_r.at[j, 0])
        add_to(self.held.at[j, 0], self.rb.at[j, 0])
        if j > 0:
            self.mail.arrived(self.rz.at[j - 1], self.z_r.at[j - 1])
            add_to(self.held.at[j, 0], self.rz.at[j - 1])
        if j < 3:
            self.mail.send(lambda: remote(self.held.at[j, 0], self.rz.at[j], self.z_s.at[j], self.z_r.at[j], (r, lax.rem(m + 1, 4))))
        else:
            self.result().start()

    def finish(self):
        self.result().wait()


def reduce_order(reduce):
    core, first, ring = reduce.from_core, reduce.to_first, reduce.ring
    groups = [
        [(core, 0, 3), (core, 1, 3), (core, 0, 1)],
        [(first, 0), (core, 0, 2), (core, 2, 3), (core, 1, 1), (core, 0, 0)],
        [(first, 1), (core, 1, 2), (core, 3, 3), (core, 2, 1), (core, 1, 0)],
        [(ring, 0)],
        [(first, 2), (core, 2, 2), (core, 3, 1), (core, 2, 0)],
        [(ring, 1)],
        [(first, 3), (core, 3, 2), (core, 3, 0)],
        [(ring, 2)],
        [(ring, 3)],
    ]

    def run(group):
        for step in group:
            step[0](*step[1:])

    return [functools.partial(run, group) for group in groups]


class GainSums:
    def __init__(self, mail, own, out, rg, gs, gz, sems):
        self.mail, self.own, self.out, self.rg, self.gs, self.gz = mail, own, out, rg, gs, gz
        self.g_s, self.g_r, self.gz_s, self.gz_r = sems

    def hop(self, n):
        r, m, core, near, first, second, both, others = self.mail.pos
        x_near = first + core * (second - first)
        y_near = second + core * (first - second)
        if n > 0:
            self.mail.arrived(self.rg.at[n - 1], self.g_r.at[n - 1])
            before = self.own[...] if n == 1 else self.gs[n - 2]
            self.gs[n - 1] = before + self.rg[n - 1]
        if n < 3:
            src = lambda: self.own if n == 0 else self.gs.at[n - 1]
            to = (near, x_near, y_near)[n]
            self.mail.send(lambda: remote(src(), self.rg.at[n], self.g_s.at[n], self.g_r.at[n], (to, m)))
            return
        self.gz[m] = self.gs[2]
        for hop in (1, 2, 3):
            self.mail.send(lambda hop=hop: remote(self.gs.at[2], self.gz.at[m], self.gz_s.at[hop - 1], self.gz_r.at[m], (r, lax.rem(m + hop, 4))))

    def finish(self):
        m = self.mail.pos[1]
        for mem in range(4):
            pl.when(m != mem)(lambda mem=mem: self.mail.arrived(self.gz.at[mem], self.gz_r.at[mem]))
        self.out[...] = (self.gz[0] + self.gz[1]) + (self.gz[2] + self.gz[3])


ANY = pl.BlockSpec(memory_space=pl.ANY)


def shaped(shape, kind=jnp.bfloat16):
    return jax.ShapeDtypeStruct(shape, kind)


def reduce_encoder_kernel(
    enc_in, x_ref, pre_ref, dq_ref, dkv_ref, w_ref, grad_h_ref, gains, gain_in,
    enc_out, q_out, gain_out, gq_ref, own_ref, *rest,
):
    mail = Mail(position())
    reduce = Reduce(mail, enc_in, enc_out, rest[:5], rest[5:15])
    tokens = TokensOut(mail, ((gq_ref, q_out),), rest[15:18])
    sums = GainSums(mail, own_ref, gain_out, *rest[18:21], rest[21:])
    greet(mail.pos)
    reduce.start()
    steps = reduce_order(reduce)
    steps[0]()
    steps[1]()
    t = x_ref.shape[0]
    back = dot_nn(dkv_ref[...], w_ref[D : 3 * D, :])
    both = back[:t] + dot_nn(dq_ref[...], w_ref[:D, :])
    grad_x, dgain = norm_back(x_ref[...].astype(jnp.float32), gains[0:1, :], both)
    gq_ref[...] = (grad_h_ref[...] + grad_x).astype(jnp.bfloat16)
    tokens.start(0)
    unused, more = norm_back(pre_ref[...].astype(jnp.float32), gains[0:1, :], back[t:])
    own_ref[...] = gain_in[...]
    own_ref[0:1, :] = dgain + more
    sums.hop(0)
    steps[2]()
    sums.hop(1)
    steps[3]()
    steps[4]()
    sums.hop(2)
    steps[5]()
    steps[6]()
    sums.hop(3)
    steps[7]()
    steps[8]()
    reduce.finish()
    tokens.finish()
    sums.finish()
    mail.finish()


def reduce_encoder(enc_g, x, pre, dq, dkv, enc_w, grad_h, gains, gain_terms):
    vmem = pl.BlockSpec(memory_space=pltpu.VMEM)
    size = enc_g.shape[0] // 32
    t = x.shape[0]
    small = lambda n: pltpu.VMEM((n, 8, D), jnp.float32)
    return pl.pallas_call(
        reduce_encoder_kernel,
        grid=(1,),
        in_specs=[ANY, whole_spec(x.shape), whole_spec(pre.shape), whole_spec(dq.shape), whole_spec(dkv.shape),
                  pl.BlockSpec((3 * D, D), lambda i: (0, 0)), whole_spec(x.shape), whole_spec(gains.shape), whole_spec((8, D))],
        out_specs=[ANY, ANY, whole_spec((8, D))],
        out_shape=[shaped((size, D)), shaped((2, t // 2, D)), shaped((8, D), jnp.float32)],
        scratch_shapes=[pltpu.VMEM(x.shape, jnp.bfloat16), pltpu.VMEM((8, D), jnp.float32)]
        + reduce_buffers(size) + reduce_sems() + token_sems(1) + [small(3), small(3), small(4)]
        + [dma(3), dma(3), dma(3), dma(4)],
        compiler_params=pltpu.CompilerParams(collective_id=3, has_side_effects=True, vmem_limit_bytes=52 * 1024 * 1024),
        name="reduce_encoder",
    )(enc_g, x, pre, dq, dkv, enc_w, grad_h, gains, gain_terms)


def fetch_kernel(ids, table, out, sems):
    n = out.shape[0]
    copies = [pltpu.make_async_copy(table.at[ids[i]], out.at[i], sems.at[i]) for i in range(n)]
    for copy in copies:
        copy.start()
    for copy in copies:
        copy.wait()


def fetch(ids, table):
    n = ids.shape[0]
    return pl.pallas_call(
        fetch_kernel,
        grid_spec=pltpu.PrefetchScalarGridSpec(
            num_scalar_prefetch=1, grid=(1,), in_specs=[ANY], out_specs=ANY,
            scratch_shapes=[dma(n)],
        ),
        out_shape=shaped((n,) + table.shape[1:], table.dtype),
        name="fetch",
    )(ids, table)


PAIRS = H // 2
CHUNKS = FF // CHUNK


def once(shape):
    return pl.BlockSpec(shape, lambda i: (0,) * len(shape), pipeline_mode=pl.Buffered(1))


def column(refs, first, i):
    return [ref.at[:, pl.ds(pl.multiple_of(first + i * 128, 128), 128)] for ref in refs]


def encode_kernel(
    enc_in, q_in, ent_in, a_in, dec_ref, g_ref, qaug_ref, kaug_ref, gains,
    nq_ref, q_ref, o_ref, lse_ref, h1_ref, nf1_ref, h2_ref, ne_ref, na_ref,
    kvo_out, kvt_out, enc_out, dec_out, x_out, pre_out, a_out, g_out,
    x_ref, a_ref, pre_ref, dect_ref, w_ref, kvo_ref, kvt_ref, s_ref, ff_ref, g_in, kv_sems, w_sems, *sems,
):
    i = pl.program_id(0)
    t = x_ref.shape[0]
    extra = pre_ref.shape[0] * pre_ref.shape[1]
    mail = Mail(position())
    encoder = Gather(mail, (enc_in,), (enc_out,), sems[:9])
    decoder = Gather(mail, (dect_ref,), (dec_out,), sems[9:18])
    tokens = TokensIn(mail, ((q_in, x_ref), (a_in, a_ref), (g_in, g_out)), sems[18:21])
    entries = EntriesIn(mail, ent_in, pre_ref, sems[21:])
    near, m = mail.pos[3], mail.pos[1]
    attention_rows, rest_rows = pl.ds(0, 3 * D), pl.ds(3 * D, w_ref.shape[0] - 3 * D)
    load = lambda rows, n: pltpu.make_async_copy(enc_out.at[rows], w_ref.at[rows], w_sems.at[n])
    kept = [
        lambda: pltpu.make_async_copy(kvo_ref, kvo_out, kv_sems.at[2]),
        lambda: pltpu.make_async_copy(kvt_ref, kvt_out, kv_sems.at[3]),
        lambda: pltpu.make_async_copy(x_ref, x_out, kv_sems.at[4]),
        lambda: pltpu.make_async_copy(pre_ref, pre_out, kv_sems.at[5]),
        lambda: pltpu.make_async_copy(a_ref, a_out, kv_sems.at[6]),
    ]

    @pl.when(i == 0)
    def _():
        greet(mail.pos)
        encoder.ring(0)
        encoder.spread(0)
        entries.start()
        dect_ref[...] = dec_ref[...].T
        encoder.ring(1)
        encoder.spread(1)
        encoder.from_first(0)
        encoder.ring(2)
        tokens.start(0)
        encoder.spread(2)
        encoder.from_first(1)
        encoder.from_second(0)
        encoder.ring(3)
        decoder.ring(0)
        encoder.spread(3)
        encoder.from_first(2)
        encoder.from_second(1)
        decoder.spread(0)
        encoder.from_first(3)
        encoder.from_second(2)
        encoder.from_second(3)
        encoder.finish()
        load(attention_rows, 0).start()
        load(rest_rows, 1).start()
        tokens.finish(0)
        entries.finish()
        nq_ref[:t, :] = rms_norm(x_ref[...].astype(jnp.float32), gains[0:1, :]).astype(jnp.bfloat16)
        pre = pre_ref[...].reshape(extra, D).astype(jnp.float32)
        nq_ref[t:, :] = rms_norm(pre, gains[0:1, :]).astype(jnp.bfloat16)
        decoder.ring(1)
        decoder.spread(1)
        load(attention_rows, 0).wait()
        for b in (1, 2):
            kvo_ref[:, (b - 1) * D : b * D] = dot_nt(nq_ref[...], w_ref[b * D : (b + 1) * D, :]).astype(jnp.bfloat16)
        mail.send(lambda: remote(kvo_ref, kvt_ref, kv_sems.at[0], kv_sems.at[1], (near, m)))
        q_ref[...] = dot_nt(nq_ref[:t, :], w_ref[:D, :]).astype(jnp.bfloat16)
        g_in[...] = g_ref[...].astype(jnp.bfloat16)
        for n in (0, 2, 3):
            kept[n]().start()

    @pl.when(i == 1)
    def _():
        mail.arrived(kvt_ref, kv_sems.at[1])
        kept[1]().start()
        load(rest_rows, 1).wait()

    @pl.when(i == 2)
    def _():
        decoder.ring(2)
        decoder.from_first(0)

    @pl.when(i == 4)
    def _():
        decoder.spread(2)

    @pl.when(i == 6)
    def _():
        decoder.from_first(1)

    @pl.when(i == 8)
    def _():
        decoder.ring(3)
        decoder.spread(3)
        tokens.start(1)
        tokens.start(2)
        decoder.from_second(0)

    @pl.when((i >= 1) & (i <= PAIRS))
    def _():
        pair = jnp.maximum(i - 1, 0)
        own_k, oth_k = column((kvo_ref, kvt_ref), 0, pair)
        own_v, oth_v = column((kvo_ref, kvt_ref), D, pair)
        q, o, lse = column((q_ref, o_ref, lse_ref), 0, pair)
        attend_pair(
            False, t, extra, chunk_sets(False, t, extra)[0], q, qaug_ref, own_k, own_v, oth_k, oth_v, kaug_ref, o, lse, s_ref
        )

    @pl.when(i == PAIRS + 1)
    def _():
        h1_ref[...] = x_ref[...].astype(jnp.float32) + dot_nn(o_ref[...], w_ref[3 * D : 4 * D, :])
        nf1_ref[...] = rms_norm(h1_ref[...], gains[1:2, :]).astype(jnp.bfloat16)
        ff_ref[...] = h1_ref[...]

    @pl.when(i > PAIRS)
    def _():
        chunk = jnp.maximum(i - PAIRS - 1, 0)
        w1 = w_ref[pl.ds(pl.multiple_of(4 * D + chunk * CHUNK, CHUNK), CHUNK), :]
        w2 = w_ref[pl.ds(pl.multiple_of(4 * D + FF + chunk * CHUNK, CHUNK), CHUNK), :]
        act = gelu_pair(dot_nt(nf1_ref[...], w1))[0].astype(jnp.bfloat16)
        ff_ref[...] += dot_nn(act, w2)

    @pl.when(i == PAIRS + CHUNKS)
    def _():
        h2_ref[...] = ff_ref[...]
        ne_ref[...] = rms_norm(ff_ref[...], gains[5:6, :]).astype(jnp.bfloat16)
        decoder.from_first(2)
        decoder.from_second(1)
        tokens.finish(1)
        kept[4]().start()
        na_ref[...] = rms_norm(a_ref[...].astype(jnp.float32), gains[2:3, :]).astype(jnp.bfloat16)
        decoder.from_first(3)
        decoder.from_second(2)
        decoder.from_second(3)
        decoder.finish()
        tokens.finish(2)
        for copy in kept:
            copy().wait()
        mail.finish()


def encode(enc_t, q, entries, a, dec_params, g, qaug, kaug, gains):
    t = 2 * q.shape[1]
    extra = 4 * entries.shape[2]
    nk = t + extra
    n_e, n_d = 32 * enc_t.shape[0], 32 * dec_params.shape[1]
    tok = whole_spec((t, D))
    dims = lambda kind, n=t, width=D: jax.ShapeDtypeStruct((n, width), kind)
    bf, f32 = jnp.bfloat16, jnp.float32
    return pl.pallas_call(
        encode_kernel,
        grid=(1 + PAIRS + CHUNKS,),
        in_specs=[ANY] * 4 + [whole_spec(v.shape) for v in (dec_params, g, qaug, kaug, gains)],
        out_specs=[whole_spec((nk, D))] + [tok] * 8 + [ANY] * 8,
        out_shape=[
            dims(bf, nk), dims(bf), dims(bf), dims(f32), dims(f32), dims(bf), dims(f32), dims(bf), dims(bf),
            dims(bf, nk, 2 * D), dims(bf, nk, 2 * D), dims(bf, n_e), dims(bf, n_d), dims(bf),
            shaped((4,) + entries.shape[2:]), dims(bf), dims(bf),
        ],
        scratch_shapes=[
            pltpu.VMEM((t, D), bf), pltpu.VMEM((t, D), bf), pltpu.VMEM((4,) + entries.shape[2:], bf), pltpu.VMEM((n_d // 32, D), bf),
            pltpu.VMEM((n_e, D), bf), pltpu.VMEM((nk, 2 * D), bf), pltpu.VMEM((nk, 2 * D), bf),
            pltpu.VMEM((t // QB, 2 * nk, 2 * QB), f32), pltpu.VMEM((t, D), f32), pltpu.VMEM(g.shape, bf), dma(7), dma(2),
        ] + gather_sems(1) + gather_sems(1) + token_sems(3) + [dma(2, 2), dma(4), dma()],
        compiler_params=pltpu.CompilerParams(collective_id=1, has_side_effects=True, vmem_limit_bytes=51 * 1024 * 1024),
        name="encode",
    )(enc_t, q, entries, a, dec_params, g, qaug, kaug, gains)


def encode_back_kernel(
    grad_ref, nf1_ref, h1_ref, nq_ref, gains, wo_ref, w1_ref, w2_ref, o_ref,
    q_ref, qaug_ref, own_k, own_v, oth_k, oth_v, kaug_ref, lse_ref, dec_g, y_in, a_in,
    whole, grad_h_ref, dgain_ref, dq_ref, dkv_ref, dec_out, y_out, a_out,
    total_ref, grad_b, mix_ref, slots, dwo_ref, sems, sem_o, dk_acc, dv_acc, dko_ref, dvo_ref, dkt_ref, dvt_ref,
    dqp_ref, own_d, sent, got, x_s, x_r, sem_w, *rest,
):
    i = pl.program_id(0)
    t = q_ref.shape[0]
    nk = own_k.shape[0]
    store = ChunkStore(slots, whole, (4 * D, 4 * D + FF), sems)
    store_o = lambda: pltpu.make_async_copy(dwo_ref, whole.at[pl.ds(3 * D, D)], sem_o)
    mail = Mail(position())
    near, m = mail.pos[3], mail.pos[1]
    reduce = Reduce(mail, dec_g, dec_out, rest[:5], rest[5:15])
    tokens = TokensOut(mail, ((y_in, y_out), (a_in, a_out)), rest[15:])
    steps = reduce_order(reduce)
    places = {1: (0,), 3: (1,), 5: (2,), 7: (3,), 9: (4,), 11: (5,)}

    @pl.when(i == 0)
    def _():
        greet(mail.pos)
        reduce.start()
        tokens.start(0)
        tokens.start(1)
        grad_b[...] = grad_ref[...].astype(jnp.bfloat16)

    for at, which in places.items():

        @pl.when(i == at)
        def _(which=which):
            for n in which:
                steps[n]()

    @pl.when(i < CHUNKS)
    def _():
        pl.when(i >= 2)(lambda: store.wait(i - 2))
        feed_back_chunk(
            nf1_ref[...], grad_b[...], w1_ref[...], w2_ref[...], slots.at[lax.rem(i, 2)], total_ref, i == 0
        )
        store.start(i)

    @pl.when(i == CHUNKS - 1)
    def _():
        grad_x, dgain = norm_back(h1_ref[...], gains[1:2, :], total_ref[...])
        dgain_ref[...] = jnp.broadcast_to(dgain, dgain_ref.shape)
        grad_h = grad_ref[...] + grad_x
        grad_h_ref[...] = grad_h
        top = grad_h.astype(jnp.bfloat16)
        dwo_ref[...] = dot_tn(o_ref[...], top).astype(jnp.bfloat16)
        store_o().start()
        mix_ref[...] = dot_nt(top, wo_ref[...]).astype(jnp.bfloat16)
        store.wait(i - 1)
        store.wait(i)

    def swap(n):
        slot = lax.rem(n, 2)
        return remote(sent.at[slot], got.at[n], x_s.at[slot], x_r.at[n], (near, m))

    @pl.when(i >= CHUNKS)
    def _():
        n = jnp.maximum(i - CHUNKS, 0)
        o, mix, dq = column((o_ref, mix_ref, dq_ref), 0, n)
        back_pair(
            False, t, nk - t, chunk_sets(False, t, nk - t)[0], q_ref, qaug_ref, own_k, own_v, oth_k, oth_v, kaug_ref,
            o, lse_ref, mix, dqp_ref, dko_ref, dvo_ref, dkt_ref, dvt_ref, dk_acc, dv_acc,
        )
        dq[...] = dqp_ref[...]
        own_d[n, 0] = dko_ref[...].astype(jnp.bfloat16)
        own_d[n, 1] = dvo_ref[...].astype(jnp.bfloat16)
        pl.when(n >= 2)(lambda: swap(n - 2).wait_send())
        sent[lax.rem(n, 2), 0] = dkt_ref[...]
        sent[lax.rem(n, 2), 1] = dvt_ref[...]
        swap(n).start()

    @pl.when(i == PAIRS + CHUNKS - 1)
    def _():
        store_o().wait()
        for n in range(PAIRS):
            swap(n).wait_recv()
            for b in (0, 1):
                at = b * D + n * 128
                dkv_ref[:, at : at + 128] = own_d[n, b] + got[n, b]
        dwo_ref[...] = dot_tn(dq_ref[...], nq_ref[:t, :]).astype(jnp.bfloat16)
        last = [pltpu.make_async_copy(dwo_ref, whole.at[pl.ds(0, D)], sem_w.at[0])]
        for b in (1, 2):
            slots[b - 1, :D, :] = dot_tn(dkv_ref[:, (b - 1) * D : b * D], nq_ref[...]).astype(jnp.bfloat16)
            last.append(pltpu.make_async_copy(slots.at[b - 1, pl.ds(0, D)], whole.at[pl.ds(b * D, D)], sem_w.at[b]))
        for copy in last:
            copy.start()
        for n in (6, 7, 8):
            steps[n]()
        reduce.finish()
        tokens.finish()
        for copy in last:
            copy.wait()
        for n in (PAIRS - 2, PAIRS - 1):
            swap(n).wait_send()
        mail.finish()


def encode_back(grad, nf1, h1, nq, gains, enc_w, o, q, qaug, own_kv, oth_kv, kaug, lse, dec_g, y, a):
    t = q.shape[0]
    nk = own_kv.shape[0]
    size = dec_g.shape[0] // 32
    pair = lambda i: jnp.maximum(i - CHUNKS, 0)
    chunk = lambda i: jnp.minimum(i, CHUNKS - 1)
    col = lambda first: pl.BlockSpec((nk, 128), lambda i: (0, first + pair(i)))
    cols = pl.BlockSpec((t, 128), lambda i: (0, pair(i)))
    tok = whole_spec((t, D))
    bf, f32 = jnp.bfloat16, jnp.float32
    dims = lambda kind, n=t, width=D: jax.ShapeDtypeStruct((n, width), kind)
    return pl.pallas_call(
        encode_back_kernel,
        grid=(PAIRS + CHUNKS,),
        in_specs=[
            once((t, D)), once((t, D)), once((t, D)), once((nk, D)), whole_spec(gains.shape),
            pl.BlockSpec((D, D), lambda i: (3, 0)),
            pl.BlockSpec((CHUNK, D), lambda i: (4 * D // CHUNK + chunk(i), 0)),
            pl.BlockSpec((CHUNK, D), lambda i: (4 * D // CHUNK + CHUNKS + chunk(i), 0)),
            once((t, D)), cols, whole_spec((t, 128)), col(0), col(PAIRS), col(0), col(PAIRS), whole_spec((2 * nk, 128)), cols,
            ANY, ANY, ANY,
        ],
        out_specs=[ANY, tok, whole_spec((8, D)), tok, whole_spec((nk, 2 * D)), ANY, ANY, ANY],
        out_shape=[
            dims(bf, enc_w.shape[0]), dims(f32), dims(f32, 8), dims(bf), dims(bf, nk, 2 * D),
            shaped((size, D)), shaped((2, t // 2, D)), shaped((2, t // 2, D)),
        ],
        scratch_shapes=[
            pltpu.VMEM((t, D), f32), pltpu.VMEM((t, D), bf), pltpu.VMEM((t, D), bf),
            pltpu.VMEM((2, 2 * CHUNK, D), bf), pltpu.VMEM((D, D), bf), dma(2, 2), dma(),
            pltpu.VMEM((2 * nk, 128), f32), pltpu.VMEM((2 * nk, 128), f32),
            pltpu.VMEM((nk, 128), f32), pltpu.VMEM((nk, 128), f32), pltpu.VMEM((nk, 128), bf), pltpu.VMEM((nk, 128), bf),
            pltpu.VMEM((t, 128), bf), pltpu.VMEM((PAIRS, 2, nk, 128), bf),
            pltpu.VMEM((2, 2, nk, 128), bf), pltpu.VMEM((PAIRS, 2, nk, 128), bf), dma(2), dma(PAIRS),
            dma(3),
        ] + reduce_buffers(size) + reduce_sems() + token_sems(2),
        compiler_params=pltpu.CompilerParams(collective_id=2, has_side_effects=True, vmem_limit_bytes=63 * 1024 * 1024),
        name="encode_back",
    )(grad, nf1, h1, nq, gains, enc_w, enc_w, enc_w, o, q, qaug, own_kv, own_kv, oth_kv, oth_kv, kaug, lse, dec_g, y, a)


def project(left, weight_t):
    return jnp.einsum("nd,ed->ne", left, weight_t, preferred_element_type=jnp.float32)


def project_back(left, weight_t):
    return jnp.einsum("ne,ed->nd", left, weight_t, preferred_element_type=jnp.float32)


def outer_sum(wide, narrow):
    return jnp.einsum("ne,nd->ed", wide, narrow, preferred_element_type=jnp.float32).astype(jnp.bfloat16)


def output_back(grad, mixed_b, w_out):
    grad_b = grad.astype(jnp.bfloat16)
    return (outer_sum(mixed_b, grad_b), project(grad_b, w_out).astype(jnp.bfloat16))


def feed_back(grad, normed_b, pre_act, act_b, w_in, w_out):
    grad_b = grad.astype(jnp.bfloat16)
    grad_wout = outer_sum(act_b, grad_b)
    grad_act = project(grad_b, w_out)
    unused, pull = jax.vjp(jax.nn.gelu, pre_act)
    grad_pre = pull(grad_act)[0].astype(jnp.bfloat16)
    return (outer_sum(grad_pre, normed_b), grad_wout, project_back(grad_pre, w_in))


def partner(values):
    n_rows = lax.axis_size("rows")
    return lax.ppermute(values, "rows", [(i, i ^ 1) for i in range(n_rows)])


def my_row(values):
    core = lax.axis_index("rows") % 2
    mem = lax.axis_index("mem")
    chosen = jnp.where(mem // 2 == core, values, partner(values))
    return lax.dynamic_index_in_dim(chosen, mem % 2, 0, keepdims=False)


def quarters_of(core):
    return (jnp.where(core == 0, 0, 1), jnp.where(core == 0, 3, 2))


def own_quarters(row, core, quarter):
    return jnp.concatenate(
        [lax.dynamic_slice_in_dim(row, place * quarter, quarter, 0) for place in quarters_of(core)], 0
    )


def to_rows(values):
    quarter = values.shape[1]
    row = my_row(lax.all_gather(values, "mem", axis=1, tiled=True))
    return own_quarters(row, lax.axis_index("rows") % 2, quarter)


def from_rows(values):
    quarter = values.shape[0] // 2
    core = lax.axis_index("rows") % 2
    mem = lax.axis_index("mem")
    gathered = lax.all_gather(values, "mem", axis=0)
    other = partner(gathered)
    holder = jnp.where((mem == 0) | (mem == 3), 0, 1)
    chosen = jnp.where(holder == core, gathered, other)
    return lax.dynamic_slice(
        chosen, (2 * core, jnp.where(mem < 2, 0, quarter), 0), (2, quarter, values.shape[1])
    )


def gather_weights(params):
    return lax.all_gather(params.T, ("rows", "mem"), axis=0, tiled=True)


def reduce_weights(grads):
    return lax.psum_scatter(grads, ("rows", "mem"), scatter_dimension=0, tiled=True)


def on_device_general(
    questions,
    answers,
    q_segments,
    a_segments,
    entry_ids,
    entry_alive_flags,
    memory_table,
    enc_params,
    dec_params,
    norm_gains,
    cotangent,
):
    quarter = questions.shape[1]
    core = lax.axis_index("rows") % 2
    per_row, slots = entry_alive_flags.shape[1], entry_alive_flags.shape[2]
    half = per_row // 2
    enc_w = gather_weights(enc_params)
    dec_w = gather_weights(dec_params)
    all_ids = lax.all_gather(entry_ids, "mem", axis=2, tiled=True)
    rows_here = questions.shape[0]
    numbers = my_row(
        jnp.concatenate(
            [
                q_segments,
                a_segments,
                entry_alive_flags.reshape(rows_here, -1),
                all_ids.reshape(rows_here, -1),
            ],
            1,
        )
    )
    row_len = q_segments.shape[1]
    q_row = numbers[:row_len]
    a_row = numbers[row_len : 2 * row_len]
    alive = numbers[2 * row_len : 2 * row_len + per_row * slots]
    ids = numbers[2 * row_len + per_row * slots :]
    x_question = to_rows(questions).astype(jnp.float32)
    x_answer = to_rows(answers).astype(jnp.float32)
    grad_top = to_rows(cotangent.astype(jnp.bfloat16)).astype(jnp.float32)

    own_ids = lax.dynamic_slice_in_dim(ids, core * half * slots, half * slots, 0)
    entry_vals = memory_table[own_ids].reshape(half * slots * 2, D).astype(jnp.float32)
    n_prefix = entry_vals.shape[0]
    extra = -(-n_prefix // 128) * 128
    place = jnp.arange(extra, dtype=jnp.int32)

    def prefix_segments(which):
        question = which * half + place // (2 * slots)
        live = lax.dynamic_slice_in_dim(alive, which * half * slots, half * slots, 0)
        live = jnp.pad(jnp.repeat(live, 2), (0, extra - n_prefix))
        return jnp.where(live == 1, question, -1)

    tokens = 2 * quarter
    own_q = own_quarters(q_row, core, quarter)
    other_q = own_quarters(q_row, 1 - core, quarter)
    own_a = own_quarters(a_row, core, quarter)
    other_a = own_quarters(a_row, 1 - core, quarter)
    q_aug, a_aug = seg_aug_q(own_q), seg_aug_q(own_a)
    enc_aug = seg_aug_k(
        jnp.concatenate([own_q, prefix_segments(core), other_q, prefix_segments(1 - core)])
    )
    self_aug = seg_aug_k(jnp.concatenate([own_a, other_a]))
    cross_aug = seg_aug_k(jnp.concatenate([own_q, other_q]))

    enc_in = jnp.concatenate([x_question, jnp.pad(entry_vals, ((0, extra - n_prefix), (0, 0)))], 0)
    normed_q = rms_norm(enc_in, norm_gains[0]).astype(jnp.bfloat16)
    query_enc = project(normed_q[:tokens], enc_w[:D]).astype(jnp.bfloat16)
    enc_kv = project(normed_q, enc_w[D : 3 * D]).astype(jnp.bfloat16)
    enc_kv_other = partner(enc_kv)

    normed_a = rms_norm(x_answer, norm_gains[2]).astype(jnp.bfloat16)
    qkv_self = project(normed_a, dec_w[: 3 * D]).astype(jnp.bfloat16)
    query_self, self_kv = qkv_self[:, :D], qkv_self[:, D:]
    self_kv_other = partner(self_kv)

    mixed_enc, logsum_enc = attend(False, core, query_enc, q_aug, enc_kv, enc_kv_other, enc_aug)
    hidden_one = x_question + project_back(mixed_enc, enc_w[3 * D : 4 * D])
    normed_f1 = rms_norm(hidden_one, norm_gains[1]).astype(jnp.bfloat16)
    pre_enc = project(normed_f1, enc_w[4 * D : 4 * D + FF])
    act_enc = jax.nn.gelu(pre_enc).astype(jnp.bfloat16)
    hidden_two = hidden_one + project_back(act_enc, enc_w[4 * D + FF :])
    encoded = rms_norm(hidden_two, norm_gains[5]).astype(jnp.bfloat16)
    cross_kv = project(encoded, dec_w[5 * D : 7 * D]).astype(jnp.bfloat16)
    cross_kv_other = partner(cross_kv)

    mixed_self, logsum_self = attend(True, core, query_self, a_aug, self_kv, self_kv_other, self_aug)
    dec_one = x_answer + project_back(mixed_self, dec_w[3 * D : 4 * D])
    normed_c = rms_norm(dec_one, norm_gains[3]).astype(jnp.bfloat16)
    query_cross = project(normed_c, dec_w[4 * D : 5 * D]).astype(jnp.bfloat16)
    mixed_cross, logsum_cross = attend(
        False, core, query_cross, a_aug, cross_kv, cross_kv_other, cross_aug
    )
    dec_two = dec_one + project_back(mixed_cross, dec_w[7 * D : 8 * D])
    normed_f2 = rms_norm(dec_two, norm_gains[4]).astype(jnp.bfloat16)
    pre_dec = project(normed_f2, dec_w[8 * D : 8 * D + FF])
    act_dec = jax.nn.gelu(pre_dec).astype(jnp.bfloat16)
    dec_three = dec_two + project_back(act_dec, dec_w[8 * D + FF :])
    decoded = from_rows(dec_three.astype(jnp.bfloat16))

    grad_w1d, grad_w2d, grad_nf2 = feed_back(
        grad_top, normed_f2, pre_dec, act_dec, dec_w[8 * D : 8 * D + FF], dec_w[8 * D + FF :]
    )
    grad_x, grad_gain4 = norm_back(dec_two, norm_gains[4], grad_nf2)
    grad_two = grad_top + grad_x
    grad_woc, grad_mixc = output_back(grad_two, mixed_cross, dec_w[7 * D : 8 * D])
    grad_qc, dk_own, dv_own, dk_other, dv_other = attend_back(
        False, core, query_cross, a_aug, cross_kv, cross_kv_other, cross_aug,
        mixed_cross, logsum_cross, grad_mixc,
    )
    more = partner(jnp.concatenate([dk_other, dv_other], 1)).astype(jnp.float32)
    grad_ckv = (jnp.concatenate([dk_own, dv_own], 1) + more).astype(jnp.bfloat16)
    grad_wqc = outer_sum(grad_qc, normed_c)
    grad_x, grad_gain3 = norm_back(
        dec_one, norm_gains[3], project_back(grad_qc, dec_w[4 * D : 5 * D])
    )
    grad_one = grad_two + grad_x
    grad_wckv = outer_sum(grad_ckv, encoded)
    grad_encoded, grad_gain5 = norm_back(
        hidden_two, norm_gains[5], project_back(grad_ckv, dec_w[5 * D : 7 * D])
    )
    grad_wos, grad_mixs = output_back(grad_one, mixed_self, dec_w[3 * D : 4 * D])
    grad_qs, dk_own, dv_own, dk_other, dv_other = attend_back(
        True, core, query_self, a_aug, self_kv, self_kv_other, self_aug,
        mixed_self, logsum_self, grad_mixs,
    )
    more = partner(jnp.concatenate([dk_other, dv_other], 1)).astype(jnp.float32)
    grad_skv = (jnp.concatenate([dk_own, dv_own], 1) + more).astype(jnp.bfloat16)
    grad_self = jnp.concatenate([grad_qs, grad_skv], 1)
    grad_wself = outer_sum(grad_self, normed_a)
    grad_x, grad_gain2 = norm_back(x_answer, norm_gains[2], project_back(grad_self, dec_w[: 3 * D]))
    grad_answers = from_rows((grad_one + grad_x).astype(jnp.bfloat16)).astype(jnp.float32)
    dec_full = jnp.concatenate(
        [grad_wself, grad_wos, grad_wqc, grad_wckv, grad_woc, grad_w1d, grad_w2d], 0
    )
    grad_decoder = reduce_weights(dec_full).astype(jnp.float32).T

    grad_w1e, grad_w2e, grad_nf1 = feed_back(
        grad_encoded, normed_f1, pre_enc, act_enc, enc_w[4 * D : 4 * D + FF], enc_w[4 * D + FF :]
    )
    grad_x, grad_gain1 = norm_back(hidden_one, norm_gains[1], grad_nf1)
    grad_hidden = grad_encoded + grad_x
    grad_woe, grad_mixe = output_back(grad_hidden, mixed_enc, enc_w[3 * D : 4 * D])
    grad_qe, dk_own, dv_own, dk_other, dv_other = attend_back(
        False, core, query_enc, q_aug, enc_kv, enc_kv_other, enc_aug,
        mixed_enc, logsum_enc, grad_mixe,
    )
    more = partner(jnp.concatenate([dk_other, dv_other], 1)).astype(jnp.float32)
    grad_ekv = (jnp.concatenate([dk_own, dv_own], 1) + more).astype(jnp.bfloat16)
    grad_wqe = outer_sum(grad_qe, normed_q[:tokens])
    grad_wkve = outer_sum(grad_ekv, normed_q)
    grad_in = project_back(grad_ekv, enc_w[D : 3 * D])
    grad_in = grad_in + jnp.pad(project_back(grad_qe, enc_w[:D]), ((0, extra), (0, 0)))
    grad_x, grad_gain0 = norm_back(enc_in, norm_gains[0], grad_in)
    grad_questions = from_rows((grad_hidden + grad_x[:tokens]).astype(jnp.bfloat16)).astype(jnp.float32)
    enc_full = jnp.concatenate([grad_wqe, grad_wkve, grad_woe, grad_w1e, grad_w2e], 0)
    gain_terms = jnp.concatenate(
        [grad_gain0, grad_gain1, grad_gain2, grad_gain3, grad_gain4, grad_gain5], 0
    )
    grad_gains = lax.psum(gain_terms, ("rows", "mem"))
    grad_encoder = reduce_weights(enc_full).astype(jnp.float32).T
    return (decoded, grad_questions, grad_answers, grad_encoder, grad_decoder, grad_gains)


def on_device_fast(
    questions,
    answers,
    q_segments,
    a_segments,
    entry_ids,
    entry_alive_flags,
    memory_table,
    enc_params,
    dec_params,
    norm_gains,
    cotangent,
):
    quarter = questions.shape[1]
    core = lax.axis_index("rows") % 2
    mem = lax.axis_index("mem")
    per_row, slots = entry_alive_flags.shape[1], entry_alive_flags.shape[2]
    half = per_row // 2
    rows_here, row_len = q_segments.shape
    n_mem = slots // entry_ids.shape[2]
    entries = fetch(entry_ids.reshape(-1), memory_table).reshape(rows_here, 2, -1, D)
    n_entry = entries.shape[2]
    piece = -(-n_entry // 32) * 32
    entries = jnp.pad(entries, ((0, 0), (0, 0), (0, piece - n_entry), (0, 0)))
    gains = norm_gains
    segs = jnp.concatenate([q_segments, a_segments, entry_alive_flags.reshape(rows_here, -1)], 1)
    numbers = my_row(segs)
    q_row, a_row, alive = numbers[:row_len], numbers[row_len : 2 * row_len], numbers[2 * row_len :]
    alive = alive.reshape(per_row, n_mem, -1)

    def prefix_segments(which):
        live = lax.dynamic_slice_in_dim(alive, which * half, half, 0)
        question = which * half + jnp.arange(half, dtype=jnp.int32)[:, None, None]
        found = jnp.where(live == 1, question, -1).transpose(1, 0, 2).reshape(n_mem, -1)
        found = jnp.repeat(found, 2, axis=1)
        return jnp.pad(found, ((0, 0), (0, piece - n_entry)), constant_values=-1).reshape(-1)

    own_q = own_quarters(q_row, core, quarter)
    other_q = own_quarters(q_row, 1 - core, quarter)
    own_a = own_quarters(a_row, core, quarter)
    other_a = own_quarters(a_row, 1 - core, quarter)
    q_aug, a_aug = seg_aug_q(own_q), seg_aug_q(own_a)
    enc_aug = seg_aug_k(
        jnp.concatenate([own_q, prefix_segments(core), other_q, prefix_segments(1 - core)])
    )
    self_aug = seg_aug_k(jnp.concatenate([own_a, other_a]))
    cross_aug = seg_aug_k(jnp.concatenate([own_q, other_q]))

    (
        normed_q, query_enc, mixed_enc, logsum_enc, hidden_one, normed_f1, hidden_two, encoded, normed_a,
        enc_kv, enc_kv_other, enc_w, dec_w, x_question, prefix, x_answer, grad_top,
    ) = encode(
        enc_params.T, questions, entries, answers, dec_params, cotangent, q_aug, enc_aug, gains
    )
    prefix = prefix.reshape(-1, D)
    qkv_self = project(normed_a, dec_w[: 3 * D]).astype(jnp.bfloat16)
    query_self, self_kv = qkv_self[:, :D], qkv_self[:, D:]
    self_kv_other = partner(self_kv)
    cross_kv = project(encoded, dec_w[5 * D : 7 * D]).astype(jnp.bfloat16)
    cross_kv_other = partner(cross_kv)

    mixed_self, logsum_self = attend(True, core, query_self, a_aug, self_kv, self_kv_other, self_aug)
    dec_one = x_answer.astype(jnp.float32) + project_back(mixed_self, dec_w[3 * D : 4 * D])
    normed_c = rms_norm(dec_one, norm_gains[3]).astype(jnp.bfloat16)
    query_cross = project(normed_c, dec_w[4 * D : 5 * D]).astype(jnp.bfloat16)
    mixed_cross, logsum_cross = attend(
        False, core, query_cross, a_aug, cross_kv, cross_kv_other, cross_aug
    )
    decoded, grad_two, grad_mixc, grad_gain4, dec_full = decode_top(
        dec_one, mixed_cross, gains, grad_top, dec_w
    )
    grad_qc, dk_own, dv_own, dk_other, dv_other = attend_back(
        False, core, query_cross, a_aug, cross_kv, cross_kv_other, cross_aug,
        mixed_cross, logsum_cross, grad_mixc,
    )
    cross_got = (partner(dk_other), partner(dv_other))
    grad_x, grad_gain3 = norm_back(dec_one, norm_gains[3], project_back(grad_qc, dec_w[4 * D : 5 * D]))
    grad_one = grad_two + grad_x
    grad_mixs = project(grad_one.astype(jnp.bfloat16), dec_w[3 * D : 4 * D]).astype(jnp.bfloat16)
    grad_qs, dk_self, dv_self, dk_other, dv_other = attend_back(
        True, core, query_self, a_aug, self_kv, self_kv_other, self_aug,
        mixed_self, logsum_self, grad_mixs,
    )
    self_got = (partner(dk_other), partner(dv_other))
    dec_full, grad_answers, grad_encoded, grad_gain2, grad_gain5 = decode_dense(
        grad_qs, dk_self, dv_self, *self_got, grad_qc, dk_own, dv_own, *cross_got, normed_a, normed_c, encoded,
        mixed_self, grad_one, x_answer, hidden_two, gains, dec_w, dec_full,
    )

    enc_full, grad_hidden, grad_gain1, grad_qe, grad_ekv, grad_decoder, decoded, grad_answers = encode_back(
        grad_encoded, normed_f1, hidden_one, normed_q, gains, enc_w, mixed_enc, query_enc, q_aug,
        enc_kv, enc_kv_other, enc_aug, logsum_enc, dec_full, decoded, grad_answers,
    )
    gain_terms = jnp.concatenate(
        [
            jnp.zeros_like(grad_gain3), grad_gain1[:1], grad_gain2[:1], grad_gain3, grad_gain4[:1], grad_gain5[:1],
            jnp.zeros((2, D), jnp.float32),
        ],
        0,
    )
    grad_encoder, grad_questions, grad_gains = reduce_encoder(
        enc_full, x_question, prefix, grad_qe, grad_ekv, enc_w, grad_hidden, gains, gain_terms
    )
    return (
        decoded,
        grad_questions.astype(jnp.float32),
        grad_answers.astype(jnp.float32),
        grad_encoder.astype(jnp.float32).T,
        grad_decoder.astype(jnp.float32).T,
        grad_gains[:6],
    )


def solution(mesh):
    fast = mesh.shape["rows"] == 8 and mesh.shape["mem"] == 4
    return jax.shard_map(
        on_device_fast if fast else on_device_general,
        mesh=mesh,
        in_specs=(
            P("rows", "mem", None),
            P("rows", "mem", None),
            P("rows", None),
            P("rows", None),
            P("rows", None, "mem"),
            P("rows", None, None),
            P(),
            P(None, ("rows", "mem")),
            P(None, ("rows", "mem")),
            P(),
            P("rows", "mem", None),
        ),
        out_specs=(
            P("rows", "mem", None),
            P("rows", "mem", None),
            P("rows", "mem", None),
            P(None, ("rows", "mem")),
            P(None, ("rows", "mem")),
            P(),
        ),
        check_vma=False,
    )
```

```python
import functools
import jax
import jax.numpy as jnp
from jax import lax
from jax.experimental import pallas as pl
from jax.experimental.pallas import tpu as pltpu
from jax.sharding import PartitionSpec as P

D = 768
H = 12
HD = 64
FF = 3072
QB = 256
masked_score = -1e30


def key_chunks(own_len, extra):
    chunks = []
    for side in (0, 1):
        for at in range(own_len // QB):
            chunks.append((side, at * QB, QB))
        if extra:
            chunks.append((side, own_len, extra))
    return chunks


def chunk_sets(causal, own_len, extra):
    chunks = key_chunks(own_len, extra)
    if not causal:
        return [[list(range(len(chunks)))] * (own_len // QB)]
    quarters = ((0, 3), (1, 2))
    sets = []
    for core in (0, 1):
        held = (quarters[core], quarters[1 - core])
        sets.append([
            [n for n, (side, at, size) in enumerate(chunks) if held[side][at // QB] <= held[0][qb]]
            for qb in range(own_len // QB)
        ])
    return sets


def attend_pair(causal, own_len, extra, use, q_ref, qaug_ref, own_k, own_v, oth_k, oth_v, kaug_ref, o_ref, lse_ref, s_ref):
    low = lax.broadcasted_iota(jnp.int32, (1, 128), 1) < HD
    chunks = key_chunks(own_len, extra)
    nk = own_len + extra
    for qb in range(own_len // QB):
        rows = pl.ds(qb * QB, QB)
        q = q_ref[rows, :] * jnp.bfloat16(HD ** (-0.5))
        qaug = qaug_ref[rows, :]
        queries = (jnp.where(low, q, qaug), jnp.where(low, qaug, q))
        tops = [None, None]
        for ci in use[qb]:
            side, at, size = chunks[ci]
            k = (own_k, oth_k)[side][at : at + size, :]
            place = slice(side * nk + at, side * nk + at + size)
            kaug = kaug_ref[place, :]
            for h in (0, 1):
                keys = jnp.where(low, k, kaug) if h == 0 else jnp.where(low, kaug, k)
                s = lax.dot_general(keys, queries[h], (((1,), (1,)), ((), ())), preferred_element_type=jnp.float32)
                if causal and side == 0 and at == qb * QB:
                    tri = lax.broadcasted_iota(jnp.int32, (size, QB), 0) <= lax.broadcasted_iota(jnp.int32, (size, QB), 1)
                    s = jnp.where(tri, s, masked_score)
                s_ref[qb, place, h * QB : (h + 1) * QB] = s
                top = jnp.max(s.reshape(size // 8, 8, QB), 0)
                tops[h] = top if tops[h] is None else jnp.maximum(tops[h], top)
        m = jnp.max(jnp.concatenate(tops, 1), 0, keepdims=True)
        total, acc = None, None
        for ci in use[qb]:
            side, at, size = chunks[ci]
            v = (own_v, oth_v)[side][at : at + size, :]
            zero = jnp.zeros_like(v)
            place = slice(side * nk + at, side * nk + at + size)
            p = jnp.exp(s_ref[qb, place, :] - m)
            part = jnp.sum(p.reshape(size // 8, 8, 2 * QB), 0)
            total = part if total is None else total + part
            pb = p.astype(jnp.bfloat16)
            pb = jnp.concatenate([pb[:, :QB], pb[:, QB:]], 0)
            v_split = jnp.concatenate([jnp.where(low, v, zero), jnp.where(low, zero, v)], 0)
            part = lax.dot_general(pb, v_split, (((0,), (0,)), ((), ())), preferred_element_type=jnp.float32)
            acc = part if acc is None else acc + part
        total = jnp.sum(total, 0, keepdims=True)
        lse = m + jnp.log(total)
        rec = 1.0 / total
        wide = lambda row, h: jnp.broadcast_to(row[:, h * QB : (h + 1) * QB], (HD, QB))
        o_ref[rows, :] = (acc * jnp.concatenate([wide(rec, 0), wide(rec, 1)], 0).T).astype(jnp.bfloat16)
        lse_ref[rows, :] = jnp.concatenate([wide(lse, 1), wide(lse, 0)], 0).T


def by_core(core, sets, work):
    if len(sets) == 1:
        work(sets[0])
        return
    for n, use in enumerate(sets):
        pl.when(core[0] == n)(functools.partial(work, use))


def attend_kernel(causal, own_len, extra, core, *refs):
    by_core(core, chunk_sets(causal, own_len, extra), lambda use: attend_pair(causal, own_len, extra, use, *refs))


def back_kernel(causal, own_len, extra, core, *refs):
    by_core(core, chunk_sets(causal, own_len, extra), lambda use: back_pair(causal, own_len, extra, use, *refs))


def attend(causal, core, q, qaug, own_kv, oth_kv, kaug):
    t = q.shape[0]
    nk = own_kv.shape[0]
    col = lambda first: pl.BlockSpec((nk, 128), lambda i, a: (0, first + i))
    return pl.pallas_call(
        functools.partial(attend_kernel, causal, t, nk - t),
        grid_spec=pltpu.PrefetchScalarGridSpec(
            num_scalar_prefetch=1,
            grid=(H // 2,),
            in_specs=[
                pl.BlockSpec((t, 128), lambda i, a: (0, i)),
                pl.BlockSpec((t, 128), lambda i, a: (0, 0)),
                col(0), col(H // 2), col(0), col(H // 2),
                pl.BlockSpec((2 * nk, 128), lambda i, a: (0, 0)),
            ],
            out_specs=[pl.BlockSpec((t, 128), lambda i, a: (0, i))] * 2,
            scratch_shapes=[pltpu.VMEM((t // QB, 2 * nk, 2 * QB), jnp.float32)],
        ),
        out_shape=[jax.ShapeDtypeStruct((t, D), jnp.bfloat16), jax.ShapeDtypeStruct((t, D), jnp.float32)],
        compiler_params=pltpu.CompilerParams(vmem_limit_bytes=32 * 1024 * 1024),
        cost_estimate=pl.CostEstimate(flops=4 * t * 2 * nk * D, bytes_accessed=8 * nk * D, transcendentals=t * 2 * nk * H),
        name="attend",
    )(core.reshape(1), q, qaug, own_kv, own_kv, oth_kv, oth_kv, kaug)


def three_parts(value):
    hi = value.astype(jnp.bfloat16).astype(jnp.float32)
    mid = (value - hi).astype(jnp.bfloat16).astype(jnp.float32)
    return hi, mid, value - hi - mid


def spread(base, lane64, value):
    hi, mid, lo = three_parts(value)
    return jnp.where(lane64 == 8, hi, jnp.where(lane64 == 9, mid, jnp.where(lane64 == 10, lo, base)))


def back_pair(causal, own_len, extra, use, q_ref, qaug_ref, own_k, own_v, oth_k, oth_v, kaug_ref, o_ref, lse_ref, g_ref, dq_ref, dko_ref, dvo_ref, dkt_ref, dvt_ref, dk_acc, dv_acc):
    lane = lax.broadcasted_iota(jnp.int32, (1, 128), 1)
    low = lane < HD
    lane64 = lane % HD
    chunks = key_chunks(own_len, extra)
    nk = own_len + extra
    begun = set()
    ones_aug = jnp.where((lane64 >= 8) & (lane64 <= 10), 1.0, 0.0).astype(jnp.bfloat16)
    def block(qb, use_here, begun):
        rows = pl.ds(pl.multiple_of(qb * QB, QB), QB)
        q = q_ref[rows, :] * jnp.bfloat16(HD ** (-0.5))
        g = g_ref[rows, :]
        qaug = spread(qaug_ref[rows, :].astype(jnp.float32), lane64, -lse_ref[rows, :]).astype(jnp.bfloat16)
        prod = g.astype(jnp.float32) * o_ref[rows, :].astype(jnp.float32)
        d_even = jnp.sum(jnp.where(low, prod, 0.0), -1, keepdims=True)
        d_odd = jnp.sum(jnp.where(low, 0.0, prod), -1, keepdims=True)
        gaug = spread(jnp.zeros((QB, 128), jnp.float32), lane64, -jnp.where(low, d_odd, d_even)).astype(jnp.bfloat16)
        queries = (jnp.where(low, q, qaug), jnp.where(low, qaug, q))
        grads = (jnp.where(low, g, gaug), jnp.where(low, gaug, g))
        zero = jnp.zeros_like(q)
        q_split = jnp.concatenate([jnp.where(low, q, zero), jnp.where(low, zero, q)], 0)
        g_split = jnp.concatenate([jnp.where(low, g, zero), jnp.where(low, zero, g)], 0)
        dq = None
        for ci in use_here:
            side, at, size = chunks[ci]
            k = (own_k, oth_k)[side][at : at + size, :]
            v = (own_v, oth_v)[side][at : at + size, :]
            place = slice(side * nk + at, side * nk + at + size)
            kaug = kaug_ref[place, :]
            vaug = jnp.broadcast_to(ones_aug, v.shape)
            zk = jnp.zeros_like(k)
            probs, dscores = [], []
            for h in (0, 1):
                keys = jnp.where(low, k, kaug) if h == 0 else jnp.where(low, kaug, k)
                vals = jnp.where(low, v, vaug) if h == 0 else jnp.where(low, vaug, v)
                s = lax.dot_general(keys, queries[h], (((1,), (1,)), ((), ())), preferred_element_type=jnp.float32)
                if causal and side == 0 and at == qb * QB:
                    tri = lax.broadcasted_iota(jnp.int32, (size, QB), 0) <= lax.broadcasted_iota(jnp.int32, (size, QB), 1)
                    s = jnp.where(tri, s, masked_score)
                p = jnp.exp(s)
                dp = lax.dot_general(vals, grads[h], (((1,), (1,)), ((), ())), preferred_element_type=jnp.float32)
                dscores.append((p * dp).astype(jnp.bfloat16))
                probs.append(p.astype(jnp.bfloat16))
            dk = jnp.dot(jnp.concatenate(dscores, 1), q_split, preferred_element_type=jnp.float32)
            dv = jnp.dot(jnp.concatenate(probs, 1), g_split, preferred_element_type=jnp.float32)
            if ci in begun:
                dk_acc[place, :] += dk
                dv_acc[place, :] += dv
            else:
                begun.add(ci)
                dk_acc[place, :] = dk
                dv_acc[place, :] = dv
            k_split = jnp.concatenate([jnp.where(low, k, zk), jnp.where(low, zk, k)], 0)
            dst = jnp.concatenate(dscores, 0)
            part = lax.dot_general(dst, k_split, (((0,), (0,)), ((), ())), preferred_element_type=jnp.float32)
            dq = part if dq is None else dq + part
        dq_ref[rows, :] = (dq * HD ** (-0.5)).astype(jnp.bfloat16)

    if causal:
        begun = set()
        for qb in range(own_len // QB):
            block(qb, use[qb], begun)
    else:
        begun = set(use[0])
        dk_acc[...] = jnp.zeros(dk_acc.shape, jnp.float32)
        dv_acc[...] = jnp.zeros(dv_acc.shape, jnp.float32)

        def step(qb, unused):
            block(qb, use[0], begun)
            return unused

        lax.fori_loop(0, own_len // QB, step, 0)
    for ci, (side, at, size) in enumerate(chunks):
        if ci not in begun:
            place = slice(side * nk + at, side * nk + at + size)
            dk_acc[place, :] = jnp.zeros((size, 128), jnp.float32)
            dv_acc[place, :] = jnp.zeros((size, 128), jnp.float32)
    dko_ref[...] = dk_acc[:nk, :]
    dvo_ref[...] = dv_acc[:nk, :]
    dkt_ref[...] = dk_acc[nk:, :].astype(jnp.bfloat16)
    dvt_ref[...] = dv_acc[nk:, :].astype(jnp.bfloat16)


def attend_back(causal, core, q, qaug, own_kv, oth_kv, kaug, mixed, lse, grad):
    t = q.shape[0]
    nk = own_kv.shape[0]
    col = lambda first: pl.BlockSpec((nk, 128), lambda i, a: (0, first + i))
    tok = pl.BlockSpec((t, 128), lambda i, a: (0, i))
    return pl.pallas_call(
        functools.partial(back_kernel, causal, t, nk - t),
        grid_spec=pltpu.PrefetchScalarGridSpec(
            num_scalar_prefetch=1,
            grid=(H // 2,),
            in_specs=[
                tok,
                pl.BlockSpec((t, 128), lambda i, a: (0, 0)),
                col(0), col(H // 2), col(0), col(H // 2),
                pl.BlockSpec((2 * nk, 128), lambda i, a: (0, 0)),
                tok, tok, tok,
            ],
            out_specs=[tok, col(0), col(0), col(0), col(0)],
            scratch_shapes=[pltpu.VMEM((2 * nk, 128), jnp.float32), pltpu.VMEM((2 * nk, 128), jnp.float32)],
        ),
        out_shape=[
            jax.ShapeDtypeStruct((t, D), jnp.bfloat16),
            jax.ShapeDtypeStruct((nk, D), jnp.float32),
            jax.ShapeDtypeStruct((nk, D), jnp.float32),
            jax.ShapeDtypeStruct((nk, D), jnp.bfloat16),
            jax.ShapeDtypeStruct((nk, D), jnp.bfloat16),
        ],
        compiler_params=pltpu.CompilerParams(vmem_limit_bytes=32 * 1024 * 1024),
        cost_estimate=pl.CostEstimate(flops=10 * t * 2 * nk * D, bytes_accessed=24 * nk * D, transcendentals=t * 2 * nk * H),
        name="attend_back",
    )(core.reshape(1), q, qaug, own_kv, own_kv, oth_kv, oth_kv, kaug, mixed, lse, grad)


def seg_aug_q(seg):
    j = jnp.arange(128, dtype=jnp.int32) % HD
    return ((j[None, :] < 8) & (j[None, :] == seg[:, None])).astype(jnp.bfloat16)


def seg_aug_k(seg):
    j = jnp.arange(128, dtype=jnp.int32)[None, :] % HD
    bad = (j < 8) & (j != seg[:, None])
    return jnp.where(bad, masked_score, jnp.where((j >= 8) & (j <= 10), 1.0, 0.0)).astype(jnp.bfloat16)


epsilon = 1e-06
CHUNK = 512
TOP_CHUNK = 1024


def dot_nt(left, right):
    return lax.dot_general(left, right, (((1,), (1,)), ((), ())), preferred_element_type=jnp.float32)


def dot_nn(left, right):
    return lax.dot_general(left, right, (((1,), (0,)), ((), ())), preferred_element_type=jnp.float32)


def dot_tn(left, right):
    return lax.dot_general(left, right, (((0,), (0,)), ((), ())), preferred_element_type=jnp.float32)


def rms_norm(values, gain):
    return values * lax.rsqrt(jnp.mean(values * values, -1, keepdims=True) + epsilon) * gain


def norm_back(values, gain, grad):
    root = lax.rsqrt(jnp.mean(values * values, -1, keepdims=True) + epsilon)
    unit = values * root
    scaled = grad * gain
    inner = jnp.mean(unit * scaled, -1, keepdims=True)
    return root * (scaled - unit * inner), jnp.sum(grad * unit, 0, keepdims=True)


def gelu_pair(pre):
    root = 0.7978845608028654
    square = pre * pre
    bent = jnp.tanh(root * pre * (1.0 + 0.044715 * square))
    half = 0.5 * (1.0 + bent)
    slope = half + 0.5 * pre * (1.0 - bent * bent) * root * (1.0 + 0.134145 * square)
    return pre * half, slope


def feed_back_chunk(normed, grad_b, w1, w2, dw, total, first):
    act, slope = gelu_pair(dot_nt(normed, w1))
    act = act.astype(jnp.bfloat16)
    grad_pre = (dot_nt(grad_b, w2) * slope).astype(jnp.bfloat16)
    size = w1.shape[0]
    dw[:size, :] = dot_tn(grad_pre, normed).astype(jnp.bfloat16)
    dw[size:, :] = dot_tn(act, grad_b).astype(jnp.bfloat16)
    part = dot_nn(grad_pre, w1)

    @pl.when(first)
    def _():
        total[...] = part

    @pl.when(jnp.logical_not(first))
    def _():
        total[...] += part

    return act


class ChunkStore:
    def __init__(self, slots, whole, places, sems):
        self.slots, self.whole, self.places, self.sems = slots, whole, places, sems

    def copy(self, i, which):
        slot = lax.rem(i, 2)
        size = self.slots.shape[1] // 2
        rows = pl.ds(pl.multiple_of(self.places[which] + i * size, size), size)
        source = self.slots.at[slot, pl.ds(which * size, size)]
        return pltpu.make_async_copy(source, self.whole.at[rows], self.sems.at[slot, which])

    def start(self, i):
        for which in (0, 1):
            self.copy(i, which).start()

    def wait(self, i):
        for which in (0, 1):
            self.copy(i, which).wait()


def whole_spec(shape):
    return pl.BlockSpec(shape, lambda i: (0,) * len(shape))


def decode_top_kernel(
    d1_ref, mixed_ref, gains, grad_ref, wo_ref, w1_ref, w2_ref,
    decoded_ref, grad_two_ref, grad_mix_ref, dgain_ref, whole,
    d2_ref, normed_ref, acc_ref, total_ref, slots, dwo_ref, sems, sem_o,
):
    i = pl.program_id(0)
    store = ChunkStore(slots, whole, (8 * D, 8 * D + FF), sems)

    @pl.when(i == 0)
    def _():
        d2_ref[...] = d1_ref[...] + dot_nn(mixed_ref[...], wo_ref[...])
        normed_ref[...] = rms_norm(d2_ref[...], gains[4:5, :]).astype(jnp.bfloat16)

    pl.when(i >= 2)(lambda: store.wait(i - 2))
    act = feed_back_chunk(
        normed_ref[...], grad_ref[...], w1_ref[...], w2_ref[...], slots.at[lax.rem(i, 2)], total_ref, i == 0
    )
    store.start(i)
    more = dot_nn(act, w2_ref[...])

    @pl.when(i == 0)
    def _():
        acc_ref[...] = d2_ref[...] + more

    @pl.when(i > 0)
    def _():
        acc_ref[...] += more

    @pl.when(i == FF // TOP_CHUNK - 1)
    def _():
        decoded_ref[...] = acc_ref[...].astype(jnp.bfloat16)
        grad_x, dgain = norm_back(d2_ref[...], gains[4:5, :], total_ref[...])
        dgain_ref[...] = jnp.broadcast_to(dgain, dgain_ref.shape)
        grad_two = grad_ref[...].astype(jnp.float32) + grad_x
        grad_two_ref[...] = grad_two
        grad_b = grad_two.astype(jnp.bfloat16)
        dwo_ref[...] = dot_tn(mixed_ref[...], grad_b).astype(jnp.bfloat16)
        last = pltpu.make_async_copy(dwo_ref, whole.at[pl.ds(7 * D, D)], sem_o)
        last.start()
        grad_mix_ref[...] = dot_nt(grad_b, wo_ref[...]).astype(jnp.bfloat16)
        store.wait(i - 1)
        store.wait(i)
        last.wait()


def decode_top(d1, mixed, gains, grad_top, dec_w):
    t = d1.shape[0]
    n = FF // TOP_CHUNK
    tok = whole_spec((t, D))
    return pl.pallas_call(
        decode_top_kernel,
        grid=(n,),
        in_specs=[
            tok, tok, whole_spec(gains.shape), tok,
            pl.BlockSpec((D, D), lambda i: (7, 0)),
            pl.BlockSpec((TOP_CHUNK, D), lambda i: (8 * D // TOP_CHUNK + i, 0)),
            pl.BlockSpec((TOP_CHUNK, D), lambda i: (8 * D // TOP_CHUNK + n + i, 0)),
        ],
        out_specs=[tok, tok, tok, whole_spec((8, D)), pl.BlockSpec(memory_space=pl.ANY)],
        out_shape=[
            jax.ShapeDtypeStruct((t, D), jnp.bfloat16),
            jax.ShapeDtypeStruct((t, D), jnp.float32),
            jax.ShapeDtypeStruct((t, D), jnp.bfloat16),
            jax.ShapeDtypeStruct((8, D), jnp.float32),
            jax.ShapeDtypeStruct(dec_w.shape, jnp.bfloat16),
        ],
        scratch_shapes=[
            pltpu.VMEM((t, D), jnp.float32),
            pltpu.VMEM((t, D), jnp.bfloat16),
            pltpu.VMEM((t, D), jnp.float32),
            pltpu.VMEM((t, D), jnp.float32),
            pltpu.VMEM((2, 2 * TOP_CHUNK, D), jnp.bfloat16),
            pltpu.VMEM((D, D), jnp.bfloat16),
            pltpu.SemaphoreType.DMA((2, 2)),
            pltpu.SemaphoreType.DMA,
        ],
        compiler_params=pltpu.CompilerParams(vmem_limit_bytes=36 * 1024 * 1024),
        cost_estimate=pl.CostEstimate(flops=14 * t * FF * D, bytes_accessed=8 * FF * D, transcendentals=t * FF),
        name="decode_top",
    )(d1, mixed, gains, grad_top, dec_w, dec_w, dec_w)


def decode_dense_kernel(*refs):
    ins, (gains, w_ref, unused, dw_ref, answers_ref, encoded_ref, dgain2_ref, dgain5_ref, g_ref, sum_ref) = refs[:17], refs[17:27]
    held, sems = refs[27:44], refs[44]
    copies = [lambda n=n: pltpu.make_async_copy(ins[n], held[n], sems.at[n]) for n in range(17)]
    (
        dqs_ref, dks_ref, dvs_ref, ks_got, vs_got, dqc_ref, dkc_ref, dvc_ref, kc_got, vc_got,
        na_ref, nc_ref, ne_ref, os_ref, one_ref, x_ref, h2_ref,
    ) = held
    i = pl.program_id(0)

    @pl.when(i == 0)
    def _():
        for n in (6, 8, 12, 7, 9, 16, 5, 11, 13, 14, 0, 10, 1, 3, 2, 4, 15):
            copies[n]().start()

    for at, which in enumerate(((6, 8, 12), (7, 9, 16), (5, 11), (13, 14), (0, 10), (1, 3), (2, 4, 15))):

        @pl.when(i == at)
        def _(which=which):
            for n in which:
                copies[n]().wait()

    def weight(n, wide, narrow):
        @pl.when(i == n)
        def _():
            dw_ref[...] = dot_tn(wide(), narrow[...]).astype(jnp.bfloat16)

    def total(own, got, slot):
        g_ref[slot] = (own[...] + got[...].astype(jnp.float32)).astype(jnp.bfloat16)
        return g_ref[slot]

    def gather_back(n, begin, grads, finish):
        @pl.when(i == n)
        def _():
            part = dot_nn(grads(), w_ref[...])
            if begin:
                sum_ref[...] = part
            else:
                sum_ref[...] += part
            if finish is not None:
                finish()

    def encoded_done():
        grad, dgain = norm_back(h2_ref[...], gains[5:6, :], sum_ref[...])
        encoded_ref[...] = grad
        dgain5_ref[...] = jnp.broadcast_to(dgain, dgain5_ref.shape)

    def answers_done():
        grad, dgain = norm_back(x_ref[...].astype(jnp.float32), gains[2:3, :], sum_ref[...])
        answers_ref[...] = (one_ref[...] + grad).astype(jnp.bfloat16)
        dgain2_ref[...] = jnp.broadcast_to(dgain, dgain2_ref.shape)

    weight(0, lambda: total(dkc_ref, kc_got, 0), ne_ref)
    gather_back(0, True, lambda: g_ref[0], None)
    weight(1, lambda: total(dvc_ref, vc_got, 1), ne_ref)
    gather_back(1, False, lambda: g_ref[1], encoded_done)
    weight(2, lambda: dqc_ref[...], nc_ref)

    @pl.when(i == 3)
    def _():
        dw_ref[...] = dot_tn(os_ref[...], one_ref[...].astype(jnp.bfloat16)).astype(jnp.bfloat16)

    weight(4, lambda: dqs_ref[...], na_ref)
    gather_back(4, True, lambda: dqs_ref[...], None)
    weight(5, lambda: total(dks_ref, ks_got, 0), na_ref)
    gather_back(5, False, lambda: g_ref[0], None)
    weight(6, lambda: total(dvs_ref, vs_got, 1), na_ref)
    gather_back(6, False, lambda: g_ref[1], answers_done)


def decode_dense(dqs, dks, dvs, ks_got, vs_got, dqc, dkc, dvc, kc_got, vc_got, na, nc, ne, os, one, x, h2, gains, dec_w, dec_g):
    t = x.shape[0]
    block = lambda i: jnp.where(i < 2, i + 5, jnp.where(i == 2, 4, jnp.where(i == 3, 3, i - 4)))
    tok = whole_spec((t, D))
    f32, bf = jnp.float32, jnp.bfloat16
    dims = lambda kind, n=t: jax.ShapeDtypeStruct((n, D), kind)
    return pl.pallas_call(
        decode_dense_kernel,
        grid=(7,),
        in_specs=[pl.BlockSpec(memory_space=pl.ANY)] * 17 + [
            whole_spec(gains.shape), pl.BlockSpec((D, D), lambda i: (block(i), 0)), pl.BlockSpec(memory_space=pl.ANY),
        ],
        out_specs=[pl.BlockSpec((D, D), lambda i: (block(i), 0)), tok, tok, whole_spec((8, D)), whole_spec((8, D))],
        out_shape=[dims(bf, dec_g.shape[0]), dims(bf), dims(f32), dims(f32, 8), dims(f32, 8)],
        scratch_shapes=[pltpu.VMEM((2, t, D), bf), pltpu.VMEM((t, D), f32)]
        + [pltpu.VMEM((t, D), v.dtype) for v in (dqs, dks, dvs, ks_got, vs_got, dqc, dkc, dvc, kc_got, vc_got, na, nc, ne, os, one, x, h2)]
        + [pltpu.SemaphoreType.DMA((17,))],
        input_output_aliases={19: 0},
        compiler_params=pltpu.CompilerParams(vmem_limit_bytes=40 * 1024 * 1024),
        cost_estimate=pl.CostEstimate(flops=24 * t * D * D, bytes_accessed=50 * t * D, transcendentals=0),
        name="decode_dense",
    )(dqs, dks, dvs, ks_got, vs_got, dqc, dkc, dvc, kc_got, vc_got, na, nc, ne, os, one, x, h2, gains, dec_w, dec_g)


MESH = pl.DeviceIdType.MESH


def position():
    r, m = lax.axis_index("rows"), lax.axis_index("mem")
    core = lax.rem(r, 2)
    near = r + 1 - 2 * core
    x_near = r + 2 - 4 * lax.rem(lax.div(r, 2), 2)
    y_near = r + 4 - 8 * lax.div(r, 4)
    first = x_near + core * (y_near - x_near)
    second = y_near + core * (x_near - y_near)
    both = first + second - r
    turn = 1 - 2 * core
    others = (near, second + turn, first + turn, both + turn)
    return r, m, core, near, first, second, both, others


def greet(pos):
    r, m, core, near, first, second = pos[:6]
    barrier = pltpu.get_barrier_semaphore()
    count = 0
    for to in (r, near):
        for step in range(4):
            if to is r and step == 0:
                continue
            pl.semaphore_signal(barrier, inc=1, device_id=(to, lax.rem(m + step, 4)), device_id_type=MESH)
            count += 1
    for to in (first, second):
        pl.semaphore_signal(barrier, inc=1, device_id=(to, m), device_id_type=MESH)
        count += 1
    pl.semaphore_wait(barrier, count)


def remote(src, dst, send, recv, to):
    return pltpu.make_async_remote_copy(
        src_ref=src, dst_ref=dst, send_sem=send, recv_sem=recv, device_id=to, device_id_type=MESH
    )


class Mail:
    def __init__(self, pos):
        self.pos = pos
        self.started = []
        self.maybe = []

    def send(self, make):
        make().start()
        self.started.append(make)

    def send_or_keep(self, here, make, keep):
        pl.when(here())(lambda: keep().start())
        pl.when(jnp.logical_not(here()))(lambda: make().start())
        self.maybe.append((here, make))

    def arrived(self, ref, sem):
        near, m = self.pos[3], self.pos[1]
        remote(ref, ref, sem, sem, (near, m)).wait_recv()

    def finish(self):
        for make in self.started:
            make().wait_send()
        for here, make in self.maybe:
            pl.when(jnp.logical_not(here()))(lambda make=make: make().wait_send())


def dma(*shape):
    return pltpu.SemaphoreType.DMA(shape)


def gather_sems(n):
    return [dma(3, n), dma(3, n), dma(4, n), dma(4, n), dma(4, 2, n), dma(4, 2, n), dma(4, 4, n), dma(4, 4, n), dma(n)]


class Gather:
    def __init__(self, mail, ins, outs, sems):
        self.mail, self.ins, self.outs = mail, ins, outs
        self.z_s, self.z_r, self.a_s, self.a_r, self.b_s, self.b_r, self.c_s, self.c_r, self.l = sems

    def at(self, w, row, step):
        m = self.mail.pos[1]
        size = self.ins[w].shape[0]
        mem = lax.rem(m - step + 4, 4)
        return self.outs[w].at[pl.ds(pl.multiple_of((row * 4 + mem) * size, 32), size)]

    def own(self, w):
        return pltpu.make_async_copy(self.ins[w], self.at(w, self.mail.pos[0], 0), self.l.at[w])

    def ring(self, step):
        r, m = self.mail.pos[:2]
        if step == 0:
            self.own(0).start()
        else:
            self.mail.arrived(self.at(0, r, step), self.z_r.at[step - 1, 0])
        if step < 3:
            self.mail.send(lambda: remote(self.source(step), self.at(0, r, step), self.z_s.at[step, 0], self.z_r.at[step, 0], (r, lax.rem(m + 1, 4))))

    def source(self, step):
        return self.ins[0] if step == 0 else self.at(0, self.mail.pos[0], step)

    def spread(self, step):
        r, m, core, near, first, second, both, others = self.mail.pos
        src, dst, send = functools.partial(self.source, step), functools.partial(self.at, 0, r, step), self.mail.send
        send(lambda: remote(src(), dst(), self.a_s.at[step, 0], self.a_r.at[step, 0], (first, m)))
        send(lambda: remote(src(), dst(), self.b_s.at[step, 0, 0], self.b_r.at[step, 0, 0], (second, m)))
        send(lambda: remote(src(), dst(), self.c_s.at[step, 0, 0], self.c_r.at[step, 0, 0], (near, m)))

    def from_first(self, step):
        r, m, core, near, first, second, both, others = self.mail.pos
        for w in range(len(self.ins)):
            here = lambda w=w: self.at(w, first, step)
            self.mail.arrived(here(), self.a_r.at[step, w])
            self.mail.send(lambda w=w, here=here: remote(here(), here(), self.b_s.at[step, 1, w], self.b_r.at[step, 1, w], (second, m)))
            self.mail.send(lambda w=w, here=here: remote(here(), here(), self.c_s.at[step, 1, w], self.c_r.at[step, 1, w], (near, m)))

    def from_second(self, step):
        r, m, core, near, first, second, both, others = self.mail.pos
        for k, row in ((0, second), (1, both)):
            for w in range(len(self.ins)):
                here = lambda w=w, row=row: self.at(w, row, step)
                self.mail.arrived(here(), self.b_r.at[step, k, w])
                self.mail.send(lambda w=w, k=k, here=here: remote(here(), here(), self.c_s.at[step, 2 + k, w], self.c_r.at[step, 2 + k, w], (near, m)))

    def finish(self):
        others = self.mail.pos[7]
        for step in range(4):
            for k in range(4):
                for w in range(len(self.ins)):
                    self.mail.arrived(self.at(w, others[k], step), self.c_r.at[step, k, w])
        for w in range(len(self.ins)):
            self.own(w).wait()


def token_sems(n):
    return [dma(n, 2), dma(n, 2), dma(n)]


class TokensIn:
    def __init__(self, mail, pairs, sems):
        self.mail, self.pairs = mail, pairs
        self.t_s, self.t_r, self.t_l = sems

    def start(self, n):
        r, m, core, near = self.mail.pos[:4]
        src, dst = self.pairs[n]
        quarter = src.shape[1]
        holder = lambda: lax.div(m * (3 - m), 2)
        slot = lambda: lax.div(m, 2)
        for i in (0, 1):
            here = lambda i=i: jnp.logical_and(2 * core + i == m, holder() == core)
            place = lambda: dst.at[pl.ds(pl.multiple_of(slot() * quarter, quarter), quarter)]
            make = lambda i=i: remote(src.at[i], place(), self.t_s.at[n, i], self.t_r.at[n, slot()], (r - core + holder(), 2 * core + i))
            keep = lambda i=i: pltpu.make_async_copy(src.at[i], place(), self.t_l.at[n])
            self.mail.send_or_keep(here, make, keep)

    def finish(self, n):
        r, m, core, near = self.mail.pos[:4]
        src, dst = self.pairs[n]
        quarter = src.shape[1]
        for li in (0, 1):
            source = core if li == 0 else 3 - core
            here = jnp.logical_and(lax.div(m, 2) == core, m == source)
            place = lambda: dst.at[pl.ds(li * quarter, quarter)]
            pl.when(here)(lambda: pltpu.make_async_copy(place(), place(), self.t_l.at[n]).wait())
            pl.when(jnp.logical_not(here))(lambda: self.mail.arrived(place(), self.t_r.at[n, li]))


class TokensOut:
    def __init__(self, mail, pairs, sems):
        self.mail, self.pairs = mail, pairs
        self.t_s, self.t_r, self.t_l = sems

    def start(self, n):
        r, m, core, near = self.mail.pos[:4]
        src, dst = self.pairs[n]
        quarter = dst.shape[1]
        row = lambda: lax.rem(m, 2)
        for li in (0, 1):
            to_mem = lambda li=li: core if li == 0 else 3 - core
            here = lambda to_mem=to_mem: jnp.logical_and(to_mem() == m, lax.div(m, 2) == core)
            place = lambda li=li: src.at[pl.ds(li * quarter, quarter)]
            make = lambda li=li, to_mem=to_mem, place=place: remote(place(), dst.at[row()], self.t_s.at[n, li], self.t_r.at[n, row()], (r - core + lax.div(m, 2), to_mem()))
            keep = lambda place=place: pltpu.make_async_copy(place(), dst.at[row()], self.t_l.at[n])
            self.mail.send_or_keep(here, make, keep)

    def finish(self):
        r, m, core, near = self.mail.pos[:4]
        holder = lax.div(m * (3 - m), 2)
        for n, (src, dst) in enumerate(self.pairs):
            for i in (0, 1):
                here = jnp.logical_and(2 * core + i == m, holder == core)
                pl.when(here)(lambda: pltpu.make_async_copy(dst.at[i], dst.at[i], self.t_l.at[n]).wait())
                pl.when(jnp.logical_not(here))(lambda: self.mail.arrived(dst.at[i], self.t_r.at[n, i]))


class EntriesIn:
    def __init__(self, mail, ent_in, ent_out, sems):
        self.mail, self.ent_in, self.ent_out = mail, ent_in, ent_out
        self.i_s, self.i_r, self.i_l = sems

    def start(self):
        r, m, core, near = self.mail.pos[:4]
        for i in (0, 1):
            make = lambda i=i, e=0, to=r: remote(self.ent_in.at[i, 1 - core if e else core], self.ent_out.at[m], self.i_s.at[i, e], self.i_r.at[m], (to, 2 * core + i))
            self.mail.send(functools.partial(make, e=1, to=near))
            here = lambda i=i: 2 * core + i == m
            keep = lambda i=i: pltpu.make_async_copy(self.ent_in.at[i, core], self.ent_out.at[m], self.i_l)
            self.mail.send_or_keep(here, make, keep)

    def finish(self):
        r, m, core, near = self.mail.pos[:4]
        for mem in range(4):
            here = jnp.logical_and(lax.div(m, 2) == core, m == mem)
            place = self.ent_out.at[mem]
            pl.when(here)(lambda: pltpu.make_async_copy(place, place, self.i_l).wait())
            pl.when(jnp.logical_not(here))(lambda: self.mail.arrived(place, self.i_r.at[mem]))


def add_to(total, more):
    def step(i, unused):
        rows = pl.ds(pl.multiple_of(i * 32, 32), 32)
        total[rows, :] = total[rows, :] + more[rows, :]
        return unused

    lax.fori_loop(0, total.shape[0] // 32, step, 0)


def reduce_buffers(size):
    block = lambda *lead: pltpu.VMEM(lead + (size, D), jnp.bfloat16)
    return [block(4, 4), block(4, 4), block(4, 2), block(4), block(3)]


def reduce_sems():
    return [dma(4, 4), dma(4, 4), dma(4, 4), dma(4, 2), dma(4, 2), dma(4), dma(4), dma(3), dma(3), dma(1)]


class Reduce:
    def __init__(self, mail, source, out, buffers, sems):
        self.mail, self.source, self.out = mail, source, out
        self.held, self.rc, self.rb, self.ra, self.rz = buffers
        self.l, self.c_s, self.c_r, self.b_s, self.b_r, self.a_s, self.a_r, self.z_s, self.z_r, self.o = sems

    def at(self, row, j):
        m = self.mail.pos[1]
        size = self.out.shape[0]
        mem = lax.rem(m + 7 - j, 4)
        return self.source.at[pl.ds(pl.multiple_of((row * 4 + mem) * size, 32), size)]

    def load(self, j, k):
        r, m, core, near, first, second, both, others = self.mail.pos
        return pltpu.make_async_copy(self.at((r, first, second, both)[k], j), self.held.at[j, k], self.l.at[j, k])

    def start(self):
        r, m, core, near, first, second, both, others = self.mail.pos
        order = [(0, 3), (1, 3), (0, 1), (0, 2), (2, 3), (1, 1), (0, 0), (1, 2), (3, 3), (2, 1), (1, 0), (2, 2), (3, 1), (2, 0), (3, 2), (3, 0)]
        for j, k in order:
            self.mail.send(lambda j=j, k=k: remote(self.at(others[k], j), self.rc.at[j, k], self.c_s.at[j, k], self.c_r.at[j, k], (near, m)))
            self.load(j, k).start()

    def from_core(self, j, k):
        second, m = self.mail.pos[5], self.mail.pos[1]
        self.load(j, k).wait()
        self.mail.arrived(self.rc.at[j, k], self.c_r.at[j, k])
        add_to(self.held.at[j, k], self.rc.at[j, k])
        if k >= 2:
            self.mail.send(lambda: remote(self.held.at[j, k], self.rb.at[j, k - 2], self.b_s.at[j, k - 2], self.b_r.at[j, k - 2], (second, m)))

    def to_first(self, j):
        first, m = self.mail.pos[4], self.mail.pos[1]
        self.mail.arrived(self.rb.at[j, 1], self.b_r.at[j, 1])
        add_to(self.held.at[j, 1], self.rb.at[j, 1])
        self.mail.send(lambda: remote(self.held.at[j, 1], self.ra.at[j], self.a_s.at[j], self.a_r.at[j], (first, m)))

    def result(self):
        return pltpu.make_async_copy(self.held.at[3, 0], self.out, self.o.at[0])

    def ring(self, j):
        r, m = self.mail.pos[:2]
        self.mail.arrived(self.ra.at[j], self.a_r.at[j])
        add_to(self.held.at[j, 0], self.ra.at[j])
        self.mail.arrived(self.rb.at[j, 0], self.b_r.at[j, 0])
        add_to(self.held.at[j, 0], self.rb.at[j, 0])
        if j > 0:
            self.mail.arrived(self.rz.at[j - 1], self.z_r.at[j - 1])
            add_to(self.held.at[j, 0], self.rz.at[j - 1])
        if j < 3:
            self.mail.send(lambda: remote(self.held.at[j, 0], self.rz.at[j], self.z_s.at[j], self.z_r.at[j], (r, lax.rem(m + 1, 4))))
        else:
            self.result().start()

    def finish(self):
        self.result().wait()


def reduce_order(reduce):
    core, first, ring = reduce.from_core, reduce.to_first, reduce.ring
    groups = [
        [(core, 0, 3), (core, 1, 3), (core, 0, 1)],
        [(first, 0), (core, 0, 2), (core, 2, 3), (core, 1, 1), (core, 0, 0)],
        [(first, 1), (core, 1, 2), (core, 3, 3), (core, 2, 1), (core, 1, 0)],
        [(ring, 0)],
        [(first, 2), (core, 2, 2), (core, 3, 1), (core, 2, 0)],
        [(ring, 1)],
        [(first, 3), (core, 3, 2), (core, 3, 0)],
        [(ring, 2)],
        [(ring, 3)],
    ]

    def run(group):
        for step in group:
            step[0](*step[1:])

    return [functools.partial(run, group) for group in groups]


class GainSums:
    def __init__(self, mail, own, out, rg, gs, gz, sems):
        self.mail, self.own, self.out, self.rg, self.gs, self.gz = mail, own, out, rg, gs, gz
        self.g_s, self.g_r, self.gz_s, self.gz_r = sems

    def hop(self, n):
        r, m, core, near, first, second, both, others = self.mail.pos
        x_near = first + core * (second - first)
        y_near = second + core * (first - second)
        if n > 0:
            self.mail.arrived(self.rg.at[n - 1], self.g_r.at[n - 1])
            before = self.own[...] if n == 1 else self.gs[n - 2]
            self.gs[n - 1] = before + self.rg[n - 1]
        if n < 3:
            src = lambda: self.own if n == 0 else self.gs.at[n - 1]
            to = (near, x_near, y_near)[n]
            self.mail.send(lambda: remote(src(), self.rg.at[n], self.g_s.at[n], self.g_r.at[n], (to, m)))
            return
        self.gz[m] = self.gs[2]
        for hop in (1, 2, 3):
            self.mail.send(lambda hop=hop: remote(self.gs.at[2], self.gz.at[m], self.gz_s.at[hop - 1], self.gz_r.at[m], (r, lax.rem(m + hop, 4))))

    def finish(self):
        m = self.mail.pos[1]
        for mem in range(4):
            pl.when(m != mem)(lambda mem=mem: self.mail.arrived(self.gz.at[mem], self.gz_r.at[mem]))
        self.out[...] = (self.gz[0] + self.gz[1]) + (self.gz[2] + self.gz[3])


ANY = pl.BlockSpec(memory_space=pl.ANY)


def shaped(shape, kind=jnp.bfloat16):
    return jax.ShapeDtypeStruct(shape, kind)


def reduce_encoder_kernel(
    enc_in, x_in, pre_in, dq_in, dkv_in, w_in, grad_h_in, gains, gain_in,
    enc_out, q_out, gain_out, gq_ref, own_ref, x_ref, pre_ref, dq_ref, dkv_ref, w_ref, grad_h_ref, in_sems, *rest,
):
    mail = Mail(position())
    held = [
        pltpu.make_async_copy(src, dst, in_sems.at[n])
        for n, (src, dst) in enumerate((
            (dkv_in, dkv_ref), (w_in.at[pl.ds(0, 3 * D)], w_ref), (dq_in, dq_ref), (x_in, x_ref), (grad_h_in, grad_h_ref),
            (pre_in, pre_ref),
        ))
    ]
    reduce = Reduce(mail, enc_in, enc_out, rest[:5], rest[5:15])
    tokens = TokensOut(mail, ((gq_ref, q_out),), rest[15:18])
    sums = GainSums(mail, own_ref, gain_out, *rest[18:21], rest[21:])
    greet(mail.pos)
    reduce.start()
    for copy in held:
        copy.start()
    steps = reduce_order(reduce)
    steps[0]()
    steps[1]()
    for copy in held:
        copy.wait()
    t = x_ref.shape[0]
    back = dot_nn(dkv_ref[...], w_ref[D : 3 * D, :])
    both = back[:t] + dot_nn(dq_ref[...], w_ref[:D, :])
    grad_x, dgain = norm_back(x_ref[...].astype(jnp.float32), gains[0:1, :], both)
    gq_ref[...] = (grad_h_ref[...] + grad_x).astype(jnp.bfloat16)
    tokens.start(0)
    unused, more = norm_back(pre_ref[...].astype(jnp.float32), gains[0:1, :], back[t:])
    own_ref[...] = gain_in[...]
    own_ref[0:1, :] = dgain + more
    sums.hop(0)
    steps[2]()
    sums.hop(1)
    steps[3]()
    steps[4]()
    sums.hop(2)
    steps[5]()
    steps[6]()
    sums.hop(3)
    steps[7]()
    steps[8]()
    reduce.finish()
    tokens.finish()
    sums.finish()
    mail.finish()


def reduce_encoder(enc_g, x, pre, dq, dkv, enc_w, grad_h, gains, gain_terms):
    vmem = pl.BlockSpec(memory_space=pltpu.VMEM)
    size = enc_g.shape[0] // 32
    t = x.shape[0]
    small = lambda n: pltpu.VMEM((n, 8, D), jnp.float32)
    return pl.pallas_call(
        reduce_encoder_kernel,
        grid=(1,),
        in_specs=[ANY] * 7 + [whole_spec(gains.shape), whole_spec((8, D))],
        out_specs=[ANY, ANY, whole_spec((8, D))],
        out_shape=[shaped((size, D)), shaped((2, t // 2, D)), shaped((8, D), jnp.float32)],
        scratch_shapes=[pltpu.VMEM(x.shape, jnp.bfloat16), pltpu.VMEM((8, D), jnp.float32)]
        + [pltpu.VMEM(v.shape, v.dtype) for v in (x, pre, dq, dkv)]
        + [pltpu.VMEM((3 * D, D), jnp.bfloat16), pltpu.VMEM(grad_h.shape, grad_h.dtype), dma(6)]
        + reduce_buffers(size) + reduce_sems() + token_sems(1) + [small(3), small(3), small(4)]
        + [dma(3), dma(3), dma(3), dma(4)],
        compiler_params=pltpu.CompilerParams(collective_id=3, has_side_effects=True, vmem_limit_bytes=52 * 1024 * 1024),
        name="reduce_encoder",
    )(enc_g, x, pre, dq, dkv, enc_w, grad_h, gains, gain_terms)


def fetch_kernel(ids, table, out, sems):
    n = out.shape[0]
    copies = [pltpu.make_async_copy(table.at[ids[i]], out.at[i], sems.at[i]) for i in range(n)]
    for copy in copies:
        copy.start()
    for copy in copies:
        copy.wait()


def fetch(ids, table):
    n = ids.shape[0]
    return pl.pallas_call(
        fetch_kernel,
        grid_spec=pltpu.PrefetchScalarGridSpec(
            num_scalar_prefetch=1, grid=(1,), in_specs=[ANY],
            out_specs=pl.BlockSpec((n,) + table.shape[1:], lambda i, ids: (0, 0, 0)),
            scratch_shapes=[dma(n)],
        ),
        out_shape=shaped((n,) + table.shape[1:], table.dtype),
        name="fetch",
    )(ids, table)


PAIRS = H // 2
CHUNKS = FF // CHUNK


def once(shape):
    return pl.BlockSpec(shape, lambda i: (0,) * len(shape), pipeline_mode=pl.Buffered(1))


def column(refs, first, i):
    return [ref.at[:, pl.ds(pl.multiple_of(first + i * 128, 128), 128)] for ref in refs]


def encode_kernel(
    enc_in, q_in, ent_in, a_in, dec_ref, g_ref, qaug_ref, kaug_ref, gains,
    nq_ref, q_ref, o_ref, lse_ref, h1_ref, nf1_ref, h2_ref, ne_ref, na_ref,
    kvo_out, kvt_out, enc_out, dec_out, x_out, pre_out, a_out, g_out,
    x_ref, a_ref, pre_ref, dect_ref, w_ref, kvo_ref, kvt_ref, s_ref, ff_ref, g_in, kv_sems, w_sems, *sems,
):
    i = pl.program_id(0)
    t = x_ref.shape[0]
    extra = pre_ref.shape[0] * pre_ref.shape[1]
    mail = Mail(position())
    encoder = Gather(mail, (enc_in,), (enc_out,), sems[:9])
    decoder = Gather(mail, (dect_ref,), (dec_out,), sems[9:18])
    tokens = TokensIn(mail, ((q_in, x_ref), (a_in, a_ref), (g_in, g_out)), sems[18:21])
    entries = EntriesIn(mail, ent_in, pre_ref, sems[21:])
    near, m = mail.pos[3], mail.pos[1]
    attention_rows, rest_rows = pl.ds(0, 3 * D), pl.ds(3 * D, w_ref.shape[0] - 3 * D)
    load = lambda rows, n: pltpu.make_async_copy(enc_out.at[rows], w_ref.at[rows], w_sems.at[n])
    kept = [
        lambda: pltpu.make_async_copy(kvo_ref, kvo_out, kv_sems.at[2]),
        lambda: pltpu.make_async_copy(kvt_ref, kvt_out, kv_sems.at[3]),
        lambda: pltpu.make_async_copy(x_ref, x_out, kv_sems.at[4]),
        lambda: pltpu.make_async_copy(pre_ref, pre_out, kv_sems.at[5]),
        lambda: pltpu.make_async_copy(a_ref, a_out, kv_sems.at[6]),
    ]

    @pl.when(i == 0)
    def _():
        greet(mail.pos)
        encoder.ring(0)
        encoder.spread(0)
        entries.start()
        dect_ref[...] = dec_ref[...].T
        encoder.ring(1)
        encoder.spread(1)
        encoder.from_first(0)
        encoder.ring(2)
        tokens.start(0)
        encoder.spread(2)
        encoder.from_first(1)
        encoder.from_second(0)
        encoder.ring(3)
        decoder.ring(0)
        encoder.spread(3)
        encoder.from_first(2)
        encoder.from_second(1)
        decoder.spread(0)
        encoder.from_first(3)
        encoder.from_second(2)
        encoder.from_second(3)
        encoder.finish()
        load(attention_rows, 0).start()
        load(rest_rows, 1).start()
        tokens.finish(0)
        entries.finish()
        nq_ref[:t, :] = rms_norm(x_ref[...].astype(jnp.float32), gains[0:1, :]).astype(jnp.bfloat16)
        pre = pre_ref[...].reshape(extra, D).astype(jnp.float32)
        nq_ref[t:, :] = rms_norm(pre, gains[0:1, :]).astype(jnp.bfloat16)
        decoder.ring(1)
        decoder.spread(1)
        load(attention_rows, 0).wait()
        for b in (1, 2):
            kvo_ref[:, (b - 1) * D : b * D] = dot_nt(nq_ref[...], w_ref[b * D : (b + 1) * D, :]).astype(jnp.bfloat16)
        mail.send(lambda: remote(kvo_ref, kvt_ref, kv_sems.at[0], kv_sems.at[1], (near, m)))
        q_ref[...] = dot_nt(nq_ref[:t, :], w_ref[:D, :]).astype(jnp.bfloat16)
        g_in[...] = g_ref[...].astype(jnp.bfloat16)
        for n in (0, 2, 3):
            kept[n]().start()

    @pl.when(i == 1)
    def _():
        mail.arrived(kvt_ref, kv_sems.at[1])
        kept[1]().start()
        load(rest_rows, 1).wait()

    @pl.when(i == 2)
    def _():
        decoder.ring(2)
        decoder.from_first(0)

    @pl.when(i == 4)
    def _():
        decoder.spread(2)

    @pl.when(i == 6)
    def _():
        decoder.from_first(1)

    @pl.when(i == 8)
    def _():
        decoder.ring(3)
        decoder.spread(3)
        tokens.start(1)
        tokens.start(2)
        decoder.from_second(0)

    @pl.when((i >= 1) & (i <= PAIRS))
    def _():
        pair = jnp.maximum(i - 1, 0)
        own_k, oth_k = column((kvo_ref, kvt_ref), 0, pair)
        own_v, oth_v = column((kvo_ref, kvt_ref), D, pair)
        q, o, lse = column((q_ref, o_ref, lse_ref), 0, pair)
        attend_pair(
            False, t, extra, chunk_sets(False, t, extra)[0], q, qaug_ref, own_k, own_v, oth_k, oth_v, kaug_ref, o, lse, s_ref
        )

    @pl.when(i == PAIRS + 1)
    def _():
        h1_ref[...] = x_ref[...].astype(jnp.float32) + dot_nn(o_ref[...], w_ref[3 * D : 4 * D, :])
        nf1_ref[...] = rms_norm(h1_ref[...], gains[1:2, :]).astype(jnp.bfloat16)
        ff_ref[...] = h1_ref[...]

    @pl.when(i > PAIRS)
    def _():
        chunk = jnp.maximum(i - PAIRS - 1, 0)
        w1 = w_ref[pl.ds(pl.multiple_of(4 * D + chunk * CHUNK, CHUNK), CHUNK), :]
        w2 = w_ref[pl.ds(pl.multiple_of(4 * D + FF + chunk * CHUNK, CHUNK), CHUNK), :]
        act = gelu_pair(dot_nt(nf1_ref[...], w1))[0].astype(jnp.bfloat16)
        ff_ref[...] += dot_nn(act, w2)

    @pl.when(i == PAIRS + CHUNKS)
    def _():
        h2_ref[...] = ff_ref[...]
        ne_ref[...] = rms_norm(ff_ref[...], gains[5:6, :]).astype(jnp.bfloat16)
        decoder.from_first(2)
        decoder.from_second(1)
        tokens.finish(1)
        kept[4]().start()
        na_ref[...] = rms_norm(a_ref[...].astype(jnp.float32), gains[2:3, :]).astype(jnp.bfloat16)
        decoder.from_first(3)
        decoder.from_second(2)
        decoder.from_second(3)
        decoder.finish()
        tokens.finish(2)
        for copy in kept:
            copy().wait()
        mail.finish()


def encode(enc_t, q, entries, a, dec_params, g, qaug, kaug, gains):
    t = 2 * q.shape[1]
    extra = 4 * entries.shape[2]
    nk = t + extra
    n_e, n_d = 32 * enc_t.shape[0], 32 * dec_params.shape[1]
    tok = whole_spec((t, D))
    dims = lambda kind, n=t, width=D: jax.ShapeDtypeStruct((n, width), kind)
    bf, f32 = jnp.bfloat16, jnp.float32
    return pl.pallas_call(
        encode_kernel,
        grid=(1 + PAIRS + CHUNKS,),
        in_specs=[ANY] * 4 + [whole_spec(v.shape) for v in (dec_params, g, qaug, kaug, gains)],
        out_specs=[whole_spec((nk, D))] + [tok] * 8 + [ANY] * 8,
        out_shape=[
            dims(bf, nk), dims(bf), dims(bf), dims(f32), dims(f32), dims(bf), dims(f32), dims(bf), dims(bf),
            dims(bf, nk, 2 * D), dims(bf, nk, 2 * D), dims(bf, n_e), dims(bf, n_d), dims(bf),
            shaped((4,) + entries.shape[2:]), dims(bf), dims(bf),
        ],
        scratch_shapes=[
            pltpu.VMEM((t, D), bf), pltpu.VMEM((t, D), bf), pltpu.VMEM((4,) + entries.shape[2:], bf), pltpu.VMEM((n_d // 32, D), bf),
            pltpu.VMEM((n_e, D), bf), pltpu.VMEM((nk, 2 * D), bf), pltpu.VMEM((nk, 2 * D), bf),
            pltpu.VMEM((t // QB, 2 * nk, 2 * QB), f32), pltpu.VMEM((t, D), f32), pltpu.VMEM(g.shape, bf), dma(7), dma(2),
        ] + gather_sems(1) + gather_sems(1) + token_sems(3) + [dma(2, 2), dma(4), dma()],
        compiler_params=pltpu.CompilerParams(collective_id=1, has_side_effects=True, vmem_limit_bytes=51 * 1024 * 1024),
        name="encode",
    )(enc_t, q, entries, a, dec_params, g, qaug, kaug, gains)


def encode_back_kernel(
    grad_ref, nf1_ref, h1_in, nq_in, gains, enc_w, w1_ref, w2_ref, o_in,
    q_ref, qaug_ref, own_k, own_v, oth_k, oth_v, kaug_ref, lse_ref, dec_g, y_in, a_in,
    whole, grad_h_ref, dgain_ref, dq_ref, dkv_ref, dec_out, y_out, a_out,
    total_ref, grad_b, mix_ref, slots, dwo_ref, sems, sem_o, dk_acc, dv_acc, dko_ref, dvo_ref, dkt_ref, dvt_ref,
    dqp_ref, own_d, sent, got, x_s, x_r, sem_w, h1_ref, nq_ref, wo_ref, o_ref, in_sems, *rest,
):
    i = pl.program_id(0)
    t = q_ref.shape[0]
    nk = own_k.shape[0]
    store = ChunkStore(slots, whole, (4 * D, 4 * D + FF), sems)
    store_o = lambda: pltpu.make_async_copy(dwo_ref, whole.at[pl.ds(3 * D, D)], sem_o)
    mail = Mail(position())
    near, m = mail.pos[3], mail.pos[1]
    reduce = Reduce(mail, dec_g, dec_out, rest[:5], rest[5:15])
    tokens = TokensOut(mail, ((y_in, y_out), (a_in, a_out)), rest[15:])
    steps = reduce_order(reduce)
    places = {1: (0,), 3: (1,), 5: (2,), 7: (3,), 9: (4,), 11: (5,)}

    loads = [
        lambda: pltpu.make_async_copy(h1_in, h1_ref, in_sems.at[0]),
        lambda: pltpu.make_async_copy(enc_w.at[pl.ds(3 * D, D)], wo_ref, in_sems.at[1]),
        lambda: pltpu.make_async_copy(o_in, o_ref, in_sems.at[2]),
        lambda: pltpu.make_async_copy(nq_in, nq_ref, in_sems.at[3]),
    ]

    @pl.when(i == 0)
    def _():
        greet(mail.pos)
        reduce.start()
        for load in loads:
            load().start()
        tokens.start(0)
        tokens.start(1)
        grad_b[...] = grad_ref[...].astype(jnp.bfloat16)

    for at, which in places.items():

        @pl.when(i == at)
        def _(which=which):
            for n in which:
                steps[n]()

    @pl.when(i < CHUNKS)
    def _():
        pl.when(i >= 2)(lambda: store.wait(i - 2))
        feed_back_chunk(
            nf1_ref[...], grad_b[...], w1_ref[...], w2_ref[...], slots.at[lax.rem(i, 2)], total_ref, i == 0
        )
        store.start(i)

    @pl.when(i == CHUNKS - 1)
    def _():
        for load in loads:
            load().wait()
        grad_x, dgain = norm_back(h1_ref[...], gains[1:2, :], total_ref[...])
        dgain_ref[...] = jnp.broadcast_to(dgain, dgain_ref.shape)
        grad_h = grad_ref[...] + grad_x
        grad_h_ref[...] = grad_h
        top = grad_h.astype(jnp.bfloat16)
        dwo_ref[...] = dot_tn(o_ref[...], top).astype(jnp.bfloat16)
        store_o().start()
        mix_ref[...] = dot_nt(top, wo_ref[...]).astype(jnp.bfloat16)
        store.wait(i - 1)
        store.wait(i)

    def swap(n):
        slot = lax.rem(n, 2)
        return remote(sent.at[slot], got.at[n], x_s.at[slot], x_r.at[n], (near, m))

    @pl.when(i >= CHUNKS)
    def _():
        n = jnp.maximum(i - CHUNKS, 0)
        o, mix, dq = column((o_ref, mix_ref, dq_ref), 0, n)
        back_pair(
            False, t, nk - t, chunk_sets(False, t, nk - t)[0], q_ref, qaug_ref, own_k, own_v, oth_k, oth_v, kaug_ref,
            o, lse_ref, mix, dqp_ref, dko_ref, dvo_ref, dkt_ref, dvt_ref, dk_acc, dv_acc,
        )
        dq[...] = dqp_ref[...]
        own_d[n, 0] = dko_ref[...].astype(jnp.bfloat16)
        own_d[n, 1] = dvo_ref[...].astype(jnp.bfloat16)
        pl.when(n >= 2)(lambda: swap(n - 2).wait_send())
        sent[lax.rem(n, 2), 0] = dkt_ref[...]
        sent[lax.rem(n, 2), 1] = dvt_ref[...]
        swap(n).start()

    @pl.when(i == PAIRS + CHUNKS - 1)
    def _():
        store_o().wait()
        for n in range(PAIRS):
            swap(n).wait_recv()
            for b in (0, 1):
                at = b * D + n * 128
                dkv_ref[:, at : at + 128] = own_d[n, b] + got[n, b]
        dwo_ref[...] = dot_tn(dq_ref[...], nq_ref[:t, :]).astype(jnp.bfloat16)
        last = [pltpu.make_async_copy(dwo_ref, whole.at[pl.ds(0, D)], sem_w.at[0])]
        for b in (1, 2):
            slots[b - 1, :D, :] = dot_tn(dkv_ref[:, (b - 1) * D : b * D], nq_ref[...]).astype(jnp.bfloat16)
            last.append(pltpu.make_async_copy(slots.at[b - 1, pl.ds(0, D)], whole.at[pl.ds(b * D, D)], sem_w.at[b]))
        for copy in last:
            copy.start()
        for n in (6, 7, 8):
            steps[n]()
        reduce.finish()
        tokens.finish()
        for copy in last:
            copy.wait()
        for n in (PAIRS - 2, PAIRS - 1):
            swap(n).wait_send()
        mail.finish()


def encode_back(grad, nf1, h1, nq, gains, enc_w, o, q, qaug, own_kv, oth_kv, kaug, lse, dec_g, y, a):
    t = q.shape[0]
    nk = own_kv.shape[0]
    size = dec_g.shape[0] // 32
    pair = lambda i: jnp.maximum(i - CHUNKS, 0)
    chunk = lambda i: jnp.minimum(i, CHUNKS - 1)
    col = lambda first: pl.BlockSpec((nk, 128), lambda i: (0, first + pair(i)))
    cols = pl.BlockSpec((t, 128), lambda i: (0, pair(i)))
    tok = whole_spec((t, D))
    bf, f32 = jnp.bfloat16, jnp.float32
    dims = lambda kind, n=t, width=D: jax.ShapeDtypeStruct((n, width), kind)
    return pl.pallas_call(
        encode_back_kernel,
        grid=(PAIRS + CHUNKS,),
        in_specs=[
            once((t, D)), once((t, D)), ANY, ANY, whole_spec(gains.shape), ANY,
            pl.BlockSpec((CHUNK, D), lambda i: (4 * D // CHUNK + chunk(i), 0)),
            pl.BlockSpec((CHUNK, D), lambda i: (4 * D // CHUNK + CHUNKS + chunk(i), 0)),
            ANY, cols, whole_spec((t, 128)), col(0), col(PAIRS), col(0), col(PAIRS), whole_spec((2 * nk, 128)), cols,
            ANY, ANY, ANY,
        ],
        out_specs=[ANY, tok, whole_spec((8, D)), tok, whole_spec((nk, 2 * D)), ANY, ANY, ANY],
        out_shape=[
            dims(bf, enc_w.shape[0]), dims(f32), dims(f32, 8), dims(bf), dims(bf, nk, 2 * D),
            shaped((size, D)), shaped((2, t // 2, D)), shaped((2, t // 2, D)),
        ],
        scratch_shapes=[
            pltpu.VMEM((t, D), f32), pltpu.VMEM((t, D), bf), pltpu.VMEM((t, D), bf),
            pltpu.VMEM((2, 2 * CHUNK, D), bf), pltpu.VMEM((D, D), bf), dma(2, 2), dma(),
            pltpu.VMEM((2 * nk, 128), f32), pltpu.VMEM((2 * nk, 128), f32),
            pltpu.VMEM((nk, 128), f32), pltpu.VMEM((nk, 128), f32), pltpu.VMEM((nk, 128), bf), pltpu.VMEM((nk, 128), bf),
            pltpu.VMEM((t, 128), bf), pltpu.VMEM((PAIRS, 2, nk, 128), bf),
            pltpu.VMEM((2, 2, nk, 128), bf), pltpu.VMEM((PAIRS, 2, nk, 128), bf), dma(2), dma(PAIRS),
            dma(3), pltpu.VMEM((t, D), f32), pltpu.VMEM((nk, D), bf), pltpu.VMEM((D, D), bf), pltpu.VMEM((t, D), bf), dma(4),
        ] + reduce_buffers(size) + reduce_sems() + token_sems(2),
        compiler_params=pltpu.CompilerParams(collective_id=2, has_side_effects=True, vmem_limit_bytes=63 * 1024 * 1024),
        name="encode_back",
    )(grad, nf1, h1, nq, gains, enc_w, enc_w, enc_w, o, q, qaug, own_kv, own_kv, oth_kv, oth_kv, kaug, lse, dec_g, y, a)


def project(left, weight_t):
    return jnp.einsum("nd,ed->ne", left, weight_t, preferred_element_type=jnp.float32)


def project_back(left, weight_t):
    return jnp.einsum("ne,ed->nd", left, weight_t, preferred_element_type=jnp.float32)


def outer_sum(wide, narrow):
    return jnp.einsum("ne,nd->ed", wide, narrow, preferred_element_type=jnp.float32).astype(jnp.bfloat16)


def output_back(grad, mixed_b, w_out):
    grad_b = grad.astype(jnp.bfloat16)
    return (outer_sum(mixed_b, grad_b), project(grad_b, w_out).astype(jnp.bfloat16))


def feed_back(grad, normed_b, pre_act, act_b, w_in, w_out):
    grad_b = grad.astype(jnp.bfloat16)
    grad_wout = outer_sum(act_b, grad_b)
    grad_act = project(grad_b, w_out)
    unused, pull = jax.vjp(jax.nn.gelu, pre_act)
    grad_pre = pull(grad_act)[0].astype(jnp.bfloat16)
    return (outer_sum(grad_pre, normed_b), grad_wout, project_back(grad_pre, w_in))


def partner(values):
    n_rows = lax.axis_size("rows")
    return lax.ppermute(values, "rows", [(i, i ^ 1) for i in range(n_rows)])


def my_row(values):
    core = lax.axis_index("rows") % 2
    mem = lax.axis_index("mem")
    chosen = jnp.where(mem // 2 == core, values, partner(values))
    return lax.dynamic_index_in_dim(chosen, mem % 2, 0, keepdims=False)


def quarters_of(core):
    return (jnp.where(core == 0, 0, 1), jnp.where(core == 0, 3, 2))


def own_quarters(row, core, quarter):
    return jnp.concatenate(
        [lax.dynamic_slice_in_dim(row, place * quarter, quarter, 0) for place in quarters_of(core)], 0
    )


def to_rows(values):
    quarter = values.shape[1]
    row = my_row(lax.all_gather(values, "mem", axis=1, tiled=True))
    return own_quarters(row, lax.axis_index("rows") % 2, quarter)


def from_rows(values):
    quarter = values.shape[0] // 2
    core = lax.axis_index("rows") % 2
    mem = lax.axis_index("mem")
    gathered = lax.all_gather(values, "mem", axis=0)
    other = partner(gathered)
    holder = jnp.where((mem == 0) | (mem == 3), 0, 1)
    chosen = jnp.where(holder == core, gathered, other)
    return lax.dynamic_slice(
        chosen, (2 * core, jnp.where(mem < 2, 0, quarter), 0), (2, quarter, values.shape[1])
    )


def gather_weights(params):
    return lax.all_gather(params.T, ("rows", "mem"), axis=0, tiled=True)


def reduce_weights(grads):
    return lax.psum_scatter(grads, ("rows", "mem"), scatter_dimension=0, tiled=True)


def on_device_general(
    questions,
    answers,
    q_segments,
    a_segments,
    entry_ids,
    entry_alive_flags,
    memory_table,
    enc_params,
    dec_params,
    norm_gains,
    cotangent,
):
    quarter = questions.shape[1]
    core = lax.axis_index("rows") % 2
    per_row, slots = entry_alive_flags.shape[1], entry_alive_flags.shape[2]
    half = per_row // 2
    enc_w = gather_weights(enc_params)
    dec_w = gather_weights(dec_params)
    all_ids = lax.all_gather(entry_ids, "mem", axis=2, tiled=True)
    rows_here = questions.shape[0]
    numbers = my_row(
        jnp.concatenate(
            [
                q_segments,
                a_segments,
                entry_alive_flags.reshape(rows_here, -1),
                all_ids.reshape(rows_here, -1),
            ],
            1,
        )
    )
    row_len = q_segments.shape[1]
    q_row = numbers[:row_len]
    a_row = numbers[row_len : 2 * row_len]
    alive = numbers[2 * row_len : 2 * row_len + per_row * slots]
    ids = numbers[2 * row_len + per_row * slots :]
    x_question = to_rows(questions).astype(jnp.float32)
    x_answer = to_rows(answers).astype(jnp.float32)
    grad_top = to_rows(cotangent.astype(jnp.bfloat16)).astype(jnp.float32)

    own_ids = lax.dynamic_slice_in_dim(ids, core * half * slots, half * slots, 0)
    entry_vals = memory_table[own_ids].reshape(half * slots * 2, D).astype(jnp.float32)
    n_prefix = entry_vals.shape[0]
    extra = -(-n_prefix // 128) * 128
    place = jnp.arange(extra, dtype=jnp.int32)

    def prefix_segments(which):
        question = which * half + place // (2 * slots)
        live = lax.dynamic_slice_in_dim(alive, which * half * slots, half * slots, 0)
        live = jnp.pad(jnp.repeat(live, 2), (0, extra - n_prefix))
        return jnp.where(live == 1, question, -1)

    tokens = 2 * quarter
    own_q = own_quarters(q_row, core, quarter)
    other_q = own_quarters(q_row, 1 - core, quarter)
    own_a = own_quarters(a_row, core, quarter)
    other_a = own_quarters(a_row, 1 - core, quarter)
    q_aug, a_aug = seg_aug_q(own_q), seg_aug_q(own_a)
    enc_aug = seg_aug_k(
        jnp.concatenate([own_q, prefix_segments(core), other_q, prefix_segments(1 - core)])
    )
    self_aug = seg_aug_k(jnp.concatenate([own_a, other_a]))
    cross_aug = seg_aug_k(jnp.concatenate([own_q, other_q]))

    enc_in = jnp.concatenate([x_question, jnp.pad(entry_vals, ((0, extra - n_prefix), (0, 0)))], 0)
    normed_q = rms_norm(enc_in, norm_gains[0]).astype(jnp.bfloat16)
    query_enc = project(normed_q[:tokens], enc_w[:D]).astype(jnp.bfloat16)
    enc_kv = project(normed_q, enc_w[D : 3 * D]).astype(jnp.bfloat16)
    enc_kv_other = partner(enc_kv)

    normed_a = rms_norm(x_answer, norm_gains[2]).astype(jnp.bfloat16)
    qkv_self = project(normed_a, dec_w[: 3 * D]).astype(jnp.bfloat16)
    query_self, self_kv = qkv_self[:, :D], qkv_self[:, D:]
    self_kv_other = partner(self_kv)

    mixed_enc, logsum_enc = attend(False, core, query_enc, q_aug, enc_kv, enc_kv_other, enc_aug)
    hidden_one = x_question + project_back(mixed_enc, enc_w[3 * D : 4 * D])
    normed_f1 = rms_norm(hidden_one, norm_gains[1]).astype(jnp.bfloat16)
    pre_enc = project(normed_f1, enc_w[4 * D : 4 * D + FF])
    act_enc = jax.nn.gelu(pre_enc).astype(jnp.bfloat16)
    hidden_two = hidden_one + project_back(act_enc, enc_w[4 * D + FF :])
    encoded = rms_norm(hidden_two, norm_gains[5]).astype(jnp.bfloat16)
    cross_kv = project(encoded, dec_w[5 * D : 7 * D]).astype(jnp.bfloat16)
    cross_kv_other = partner(cross_kv)

    mixed_self, logsum_self = attend(True, core, query_self, a_aug, self_kv, self_kv_other, self_aug)
    dec_one = x_answer + project_back(mixed_self, dec_w[3 * D : 4 * D])
    normed_c = rms_norm(dec_one, norm_gains[3]).astype(jnp.bfloat16)
    query_cross = project(normed_c, dec_w[4 * D : 5 * D]).astype(jnp.bfloat16)
    mixed_cross, logsum_cross = attend(
        False, core, query_cross, a_aug, cross_kv, cross_kv_other, cross_aug
    )
    dec_two = dec_one + project_back(mixed_cross, dec_w[7 * D : 8 * D])
    normed_f2 = rms_norm(dec_two, norm_gains[4]).astype(jnp.bfloat16)
    pre_dec = project(normed_f2, dec_w[8 * D : 8 * D + FF])
    act_dec = jax.nn.gelu(pre_dec).astype(jnp.bfloat16)
    dec_three = dec_two + project_back(act_dec, dec_w[8 * D + FF :])
    decoded = from_rows(dec_three.astype(jnp.bfloat16))

    grad_w1d, grad_w2d, grad_nf2 = feed_back(
        grad_top, normed_f2, pre_dec, act_dec, dec_w[8 * D : 8 * D + FF], dec_w[8 * D + FF :]
    )
    grad_x, grad_gain4 = norm_back(dec_two, norm_gains[4], grad_nf2)
    grad_two = grad_top + grad_x
    grad_woc, grad_mixc = output_back(grad_two, mixed_cross, dec_w[7 * D : 8 * D])
    grad_qc, dk_own, dv_own, dk_other, dv_other = attend_back(
        False, core, query_cross, a_aug, cross_kv, cross_kv_other, cross_aug,
        mixed_cross, logsum_cross, grad_mixc,
    )
    more = partner(jnp.concatenate([dk_other, dv_other], 1)).astype(jnp.float32)
    grad_ckv = (jnp.concatenate([dk_own, dv_own], 1) + more).astype(jnp.bfloat16)
    grad_wqc = outer_sum(grad_qc, normed_c)
    grad_x, grad_gain3 = norm_back(
        dec_one, norm_gains[3], project_back(grad_qc, dec_w[4 * D : 5 * D])
    )
    grad_one = grad_two + grad_x
    grad_wckv = outer_sum(grad_ckv, encoded)
    grad_encoded, grad_gain5 = norm_back(
        hidden_two, norm_gains[5], project_back(grad_ckv, dec_w[5 * D : 7 * D])
    )
    grad_wos, grad_mixs = output_back(grad_one, mixed_self, dec_w[3 * D : 4 * D])
    grad_qs, dk_own, dv_own, dk_other, dv_other = attend_back(
        True, core, query_self, a_aug, self_kv, self_kv_other, self_aug,
        mixed_self, logsum_self, grad_mixs,
    )
    more = partner(jnp.concatenate([dk_other, dv_other], 1)).astype(jnp.float32)
    grad_skv = (jnp.concatenate([dk_own, dv_own], 1) + more).astype(jnp.bfloat16)
    grad_self = jnp.concatenate([grad_qs, grad_skv], 1)
    grad_wself = outer_sum(grad_self, normed_a)
    grad_x, grad_gain2 = norm_back(x_answer, norm_gains[2], project_back(grad_self, dec_w[: 3 * D]))
    grad_answers = from_rows((grad_one + grad_x).astype(jnp.bfloat16)).astype(jnp.float32)
    dec_full = jnp.concatenate(
        [grad_wself, grad_wos, grad_wqc, grad_wckv, grad_woc, grad_w1d, grad_w2d], 0
    )
    grad_decoder = reduce_weights(dec_full).astype(jnp.float32).T

    grad_w1e, grad_w2e, grad_nf1 = feed_back(
        grad_encoded, normed_f1, pre_enc, act_enc, enc_w[4 * D : 4 * D + FF], enc_w[4 * D + FF :]
    )
    grad_x, grad_gain1 = norm_back(hidden_one, norm_gains[1], grad_nf1)
    grad_hidden = grad_encoded + grad_x
    grad_woe, grad_mixe = output_back(grad_hidden, mixed_enc, enc_w[3 * D : 4 * D])
    grad_qe, dk_own, dv_own, dk_other, dv_other = attend_back(
        False, core, query_enc, q_aug, enc_kv, enc_kv_other, enc_aug,
        mixed_enc, logsum_enc, grad_mixe,
    )
    more = partner(jnp.concatenate([dk_other, dv_other], 1)).astype(jnp.float32)
    grad_ekv = (jnp.concatenate([dk_own, dv_own], 1) + more).astype(jnp.bfloat16)
    grad_wqe = outer_sum(grad_qe, normed_q[:tokens])
    grad_wkve = outer_sum(grad_ekv, normed_q)
    grad_in = project_back(grad_ekv, enc_w[D : 3 * D])
    grad_in = grad_in + jnp.pad(project_back(grad_qe, enc_w[:D]), ((0, extra), (0, 0)))
    grad_x, grad_gain0 = norm_back(enc_in, norm_gains[0], grad_in)
    grad_questions = from_rows((grad_hidden + grad_x[:tokens]).astype(jnp.bfloat16)).astype(jnp.float32)
    enc_full = jnp.concatenate([grad_wqe, grad_wkve, grad_woe, grad_w1e, grad_w2e], 0)
    gain_terms = jnp.concatenate(
        [grad_gain0, grad_gain1, grad_gain2, grad_gain3, grad_gain4, grad_gain5], 0
    )
    grad_gains = lax.psum(gain_terms, ("rows", "mem"))
    grad_encoder = reduce_weights(enc_full).astype(jnp.float32).T
    return (decoded, grad_questions, grad_answers, grad_encoder, grad_decoder, grad_gains)


def on_device_fast(
    questions,
    answers,
    q_segments,
    a_segments,
    entry_ids,
    entry_alive_flags,
    memory_table,
    enc_params,
    dec_params,
    norm_gains,
    cotangent,
):
    quarter = questions.shape[1]
    core = lax.axis_index("rows") % 2
    mem = lax.axis_index("mem")
    per_row, slots = entry_alive_flags.shape[1], entry_alive_flags.shape[2]
    half = per_row // 2
    rows_here, row_len = q_segments.shape
    n_mem = slots // entry_ids.shape[2]
    entries = fetch(entry_ids.reshape(-1), memory_table).reshape(rows_here, 2, -1, D)
    n_entry = entries.shape[2]
    piece = -(-n_entry // 32) * 32
    entries = jnp.pad(entries, ((0, 0), (0, 0), (0, piece - n_entry), (0, 0)))
    gains = norm_gains
    segs = jnp.concatenate([q_segments, a_segments, entry_alive_flags.reshape(rows_here, -1)], 1)
    numbers = my_row(segs)
    q_row, a_row, alive = numbers[:row_len], numbers[row_len : 2 * row_len], numbers[2 * row_len :]
    alive = alive.reshape(per_row, n_mem, -1)

    def prefix_segments(which):
        live = lax.dynamic_slice_in_dim(alive, which * half, half, 0)
        question = which * half + jnp.arange(half, dtype=jnp.int32)[:, None, None]
        found = jnp.where(live == 1, question, -1).transpose(1, 0, 2).reshape(n_mem, -1)
        found = jnp.repeat(found, 2, axis=1)
        return jnp.pad(found, ((0, 0), (0, piece - n_entry)), constant_values=-1).reshape(-1)

    own_q = own_quarters(q_row, core, quarter)
    other_q = own_quarters(q_row, 1 - core, quarter)
    own_a = own_quarters(a_row, core, quarter)
    other_a = own_quarters(a_row, 1 - core, quarter)
    q_aug, a_aug = seg_aug_q(own_q), seg_aug_q(own_a)
    enc_aug = seg_aug_k(
        jnp.concatenate([own_q, prefix_segments(core), other_q, prefix_segments(1 - core)])
    )
    self_aug = seg_aug_k(jnp.concatenate([own_a, other_a]))
    cross_aug = seg_aug_k(jnp.concatenate([own_q, other_q]))

    (
        normed_q, query_enc, mixed_enc, logsum_enc, hidden_one, normed_f1, hidden_two, encoded, normed_a,
        enc_kv, enc_kv_other, enc_w, dec_w, x_question, prefix, x_answer, grad_top,
    ) = encode(
        enc_params.T, questions, entries, answers, dec_params, cotangent, q_aug, enc_aug, gains
    )
    prefix = prefix.reshape(-1, D)
    qkv_self = project(normed_a, dec_w[: 3 * D]).astype(jnp.bfloat16)
    query_self, self_kv = qkv_self[:, :D], qkv_self[:, D:]
    self_kv_other = partner(self_kv)
    cross_kv = project(encoded, dec_w[5 * D : 7 * D]).astype(jnp.bfloat16)
    cross_kv_other = partner(cross_kv)

    mixed_self, logsum_self = attend(True, core, query_self, a_aug, self_kv, self_kv_other, self_aug)
    dec_one = x_answer.astype(jnp.float32) + project_back(mixed_self, dec_w[3 * D : 4 * D])
    normed_c = rms_norm(dec_one, norm_gains[3]).astype(jnp.bfloat16)
    query_cross = project(normed_c, dec_w[4 * D : 5 * D]).astype(jnp.bfloat16)
    mixed_cross, logsum_cross = attend(
        False, core, query_cross, a_aug, cross_kv, cross_kv_other, cross_aug
    )
    decoded, grad_two, grad_mixc, grad_gain4, dec_full = decode_top(
        dec_one, mixed_cross, gains, grad_top, dec_w
    )
    grad_qc, dk_own, dv_own, dk_other, dv_other = attend_back(
        False, core, query_cross, a_aug, cross_kv, cross_kv_other, cross_aug,
        mixed_cross, logsum_cross, grad_mixc,
    )
    cross_got = (partner(dk_other), partner(dv_other))
    grad_x, grad_gain3 = norm_back(dec_one, norm_gains[3], project_back(grad_qc, dec_w[4 * D : 5 * D]))
    grad_one = grad_two + grad_x
    grad_mixs = project(grad_one.astype(jnp.bfloat16), dec_w[3 * D : 4 * D]).astype(jnp.bfloat16)
    grad_qs, dk_self, dv_self, dk_other, dv_other = attend_back(
        True, core, query_self, a_aug, self_kv, self_kv_other, self_aug,
        mixed_self, logsum_self, grad_mixs,
    )
    self_got = (partner(dk_other), partner(dv_other))
    dec_full, grad_answers, grad_encoded, grad_gain2, grad_gain5 = decode_dense(
        grad_qs, dk_self, dv_self, *self_got, grad_qc, dk_own, dv_own, *cross_got, normed_a, normed_c, encoded,
        mixed_self, grad_one, x_answer, hidden_two, gains, dec_w, dec_full,
    )

    enc_full, grad_hidden, grad_gain1, grad_qe, grad_ekv, grad_decoder, decoded, grad_answers = encode_back(
        grad_encoded, normed_f1, hidden_one, normed_q, gains, enc_w, mixed_enc, query_enc, q_aug,
        enc_kv, enc_kv_other, enc_aug, logsum_enc, dec_full, decoded, grad_answers,
    )
    gain_terms = jnp.concatenate(
        [
            jnp.zeros_like(grad_gain3), grad_gain1[:1], grad_gain2[:1], grad_gain3, grad_gain4[:1], grad_gain5[:1],
            jnp.zeros((2, D), jnp.float32),
        ],
        0,
    )
    grad_encoder, grad_questions, grad_gains = reduce_encoder(
        enc_full, x_question, prefix, grad_qe, grad_ekv, enc_w, grad_hidden, gains, gain_terms
    )
    return (
        decoded,
        grad_questions.astype(jnp.float32),
        grad_answers.astype(jnp.float32),
        grad_encoder.astype(jnp.float32).T,
        grad_decoder.astype(jnp.float32).T,
        grad_gains[:6],
    )


def solution(mesh):
    fast = mesh.shape["rows"] == 8 and mesh.shape["mem"] == 4
    return jax.shard_map(
        on_device_fast if fast else on_device_general,
        mesh=mesh,
        in_specs=(
            P("rows", "mem", None),
            P("rows", "mem", None),
            P("rows", None),
            P("rows", None),
            P("rows", None, "mem"),
            P("rows", None, None),
            P(),
            P(None, ("rows", "mem")),
            P(None, ("rows", "mem")),
            P(),
            P("rows", "mem", None),
        ),
        out_specs=(
            P("rows", "mem", None),
            P("rows", "mem", None),
            P("rows", "mem", None),
            P(None, ("rows", "mem")),
            P(None, ("rows", "mem")),
            P(),
        ),
        check_vma=False,
    )
```
